32 devices in a mesh: ctx: 8 (over z, y), head: 4 (over x, core).
Axes of the slice: x: 2, y: 2, z: 4, core: 2. Of those that a mesh axis runs over, the one named last changes fastest.
Arguments:
- q_rows: bfloat16 [2048, 2048], P(('ctx', 'head')), may hold values from -6 to 6
- k_rows: bfloat16 [2048, 2048], P(('ctx', 'head')), may hold values from -6 to 6
- v_rows: bfloat16 [2048, 4096], P(('ctx', 'head')), may hold values from -6 to 6
- z_rows: bfloat16 [2048, 4096], P(('ctx', 'head')), may hold values from -6 to 6
- a_rows: bfloat16 [2048, 32], P(('ctx', 'head')), may hold values from -5 to 5
- b_rows: bfloat16 [2048, 32], P(('ctx', 'head')), may hold values from -11 to 5
- conv_q: float32 [4, 2048], P(None, 'head'), may hold values from -3 to 3
- conv_k: float32 [4, 2048], P(None, 'head'), may hold values from -3 to 3
- conv_v: float32 [4, 4096], P(None, 'head'), may hold values from -3 to 3
- a_log: float32 [32], P('head'), may hold values from -11 to -1
- dt_bias: float32 [32], P('head'), may hold values from -2 to 1
- norm_gain: float32 [128], replicated, may hold values from 0.5 to 1.5
Outputs:
- gated_out: bfloat16 [2048, 4096], P(('ctx', 'head'))
The draws below stay inside these ranges and needn't reach their ends.
All inputs are finite; a program needn't handle non-finite values.
Results may differ from the reference program's by a relative error of at most 0.0075.
Values may be sent and summed in bfloat16 or wider, within the bound.
No kernel may reach another device: no remote copies, remote signals or barrier semaphores. Data moves between devices by JAX's collectives and lax.ppermute only.
A program may use at most 128 MiB of HBM per device.

```python
import jax
import jax.numpy as jnp
from jax import lax

KH = 16
VH = 32
DK = 128
DV = 128
CONV = 4
SPAN = 64
TOKENS = 2048


def draw_b_rows(key, part):
    level_key, noise_key = jax.random.split(jax.random.fold_in(key, 7))
    levels = jax.random.uniform(level_key, (VH,), jnp.float32, -7.0, 1.0)
    noise = jnp.clip(jax.random.normal(noise_key, (TOKENS, VH), jnp.float32), -4.0, 4.0)
    return (levels[None, :] + noise).astype(jnp.bfloat16)


def block_scale(own_key, shape, cuts, smallest, top_value):
    loudness, own = 1.0, jax.random.fold_in(own_key, 6)
    for dim, parts in cuts:
        heights = jnp.exp(jax.random.uniform(jax.random.fold_in(own, dim), (parts,), jnp.float32, smallest / len(cuts), top_value / len(cuts)))
        loudness = loudness * jnp.repeat(heights, shape[dim] // parts).reshape([-1 if axis == dim else 1 for axis in range(len(shape))])
    return loudness


def gaussian(stream_key, dims, deviation, limit, cuts=(), kind=jnp.bfloat16):
    entries = jax.random.normal(stream_key, dims, jnp.float32) * deviation
    if len(cuts) > 0:
        entries = block_scale(stream_key, dims, cuts, -0.22, 0.18) * entries
    return jnp.clip(entries, min=-limit, max=limit).astype(kind)


def setup_inputs(seed: int = 0) -> dict:
    key_of = jax.random.split(jax.random.key(seed), 13)
    return {
        "q_rows": gaussian(key_of[0], (TOKENS, KH * DK), 1.0, 6.0, ((0, 32),)),
        "k_rows": gaussian(key_of[1], (TOKENS, KH * DK), 1.0, 6.0, ((0, 32),)),
        "v_rows": gaussian(key_of[2], (TOKENS, VH * DV), 1.0, 6.0, ((0, 32),)),
        "z_rows": gaussian(key_of[3], (TOKENS, VH * DV), 1.0, 6.0, ((0, 32),)),
        "a_rows": gaussian(key_of[4], (TOKENS, VH), 1.0, 5.0, ((0, 32),)),
        "b_rows": draw_b_rows(jax.random.fold_in(key_of[12], 71), 0),
        "conv_q": gaussian(key_of[6], (CONV, KH * DK), 0.6, 3.0, ((1, 4),), jnp.float32),
        "conv_k": gaussian(key_of[7], (CONV, KH * DK), 0.6, 3.0, ((1, 4),), jnp.float32),
        "conv_v": gaussian(key_of[8], (CONV, VH * DV), 0.6, 3.0, ((1, 4),), jnp.float32),
        "a_log": jnp.clip(-11.0 + 10.0 * jax.random.uniform(key_of[9], (VH,), jnp.float32) ** block_scale(key_of[9], (VH,), ((0, 4),), -0.2, 0.2), -11.0, -1.0),
        "dt_bias": jnp.clip(-2.0 + 3.0 * jax.random.uniform(key_of[10], (VH,), jnp.float32) ** block_scale(key_of[10], (VH,), ((0, 4),), -0.2, 0.2), -2.0, 1.0),
        "norm_gain": jnp.clip(1.0 + 0.1 * jax.random.normal(key_of[11], (DV,), jnp.float32), 0.5, 1.5),
    }


HIGHEST = lax.Precision.HIGHEST

def conv_silu(seq_rows, rim_rows, weight):
    padded = jnp.concatenate([rim_rows, seq_rows], axis=0).astype(jnp.float32)
    length_rows = seq_rows.shape[0]
    summed = weight[0] * padded[0:length_rows]
    for offset in range(1, weight.shape[0]):
        summed = summed + weight[offset] * padded[offset:offset + length_rows]
    return jax.nn.silu(summed)

def unit_norm(conv_out, head_width, factor):
    shaped = conv_out.reshape(conv_out.shape[0], -1, head_width)
    scaled = shaped * lax.rsqrt(lax.optimization_barrier(jnp.sum(shaped * shaped, axis=-1, keepdims=True)) + 1e-06) * factor
    return scaled.astype(jnp.bfloat16)

def span_parts(q_block, k_block, v_block, g_block, b_block):
    length_rows = g_block.shape[1]
    cum_decay = jnp.cumsum(g_block, axis=1)
    row_ids = lax.broadcasted_iota(jnp.int32, (length_rows, length_rows), 0)
    col_ids = lax.broadcasted_iota(jnp.int32, (length_rows, length_rows), 1)
    lower_mask = row_ids >= col_ids
    gap_log = cum_decay[:, :, None] - cum_decay[:, None, :]
    within = jnp.where(lower_mask, jnp.exp(jnp.where(lower_mask, gap_log, 0.0)), 0.0)
    k_gram = jnp.einsum('hid,hjd->hij', k_block, k_block, precision=HIGHEST)
    strict_part = jnp.where(row_ids > col_ids, b_block[:, :, None] * within * k_gram, 0.0)
    system_mat = strict_part + jnp.eye(length_rows, dtype=jnp.float32)
    growth = jnp.exp(cum_decay)
    right_side = jnp.concatenate([(b_block * growth)[:, :, None] * k_block, b_block[:, :, None] * v_block], axis=2)
    solved = jax.scipy.linalg.solve_triangular(system_mat, right_side, lower=True, unit_diagonal=True)
    key_width = k_block.shape[2]
    w_mat = solved[:, :, :key_width]
    u_mat = solved[:, :, key_width:]
    scores = jnp.einsum('hid,hjd->hij', q_block, k_block, precision=HIGHEST) * within
    q_decay = growth[:, :, None] * q_block
    end_decay = growth[:, -1]
    k_decay = jnp.exp(cum_decay[:, -1:] - cum_decay)[:, :, None] * k_block
    return (q_decay, scores, w_mat, u_mat, k_decay, end_decay)

def reference(q_rows, k_rows, v_rows, z_rows, a_rows, b_rows, conv_q, conv_k, conv_v, a_log, dt_bias, norm_gain):
    rim_keys = jnp.zeros((CONV - 1, KH * DK), jnp.bfloat16)
    rim_vals = jnp.zeros((CONV - 1, VH * DV), jnp.bfloat16)
    queries = unit_norm(conv_silu(q_rows, rim_keys, conv_q), DK, DK ** (-0.5))
    keys_unit = unit_norm(conv_silu(k_rows, rim_keys, conv_k), DK, 1.0)
    values = conv_silu(v_rows, rim_vals, conv_v).astype(jnp.bfloat16).reshape(TOKENS, VH, DV)
    write_rate = jax.nn.sigmoid(b_rows.astype(jnp.float32))
    log_decay = -jnp.exp(a_log)[None, :] * jax.nn.softplus(a_rows.astype(jnp.float32) + dt_bias[None, :])
    span_count = TOKENS // SPAN
    q_all = queries.reshape(span_count, SPAN, KH, DK).transpose(0, 2, 1, 3)
    k_all = keys_unit.reshape(span_count, SPAN, KH, DK).transpose(0, 2, 1, 3)
    v_all = values.reshape(span_count, SPAN, VH, DV).transpose(0, 2, 1, 3)
    g_all = log_decay.reshape(span_count, SPAN, VH).transpose(0, 2, 1)
    b_all = write_rate.reshape(span_count, SPAN, VH).transpose(0, 2, 1)
    share_ratio = VH // KH

    def advance(state_now, pieces):
        q_block, k_block, v_block, g_block, b_block = pieces
        q_full = jnp.repeat(q_block.astype(jnp.float32), share_ratio, axis=0)
        k_full = jnp.repeat(k_block.astype(jnp.float32), share_ratio, axis=0)
        q_decay, scores, w_mat, u_mat, k_decay, end_decay = span_parts(q_full, k_full, v_block.astype(jnp.float32), g_block, b_block)
        fresh_vals = u_mat - jnp.einsum('hcd,hde->hce', w_mat, state_now, precision=HIGHEST)
        output = jnp.einsum('hcd,hde->hce', q_decay, state_now, precision=HIGHEST) + jnp.einsum('hij,hje->hie', scores, fresh_vals, precision=HIGHEST)
        state_next = end_decay[:, None, None] * state_now + jnp.einsum('hcd,hce->hde', k_decay, fresh_vals, precision=HIGHEST)
        return (state_next, output)
    state_first = jnp.zeros((VH, DK, DV), jnp.float32)
    _, outputs = lax.scan(advance, state_first, (q_all, k_all, v_all, g_all, b_all))
    core_out = outputs.transpose(0, 2, 1, 3).reshape(TOKENS, VH, DV)
    normed = (core_out * lax.rsqrt(lax.optimization_barrier(jnp.mean(core_out * core_out, axis=-1, keepdims=True)) + 1e-06) * norm_gain).astype(jnp.bfloat16)
    normed = lax.optimization_barrier(normed)
    gated_out = normed.astype(jnp.float32).reshape(TOKENS, VH * DV) * jax.nn.silu(z_rows.astype(jnp.float32))
    return gated_out.astype(jnp.bfloat16)
```

```python
import jax
import jax.numpy as jnp
from jax import lax
from jax.experimental import pallas as pl
from jax.experimental.pallas import tpu as pltpu
from jax.sharding import Mesh, PartitionSpec as P

DK = 128
DV = 128
CONV = 4
SUB = 8
KH = 16
EPS = 1e-06
F32 = jnp.float32
BF16 = jnp.bfloat16
VMEM_BYTES = 56 * 1024 * 1024


def dot(a, b, dims=((1,), (0,))):
    return lax.dot_general(a, b, (dims, ((), ())), preferred_element_type=F32)


def halves(x):
    high = x.astype(BF16)
    return high, (x - high.astype(F32)).astype(BF16)


def mm_left(a, b):
    return dot(jnp.concatenate(halves(a), axis=1), jnp.concatenate([b, b], axis=0))


def mm_right(a, b):
    return dot(jnp.concatenate([a, a], axis=1), jnp.concatenate(halves(b), axis=0))


def mm(a, b):
    a_high, a_low = halves(a)
    b_high, b_low = halves(b)
    both = jnp.concatenate([a_high, a_low], axis=1)
    return dot(both, jnp.concatenate([b_high, b_high], axis=0)) + dot(a_high, b_low)


def silu(x):
    return x / (1.0 + jnp.exp(-x))


def iota(shape, dim):
    return lax.broadcasted_iota(jnp.int32, shape, dim)


def pack_kernel(heads_axis, q_ref, k_ref, v_ref, a_ref, b_ref, out_ref):
    peers, tokens = out_ref.shape[0], q_ref.shape[0]
    heads = peers // (q_ref.shape[1] // DK // heads_axis)
    subs = peers // heads_axis
    for sub in range(subs):
        for head in range(heads_axis):
            dest, key_head = sub * heads_axis + head, head * subs + sub
            out_ref[dest, 0:tokens, :] = q_ref[:, key_head * DK : (key_head + 1) * DK]
            out_ref[dest, tokens : 2 * tokens, :] = k_ref[:, key_head * DK : (key_head + 1) * DK]
            for r in range(2):
                value_head = 2 * key_head + r
                out_ref[dest, (2 + r) * tokens : (3 + r) * tokens, :] = v_ref[
                    :, value_head * DV : (value_head + 1) * DV
                ]
    del heads
    value_heads = a_ref.shape[1]
    row = iota((value_heads, peers * 16), 0)
    col = iota((value_heads, peers * 16), 1)
    dest, entry = col // 16, col % 16
    first = 2 * ((dest % heads_axis) * subs + dest // heads_axis)
    pick_a = jnp.where((entry < 2) & (row == first + entry), 1.0, 0.0).astype(BF16)
    pick_b = jnp.where(
        (entry >= 2) & (entry < 4) & (row == first + entry - 2), 1.0, 0.0
    ).astype(BF16)
    picked = (dot(a_ref[...], pick_a) + dot(b_ref[...], pick_b)).astype(BF16)
    lane_shift = tokens * lax.rem(lax.axis_index("head"), 2)
    place = jnp.where(
        iota((tokens, 128), 1) == iota((tokens, 128), 0) + lane_shift, 1.0, 0.0
    ).astype(BF16)
    gates = dot(picked, place, ((0,), (0,))).astype(BF16)
    for d in range(peers):
        out_ref[d, 4 * tokens :, :] = gates[16 * d : 16 * (d + 1), :]


def invert(systems):
    size = systems[0].shape[0]
    blocks = size // SUB
    row, col = iota((size, size), 0), iota((size, size), 1)
    diagonal = (row // SUB) == (col // SUB)
    compact = jnp.concatenate(
        [
            jnp.sum(jnp.where(diagonal, n, 0.0).reshape(blocks, SUB, size), axis=0)
            for n in systems
        ],
        axis=0,
    )
    count = len(systems)
    lane, line = iota(compact.shape, 1), iota(compact.shape, 0)
    solved = jnp.where(lane % SUB == line % SUB, 1.0, 0.0).reshape(count, SUB, size)
    for m in range(SUB - 1):
        spread = jnp.take_along_axis(compact, (lane // SUB) * SUB + m, axis=1)
        solved = solved - spread.reshape(count, SUB, size) * solved[:, m : m + 1, :]
    inverses = [
        jnp.where(
            diagonal.reshape(blocks, SUB, size), solved[i : i + 1, :, :], 0.0
        ).reshape(size, size)
        for i in range(count)
    ]
    width = SUB
    while width < size:
        odd = [(j, j + width) for j in range(width, size, 2 * width)]

        def rows_of(x):
            return jnp.concatenate([x[lo:hi] for lo, hi in odd], axis=0)

        below = rows_of(
            ((row // (2 * width)) == (col // (2 * width))) & ((col // width) % 2 == 0)
        )
        firsts = [
            mm(jnp.where(below, rows_of(n), 0.0), inv) for n, inv in zip(systems, inverses)
        ]
        zero = jnp.zeros((width, size), F32)
        spreads = []
        for first in firsts:
            parts = []
            for j in range(len(odd)):
                parts += [zero, first[j * width : (j + 1) * width]]
            spreads.append(jnp.concatenate(parts, axis=0))
        seconds = [mm(rows_of(inv), spread) for inv, spread in zip(inverses, spreads)]
        grown = []
        for inv, second in zip(inverses, seconds):
            parts = []
            for j, (lo, hi) in enumerate(odd):
                parts += [inv[lo - width : lo], inv[lo:hi] - second[j * width : (j + 1) * width]]
            grown.append(jnp.concatenate(parts, axis=0))
        inverses = grown
        width *= 2
    return inverses


def core_kernel(
    recv_ref, rim_ref, cq_ref, ck_ref, cv_ref, alog_ref, dt_ref, o_ref, x_ref, rows, qs, ks, vs
):
    sub = lax.axis_index("sub")
    peers = recv_ref.shape[0]
    tokens = (recv_ref.shape[1] - 16) // 4
    total = peers * tokens
    span = 128
    spans = total // span
    for g in range(4):
        rows[0:8, g * 128 : (g + 1) * 128] = rim_ref[16 * g : 16 * (g + 1), :].astype(F32)[8:]

    def widen(s, carry):
        start = pl.multiple_of(8 + s * tokens, 8)
        for g in range(4):
            rows[pl.ds(start, tokens), g * 128 : (g + 1) * 128] = recv_ref[
                s, g * tokens : (g + 1) * tokens, :
            ].astype(F32)
        return carry

    lax.fori_loop(0, peers, widen, 0)
    key_lane = pl.multiple_of(sub * DK, 128)
    value_lane = pl.multiple_of(sub * 2 * DV, 128)
    taps = [
        cq_ref[:, pl.ds(key_lane, DK)],
        ck_ref[:, pl.ds(key_lane, DK)],
        cv_ref[:, pl.ds(value_lane, DV)],
        cv_ref[:, pl.ds(pl.multiple_of(value_lane + DV, 128), DV)],
    ]
    for n in range(spans):
        at = n * span
        results = []
        for g in range(4):
            lanes = slice(g * 128, (g + 1) * 128)
            tap = taps[g]
            summed = tap[0:1] * rows[at + 5 : at + 5 + span, lanes]
            for j in range(1, CONV):
                summed = summed + tap[j : j + 1] * rows[at + 5 + j : at + 5 + j + span, lanes]
            results.append(silu(summed))
        for ref, y, factor in ((qs, results[0], DK**-0.5), (ks, results[1], 1.0)):
            scale = lax.rsqrt(jnp.sum(y * y, axis=-1, keepdims=True) + EPS)
            ref[at : at + span, :] = (y * scale * factor).astype(BF16)
        vs[at : at + span, 0:128] = results[2].astype(BF16)
        vs[at : at + span, 128:256] = results[3].astype(BF16)
    gates = jnp.concatenate(
        [
            recv_ref[2 * n, 4 * tokens :, :].astype(F32)
            + recv_ref[2 * n + 1, 4 * tokens :, :].astype(F32)
            for n in range(spans)
        ],
        axis=0,
    )
    second = iota(gates.shape, 0) % 16 == 1
    a_log = jnp.where(second, alog_ref[2 * sub + 1], alog_ref[2 * sub])
    dt_bias = jnp.where(second, dt_ref[2 * sub + 1], dt_ref[2 * sub])
    shifted = gates + dt_bias
    soft = jnp.maximum(shifted, 0.0) + jnp.log1p(jnp.exp(-jnp.abs(shifted)))
    decay = -jnp.exp(a_log) * soft
    rate = 1.0 / (1.0 + jnp.exp(-gates))
    lane_r, lane_c = iota((span, span), 0), iota((span, span), 1)
    upto = jnp.where(lane_r <= lane_c, 1.0, 0.0).astype(BF16)
    d_high, d_rest = halves(decay)
    d_mid, d_low = halves(decay - d_high.astype(F32))
    cum = dot(d_high, upto) + (dot(d_mid, upto) + dot(d_low, upto))
    growth = jnp.exp(cum)
    mixed = jnp.where(iota(gates.shape, 0) % 16 < 2, cum, rate)
    columns = jnp.transpose(mixed)
    lower = lane_r >= lane_c
    strict = lane_r > lane_c
    keys, keys_t, queries, scores, systems = [], [], [], [], []
    for n in range(spans):
        q_n = qs[n * span : (n + 1) * span, :]
        k_n = ks[n * span : (n + 1) * span, :]
        kt_n = jnp.transpose(k_n.astype(F32)).astype(BF16)
        grams = dot(jnp.concatenate([k_n, q_n], axis=0), kt_n)
        keys.append(k_n)
        keys_t.append(kt_n)
        queries.append(q_n)
        for r in range(2):
            c_col = columns[:, 16 * n + r : 16 * n + r + 1]
            c_row = cum[16 * n + r : 16 * n + r + 1, :]
            b_col = columns[:, 16 * n + 2 + r : 16 * n + 3 + r]
            within = jnp.where(lower, jnp.exp(jnp.where(lower, c_col - c_row, 0.0)), 0.0)
            systems.append(jnp.where(strict, b_col * within * grams[:span], 0.0))
            scores.append(within * grams[span:])
    inverses = invert(systems)
    states = [
        jnp.concatenate([jnp.zeros((DK, DV), F32), jnp.where(lane_r == lane_c, 1.0, 0.0)], axis=1)
        for r in range(2)
    ]
    zero_half = jnp.zeros((span, DV), F32)
    for n in range(spans):
        for r in range(2):
            at = 16 * n + r
            b_row = rate[at + 2 : at + 3, :]
            c_col = columns[:, at : at + 1]
            t_b = inverses[2 * n + r] * b_row
            w_mat = mm_left(t_b * growth[at : at + 1, :], keys[n])
            u_mat = mm_left(t_b, vs[n * span : (n + 1) * span, r * DV : (r + 1) * DV])
            x = states[r]
            fresh = jnp.concatenate([u_mat, zero_half], axis=1) - mm(w_mat, x)
            out = jnp.exp(c_col) * mm_right(queries[n], x) + mm(scores[2 * n + r], fresh)
            o_ref[r, n * span : (n + 1) * span, :] = out
            c_end = c_col[span - 1 : span, :]
            states[r] = jnp.exp(c_end) * x + mm_right(
                keys_t[n], jnp.exp(c_end - c_col) * fresh
            )
    for r in range(2):
        x_ref[r] = states[r]


def finish_kernel(o_ref, s_ref, gain_ref, out_ref):
    peers, tokens = out_ref.shape[0], out_ref.shape[1]
    gain = gain_ref[...]
    group = 2
    for r in range(2):
        s_in = s_ref[r].astype(F32)
        for i in range(0, peers, group):
            at = i * tokens
            ext = o_ref[r, at : at + group * tokens, :]
            core = ext[:, :DV] + mm(ext[:, DV:], s_in)
            scale = lax.rsqrt(jnp.mean(core * core, axis=-1, keepdims=True) + EPS)
            normed = (core * scale * gain).astype(BF16)
            out_ref[i : i + group, :, r * DV : (r + 1) * DV] = normed.reshape(group, tokens, DV)


def gate_kernel(heads_axis, normed_ref, z_ref, out_ref):
    peers = normed_ref.shape[0]
    subs = peers // heads_axis
    for sub in range(subs):
        for head in range(heads_axis):
            key_head = head * subs + sub
            lanes = slice(key_head * 2 * DV, (key_head + 1) * 2 * DV)
            gate = silu(z_ref[:, lanes].astype(F32))
            value = normed_ref[sub * heads_axis + head].astype(F32)
            out_ref[:, lanes] = (value * gate).astype(BF16)


def call(kernel, outs, n_in, scratch=(), smem=()):
    specs = [
        pl.BlockSpec(memory_space=pltpu.SMEM if i in smem else pltpu.VMEM) for i in range(n_in)
    ]
    return pl.pallas_call(
        kernel,
        out_shape=outs,
        in_specs=specs,
        out_specs=jax.tree.map(lambda _: pl.BlockSpec(memory_space=pltpu.VMEM), outs),
        scratch_shapes=list(scratch),
        compiler_params=pltpu.CompilerParams(vmem_limit_bytes=VMEM_BYTES),
    )


def local(
    q_rows,
    k_rows,
    v_rows,
    z_rows,
    a_rows,
    b_rows,
    conv_q,
    conv_k,
    conv_v,
    a_log,
    dt_bias,
    norm_gain,
):
    shards, subs, heads_axis = (lax.axis_size(a) for a in ("half", "sub", "head"))
    peers, tokens = subs * heads_axis, q_rows.shape[0]
    total = peers * tokens
    group = ("sub", "head")
    route = [(i, i + 1) for i in range(shards - 1)]
    shape = jax.ShapeDtypeStruct
    packed = call(
        lambda *refs: pack_kernel(heads_axis, *refs),
        shape((peers, 4 * tokens + 16, 128), BF16),
        5,
    )(q_rows, k_rows, v_rows, a_rows, b_rows)
    received = lax.all_to_all(packed, group, 0, 0, tiled=True)
    tail = jnp.concatenate(
        [received[peers - 1, (g + 1) * tokens - 16 : (g + 1) * tokens] for g in range(4)], axis=0
    )
    rim = lax.ppermute(tail, "half", route)
    partial, state = call(
        core_kernel,
        (shape((2, total, 2 * DV), F32), shape((2, DK, 2 * DV), F32)),
        7,
        scratch=(
            pltpu.VMEM((8 + total, 512), F32),
            pltpu.VMEM((total, DK), BF16),
            pltpu.VMEM((total, DK), BF16),
            pltpu.VMEM((total, 2 * DV), BF16),
        ),
        smem=(5, 6),
    )(received, rim, conv_q, conv_k, conv_v, a_log, dt_bias)
    add, lin = state[:, :, :DV], state[:, :, DV:]
    entering = lax.ppermute(add, "half", route)
    for _ in range(shards - 2):
        moved = jnp.einsum("hde,hef->hdf", lin, entering, precision=lax.Precision.HIGHEST) + add
        entering = lax.ppermute(moved, "half", route)
    normed = call(finish_kernel, shape((peers, tokens, 2 * DV), BF16), 3)(
        partial, entering, norm_gain.reshape(1, DV)
    )
    returned = lax.all_to_all(normed, group, 0, 0, tiled=True)
    return call(
        lambda *refs: gate_kernel(heads_axis, *refs),
        shape((tokens, z_rows.shape[1]), BF16),
        2,
    )(returned, z_rows)


def solution(mesh):
    heads_axis = mesh.shape["head"]
    subs = KH // heads_axis
    regrouped = Mesh(
        mesh.devices.reshape(mesh.shape["ctx"] // subs, subs, heads_axis), ("half", "sub", "head")
    )
    row = P(("half", "sub", "head"), None)
    placed = (row,) * 6 + (P(None, "head"),) * 3 + (P("head"),) * 2 + (P(),)
    return jax.shard_map(local, mesh=regrouped, in_specs=placed, out_specs=row, check_vma=False)
```

```python
import jax
import jax.numpy as jnp
from jax import lax
from jax.experimental import pallas as pl
from jax.experimental.pallas import tpu as pltpu
from jax.sharding import Mesh, PartitionSpec as P

DK = 128
DV = 128
CONV = 4
KH = 16
SUB = 8
SPAN = 128
EDGE = CONV - 1
EPS = 1e-06
F32 = jnp.float32
BF16 = jnp.bfloat16
VMEM_BYTES = 56 * 1024 * 1024
GATES = 16


def dot(a, b, dims=((1,), (0,))):
    return lax.dot_general(a, b, (dims, ((), ())), preferred_element_type=F32)


def halves(x):
    high = x.astype(BF16)
    return high, (x - high.astype(F32)).astype(BF16)


def mm_left(a, b):
    return dot(jnp.concatenate(halves(a), axis=1), jnp.concatenate([b, b], axis=0))


def mm_right(a, b):
    return dot(jnp.concatenate([a, a], axis=1), jnp.concatenate(halves(b), axis=0))


def mm(a, b):
    a_high, a_low = halves(a)
    b_high, b_low = halves(b)
    both = jnp.concatenate([a_high, a_low], axis=1)
    return dot(both, jnp.concatenate([b_high, b_high], axis=0)) + dot(a_high, b_low)


def silu(x):
    return x / (1.0 + jnp.exp(-x))


def unit(y, factor):
    scale = lax.rsqrt(jnp.sum(y * y, axis=-1, keepdims=True) + EPS)
    return (y * scale * factor).astype(BF16)


def iota(shape, dim):
    return lax.broadcasted_iota(jnp.int32, shape, dim)


def pack_kernel(q_ref, k_ref, v_ref, at_ref, bt_ref, out_ref):
    head = pl.program_id(0)
    subs, tokens = out_ref.shape[0], q_ref.shape[0]
    for sub in range(subs):
        lanes = slice(sub * DK, (sub + 1) * DK)
        out_ref[sub, 0, GATES : GATES + tokens, :] = k_ref[:, lanes]
        for r in range(2):
            value_head = 2 * sub + r
            out_ref[sub, 0, GATES + (1 + r) * tokens : GATES + (2 + r) * tokens, :] = v_ref[
                :, value_head * DV : (value_head + 1) * DV
            ]
        out_ref[sub, 0, GATES + 3 * tokens :, :] = q_ref[:, lanes]
    value_heads = at_ref.shape[0]
    row, entry = iota((subs * GATES, value_heads), 0), iota((subs * GATES, value_heads), 1)
    sub, which = row // GATES, row % GATES
    first = 2 * (head * subs + sub)
    pick_a = jnp.where((which < 2) & (entry == first + which), 1.0, 0.0).astype(BF16)
    pick_b = jnp.where(
        (which >= 2) & (which < 4) & (entry == first + which - 2), 1.0, 0.0
    ).astype(BF16)
    picked = (dot(pick_a, at_ref[...]) + dot(pick_b, bt_ref[...])).astype(BF16)
    lane_shift = tokens * lax.rem(lax.axis_index("head"), SPAN // tokens)
    place = jnp.where(
        iota((tokens, SPAN), 1) == iota((tokens, SPAN), 0) + lane_shift, 1.0, 0.0
    ).astype(BF16)
    gates = dot(picked, place).astype(BF16)
    for sub in range(subs):
        out_ref[sub, 0, 0:GATES, :] = gates[GATES * sub : GATES * (sub + 1), :]


def invert(systems):
    size = systems[0].shape[0]
    blocks = size // SUB
    row, col = iota((size, size), 0), iota((size, size), 1)
    diagonal = (row // SUB) == (col // SUB)
    compact = jnp.concatenate(
        [
            jnp.sum(jnp.where(diagonal, n, 0.0).reshape(blocks, SUB, size), axis=0)
            for n in systems
        ],
        axis=0,
    )
    count = len(systems)
    lane, line = iota(compact.shape, 1), iota(compact.shape, 0)
    solved = jnp.where(lane % SUB == line % SUB, 1.0, 0.0).reshape(count, SUB, size)
    for m in range(SUB - 1):
        spread = jnp.take_along_axis(compact, (lane // SUB) * SUB + m, axis=1)
        solved = solved - spread.reshape(count, SUB, size) * solved[:, m : m + 1, :]
    inverses = [
        jnp.where(
            diagonal.reshape(blocks, SUB, size), solved[i : i + 1, :, :], 0.0
        ).reshape(size, size)
        for i in range(count)
    ]
    width = SUB
    while width < size:
        odd = [(j, j + width) for j in range(width, size, 2 * width)]

        def rows_of(x):
            return jnp.concatenate([x[lo:hi] for lo, hi in odd], axis=0)

        below = rows_of(
            ((row // (2 * width)) == (col // (2 * width))) & ((col // width) % 2 == 0)
        )
        firsts = [
            mm(jnp.where(below, rows_of(n), 0.0), inv) for n, inv in zip(systems, inverses)
        ]
        zero = jnp.zeros((width, size), F32)
        spreads = []
        for first in firsts:
            parts = []
            for j in range(len(odd)):
                parts += [zero, first[j * width : (j + 1) * width]]
            spreads.append(jnp.concatenate(parts, axis=0))
        seconds = [mm(rows_of(inv), spread) for inv, spread in zip(inverses, spreads)]
        grown = []
        for inv, second in zip(inverses, seconds):
            parts = []
            for j, (lo, hi) in enumerate(odd):
                parts += [inv[lo - width : lo], inv[lo:hi] - second[j * width : (j + 1) * width]]
            grown.append(jnp.concatenate(parts, axis=0))
        inverses = grown
        width *= 2
    return inverses


def gate_values(gates, sub, alog_ref, dt_ref):
    second = iota(gates.shape, 0) % GATES == 1
    a_log = jnp.where(second, alog_ref[2 * sub + 1], alog_ref[2 * sub])
    dt_bias = jnp.where(second, dt_ref[2 * sub + 1], dt_ref[2 * sub])
    shifted = gates + dt_bias
    soft = jnp.maximum(shifted, 0.0) + jnp.log1p(jnp.exp(-jnp.abs(shifted)))
    return -jnp.exp(a_log) * soft, 1.0 / (1.0 + jnp.exp(-gates))


def convolved(rows, at, count, lanes, tap):
    summed = tap[0:1] * rows[at : at + count, lanes]
    for j in range(1, CONV):
        summed = summed + tap[j : j + 1] * rows[at + j : at + j + count, lanes]
    return silu(summed)


def taps_of(sub, ck_ref, cv_ref):
    key_lane = pl.multiple_of(sub * DK, 128)
    value_lane = pl.multiple_of(sub * 2 * DV, 128)
    return [
        ck_ref[:, pl.ds(key_lane, DK)],
        cv_ref[:, pl.ds(value_lane, DV)],
        cv_ref[:, pl.ds(pl.multiple_of(value_lane + DV, 128), DV)],
    ]


def state_kernel(
    recv_ref,
    ck_ref,
    cv_ref,
    alog_ref,
    dt_ref,
    hop_ref,
    keys_ref,
    wu_ref,
    xs_ref,
    cols_ref,
    cum_ref,
    early_ref,
    last_ref,
    raw,
    edge,
    rows,
    vs,
    sems,
):
    sub = lax.axis_index("sub")
    later = lax.axis_index("half") > 0
    peers = recv_ref.shape[0]
    tokens = (recv_ref.shape[1] - GATES) // 4
    total = peers * tokens
    spans = total // SPAN
    width = GATES + 3 * tokens
    fetch = pltpu.make_async_copy(recv_ref.at[:, pl.ds(0, width), :], raw, sems.at[0])
    fetch_edge = pltpu.make_async_copy(
        recv_ref.at[peers - 1, pl.ds(GATES + 4 * tokens - 16, 16), :], edge, sems.at[1]
    )
    fetch.start()
    fetch_edge.start()
    taps = taps_of(sub, ck_ref, cv_ref)
    rows[0:8, :] = jnp.zeros((8, 3 * 128), F32)
    fetch.wait()
    fetch_edge.wait()
    hop_ref[2 * DK : 2 * DK + 16, :] = edge[...]
    for g in range(3):
        hop_ref[2 * DK + 16 * (g + 1) : 2 * DK + 16 * (g + 2), :] = raw[
            peers - 1, GATES + (g + 1) * tokens - 16 : GATES + (g + 1) * tokens, :
        ]

    def widen(s, carry):
        start = pl.multiple_of(8 + s * tokens, 8)
        for g in range(3):
            rows[pl.ds(start, tokens), g * 128 : (g + 1) * 128] = raw[
                s, GATES + g * tokens : GATES + (g + 1) * tokens, :
            ].astype(F32)
        return carry

    lax.fori_loop(0, peers, widen, 0)
    for n in range(spans):
        at = n * SPAN
        results = [
            convolved(rows, at + 8 - EDGE, SPAN, slice(g * 128, (g + 1) * 128), taps[g])
            for g in range(3)
        ]
        keys_ref[at : at + SPAN, :] = unit(results[0], 1.0)
        vs[at : at + SPAN, 0:DV] = results[1].astype(BF16)
        vs[at : at + SPAN, DV : 2 * DV] = results[2].astype(BF16)
    gates = jnp.concatenate(
        [
            sum(raw[s, 0:GATES, :].astype(F32) for s in range(n, n + SPAN // tokens))
            for n in range(0, peers, SPAN // tokens)
        ],
        axis=0,
    )
    decay, rate = gate_values(gates, sub, alog_ref, dt_ref)
    early_ref[...] = jnp.where(iota((8, SPAN), 0) < 2, decay[0:8], rate[0:8])
    skipped = later & (iota(gates.shape, 0) < GATES) & (iota(gates.shape, 1) < EDGE)
    decay = jnp.where(skipped, 0.0, decay)
    rate = jnp.where(skipped, 0.0, rate)
    lane_r, lane_c = iota((SPAN, SPAN), 0), iota((SPAN, SPAN), 1)
    upto = jnp.where(lane_r <= lane_c, 1.0, 0.0).astype(BF16)
    d_high, d_rest = halves(decay)
    d_mid, d_low = halves(decay - d_high.astype(F32))
    cum = dot(d_high, upto) + (dot(d_mid, upto) + dot(d_low, upto))
    growth = jnp.exp(cum)
    columns = jnp.transpose(jnp.where(iota(gates.shape, 0) % GATES < 2, cum, rate))
    cum_ref[...] = cum
    cols_ref[...] = columns
    lower = lane_r >= lane_c
    strict = lane_r > lane_c
    keys, keys_t, systems = [], [], []
    for n in range(spans):
        k_n = keys_ref[n * SPAN : (n + 1) * SPAN, :]
        kt_n = jnp.transpose(k_n.astype(F32)).astype(BF16)
        gram = dot(k_n, kt_n)
        keys.append(k_n)
        keys_t.append(kt_n)
        for r in range(2):
            at = GATES * n + r
            gap = columns[:, at : at + 1] - cum[at : at + 1, :]
            within = jnp.exp(jnp.where(lower, gap, 0.0))
            systems.append(jnp.where(strict, columns[:, at + 2 : at + 3] * within * gram, 0.0))
    inverses = invert(systems)
    identity = jnp.where(lane_r == lane_c, 1.0, 0.0)
    maps = []
    for n in range(spans):
        for r in range(2):
            at = GATES * n + r
            c_col = columns[:, at : at + 1]
            t_b = inverses[2 * n + r] * rate[at + 2 : at + 3, :]
            w_mat = mm_left(t_b * growth[at : at + 1, :], keys[n])
            u_mat = mm_left(t_b, vs[n * SPAN : (n + 1) * SPAN, r * DV : (r + 1) * DV])
            both = jnp.concatenate([w_mat, u_mat], axis=1)
            wu_ref[r, n * SPAN : (n + 1) * SPAN, :] = both.astype(BF16)
            c_end = c_col[SPAN - 1 : SPAN, :]
            moved = mm_right(keys_t[n], jnp.exp(c_end - c_col) * both)
            maps.append((jnp.exp(c_end) * identity - moved[:, :DK], moved[:, DK:]))
    states = [jnp.concatenate([jnp.zeros((DK, DV), F32), identity], axis=1) for r in range(2)]
    zero_half = jnp.zeros((DK, DV), F32)
    for n in range(spans):
        for r in range(2):
            xs_ref[r, n] = states[r].astype(BF16)
            lin, add = maps[2 * n + r]
            if n == 0:
                states[r] = jnp.concatenate([add, lin], axis=1)
            else:
                states[r] = mm(lin, states[r]) + jnp.concatenate([add, zero_half], axis=1)
    for r in range(2):
        last_ref[r] = states[r]
        hop_ref[r * DK : (r + 1) * DK, :] = states[r][:, :DV].astype(BF16)


def output_kernel(
    recv_ref, cq_ref, keys_ref, wu_ref, xs_ref, cols_ref, cum_ref, oa_ref, om_ref, raw, rows, sem
):
    sub = lax.axis_index("sub")
    peers = recv_ref.shape[0]
    tokens = (recv_ref.shape[1] - GATES) // 4
    total = peers * tokens
    spans = total // SPAN
    fetch = pltpu.make_async_copy(
        recv_ref.at[:, pl.ds(GATES + 3 * tokens, tokens), :], raw, sem.at[0]
    )
    fetch.start()
    tap = cq_ref[:, pl.ds(pl.multiple_of(sub * DK, 128), DK)]
    rows[0:8, :] = jnp.zeros((8, DK), F32)
    fetch.wait()
    rows[8 : 8 + total, :] = raw[...].astype(F32).reshape(total, DK)
    lane_r, lane_c = iota((SPAN, SPAN), 0), iota((SPAN, SPAN), 1)
    lower = lane_r >= lane_c
    for n in range(spans):
        at = n * SPAN
        q_n = unit(convolved(rows, at + 8 - EDGE, SPAN, slice(0, DK), tap), DK**-0.5)
        k_n = keys_ref[at : at + SPAN, :]
        scores = dot(q_n, k_n, ((1,), (1,)))
        for r in range(2):
            c_col = cols_ref[:, GATES * n + r : GATES * n + r + 1]
            c_row = cum_ref[GATES * n + r : GATES * n + r + 1, :]
            within = jnp.exp(jnp.where(lower, c_col - c_row, 0.0))
            inner = jnp.where(lower, within * scores, 0.0).astype(BF16)
            x_n = xs_ref[r, n]
            both = wu_ref[r, at : at + SPAN, :]
            held = dot(both[:, :DK], x_n)
            fresh_a = (both[:, DK:].astype(F32) - held[:, :DV]).astype(BF16)
            fresh_m = (-held[:, DV:]).astype(BF16)
            out = jnp.exp(c_col) * dot(q_n, x_n) + dot(
                inner, jnp.concatenate([fresh_a, fresh_m], axis=1)
            )
            oa_ref[r, at : at + SPAN, :] = out[:, :DV]
            om_ref[r, at : at + SPAN, :] = out[:, DV:].astype(BF16)


def first_tokens(hop_ref, head_ref, early_ref, cq_ref, ck_ref, cv_ref, rows):
    sub = lax.axis_index("sub")
    later = lax.axis_index("half") > 0
    tokens = (head_ref.shape[0] - GATES) // 4
    starts = [GATES + 3 * tokens, GATES, GATES + tokens, GATES + 2 * tokens]
    taps = [cq_ref[:, pl.ds(pl.multiple_of(sub * DK, 128), DK)]] + taps_of(sub, ck_ref, cv_ref)
    results = []
    for g in range(4):
        lanes = slice(g * 128, (g + 1) * 128)
        rows[0:16, lanes] = hop_ref[2 * DK + 16 * g : 2 * DK + 16 * (g + 1), :].astype(F32)
        rows[16:32, lanes] = head_ref[starts[g] : starts[g] + 16, :].astype(F32)
        results.append(convolved(rows, 16 - EDGE, 8, lanes, taps[g]))
    q_cols = jnp.transpose(unit(results[0], DK**-0.5).astype(F32))
    k_cols = jnp.transpose(unit(results[1], 1.0).astype(F32))
    gates = early_ref[...]
    line = iota((8, DV), 0)
    finals, outputs = [], []
    for r in range(2):
        values = results[2 + r].astype(BF16).astype(F32)
        entering = hop_ref[r * DK : (r + 1) * DK, :].astype(F32)
        state, out = entering, jnp.zeros((8, DV), F32)
        for t in range(EDGE):
            k_t, q_t = k_cols[:, t : t + 1], q_cols[:, t : t + 1]
            state = jnp.exp(gates[r : r + 1, t : t + 1]) * state
            held = jnp.sum(k_t * state, axis=0, keepdims=True)
            state = state + k_t * (
                gates[2 + r : 3 + r, t : t + 1] * (values[t : t + 1, :] - held)
            )
            out = jnp.where(line == t, jnp.sum(q_t * state, axis=0, keepdims=True), out)
        finals.append(jnp.where(later, state, entering))
        outputs.append(out)
    return finals, outputs, later


def finish_kernel(
    hop_ref,
    head_ref,
    early_ref,
    cq_ref,
    ck_ref,
    cv_ref,
    gain_ref,
    oa_ref,
    om_ref,
    out_ref,
    rows,
    states,
    starts,
):
    step = pl.program_id(0)

    @pl.when(step == 0)
    def _():
        finals, outputs, _ = first_tokens(
            hop_ref, head_ref, early_ref, cq_ref, ck_ref, cv_ref, rows
        )
        for r in range(2):
            states[r] = finals[r].astype(BF16)
            starts[r] = outputs[r]

    gain = gain_ref[...]
    peers, tokens = out_ref.shape[0], out_ref.shape[1]
    opening = (step == 0) & (lax.axis_index("half") > 0)
    for r in range(2):
        core = oa_ref[r] + dot(om_ref[r], states[r])
        replaced = opening & (iota((8, DV), 0) < EDGE)
        core = jnp.concatenate([jnp.where(replaced, starts[r], core[0:8]), core[8:]], axis=0)
        scale = lax.rsqrt(jnp.mean(core * core, axis=-1, keepdims=True) + EPS)
        normed = (core * scale * gain).astype(BF16)
        out_ref[:, :, r * DV : (r + 1) * DV] = normed.reshape(peers, tokens, DV)


def advance_kernel(
    hop_ref, head_ref, early_ref, cq_ref, ck_ref, cv_ref, last_ref, next_ref, rows
):
    finals, _, _ = first_tokens(hop_ref, head_ref, early_ref, cq_ref, ck_ref, cv_ref, rows)
    for r in range(2):
        x = last_ref[r]
        next_ref[r * DK : (r + 1) * DK, :] = (mm(x[:, DV:], finals[r]) + x[:, :DV]).astype(BF16)
    next_ref[2 * DK :, :] = hop_ref[2 * DK :, :]


def gate_kernel(normed_ref, z_ref, out_ref):
    subs = normed_ref.shape[0]
    for sub in range(subs):
        lanes = slice(sub * 2 * DV, (sub + 1) * 2 * DV)
        gate = silu(z_ref[:, lanes].astype(F32))
        out_ref[:, lanes] = (normed_ref[sub, 0].astype(F32) * gate).astype(BF16)


VMEM = pl.BlockSpec(memory_space=pltpu.VMEM)
SMEM = pl.BlockSpec(memory_space=pltpu.SMEM)
ANY = pl.BlockSpec(memory_space=pl.ANY)


def call(kernel, outs, in_specs, out_specs=None, grid=(), scratch=(), flops=1 << 26, moved=1 << 21):
    return pl.pallas_call(
        kernel,
        grid=grid,
        out_shape=outs,
        in_specs=in_specs,
        out_specs=jax.tree.map(lambda _: VMEM, outs) if out_specs is None else out_specs,
        scratch_shapes=list(scratch),
        compiler_params=pltpu.CompilerParams(vmem_limit_bytes=VMEM_BYTES),
        cost_estimate=pl.CostEstimate(flops=flops, bytes_accessed=moved, transcendentals=0),
    )


def whole(shape):
    return pl.BlockSpec(shape, lambda i: (0,) * len(shape))


def local(
    q_rows,
    k_rows,
    v_rows,
    z_rows,
    a_rows,
    b_rows,
    conv_q,
    conv_k,
    conv_v,
    a_log,
    dt_bias,
    norm_gain,
):
    shards, subs, heads_axis = (lax.axis_size(a) for a in ("half", "sub", "head"))
    peers, tokens = subs * heads_axis, q_rows.shape[0]
    total = peers * tokens
    spans = total // SPAN
    block = GATES + 4 * tokens
    group = ("sub", "head")
    route = [(i, i + 1) for i in range(shards - 1)]
    shape = jax.ShapeDtypeStruct
    heads_in_all = a_rows.shape[1]
    columns = lambda width: pl.BlockSpec((tokens, width), lambda i: (0, i))
    packed = call(
        pack_kernel,
        shape((subs, heads_axis, block, 128), BF16),
        [columns(subs * DK), columns(subs * DK), columns(2 * subs * DV)]
        + [whole((heads_in_all, tokens))] * 2,
        pl.BlockSpec((subs, 1, block, 128), lambda i: (0, i, 0, 0)),
        (heads_axis,),
    )(q_rows, k_rows, v_rows, a_rows.T, b_rows.T)
    received = lax.all_to_all(
        packed.reshape(peers, block, 128), group, 0, 0, tiled=True
    )
    hop, keys, both, starts, cols, cum, early, last = call(
        state_kernel,
        (
            shape((2 * DK + 64, 128), BF16),
            shape((total, DK), BF16),
            shape((2, total, 2 * DV), BF16),
            shape((2, spans, DK, 2 * DV), BF16),
            shape((SPAN, spans * GATES), F32),
            shape((spans * GATES, SPAN), F32),
            shape((8, SPAN), F32),
            shape((2, DK, 2 * DV), F32),
        ),
        [ANY, VMEM, VMEM, SMEM, SMEM],
        scratch=(
            pltpu.VMEM((peers, GATES + 3 * tokens, 128), BF16),
            pltpu.VMEM((16, 128), BF16),
            pltpu.VMEM((8 + total, 384), F32),
            pltpu.VMEM((total, 2 * DV), BF16),
            pltpu.SemaphoreType.DMA((2,)),
        ),
    )(received, conv_k, conv_v, a_log, dt_bias)
    entering = lax.ppermute(hop, "half", route)
    out_a, out_m = call(
        output_kernel,
        (shape((2, total, DV), F32), shape((2, total, DV), BF16)),
        [ANY] + [VMEM] * 6,
        scratch=(
            pltpu.VMEM((peers, tokens, 128), BF16),
            pltpu.VMEM((8 + total, DK), F32),
            pltpu.SemaphoreType.DMA((1,)),
        ),
    )(received, conv_q, keys, both, starts, cols, cum)
    head_rows = pl.BlockSpec((None, block, 128), lambda i: (0, 0, 0))
    fixed = [
        whole(entering.shape),
        head_rows,
        whole(early.shape),
        whole(conv_q.shape),
        whole(conv_k.shape),
        whole(conv_v.shape),
    ]
    fixed_values = (received, early, conv_q, conv_k, conv_v)
    for _ in range(shards - 2):
        moved = call(
            advance_kernel,
            shape(hop.shape, BF16),
            fixed + [whole(last.shape)],
            whole(hop.shape),
            (1,),
            (pltpu.VMEM((32, 512), F32),),
        )(entering, *fixed_values, last)
        fresh_hop = jnp.concatenate([moved[: 2 * DK], hop[2 * DK :]], axis=0)
        entering = lax.ppermute(fresh_hop, "half", route)
    steps = 4
    normed = call(
        finish_kernel,
        shape((peers, tokens, 2 * DV), BF16),
        fixed
        + [whole((1, DV))]
        + [pl.BlockSpec((2, total // steps, DV), lambda i: (0, i, 0))] * 2,
        pl.BlockSpec((peers // steps, tokens, 2 * DV), lambda i: (i, 0, 0)),
        (steps,),
        (
            pltpu.VMEM((32, 512), F32),
            pltpu.VMEM((2, DK, DV), BF16),
            pltpu.VMEM((2, 8, DV), F32),
        ),
    )(entering, *fixed_values, norm_gain.reshape(1, DV), out_a, out_m)
    returned = lax.all_to_all(normed, group, 0, 0, tiled=True)
    return call(
        gate_kernel,
        shape((tokens, z_rows.shape[1]), BF16),
        [
            pl.BlockSpec((subs, 1, tokens, 2 * DV), lambda i: (0, i, 0, 0)),
            columns(2 * subs * DV),
        ],
        columns(2 * subs * DV),
        (heads_axis,),
    )(returned.reshape(subs, heads_axis, tokens, 2 * DV), z_rows)


def solution(mesh):
    heads_axis = mesh.shape["head"]
    subs = KH // heads_axis
    regrouped = Mesh(
        mesh.devices.reshape(mesh.shape["ctx"] // subs, subs, heads_axis), ("half", "sub", "head")
    )
    row = P(("half", "sub", "head"), None)
    placed = (row,) * 6 + (P(None, "head"),) * 3 + (P("head"),) * 2 + (P(),)
    return jax.shard_map(local, mesh=regrouped, in_specs=placed, out_specs=row, check_vma=False)
```

```python
import functools

import jax
import jax.numpy as jnp
from jax import lax
from jax.experimental import pallas as pl
from jax.experimental.pallas import tpu as pltpu
from jax.sharding import Mesh, PartitionSpec as P

DK = 128
DV = 128
CONV = 4
KH = 16
SUB = 8
SPAN = 128
EDGE = CONV - 1
EPS = 1e-06
F32 = jnp.float32
BF16 = jnp.bfloat16
VMEM_BYTES = 56 * 1024 * 1024
GATES = 16


def dot(a, b, dims=((1,), (0,))):
    return lax.dot_general(a, b, (dims, ((), ())), preferred_element_type=F32)


def halves(x):
    high = x.astype(BF16)
    return high, (x - high.astype(F32)).astype(BF16)


def mm_left(a, b):
    return dot(jnp.concatenate(halves(a), axis=1), jnp.concatenate([b, b], axis=0))


def mm_right(a, b):
    return dot(jnp.concatenate([a, a], axis=1), jnp.concatenate(halves(b), axis=0))


def mm(a, b):
    a_high, a_low = halves(a)
    b_high, b_low = halves(b)
    both = jnp.concatenate([a_high, a_low], axis=1)
    return dot(both, jnp.concatenate([b_high, b_high], axis=0)) + dot(a_high, b_low)


def silu(x):
    return x / (1.0 + jnp.exp(-x))


def unit(y, factor):
    scale = lax.rsqrt(jnp.sum(y * y, axis=-1, keepdims=True) + EPS)
    return (y * scale * factor).astype(BF16)


def iota(shape, dim):
    return lax.broadcasted_iota(jnp.int32, shape, dim)


def pack_keys_kernel(heads_axis, k_ref, at_ref, bt_ref, out_ref):
    peers, tokens = out_ref.shape[0], k_ref.shape[0]
    subs = peers // heads_axis
    for dest in range(peers):
        key_head = (dest % heads_axis) * subs + dest // heads_axis
        out_ref[dest, GATES:, :] = k_ref[:, key_head * DK : (key_head + 1) * DK]
    value_heads = at_ref.shape[0]
    row, entry = iota((peers * GATES, value_heads), 0), iota((peers * GATES, value_heads), 1)
    dest, which = row // GATES, row % GATES
    first = 2 * ((dest % heads_axis) * subs + dest // heads_axis)
    pick_a = jnp.where((which < 2) & (entry == first + which), 1.0, 0.0).astype(BF16)
    pick_b = jnp.where(
        (which >= 2) & (which < 4) & (entry == first + which - 2), 1.0, 0.0
    ).astype(BF16)
    picked = (dot(pick_a, at_ref[...]) + dot(pick_b, bt_ref[...])).astype(BF16)
    lane_shift = tokens * lax.rem(lax.axis_index("head"), SPAN // tokens)
    place = jnp.where(
        iota((tokens, SPAN), 1) == iota((tokens, SPAN), 0) + lane_shift, 1.0, 0.0
    ).astype(BF16)
    gates = dot(picked, place).astype(BF16)
    for dest in range(peers):
        out_ref[dest, 0:GATES, :] = gates[GATES * dest : GATES * (dest + 1), :]


def pack_values_kernel(heads_axis, v_ref, q_ref, out_ref):
    peers, tokens = out_ref.shape[0], q_ref.shape[0]
    subs = peers // heads_axis
    for dest in range(peers):
        key_head = (dest % heads_axis) * subs + dest // heads_axis
        for r in range(2):
            lanes = slice((2 * key_head + r) * DV, (2 * key_head + r + 1) * DV)
            out_ref[dest, r * tokens : (r + 1) * tokens, :] = v_ref[:, lanes]
        out_ref[dest, 2 * tokens :, :] = q_ref[:, key_head * DK : (key_head + 1) * DK]


def invert(systems):
    size = systems[0].shape[0]
    blocks = size // SUB
    row, col = iota((size, size), 0), iota((size, size), 1)
    diagonal = (row // SUB) == (col // SUB)
    compact = jnp.concatenate(
        [
            jnp.sum(jnp.where(diagonal, n, 0.0).reshape(blocks, SUB, size), axis=0)
            for n in systems
        ],
        axis=0,
    )
    count = len(systems)
    lane, line = iota(compact.shape, 1), iota(compact.shape, 0)
    solved = jnp.where(lane % SUB == line % SUB, 1.0, 0.0).reshape(count, SUB, size)
    for m in range(SUB - 1):
        spread = jnp.take_along_axis(compact, (lane // SUB) * SUB + m, axis=1)
        solved = solved - spread.reshape(count, SUB, size) * solved[:, m : m + 1, :]
    inverses = [
        jnp.where(
            diagonal.reshape(blocks, SUB, size), solved[i : i + 1, :, :], 0.0
        ).reshape(size, size)
        for i in range(count)
    ]
    width = SUB
    while width < size:
        odd = [(j, j + width) for j in range(width, size, 2 * width)]

        def rows_of(x):
            return jnp.concatenate([x[lo:hi] for lo, hi in odd], axis=0)

        below = rows_of(
            ((row // (2 * width)) == (col // (2 * width))) & ((col // width) % 2 == 0)
        )
        firsts = [
            mm(jnp.where(below, rows_of(n), 0.0), inv) for n, inv in zip(systems, inverses)
        ]
        zero = jnp.zeros((width, size), F32)
        spreads = []
        for first in firsts:
            parts = []
            for j in range(len(odd)):
                parts += [zero, first[j * width : (j + 1) * width]]
            spreads.append(jnp.concatenate(parts, axis=0))
        seconds = [mm(rows_of(inv), spread) for inv, spread in zip(inverses, spreads)]
        grown = []
        for inv, second in zip(inverses, seconds):
            parts = []
            for j, (lo, hi) in enumerate(odd):
                parts += [inv[lo - width : lo], inv[lo:hi] - second[j * width : (j + 1) * width]]
            grown.append(jnp.concatenate(parts, axis=0))
        inverses = grown
        width *= 2
    return inverses


def gate_values(gates, sub, alog_ref, dt_ref):
    second = iota(gates.shape, 0) % GATES == 1
    a_log = jnp.where(second, alog_ref[2 * sub + 1], alog_ref[2 * sub])
    dt_bias = jnp.where(second, dt_ref[2 * sub + 1], dt_ref[2 * sub])
    shifted = gates + dt_bias
    soft = jnp.maximum(shifted, 0.0) + jnp.log1p(jnp.exp(-jnp.abs(shifted)))
    return -jnp.exp(a_log) * soft, 1.0 / (1.0 + jnp.exp(-gates))


def convolved(rows, at, count, lanes, tap):
    summed = tap[0:1] * rows[at : at + count, lanes]
    for j in range(1, CONV):
        summed = summed + tap[j : j + 1] * rows[at + j : at + j + count, lanes]
    return silu(summed)


def key_tap(sub, tap_ref):
    return tap_ref[:, pl.ds(pl.multiple_of(sub * DK, 128), DK)]


def value_taps(sub, cv_ref):
    lane = pl.multiple_of(sub * 2 * DV, 128)
    return [cv_ref[:, pl.ds(pl.multiple_of(lane + r * DV, 128), DV)] for r in range(2)]


def inverse_kernel(
    recv_ref,
    ck_ref,
    alog_ref,
    dt_ref,
    keys_ref,
    tb_ref,
    w_ref,
    lin_ref,
    ms_ref,
    cols_ref,
    cum_ref,
    early_ref,
    edge_ref,
    rows,
):
    sub = lax.axis_index("sub")
    later = lax.axis_index("half") > 0
    peers = recv_ref.shape[0]
    tokens = recv_ref.shape[1] - GATES
    total = peers * tokens
    spans = total // SPAN
    edge_ref[...] = recv_ref[peers - 1, GATES + tokens - 16 :, :]
    tap = key_tap(sub, ck_ref)
    rows[0:8, :] = jnp.zeros((8, DK), F32)
    for s in range(peers):
        rows[8 + s * tokens : 8 + (s + 1) * tokens, :] = recv_ref[s, GATES:, :].astype(F32)
    gates = jnp.concatenate(
        [
            sum(recv_ref[s, 0:GATES, :].astype(F32) for s in range(n, n + SPAN // tokens))
            for n in range(0, peers, SPAN // tokens)
        ],
        axis=0,
    )
    decay, rate = gate_values(gates, sub, alog_ref, dt_ref)
    early_ref[...] = jnp.where(iota((8, SPAN), 0) < 2, decay[0:8], rate[0:8])
    skipped = later & (iota(gates.shape, 0) < GATES) & (iota(gates.shape, 1) < EDGE)
    decay = jnp.where(skipped, 0.0, decay)
    rate = jnp.where(skipped, 0.0, rate)
    lane_r, lane_c = iota((SPAN, SPAN), 0), iota((SPAN, SPAN), 1)
    upto = jnp.where(lane_r <= lane_c, 1.0, 0.0).astype(BF16)
    d_high, d_rest = halves(decay)
    d_mid, d_low = halves(decay - d_high.astype(F32))
    cum = dot(d_high, upto) + (dot(d_mid, upto) + dot(d_low, upto))
    growth = jnp.exp(cum)
    columns = jnp.transpose(jnp.where(iota(gates.shape, 0) % GATES < 2, cum, rate))
    cum_ref[...] = cum
    cols_ref[...] = columns
    lower = lane_r >= lane_c
    strict = lane_r > lane_c
    keys, keys_t, systems = [], [], []
    for n in range(spans):
        k_n = unit(convolved(rows, n * SPAN + 8 - EDGE, SPAN, slice(0, DK), tap), 1.0)
        keys_ref[n * SPAN : (n + 1) * SPAN, :] = k_n
        kt_n = jnp.transpose(k_n.astype(F32)).astype(BF16)
        gram = dot(k_n, kt_n)
        keys.append(k_n)
        keys_t.append(kt_n)
        for r in range(2):
            at = GATES * n + r
            gap = columns[:, at : at + 1] - cum[at : at + 1, :]
            within = jnp.exp(jnp.where(lower, gap, 0.0))
            systems.append(jnp.where(strict, columns[:, at + 2 : at + 3] * within * gram, 0.0))
    inverses = invert(systems)
    identity = jnp.where(lane_r == lane_c, 1.0, 0.0)
    lins = []
    for n in range(spans):
        for r in range(2):
            at = GATES * n + r
            c_col = columns[:, at : at + 1]
            t_b = inverses[2 * n + r] * rate[at + 2 : at + 3, :]
            tb_ref[r, n] = jnp.concatenate(halves(t_b), axis=1)
            w_mat = mm_left(t_b * growth[at : at + 1, :], keys[n])
            w_ref[r, n * SPAN : (n + 1) * SPAN, :] = w_mat.astype(BF16)
            c_end = c_col[SPAN - 1 : SPAN, :]
            lin = jnp.exp(c_end) * identity - mm_right(keys_t[n], jnp.exp(c_end - c_col) * w_mat)
            lin_ref[r, n] = jnp.concatenate(halves(lin), axis=1)
            lins.append(lin)
    states = [identity, identity]
    for n in range(spans):
        for r in range(2):
            ms_ref[r, n] = states[r].astype(BF16)
            states[r] = lins[r] if n == 0 else mm(lins[2 * n + r], states[r])
    for r in range(2):
        ms_ref[r, spans] = states[r].astype(BF16)


def state_kernel(
    recv_ref, cv_ref, keys_ref, tb_ref, lin_ref, cols_ref, edge_ref, hop_ref, u_ref, xs_ref, raw, rows, sem
):
    sub = lax.axis_index("sub")
    peers = recv_ref.shape[0]
    tokens = recv_ref.shape[1] // 3
    total = peers * tokens
    spans = total // SPAN
    fetch = pltpu.make_async_copy(recv_ref, raw, sem.at[0])
    fetch.start()
    taps = value_taps(sub, cv_ref)
    rows[0:8, :] = jnp.zeros((8, 2 * DV), F32)
    hop_ref[2 * DK + 16 : 2 * DK + 32, :] = edge_ref[...]
    fetch.wait()
    for at, first in ((0, 2 * tokens), (32, 0), (48, tokens)):
        hop_ref[2 * DK + at : 2 * DK + at + 16, :] = raw[
            peers - 1, first + tokens - 16 : first + tokens, :
        ]
    for s in range(peers):
        for r in range(2):
            rows[8 + s * tokens : 8 + (s + 1) * tokens, r * DV : (r + 1) * DV] = raw[
                s, r * tokens : (r + 1) * tokens, :
            ].astype(F32)
    adds = []
    for n in range(spans):
        at = n * SPAN
        kt_n = jnp.transpose(keys_ref[at : at + SPAN, :].astype(F32)).astype(BF16)
        for r in range(2):
            v_n = convolved(
                rows, at + 8 - EDGE, SPAN, slice(r * DV, (r + 1) * DV), taps[r]
            ).astype(BF16)
            u_mat = dot(tb_ref[r, n], jnp.concatenate([v_n, v_n], axis=0))
            u_ref[r, at : at + SPAN, :] = u_mat.astype(BF16)
            c_col = cols_ref[:, GATES * n + r : GATES * n + r + 1]
            adds.append(mm_right(kt_n, jnp.exp(c_col[SPAN - 1 : SPAN, :] - c_col) * u_mat))
    states = [None, None]
    for r in range(2):
        xs_ref[r, 0] = jnp.zeros((DK, DV), BF16)
    for n in range(spans):
        for r in range(2):
            if n == 0:
                states[r] = adds[r]
            else:
                high, low = halves(states[r])
                xs_ref[r, n] = high
                lin = lin_ref[r, n]
                states[r] = (
                    dot(lin, jnp.concatenate([high, high], axis=0))
                    + dot(lin[:, :DK], low)
                    + adds[2 * n + r]
                )
    for r in range(2):
        hop_ref[r * DK : (r + 1) * DK, :] = states[r].astype(BF16)


def output_kernel(
    recv_ref,
    cq_ref,
    keys_ref,
    w_ref,
    u_ref,
    xs_ref,
    ms_ref,
    cols_ref,
    cum_ref,
    oa_ref,
    om_ref,
    raw,
    rows,
    sem,
):
    sub = lax.axis_index("sub")
    peers = recv_ref.shape[0]
    tokens = recv_ref.shape[1] // 3
    total = peers * tokens
    spans = total // SPAN
    fetch = pltpu.make_async_copy(
        recv_ref.at[:, pl.ds(2 * tokens, tokens), :], raw, sem.at[0]
    )
    fetch.start()
    tap = key_tap(sub, cq_ref)
    rows[0:8, :] = jnp.zeros((8, DK), F32)
    fetch.wait()
    rows[8 : 8 + total, :] = raw[...].astype(F32).reshape(total, DK)
    lane_r, lane_c = iota((SPAN, SPAN), 0), iota((SPAN, SPAN), 1)
    lower = lane_r >= lane_c
    for n in range(spans):
        at = n * SPAN
        q_n = unit(convolved(rows, at + 8 - EDGE, SPAN, slice(0, DK), tap), DK**-0.5)
        k_n = keys_ref[at : at + SPAN, :]
        scores = dot(q_n, k_n, ((1,), (1,)))
        for r in range(2):
            c_col = cols_ref[:, GATES * n + r : GATES * n + r + 1]
            c_row = cum_ref[GATES * n + r : GATES * n + r + 1, :]
            within = jnp.exp(jnp.where(lower, c_col - c_row, 0.0))
            inner = jnp.where(lower, within * scores, 0.0).astype(BF16)
            x_n = jnp.concatenate([xs_ref[r, n], ms_ref[r, n]], axis=1)
            held = dot(w_ref[r, at : at + SPAN, :], x_n)
            fresh_a = (u_ref[r, at : at + SPAN, :].astype(F32) - held[:, :DV]).astype(BF16)
            fresh_m = (-held[:, DV:]).astype(BF16)
            out = jnp.exp(c_col) * dot(q_n, x_n) + dot(
                inner, jnp.concatenate([fresh_a, fresh_m], axis=1)
            )
            oa_ref[r, at : at + SPAN, :] = out[:, :DV]
            om_ref[r, at : at + SPAN, :] = out[:, DV:].astype(BF16)


def first_tokens(hop_ref, keys_head, values_head, early_ref, cq_ref, ck_ref, cv_ref, rows):
    sub = lax.axis_index("sub")
    later = lax.axis_index("half") > 0
    tokens = values_head.shape[0] // 3
    opening = [values_head[2 * tokens : 2 * tokens + 16, :], keys_head[GATES : GATES + 16, :]]
    opening += [values_head[r * tokens : r * tokens + 16, :] for r in range(2)]
    taps = [key_tap(sub, cq_ref), key_tap(sub, ck_ref)] + value_taps(sub, cv_ref)
    results = []
    for g in range(4):
        lanes = slice(g * 128, (g + 1) * 128)
        rows[0:16, lanes] = hop_ref[2 * DK + 16 * g : 2 * DK + 16 * (g + 1), :].astype(F32)
        rows[16:32, lanes] = opening[g].astype(F32)
        results.append(convolved(rows, 16 - EDGE, 8, lanes, taps[g]))
    q_cols = jnp.transpose(unit(results[0], DK**-0.5).astype(F32))
    k_cols = jnp.transpose(unit(results[1], 1.0).astype(F32))
    gates = early_ref[...]
    line = iota((8, DV), 0)
    finals, outputs = [], []
    for r in range(2):
        values = results[2 + r].astype(BF16).astype(F32)
        entering = hop_ref[r * DK : (r + 1) * DK, :].astype(F32)
        state, out = entering, jnp.zeros((8, DV), F32)
        for t in range(EDGE):
            k_t, q_t = k_cols[:, t : t + 1], q_cols[:, t : t + 1]
            state = jnp.exp(gates[r : r + 1, t : t + 1]) * state
            held = jnp.sum(k_t * state, axis=0, keepdims=True)
            state = state + k_t * (
                gates[2 + r : 3 + r, t : t + 1] * (values[t : t + 1, :] - held)
            )
            out = jnp.where(line == t, jnp.sum(q_t * state, axis=0, keepdims=True), out)
        finals.append(jnp.where(later, state, entering))
        outputs.append(out)
    return finals, outputs, later


def finish_kernel(
    hop_in,
    keys_head,
    values_head,
    early_ref,
    cq_ref,
    ck_ref,
    cv_ref,
    gain_ref,
    oa_ref,
    om_ref,
    out_ref,
    hop,
    heads_k,
    heads_v,
    oa,
    om,
    made,
    rows,
    sems,
):
    peers, tokens = out_ref.shape[0], out_ref.shape[1]
    total = peers * tokens
    chunks = 4
    part, peer_part = total // chunks, peers // chunks
    first = [
        pltpu.make_async_copy(hop_in, hop, sems.at[0]),
        pltpu.make_async_copy(keys_head.at[0], heads_k, sems.at[1]),
        pltpu.make_async_copy(values_head.at[0], heads_v, sems.at[2]),
    ]
    fetches = []
    for c in range(chunks):
        here = pl.ds(c * part, part)
        fetches.append(
            [
                pltpu.make_async_copy(oa_ref.at[:, here, :], oa.at[:, here, :], sems.at[3 + 2 * c]),
                pltpu.make_async_copy(om_ref.at[:, here, :], om.at[:, here, :], sems.at[4 + 2 * c]),
            ]
        )
    for copy in first:
        copy.start()
    for pair in fetches:
        for copy in pair:
            copy.start()
    for copy in first:
        copy.wait()
    finals, outputs, later = first_tokens(
        hop, heads_k, heads_v, early_ref, cq_ref, ck_ref, cv_ref, rows
    )
    states = [x.astype(BF16) for x in finals]
    gain = gain_ref[...]
    replaced = later & (iota((8, DV), 0) < EDGE)
    stores = []
    for c in range(chunks):
        for copy in fetches[c]:
            copy.wait()
        at = c * part
        for r in range(2):
            core = oa[r, at : at + part, :] + dot(om[r, at : at + part, :], states[r])
            if c == 0:
                core = jnp.concatenate(
                    [jnp.where(replaced, outputs[r], core[0:8]), core[8:]], axis=0
                )
            scale = lax.rsqrt(jnp.mean(core * core, axis=-1, keepdims=True) + EPS)
            normed = (core * scale * gain).astype(BF16)
            made[c * peer_part : (c + 1) * peer_part, :, r * DV : (r + 1) * DV] = normed.reshape(
                peer_part, tokens, DV
            )
        here = pl.ds(c * peer_part, peer_part)
        store = pltpu.make_async_copy(made.at[here], out_ref.at[here], sems.at[3 + 2 * chunks + c])
        store.start()
        stores.append(store)
    for store in stores:
        store.wait()


def advance_kernel(
    hop_in,
    keys_head,
    values_head,
    early_ref,
    cq_ref,
    ck_ref,
    cv_ref,
    hop_own,
    ms_ref,
    next_ref,
    rows,
):
    finals, _, _ = first_tokens(
        hop_in, keys_head.at[0], values_head.at[0], early_ref, cq_ref, ck_ref, cv_ref, rows
    )
    last = ms_ref.shape[1] - 1
    for r in range(2):
        own = hop_own[r * DK : (r + 1) * DK, :].astype(F32)
        next_ref[r * DK : (r + 1) * DK, :] = (mm_right(ms_ref[r, last], finals[r]) + own).astype(
            BF16
        )
    next_ref[2 * DK :, :] = hop_own[2 * DK :, :]


def gate_kernel(heads_axis, normed_ref, z_ref, out_ref, normed, z, made, sems):
    peers, tokens = normed_ref.shape[0], normed_ref.shape[1]
    subs = peers // heads_axis
    width = subs * 2 * DV
    fetches, stores = [], []
    for head in range(heads_axis):
        lanes = pl.ds(head * width, width)
        fetches.append([pltpu.make_async_copy(z_ref.at[:, lanes], z.at[:, lanes], sems.at[0, head])])
    for sub in range(subs):
        here = pl.ds(sub * heads_axis, heads_axis)
        fetches[sub % heads_axis].append(
            pltpu.make_async_copy(normed_ref.at[here], normed.at[here], sems.at[1, sub])
        )
    for copies in fetches:
        for copy in copies:
            copy.start()
    for copies in fetches:
        for copy in copies:
            copy.wait()
    for head in range(heads_axis):
        for sub in range(subs):
            at = (head * subs + sub) * 2 * DV
            gate = silu(z[:, at : at + 2 * DV].astype(F32))
            value = normed[sub * heads_axis + head].astype(F32)
            made[:, at : at + 2 * DV] = (value * gate).astype(BF16)
        lanes = pl.ds(head * width, width)
        store = pltpu.make_async_copy(made.at[:, lanes], out_ref.at[:, lanes], sems.at[2, head])
        store.start()
        stores.append(store)
    for store in stores:
        store.wait()


VMEM = pl.BlockSpec(memory_space=pltpu.VMEM)
SMEM = pl.BlockSpec(memory_space=pltpu.SMEM)
ANY = pl.BlockSpec(memory_space=pl.ANY)


def call(kernel, outs, in_specs, out_specs=None, scratch=(), flops=1 << 26, moved=1 << 21):
    return pl.pallas_call(
        kernel,
        out_shape=outs,
        in_specs=in_specs,
        out_specs=jax.tree.map(lambda _: VMEM, outs) if out_specs is None else out_specs,
        scratch_shapes=list(scratch),
        compiler_params=pltpu.CompilerParams(vmem_limit_bytes=VMEM_BYTES),
        cost_estimate=pl.CostEstimate(flops=flops, bytes_accessed=moved, transcendentals=0),
    )


def local(
    q_rows,
    k_rows,
    v_rows,
    z_rows,
    a_rows,
    b_rows,
    conv_q,
    conv_k,
    conv_v,
    a_log,
    dt_bias,
    norm_gain,
):
    shards, subs, heads_axis = (lax.axis_size(a) for a in ("half", "sub", "head"))
    peers, tokens = subs * heads_axis, q_rows.shape[0]
    total = peers * tokens
    spans = total // SPAN
    group = ("sub", "head")
    route = [(i, i + 1) for i in range(shards - 1)]
    shape = jax.ShapeDtypeStruct
    key_block, value_block = GATES + tokens, 3 * tokens
    packed_keys = call(
        functools.partial(pack_keys_kernel, heads_axis),
        shape((peers, key_block, 128), BF16),
        [VMEM] * 3,
        flops=1 << 20,
    )(k_rows, a_rows.T, b_rows.T)
    key_blocks = lax.all_to_all(packed_keys, group, 0, 0, tiled=True)
    packed_values = call(
        functools.partial(pack_values_kernel, heads_axis),
        shape((peers, value_block, 128), BF16),
        [VMEM] * 2,
        flops=1 << 20,
    )(v_rows, q_rows)
    value_blocks = lax.all_to_all(packed_values, group, 0, 0, tiled=True)
    keys, t_b, w_mats, lins, ms, cols, cum, early, edge = call(
        inverse_kernel,
        (
            shape((total, DK), BF16),
            shape((2, spans, SPAN, 2 * SPAN), BF16),
            shape((2, total, DK), BF16),
            shape((2, spans, DK, 2 * DK), BF16),
            shape((2, spans + 1, DK, DK), BF16),
            shape((SPAN, spans * GATES), F32),
            shape((spans * GATES, SPAN), F32),
            shape((8, SPAN), F32),
            shape((16, 128), BF16),
        ),
        [VMEM, VMEM, SMEM, SMEM],
        scratch=(pltpu.VMEM((8 + total, DK), F32),),
        flops=1 << 32,
    )(key_blocks, conv_k, a_log, dt_bias)
    hop, u_mats, starts = call(
        state_kernel,
        (
            shape((2 * DK + 64, 128), BF16),
            shape((2, total, DV), BF16),
            shape((2, spans, DK, DV), BF16),
        ),
        [ANY] + [VMEM] * 6,
        scratch=(
            pltpu.VMEM((peers, value_block, 128), BF16),
            pltpu.VMEM((8 + total, 2 * DV), F32),
            pltpu.SemaphoreType.DMA((1,)),
        ),
    )(value_blocks, conv_v, keys, t_b, lins, cols, edge)
    entering = lax.ppermute(hop, "half", route)
    out_a, out_m = call(
        output_kernel,
        (shape((2, total, DV), F32), shape((2, total, DV), BF16)),
        [ANY] + [VMEM] * 8,
        scratch=(
            pltpu.VMEM((peers, tokens, 128), BF16),
            pltpu.VMEM((8 + total, DK), F32),
            pltpu.SemaphoreType.DMA((1,)),
        ),
        flops=1 << 32,
    )(value_blocks, conv_q, keys, w_mats, u_mats, starts, ms, cols, cum)
    for _ in range(shards - 2):
        moved = call(
            advance_kernel,
            shape(hop.shape, BF16),
            [VMEM] * 9,
            scratch=(pltpu.VMEM((32, 512), F32),),
        )(entering, key_blocks[:1], value_blocks[:1], early, conv_q, conv_k, conv_v, hop, ms)
        entering = lax.ppermute(moved, "half", route)
    chunks = 4
    normed = call(
        finish_kernel,
        shape((peers, tokens, 2 * DV), BF16),
        [ANY] * 3 + [VMEM] * 5 + [ANY] * 2,
        ANY,
        (
            pltpu.VMEM(hop.shape, BF16),
            pltpu.VMEM((key_block, 128), BF16),
            pltpu.VMEM((value_block, 128), BF16),
            pltpu.VMEM((2, total, DV), F32),
            pltpu.VMEM((2, total, DV), BF16),
            pltpu.VMEM((peers, tokens, 2 * DV), BF16),
            pltpu.VMEM((32, 512), F32),
            pltpu.SemaphoreType.DMA((3 + 3 * chunks,)),
        ),
    )(
        entering,
        key_blocks,
        value_blocks,
        early,
        conv_q,
        conv_k,
        conv_v,
        norm_gain.reshape(1, DV),
        out_a,
        out_m,
    )
    returned = lax.all_to_all(normed, group, 0, 0, tiled=True)
    return call(
        functools.partial(gate_kernel, heads_axis),
        shape(z_rows.shape, BF16),
        [ANY] * 2,
        ANY,
        (
            pltpu.VMEM(normed.shape, BF16),
            pltpu.VMEM(z_rows.shape, BF16),
            pltpu.VMEM(z_rows.shape, BF16),
            pltpu.SemaphoreType.DMA((3, max(heads_axis, subs))),
        ),
    )(returned, z_rows)


def solution(mesh):
    heads_axis = mesh.shape["head"]
    subs = KH // heads_axis
    regrouped = Mesh(
        mesh.devices.reshape(mesh.shape["ctx"] // subs, subs, heads_axis), ("half", "sub", "head")
    )
    row = P(("half", "sub", "head"), None)
    placed = (row,) * 6 + (P(None, "head"),) * 3 + (P("head"),) * 2 + (P(),)
    return jax.shard_map(local, mesh=regrouped, in_specs=placed, out_specs=row, check_vma=False)
```

```python
import functools

import jax
import jax.numpy as jnp
from jax import lax
from jax.experimental import pallas as pl
from jax.experimental.pallas import tpu as pltpu
from jax.sharding import Mesh, PartitionSpec as P

DK = 128
DV = 128
CONV = 4
KH = 16
SUB = 16
SPAN = 128
EDGE = CONV - 1
EPS = 1e-06
F32 = jnp.float32
BF16 = jnp.bfloat16
VMEM_BYTES = 24 * 1024 * 1024
GATES = 16


def dot(a, b, dims=((1,), (0,))):
    return lax.dot_general(a, b, (dims, ((), ())), preferred_element_type=F32)


def halves(x):
    high = x.astype(BF16)
    return high, (x - high.astype(F32)).astype(BF16)


def mm_left(a, b):
    return dot(jnp.concatenate(halves(a), axis=1), jnp.concatenate([b, b], axis=0))


def mm_right(a, b):
    return dot(jnp.concatenate([a, a], axis=1), jnp.concatenate(halves(b), axis=0))


def mm(a, b):
    a_high, a_low = halves(a)
    b_high, b_low = halves(b)
    both = jnp.concatenate([a_high, a_low], axis=1)
    return dot(both, jnp.concatenate([b_high, b_high], axis=0)) + dot(a_high, b_low)


def silu(x):
    return x / (1.0 + jnp.exp(-x))


def unit(y, factor):
    scale = lax.rsqrt(jnp.sum(y * y, axis=-1, keepdims=True) + EPS)
    return (y * scale * factor).astype(BF16)


def iota(shape, dim):
    return lax.broadcasted_iota(jnp.int32, shape, dim)


def pack_kernel(heads_axis, q_ref, k_ref, v_ref, at_ref, bt_ref, out_ref):
    peers, tokens = out_ref.shape[0], q_ref.shape[0]
    subs = peers // heads_axis
    for dest in range(peers):
        key_head = (dest % heads_axis) * subs + dest // heads_axis
        lanes = slice(key_head * DK, (key_head + 1) * DK)
        out_ref[dest, GATES : GATES + tokens, :] = k_ref[:, lanes]
        for r in range(2):
            value_lanes = slice((2 * key_head + r) * DV, (2 * key_head + r + 1) * DV)
            out_ref[dest, GATES + (1 + r) * tokens : GATES + (2 + r) * tokens, :] = v_ref[
                :, value_lanes
            ]
        out_ref[dest, GATES + 3 * tokens :, :] = q_ref[:, lanes]
    value_heads = at_ref.shape[0]
    row, entry = iota((peers * GATES, value_heads), 0), iota((peers * GATES, value_heads), 1)
    dest, which = row // GATES, row % GATES
    first = 2 * ((dest % heads_axis) * subs + dest // heads_axis)
    pick_a = jnp.where((which < 2) & (entry == first + which), 1.0, 0.0).astype(BF16)
    pick_b = jnp.where(
        (which >= 2) & (which < 4) & (entry == first + which - 2), 1.0, 0.0
    ).astype(BF16)
    picked = (dot(pick_a, at_ref[...]) + dot(pick_b, bt_ref[...])).astype(BF16)
    lane_shift = tokens * lax.rem(lax.axis_index("head"), SPAN // tokens)
    place = jnp.where(
        iota((tokens, SPAN), 1) == iota((tokens, SPAN), 0) + lane_shift, 1.0, 0.0
    ).astype(BF16)
    gates = dot(picked, place).astype(BF16)
    for dest in range(peers):
        out_ref[dest, 0:GATES, :] = gates[GATES * dest : GATES * (dest + 1), :]


def invert(systems):
    size = systems[0].shape[0]
    blocks = size // SUB
    row, col = iota((size, size), 0), iota((size, size), 1)
    diagonal = (row // SUB) == (col // SUB)
    compact = jnp.concatenate(
        [
            jnp.sum(jnp.where(diagonal, n, 0.0).reshape(blocks, SUB, size), axis=0)
            for n in systems
        ],
        axis=0,
    )
    count = len(systems)
    lane, line = iota(compact.shape, 1), iota(compact.shape, 0)
    solved = jnp.where(lane % SUB == line % SUB, 1.0, 0.0).reshape(count, SUB, size)
    for m in range(SUB - 1):
        spread = jnp.take_along_axis(compact, (lane // SUB) * SUB + m, axis=1)
        solved = solved - spread.reshape(count, SUB, size) * solved[:, m : m + 1, :]
    inverses = [
        jnp.where(
            diagonal.reshape(blocks, SUB, size), solved[i : i + 1, :, :], 0.0
        ).reshape(size, size)
        for i in range(count)
    ]
    width = SUB
    while width < size:
        odd = [(j, j + width) for j in range(width, size, 2 * width)]

        def rows_of(x):
            return jnp.concatenate([x[lo:hi] for lo, hi in odd], axis=0)

        below = rows_of(
            ((row // (2 * width)) == (col // (2 * width))) & ((col // width) % 2 == 0)
        )
        firsts = [
            mm(jnp.where(below, rows_of(n), 0.0), inv) for n, inv in zip(systems, inverses)
        ]
        zero = jnp.zeros((width, size), F32)
        spreads = []
        for first in firsts:
            parts = []
            for j in range(len(odd)):
                parts += [zero, first[j * width : (j + 1) * width]]
            spreads.append(jnp.concatenate(parts, axis=0))
        seconds = [mm(rows_of(inv), spread) for inv, spread in zip(inverses, spreads)]
        grown = []
        for inv, second in zip(inverses, seconds):
            parts = []
            for j, (lo, hi) in enumerate(odd):
                parts += [inv[lo - width : lo], inv[lo:hi] - second[j * width : (j + 1) * width]]
            grown.append(jnp.concatenate(parts, axis=0))
        inverses = grown
        width *= 2
    return inverses


def gate_values(gates, sub, alog_ref, dt_ref):
    second = iota(gates.shape, 0) % GATES == 1
    a_log = jnp.where(second, alog_ref[2 * sub + 1], alog_ref[2 * sub])
    dt_bias = jnp.where(second, dt_ref[2 * sub + 1], dt_ref[2 * sub])
    shifted = gates + dt_bias
    soft = jnp.maximum(shifted, 0.0) + jnp.log1p(jnp.exp(-jnp.abs(shifted)))
    return -jnp.exp(a_log) * soft, 1.0 / (1.0 + jnp.exp(-gates))


def convolved(rows, at, count, lanes, tap):
    summed = tap[0:1] * rows[at : at + count, lanes]
    for j in range(1, CONV):
        summed = summed + tap[j : j + 1] * rows[at + j : at + j + count, lanes]
    return silu(summed)


def key_tap(sub, tap_ref):
    return tap_ref[:, pl.ds(pl.multiple_of(sub * DK, 128), DK)]


def value_taps(sub, cv_ref):
    lane = pl.multiple_of(sub * 2 * DV, 128)
    return [cv_ref[:, pl.ds(pl.multiple_of(lane + r * DV, 128), DV)] for r in range(2)]


def state_kernel(
    recv_ref,
    ck_ref,
    cv_ref,
    alog_ref,
    dt_ref,
    hop_ref,
    keys_ref,
    w_ref,
    u_ref,
    within_ref,
    xs_ref,
    cols_ref,
    early_ref,
    rows,
):
    sub = lax.axis_index("sub")
    later = lax.axis_index("half") > 0
    peers = recv_ref.shape[0]
    tokens = (recv_ref.shape[1] - GATES) // 4
    total = peers * tokens
    spans = total // SPAN
    starts = [GATES + i * tokens for i in range(4)]
    for at, first in ((0, 3), (16, 0), (32, 1), (48, 2)):
        hop_ref[2 * DK + at : 2 * DK + at + 16, :] = recv_ref[
            peers - 1, starts[first] + tokens - 16 : starts[first] + tokens, :
        ]
    taps = [key_tap(sub, ck_ref)] + value_taps(sub, cv_ref)
    rows[0:8, :] = jnp.zeros((8, 384), F32)
    for s in range(peers):
        for g in range(3):
            rows[8 + s * tokens : 8 + (s + 1) * tokens, g * 128 : (g + 1) * 128] = recv_ref[
                s, starts[g] : starts[g] + tokens, :
            ].astype(F32)
    gates = jnp.concatenate(
        [
            sum(recv_ref[s, 0:GATES, :].astype(F32) for s in range(n, n + SPAN // tokens))
            for n in range(0, peers, SPAN // tokens)
        ],
        axis=0,
    )
    decay, rate = gate_values(gates, sub, alog_ref, dt_ref)
    early_ref[...] = jnp.where(iota((8, SPAN), 0) < 2, decay[0:8], rate[0:8])
    skipped = later & (iota(gates.shape, 0) < GATES) & (iota(gates.shape, 1) < EDGE)
    decay = jnp.where(skipped, 0.0, decay)
    rate = jnp.where(skipped, 0.0, rate)
    lane_r, lane_c = iota((SPAN, SPAN), 0), iota((SPAN, SPAN), 1)
    upto = jnp.where(lane_r <= lane_c, 1.0, 0.0).astype(BF16)
    d_high, d_rest = halves(decay)
    d_mid, d_low = halves(decay - d_high.astype(F32))
    cum = dot(d_high, upto) + (dot(d_mid, upto) + dot(d_low, upto))
    growth = jnp.exp(cum)
    columns = jnp.transpose(jnp.where(iota(gates.shape, 0) % GATES < 2, cum, rate))
    cols_ref[...] = columns
    lower = lane_r >= lane_c
    strict = lane_r > lane_c
    keys, keys_t, systems = [], [], []
    for n in range(spans):
        k_n = unit(convolved(rows, n * SPAN + 8 - EDGE, SPAN, slice(0, DK), taps[0]), 1.0)
        keys_ref[n * SPAN : (n + 1) * SPAN, :] = k_n
        kt_n = jnp.transpose(k_n.astype(F32)).astype(BF16)
        gram = dot(k_n, kt_n)
        keys.append(k_n)
        keys_t.append(kt_n)
        for r in range(2):
            at = GATES * n + r
            gap = columns[:, at : at + 1] - cum[at : at + 1, :]
            within = jnp.where(lower, jnp.exp(jnp.where(lower, gap, 0.0)), 0.0)
            within_ref[r, n * SPAN : (n + 1) * SPAN, :] = within.astype(BF16)
            systems.append(jnp.where(strict, columns[:, at + 2 : at + 3] * within * gram, 0.0))
    inverses = invert(systems)
    identity = jnp.where(lane_r == lane_c, 1.0, 0.0)
    maps = []
    for n in range(spans):
        at_rows = slice(n * SPAN, (n + 1) * SPAN)
        for r in range(2):
            at = GATES * n + r
            c_col = columns[:, at : at + 1]
            v_n = convolved(
                rows, n * SPAN + 8 - EDGE, SPAN, slice((1 + r) * DV, (2 + r) * DV), taps[1 + r]
            ).astype(BF16)
            t_b = inverses[2 * n + r] * rate[at + 2 : at + 3, :]
            w_mat = mm_left(t_b * growth[at : at + 1, :], keys[n])
            u_mat = mm_left(t_b, v_n)
            w_ref[r, at_rows, :] = w_mat.astype(BF16)
            u_ref[r, at_rows, :] = u_mat.astype(BF16)
            c_end = c_col[SPAN - 1 : SPAN, :]
            both = jnp.concatenate([w_mat, u_mat], axis=1)
            moved = mm_right(keys_t[n], jnp.exp(c_end - c_col) * both)
            maps.append((jnp.exp(c_end) * identity - moved[:, :DK], moved[:, DK:]))
    zero_half = jnp.zeros((DK, DV), F32)
    states = [jnp.concatenate([zero_half, identity], axis=1) for r in range(2)]
    for n in range(spans):
        for r in range(2):
            xs_ref[r, n] = states[r].astype(BF16)
            lin, add = maps[2 * n + r]
            if n == 0:
                states[r] = jnp.concatenate([add, lin], axis=1)
            else:
                states[r] = mm(lin, states[r]) + jnp.concatenate([add, zero_half], axis=1)
    for r in range(2):
        xs_ref[r, spans] = states[r].astype(BF16)
        hop_ref[r * DK : (r + 1) * DK, :] = states[r][:, :DV].astype(BF16)


def output_kernel(
    recv_ref, cq_ref, keys_ref, w_ref, u_ref, within_ref, xs_ref, cols_ref, oa_ref, om_ref, rows
):
    sub = lax.axis_index("sub")
    peers = recv_ref.shape[0]
    tokens = (recv_ref.shape[1] - GATES) // 4
    total = peers * tokens
    spans = total // SPAN
    tap = key_tap(sub, cq_ref)
    rows[0:8, :] = jnp.zeros((8, DK), F32)
    for s in range(peers):
        rows[8 + s * tokens : 8 + (s + 1) * tokens, :] = recv_ref[
            s, GATES + 3 * tokens :, :
        ].astype(F32)
    for n in range(spans):
        at = n * SPAN
        q_n = unit(convolved(rows, at + 8 - EDGE, SPAN, slice(0, DK), tap), DK**-0.5)
        scores = dot(q_n, keys_ref[at : at + SPAN, :], ((1,), (1,)))
        for r in range(2):
            c_col = cols_ref[:, GATES * n + r : GATES * n + r + 1]
            inner = (within_ref[r, at : at + SPAN, :].astype(F32) * scores).astype(BF16)
            x_n = xs_ref[r, n]
            held = dot(w_ref[r, at : at + SPAN, :], x_n)
            fresh_a = (u_ref[r, at : at + SPAN, :].astype(F32) - held[:, :DV]).astype(BF16)
            fresh_m = (-held[:, DV:]).astype(BF16)
            out = jnp.exp(c_col) * dot(q_n, x_n) + dot(
                inner, jnp.concatenate([fresh_a, fresh_m], axis=1)
            )
            oa_ref[r, at : at + SPAN, :] = out[:, :DV]
            om_ref[r, at : at + SPAN, :] = out[:, DV:].astype(BF16)


def first_tokens(hop_ref, recv_ref, early_ref, cq_ref, ck_ref, cv_ref, rows):
    sub = lax.axis_index("sub")
    later = lax.axis_index("half") > 0
    tokens = (recv_ref.shape[1] - GATES) // 4
    taps = [key_tap(sub, cq_ref), key_tap(sub, ck_ref)] + value_taps(sub, cv_ref)
    results = []
    for g, first in enumerate((3, 0, 1, 2)):
        lanes = slice(g * 128, (g + 1) * 128)
        start = GATES + first * tokens
        rows[0:16, lanes] = hop_ref[2 * DK + 16 * g : 2 * DK + 16 * (g + 1), :].astype(F32)
        rows[16:32, lanes] = recv_ref[0, start : start + 16, :].astype(F32)
        results.append(convolved(rows, 16 - EDGE, 8, lanes, taps[g]))
    q_cols = jnp.transpose(unit(results[0], DK**-0.5).astype(F32))
    k_cols = jnp.transpose(unit(results[1], 1.0).astype(F32))
    gates = early_ref[...]
    line = iota((8, DV), 0)
    finals, outputs = [], []
    for r in range(2):
        values = results[2 + r].astype(BF16).astype(F32)
        entering = hop_ref[r * DK : (r + 1) * DK, :].astype(F32)
        state, out = entering, jnp.zeros((8, DV), F32)
        for t in range(EDGE):
            k_t, q_t = k_cols[:, t : t + 1], q_cols[:, t : t + 1]
            state = jnp.exp(gates[r : r + 1, t : t + 1]) * state
            held = jnp.sum(k_t * state, axis=0, keepdims=True)
            state = state + k_t * (
                gates[2 + r : 3 + r, t : t + 1] * (values[t : t + 1, :] - held)
            )
            out = jnp.where(line == t, jnp.sum(q_t * state, axis=0, keepdims=True), out)
        finals.append(jnp.where(later, state, entering))
        outputs.append(out)
    return finals, outputs, later


def finish_kernel(
    hop_ref, recv_ref, early_ref, cq_ref, ck_ref, cv_ref, gain_ref, oa_ref, om_ref, out_ref, rows
):
    peers, tokens = out_ref.shape[0], out_ref.shape[1]
    finals, outputs, later = first_tokens(
        hop_ref, recv_ref, early_ref, cq_ref, ck_ref, cv_ref, rows
    )
    states = [x.astype(BF16) for x in finals]
    gain = gain_ref[...]
    replaced = later & (iota((8, DV), 0) < EDGE)
    chunks = 4
    part, peer_part = peers * tokens // chunks, peers // chunks
    for c in range(chunks):
        at = c * part
        for r in range(2):
            core = oa_ref[r, at : at + part, :] + dot(om_ref[r, at : at + part, :], states[r])
            if c == 0:
                core = jnp.concatenate(
                    [jnp.where(replaced, outputs[r], core[0:8]), core[8:]], axis=0
                )
            scale = lax.rsqrt(jnp.mean(core * core, axis=-1, keepdims=True) + EPS)
            normed = (core * scale * gain).astype(BF16)
            out_ref[c * peer_part : (c + 1) * peer_part, :, r * DV : (r + 1) * DV] = (
                normed.reshape(peer_part, tokens, DV)
            )


def advance_kernel(
    hop_ref, recv_ref, early_ref, cq_ref, ck_ref, cv_ref, hop_own, xs_ref, next_ref, rows
):
    finals, _, _ = first_tokens(hop_ref, recv_ref, early_ref, cq_ref, ck_ref, cv_ref, rows)
    last = xs_ref.shape[1] - 1
    for r in range(2):
        own = hop_own[r * DK : (r + 1) * DK, :].astype(F32)
        through = mm_right(xs_ref[r, last][:, DV:], finals[r])
        next_ref[r * DK : (r + 1) * DK, :] = (through + own).astype(BF16)
    next_ref[2 * DK :, :] = hop_own[2 * DK :, :]


def gate_kernel(heads_axis, normed_ref, z_ref, out_ref):
    subs = normed_ref.shape[0] // heads_axis
    for sub in range(subs):
        for head in range(heads_axis):
            at = (head * subs + sub) * 2 * DV
            gate = silu(z_ref[:, at : at + 2 * DV].astype(F32))
            value = normed_ref[sub * heads_axis + head].astype(F32)
            out_ref[:, at : at + 2 * DV] = (value * gate).astype(BF16)


VMEM = pl.BlockSpec(memory_space=pltpu.VMEM)
SMEM = pl.BlockSpec(memory_space=pltpu.SMEM)


def near(x):
    return pltpu.with_memory_space_constraint(x, pltpu.VMEM)


def call(kernel, outs, in_specs, scratch=(), flops=1 << 26, moved=1 << 21):
    return pl.pallas_call(
        kernel,
        out_shape=outs,
        in_specs=in_specs,
        out_specs=jax.tree.map(lambda _: VMEM, outs),
        scratch_shapes=list(scratch),
        compiler_params=pltpu.CompilerParams(vmem_limit_bytes=VMEM_BYTES),
        cost_estimate=pl.CostEstimate(flops=flops, bytes_accessed=moved, transcendentals=0),
    )


def local(
    q_rows,
    k_rows,
    v_rows,
    z_rows,
    a_rows,
    b_rows,
    conv_q,
    conv_k,
    conv_v,
    a_log,
    dt_bias,
    norm_gain,
):
    shards, subs, heads_axis = (lax.axis_size(a) for a in ("half", "sub", "head"))
    peers, tokens = subs * heads_axis, q_rows.shape[0]
    total = peers * tokens
    spans = total // SPAN
    group = ("sub", "head")
    route = [(i, i + 1) for i in range(shards - 1)]
    packed = call(
        functools.partial(pack_kernel, heads_axis),
        pltpu.VMEM((peers, GATES + 4 * tokens, 128), BF16),
        [VMEM] * 5,
        flops=1 << 20,
    )(q_rows, k_rows, v_rows, a_rows.T, b_rows.T)
    blocks = lax.all_to_all(packed, group, 0, 0, tiled=True)
    hop, keys, w_mats, u_mats, within, starts, cols, early = call(
        state_kernel,
        (
            pltpu.VMEM((2 * DK + 64, 128), BF16),
            pltpu.VMEM((total, DK), BF16),
            pltpu.VMEM((2, total, DK), BF16),
            pltpu.VMEM((2, total, DV), BF16),
            pltpu.VMEM((2, total, SPAN), BF16),
            pltpu.VMEM((2, spans + 1, DK, 2 * DV), BF16),
            pltpu.VMEM((SPAN, spans * GATES), F32),
            pltpu.VMEM((8, SPAN), F32),
        ),
        [VMEM, VMEM, VMEM, SMEM, SMEM],
        scratch=(pltpu.VMEM((8 + total, 384), F32),),
        flops=1 << 32,
    )(near(blocks), conv_k, conv_v, a_log, dt_bias)
    entering = lax.ppermute(hop, "half", route)
    out_a, out_m = call(
        output_kernel,
        (pltpu.VMEM((2, total, DV), F32), pltpu.VMEM((2, total, DV), BF16)),
        [VMEM] * 8,
        scratch=(pltpu.VMEM((8 + total, DK), F32),),
        flops=1 << 32,
    )(
        near(blocks),
        conv_q,
        near(keys),
        near(w_mats),
        near(u_mats),
        near(within),
        near(starts),
        near(cols),
    )
    for _ in range(shards - 2):
        moved = call(
            advance_kernel,
            pltpu.VMEM(hop.shape, BF16),
            [VMEM] * 8,
            scratch=(pltpu.VMEM((32, 512), F32),),
        )(near(entering), near(blocks), near(early), conv_q, conv_k, conv_v, near(hop), near(starts))
        entering = lax.ppermute(moved, "half", route)
    normed = call(
        finish_kernel,
        pltpu.VMEM((peers, tokens, 2 * DV), BF16),
        [VMEM] * 9,
        scratch=(pltpu.VMEM((32, 512), F32),),
    )(
        near(entering),
        near(blocks),
        near(early),
        conv_q,
        conv_k,
        conv_v,
        norm_gain.reshape(1, DV),
        near(out_a),
        near(out_m),
    )
    returned = lax.all_to_all(normed, group, 0, 0, tiled=True)
    return call(
        functools.partial(gate_kernel, heads_axis),
        jax.ShapeDtypeStruct(z_rows.shape, BF16),
        [VMEM] * 2,
    )(near(returned), z_rows)


def solution(mesh):
    heads_axis = mesh.shape["head"]
    subs = KH // heads_axis
    regrouped = Mesh(
        mesh.devices.reshape(mesh.shape["ctx"] // subs, subs, heads_axis), ("half", "sub", "head")
    )
    row = P(("half", "sub", "head"), None)
    placed = (row,) * 6 + (P(None, "head"),) * 3 + (P("head"),) * 2 + (P(),)
    return jax.shard_map(local, mesh=regrouped, in_specs=placed, out_specs=row, check_vma=False)
```

```python
import functools

import jax
import jax.numpy as jnp
from jax import lax
from jax.experimental import pallas as pl
from jax.experimental.pallas import tpu as pltpu
from jax.sharding import Mesh, PartitionSpec as P

DK = 128
DV = 128
CONV = 4
KH = 16
SUB = 16
SPAN = 128
EDGE = CONV - 1
EPS = 1e-06
F32 = jnp.float32
BF16 = jnp.bfloat16
VMEM_BYTES = 24 * 1024 * 1024
GATES = 16


def dot(a, b, dims=((1,), (0,))):
    return lax.dot_general(a, b, (dims, ((), ())), preferred_element_type=F32)


def halves(x):
    high = x.astype(BF16)
    return high, (x - high.astype(F32)).astype(BF16)


def mm_right(a, b):
    return dot(jnp.concatenate([a, a], axis=1), jnp.concatenate(halves(b), axis=0))


def mm_parts(a, b):
    both = jnp.concatenate(a, axis=1)
    return dot(both, jnp.concatenate([b[0], b[0]], axis=0)) + dot(a[0], b[1])


def silu(x):
    half = 0.5 * x
    return half + half * jnp.tanh(half)


def unit(y, factor):
    scale = lax.rsqrt(jnp.sum(y * y, axis=-1, keepdims=True) + EPS)
    return (y * scale * factor).astype(BF16)


def iota(shape, dim):
    return lax.broadcasted_iota(jnp.int32, shape, dim)


def pack_kernel(
    heads_axis, q_in, k_in, v_in, at_in, bt_in, out_ref, q_ref, k_ref, v_ref, at_ref, bt_ref, sems
):
    peers, tokens = out_ref.shape[0], q_ref.shape[0]
    pairs = ((at_in, at_ref), (bt_in, bt_ref), (k_in, k_ref), (v_in, v_ref), (q_in, q_ref))
    copies = [pltpu.make_async_copy(a, b, sems.at[i]) for i, (a, b) in enumerate(pairs)]
    for copy in copies:
        copy.start()
    for copy in copies:
        copy.wait()
    subs = peers // heads_axis
    for dest in range(peers):
        key_head = (dest % heads_axis) * subs + dest // heads_axis
        lanes = slice(key_head * DK, (key_head + 1) * DK)
        out_ref[dest, GATES : GATES + tokens, :] = k_ref[:, lanes]
        for r in range(2):
            value_lanes = slice((2 * key_head + r) * DV, (2 * key_head + r + 1) * DV)
            out_ref[dest, GATES + (1 + r) * tokens : GATES + (2 + r) * tokens, :] = v_ref[
                :, value_lanes
            ]
        out_ref[dest, GATES + 3 * tokens :, :] = q_ref[:, lanes]
    value_heads = at_ref.shape[0]
    row, entry = iota((peers * GATES, value_heads), 0), iota((peers * GATES, value_heads), 1)
    dest, which = row // GATES, row % GATES
    first = 2 * ((dest % heads_axis) * subs + dest // heads_axis)
    pick_a = jnp.where((which < 2) & (entry == first + which), 1.0, 0.0).astype(BF16)
    pick_b = jnp.where(
        (which >= 2) & (which < 4) & (entry == first + which - 2), 1.0, 0.0
    ).astype(BF16)
    picked = (dot(pick_a, at_ref[...]) + dot(pick_b, bt_ref[...])).astype(BF16)
    lane_shift = tokens * lax.rem(lax.axis_index("head"), SPAN // tokens)
    place = jnp.where(
        iota((tokens, SPAN), 1) == iota((tokens, SPAN), 0) + lane_shift, 1.0, 0.0
    ).astype(BF16)
    gates = dot(picked, place).astype(BF16)
    for dest in range(peers):
        out_ref[dest, 0:GATES, :] = gates[GATES * dest : GATES * (dest + 1), :]


def invert(systems):
    size = systems[0].shape[0]
    blocks = size // SUB
    row, col = iota((size, size), 0), iota((size, size), 1)
    diagonal = (row // SUB) == (col // SUB)
    compact = jnp.concatenate(
        [
            jnp.sum(jnp.where(diagonal, n, 0.0).reshape(blocks, SUB, size), axis=0)
            for n in systems
        ],
        axis=0,
    )
    count = len(systems)
    lane, line = iota(compact.shape, 1), iota(compact.shape, 0)
    solved = jnp.where(lane % SUB == line % SUB, 1.0, 0.0).reshape(count, SUB, size)
    for m in range(SUB - 1):
        spread = jnp.take_along_axis(compact, (lane // SUB) * SUB + m, axis=1)
        solved = solved - spread.reshape(count, SUB, size) * solved[:, m : m + 1, :]
    inverses = [
        jnp.where(
            diagonal.reshape(blocks, SUB, size), solved[i : i + 1, :, :], 0.0
        ).reshape(size, size)
        for i in range(count)
    ]
    lows = [halves(n) for n in systems]
    parts = [halves(inv) for inv in inverses]
    width = SUB
    while width < size:
        odd = [(j, j + width) for j in range(width, size, 2 * width)]

        def rows_of(x):
            return jnp.concatenate([x[lo:hi] for lo, hi in odd], axis=0)

        def woven(even, x):
            pieces = []
            for j, (lo, hi) in enumerate(odd):
                pieces += [even[lo - width : lo], x[j * width : (j + 1) * width]]
            return jnp.concatenate(pieces, axis=0)

        below = ((row // (2 * width)) == (col // (2 * width))) & ((col // width) % 2 == 0)
        mask = rows_of(jnp.where(below, 1.0, 0.0).astype(BF16))
        blank = jnp.zeros((size, size), BF16)
        firsts = [
            mm_parts((rows_of(n[0]) * mask, rows_of(n[1]) * mask), t) for n, t in zip(lows, parts)
        ]
        spreads = [tuple(woven(blank, x) for x in halves(first)) for first in firsts]
        odds = [(rows_of(t[0]), rows_of(t[1])) for t in parts]
        seconds = [halves(-mm_parts(o, spread)) for o, spread in zip(odds, spreads)]
        parts = [
            tuple(woven(t[i], o[i] + second[i]) for i in range(2))
            for t, o, second in zip(parts, odds, seconds)
        ]
        width *= 2
    return parts


def gate_values(gates, sub, alog_ref, dt_ref):
    second = iota(gates.shape, 0) % GATES == 1
    a_log = jnp.where(second, alog_ref[2 * sub + 1], alog_ref[2 * sub])
    dt_bias = jnp.where(second, dt_ref[2 * sub + 1], dt_ref[2 * sub])
    shifted = gates + dt_bias
    soft = jnp.maximum(shifted, 0.0) + jnp.log1p(jnp.exp(-jnp.abs(shifted)))
    return -jnp.exp(a_log) * soft, 1.0 / (1.0 + jnp.exp(-gates))


def convolved(rows, at, count, lanes, tap):
    summed = tap[0:1] * rows[at : at + count, lanes]
    for j in range(1, CONV):
        summed = summed + tap[j : j + 1] * rows[at + j : at + j + count, lanes]
    return silu(summed)


def key_tap(sub, tap_ref):
    return tap_ref[:, pl.ds(pl.multiple_of(sub * DK, 128), DK)]


def value_taps(sub, cv_ref):
    lane = pl.multiple_of(sub * 2 * DV, 128)
    return [cv_ref[:, pl.ds(pl.multiple_of(lane + r * DV, 128), DV)] for r in range(2)]


def widened(rows, recv_ref, starts, tokens):
    rows[0:8, :] = jnp.zeros((8, rows.shape[1]), F32)
    for s in range(recv_ref.shape[0]):
        for g, start in enumerate(starts):
            rows[8 + s * tokens : 8 + (s + 1) * tokens, g * 128 : (g + 1) * 128] = recv_ref[
                s, start : start + tokens, :
            ].astype(F32)


def keys_kernel(
    recv_ref,
    ck_ref,
    alog_ref,
    dt_ref,
    keys_ref,
    keys_t_ref,
    t_ref,
    lin_ref,
    within_ref,
    cols_ref,
    early_ref,
    rows,
):
    sub = lax.axis_index("sub")
    later = lax.axis_index("half") > 0
    peers = recv_ref.shape[0]
    tokens = (recv_ref.shape[1] - GATES) // 4
    spans = peers * tokens // SPAN
    tap = key_tap(sub, ck_ref)
    widened(rows, recv_ref, [GATES], tokens)
    gates = jnp.concatenate(
        [
            sum(recv_ref[s, 0:GATES, :].astype(F32) for s in range(n, n + SPAN // tokens))
            for n in range(0, peers, SPAN // tokens)
        ],
        axis=0,
    )
    decay, rate = gate_values(gates, sub, alog_ref, dt_ref)
    early_ref[...] = jnp.where(iota((8, SPAN), 0) < 2, decay[0:8], rate[0:8])
    skipped = later & (iota(gates.shape, 0) < GATES) & (iota(gates.shape, 1) < EDGE)
    decay = jnp.where(skipped, 0.0, decay)
    rate = jnp.where(skipped, 0.0, rate)
    lane_r, lane_c = iota((SPAN, SPAN), 0), iota((SPAN, SPAN), 1)
    upto = jnp.where(lane_r <= lane_c, 1.0, 0.0).astype(BF16)
    d_high, d_rest = halves(decay)
    d_mid, d_low = halves(decay - d_high.astype(F32))
    cum = dot(d_high, upto) + (dot(d_mid, upto) + dot(d_low, upto))
    columns = jnp.transpose(jnp.where(iota(gates.shape, 0) % GATES < 2, cum, rate))
    cols_ref[...] = columns
    lower = lane_r >= lane_c
    strict = lane_r > lane_c
    keys, keys_t, systems = [], [], []
    for n in range(spans):
        k_n = unit(convolved(rows, n * SPAN + 8 - EDGE, SPAN, slice(0, DK), tap), 1.0)
        kt_n = jnp.transpose(k_n.astype(F32)).astype(BF16)
        keys_ref[n * SPAN : (n + 1) * SPAN, :] = k_n
        keys_t_ref[n] = kt_n
        gram = dot(k_n, kt_n)
        keys.append(k_n)
        keys_t.append(kt_n)
        for r in range(2):
            at = GATES * n + r
            gap = columns[:, at : at + 1] - cum[at : at + 1, :]
            within = jnp.where(lower, jnp.exp(jnp.where(lower, gap, 0.0)), 0.0)
            within_ref[r, n * SPAN : (n + 1) * SPAN, :] = within.astype(BF16)
            systems.append(jnp.where(strict, columns[:, at + 2 : at + 3] * within * gram, 0.0))
    inverses = invert(systems)
    identity = jnp.where(lane_r == lane_c, 1.0, 0.0)
    for n in range(spans):
        for r in range(2):
            at = GATES * n + r
            c_col = columns[:, at : at + 1]
            t_parts = inverses[2 * n + r]
            t_ref[r, n] = jnp.concatenate(t_parts, axis=1)
            scaled = (columns[:, at + 2 : at + 3] * jnp.exp(c_col)) * keys[n].astype(F32)
            w_mat = mm_parts(t_parts, halves(scaled))
            c_end = c_col[SPAN - 1 : SPAN, :]
            moved = mm_right(keys_t[n], jnp.exp(c_end - c_col) * w_mat)
            lin = jnp.exp(c_end) * identity - moved
            lin_ref[r, n] = jnp.concatenate(halves(lin), axis=1)


def step(lin, parts):
    high, low = parts
    return dot(lin, jnp.concatenate([high, high], axis=0)) + dot(lin[:, :DK], low)


def values_part(recv_ref, cv_ref, keys_t_ref, t_ref, cols_ref, rows, vs):
    sub = lax.axis_index("sub")
    tokens = (recv_ref.shape[1] - GATES) // 4
    spans = t_ref.shape[1]
    taps = value_taps(sub, cv_ref)
    widened(rows, recv_ref, [GATES + tokens, GATES + 2 * tokens], tokens)
    adds = []
    for n in range(spans):
        for r in range(2):
            lanes = slice(r * DV, (r + 1) * DV)
            at = GATES * n + r
            v_n = convolved(rows, n * SPAN + 8 - EDGE, SPAN, lanes, taps[r]).astype(BF16)
            vs[n * SPAN : (n + 1) * SPAN, lanes] = v_n
            t_n = t_ref[r, n]
            high, low = halves(cols_ref[:, at + 2 : at + 3] * v_n.astype(F32))
            u_mat = step(t_n, (high, low))
            c_col = cols_ref[:, at : at + 1]
            adds.append(mm_right(keys_t_ref[n], jnp.exp(c_col[SPAN - 1 : SPAN, :] - c_col) * u_mat))
    return adds


def opening_kernel(
    recv_ref, cv_ref, keys_t_ref, t_ref, lin_ref, cols_ref, hop_ref, vs_ref, xs_ref, rows
):
    first = lax.axis_index("half") == 0
    peers = recv_ref.shape[0]
    tokens = (recv_ref.shape[1] - GATES) // 4
    spans = t_ref.shape[1]
    for at, which in ((0, 3), (16, 0), (32, 1), (48, 2)):
        end = GATES + (which + 1) * tokens
        hop_ref[2 * DK + at : 2 * DK + at + 16, :] = recv_ref[peers - 1, end - 16 : end, :]

    @pl.when(first)
    def _():
        adds = values_part(recv_ref, cv_ref, keys_t_ref, t_ref, cols_ref, rows, vs_ref)
        states = [adds[0], adds[1]]
        for n in range(1, spans):
            for r in range(2):
                parts = halves(states[r])
                xs_ref[r, n] = jnp.concatenate(parts, axis=0)
                states[r] = step(lin_ref[r, n], parts) + adds[2 * n + r]
        for r in range(2):
            hop_ref[r * DK : (r + 1) * DK, :] = states[r].astype(BF16)

    @pl.when(jnp.logical_not(first))
    def _():
        hop_ref[0 : 2 * DK, :] = jnp.zeros((2 * DK, DV), BF16)


def output_kernel(
    recv_ref,
    cq_ref,
    cv_ref,
    keys_ref,
    keys_t_ref,
    t_ref,
    lin_ref,
    within_ref,
    cols_ref,
    hop_ref,
    vs_ref,
    xs_ref,
    oa_ref,
    om_ref,
    last_ref,
    rows,
    query_rows,
    values,
):
    sub = lax.axis_index("sub")
    first = lax.axis_index("half") == 0
    tokens = (recv_ref.shape[1] - GATES) // 4
    spans = t_ref.shape[1]
    tap = key_tap(sub, cq_ref)
    widened(query_rows, recv_ref, [GATES + 3 * tokens], tokens)

    def seen(n):
        at = n * SPAN
        q_n = unit(convolved(query_rows, at + 8 - EDGE, SPAN, slice(0, DK), tap), DK**-0.5)
        k_n = keys_ref[at : at + SPAN, :]
        readers = jnp.concatenate([k_n, q_n], axis=0)
        return readers, dot(q_n, keys_t_ref[n])

    def weights(n, r, scores):
        return (within_ref[r, n * SPAN : (n + 1) * SPAN, :].astype(F32) * scores).astype(BF16)

    def spread(t_n, rest, inner):
        rest = rest.astype(BF16)
        fresh = dot(t_n, jnp.concatenate([rest, rest], axis=0))
        return dot(inner, fresh.astype(BF16))

    @pl.when(first)
    def _():
        for n in range(spans):
            at = slice(n * SPAN, (n + 1) * SPAN)
            readers, scores = seen(n)
            readers = jnp.concatenate([readers, readers], axis=1)
            for r in range(2):
                growth = jnp.exp(cols_ref[:, GATES * n + r : GATES * n + r + 1])
                rate = cols_ref[:, GATES * n + 2 + r : GATES * n + 3 + r]
                value = vs_ref[at, r * DV : (r + 1) * DV].astype(F32)
                inner = weights(n, r, scores)
                if n == 0:
                    oa_ref[r, at, :] = spread(t_ref[r, n], rate * value, inner)
                else:
                    read = dot(readers, xs_ref[r, n])
                    rest = rate * (value - growth * read[:SPAN])
                    oa_ref[r, at, :] = growth * read[SPAN:] + spread(t_ref[r, n], rest, inner)
        for r in range(2):
            last_ref[r, :, 0:DV] = hop_ref[r * DK : (r + 1) * DK, :].astype(F32)
            last_ref[r, :, DV:] = jnp.zeros((DK, DV), F32)

    @pl.when(jnp.logical_not(first))
    def _():
        adds = values_part(recv_ref, cv_ref, keys_t_ref, t_ref, cols_ref, rows, values)
        zero_half = jnp.zeros((SPAN, DV), F32)
        identity = jnp.where(iota((DK, DK), 0) == iota((DK, DK), 1), 1.0, 0.0)
        states = [jnp.concatenate([zero_half, identity], axis=1) for r in range(2)]
        for n in range(spans):
            at = slice(n * SPAN, (n + 1) * SPAN)
            readers, scores = seen(n)
            readers = jnp.concatenate([readers, readers], axis=1)
            for r in range(2):
                parts = halves(states[r])
                growth = jnp.exp(cols_ref[:, GATES * n + r : GATES * n + r + 1])
                rate = cols_ref[:, GATES * n + 2 + r : GATES * n + 3 + r]
                value = values[at, r * DV : (r + 1) * DV].astype(F32)
                inner = weights(n, r, scores)
                read = dot(readers, jnp.concatenate(parts, axis=0))
                rest = rate * (jnp.concatenate([value, zero_half], axis=1) - growth * read[:SPAN])
                out = growth * read[SPAN:] + spread(t_ref[r, n], rest, inner)
                oa_ref[r, at, :] = out[:, :DV]
                om_ref[r, at, :] = out[:, DV:].astype(BF16)
                add = jnp.concatenate([adds[2 * n + r], zero_half], axis=1)
                states[r] = step(lin_ref[r, n], parts) + add
        for r in range(2):
            last_ref[r] = states[r]


def first_tokens(hop_ref, recv_ref, early_ref, cq_ref, ck_ref, cv_ref, rows):
    sub = lax.axis_index("sub")
    later = lax.axis_index("half") > 0
    tokens = (recv_ref.shape[1] - GATES) // 4
    taps = [key_tap(sub, cq_ref), key_tap(sub, ck_ref)] + value_taps(sub, cv_ref)
    results = []
    for g, first in enumerate((3, 0, 1, 2)):
        lanes = slice(g * 128, (g + 1) * 128)
        start = GATES + first * tokens
        rows[0:16, lanes] = hop_ref[2 * DK + 16 * g : 2 * DK + 16 * (g + 1), :].astype(F32)
        rows[16:32, lanes] = recv_ref[0, start : start + 16, :].astype(F32)
        results.append(convolved(rows, 16 - EDGE, 8, lanes, taps[g]))
    q_cols = jnp.transpose(unit(results[0], DK**-0.5).astype(F32))
    k_cols = jnp.transpose(unit(results[1], 1.0).astype(F32))
    gates = early_ref[...]
    line = iota((8, DV), 0)
    finals, outputs = [], []
    for r in range(2):
        values = results[2 + r].astype(BF16).astype(F32)
        entering = hop_ref[r * DK : (r + 1) * DK, :].astype(F32)
        state, out = entering, jnp.zeros((8, DV), F32)
        for t in range(EDGE):
            k_t, q_t = k_cols[:, t : t + 1], q_cols[:, t : t + 1]
            state = jnp.exp(gates[r : r + 1, t : t + 1]) * state
            held = jnp.sum(k_t * state, axis=0, keepdims=True)
            state = state + k_t * (
                gates[2 + r : 3 + r, t : t + 1] * (values[t : t + 1, :] - held)
            )
            out = jnp.where(line == t, jnp.sum(q_t * state, axis=0, keepdims=True), out)
        finals.append(jnp.where(later, state, entering))
        outputs.append(out)
    return finals, outputs, later


def finish_kernel(
    hop_ref, recv_ref, early_ref, cq_ref, ck_ref, cv_ref, gain_ref, oa_ref, om_ref, out_ref, rows
):
    peers, tokens = out_ref.shape[0], out_ref.shape[1]
    finals, outputs, later = first_tokens(
        hop_ref, recv_ref, early_ref, cq_ref, ck_ref, cv_ref, rows
    )
    states = [x.astype(BF16) for x in finals]
    gain = gain_ref[...]
    replaced = later & (iota((8, DV), 0) < EDGE)
    chunks = 4
    part, peer_part = peers * tokens // chunks, peers // chunks
    for c in range(chunks):
        at = c * part
        for r in range(2):
            passed = dot(om_ref[r, at : at + part, :], states[r])
            core = oa_ref[r, at : at + part, :] + jnp.where(later, passed, 0.0)
            if c == 0:
                core = jnp.concatenate(
                    [jnp.where(replaced, outputs[r], core[0:8]), core[8:]], axis=0
                )
            scale = lax.rsqrt(jnp.mean(core * core, axis=-1, keepdims=True) + EPS)
            normed = (core * scale * gain).astype(BF16)
            out_ref[c * peer_part : (c + 1) * peer_part, :, r * DV : (r + 1) * DV] = (
                normed.reshape(peer_part, tokens, DV)
            )


def advance_kernel(
    hop_ref, recv_ref, early_ref, cq_ref, ck_ref, cv_ref, hop_own, last_ref, next_ref, rows
):
    finals, _, _ = first_tokens(hop_ref, recv_ref, early_ref, cq_ref, ck_ref, cv_ref, rows)
    for r in range(2):
        last = last_ref[r]
        through = mm_parts(halves(last[:, DV:]), halves(finals[r]))
        next_ref[r * DK : (r + 1) * DK, :] = (through + last[:, :DV]).astype(BF16)
    next_ref[2 * DK :, :] = hop_own[2 * DK :, :]


def gate_kernel(heads_axis, normed_ref, z_ref, out_ref, made, sems):
    subs = normed_ref.shape[0] // heads_axis
    width = subs * 2 * DV
    copies = []
    for head in range(heads_axis):
        for sub in range(subs):
            at = (head * subs + sub) * 2 * DV
            gate = silu(z_ref[:, at : at + 2 * DV].astype(F32))
            value = normed_ref[sub * heads_axis + head].astype(F32)
            made[:, at : at + 2 * DV] = (value * gate).astype(BF16)
        lanes = pl.ds(head * width, width)
        copy = pltpu.make_async_copy(made.at[:, lanes], out_ref.at[:, lanes], sems.at[head])
        copy.start()
        copies.append(copy)
    for copy in copies:
        copy.wait()


VMEM = pl.BlockSpec(memory_space=pltpu.VMEM)
SMEM = pl.BlockSpec(memory_space=pltpu.SMEM)
ANY = pl.BlockSpec(memory_space=pl.ANY)


def near(x):
    return pltpu.with_memory_space_constraint(x, pltpu.VMEM)


def far(x):
    return pltpu.with_memory_space_constraint(x, pltpu.HBM)


def call(kernel, outs, in_specs, scratch=(), out_spec=VMEM, flops=1 << 26, moved=1 << 21):
    return pl.pallas_call(
        kernel,
        out_shape=outs,
        in_specs=in_specs,
        out_specs=jax.tree.map(lambda _: out_spec, outs),
        scratch_shapes=list(scratch),
        compiler_params=pltpu.CompilerParams(vmem_limit_bytes=VMEM_BYTES),
        cost_estimate=pl.CostEstimate(flops=flops, bytes_accessed=moved, transcendentals=0),
    )


def local(
    q_rows,
    k_rows,
    v_rows,
    z_rows,
    a_rows,
    b_rows,
    conv_q,
    conv_k,
    conv_v,
    a_log,
    dt_bias,
    norm_gain,
):
    shards, subs, heads_axis = (lax.axis_size(a) for a in ("half", "sub", "head"))
    peers, tokens = subs * heads_axis, q_rows.shape[0]
    total = peers * tokens
    spans = total // SPAN
    group = ("sub", "head")
    route = [(i, i + 1) for i in range(shards - 1)]
    inputs = [far(x) for x in (q_rows, k_rows, v_rows, a_rows.T, b_rows.T)]
    packed = call(
        functools.partial(pack_kernel, heads_axis),
        pltpu.VMEM((peers, GATES + 4 * tokens, 128), BF16),
        [ANY] * 5,
        [pltpu.VMEM(x.shape, BF16) for x in inputs] + [pltpu.SemaphoreType.DMA((5,))],
        flops=1 << 20,
    )(*inputs)
    blocks = near(lax.all_to_all(packed, group, 0, 0, tiled=True))
    keys, keys_t, inverses, lins, within, cols, early = call(
        keys_kernel,
        (
            pltpu.VMEM((total, DK), BF16),
            pltpu.VMEM((spans, DK, SPAN), BF16),
            pltpu.VMEM((2, spans, SPAN, 2 * SPAN), BF16),
            pltpu.VMEM((2, spans, DK, 2 * DK), BF16),
            pltpu.VMEM((2, total, SPAN), BF16),
            pltpu.VMEM((SPAN, spans * GATES), F32),
            pltpu.VMEM((8, SPAN), F32),
        ),
        [VMEM, VMEM, SMEM, SMEM],
        [pltpu.VMEM((8 + total, DK), F32)],
        flops=1 << 32,
    )(blocks, conv_k, a_log, dt_bias)
    keys, keys_t, inverses, lins, within, cols, early = (
        near(x) for x in (keys, keys_t, inverses, lins, within, cols, early)
    )
    hop, values, starts = call(
        opening_kernel,
        (
            pltpu.VMEM((2 * DK + 64, 128), BF16),
            pltpu.VMEM((total, 2 * DV), BF16),
            pltpu.VMEM((2, spans, 2 * DK, DV), BF16),
        ),
        [VMEM] * 6,
        [pltpu.VMEM((8 + total, 2 * DV), F32)],
        flops=1 << 32,
    )(blocks, conv_v, keys_t, inverses, lins, cols)
    entering = near(lax.ppermute(hop, "half", route))
    hop, values, starts = near(hop), near(values), near(starts)
    out_a, out_m, last = call(
        output_kernel,
        (
            pltpu.VMEM((2, total, DV), F32),
            pltpu.VMEM((2, total, DV), BF16),
            pltpu.VMEM((2, DK, 2 * DV), F32),
        ),
        [VMEM] * 12,
        [
            pltpu.VMEM((8 + total, 2 * DV), F32),
            pltpu.VMEM((8 + total, DK), F32),
            pltpu.VMEM((total, 2 * DV), BF16),
        ],
        flops=1 << 32,
    )(
        blocks,
        conv_q,
        conv_v,
        keys,
        keys_t,
        inverses,
        lins,
        within,
        cols,
        hop,
        values,
        starts,
    )
    for _ in range(shards - 2):
        moved = call(
            advance_kernel,
            pltpu.VMEM(hop.shape, BF16),
            [VMEM] * 8,
            [pltpu.VMEM((32, 512), F32)],
        )(entering, blocks, early, conv_q, conv_k, conv_v, hop, near(last))
        entering = near(lax.ppermute(moved, "half", route))
    normed = call(
        finish_kernel,
        pltpu.VMEM((peers, tokens, 2 * DV), BF16),
        [VMEM] * 9,
        [pltpu.VMEM((32, 512), F32)],
    )(
        entering,
        blocks,
        early,
        conv_q,
        conv_k,
        conv_v,
        norm_gain.reshape(1, DV),
        near(out_a),
        near(out_m),
    )
    returned = near(lax.all_to_all(normed, group, 0, 0, tiled=True))
    return call(
        functools.partial(gate_kernel, heads_axis),
        jax.ShapeDtypeStruct(z_rows.shape, BF16),
        [VMEM] * 2,
        [pltpu.VMEM(z_rows.shape, BF16), pltpu.SemaphoreType.DMA((heads_axis,))],
        ANY,
    )(returned, z_rows)


def solution(mesh):
    heads_axis = mesh.shape["head"]
    subs = KH // heads_axis
    regrouped = Mesh(
        mesh.devices.reshape(mesh.shape["ctx"] // subs, subs, heads_axis), ("half", "sub", "head")
    )
    row = P(("half", "sub", "head"), None)
    placed = (row,) * 6 + (P(None, "head"),) * 3 + (P("head"),) * 2 + (P(),)
    return jax.shard_map(local, mesh=regrouped, in_specs=placed, out_specs=row, check_vma=False)
```

```python
import functools

import jax
import jax.numpy as jnp
from jax import lax
from jax.experimental import pallas as pl
from jax.experimental.pallas import tpu as pltpu
from jax.sharding import Mesh, PartitionSpec as P

DK = 128
DV = 128
CONV = 4
KH = 16
SUB = 16
SPAN = 128
EDGE = CONV - 1
EPS = 1e-06
F32 = jnp.float32
BF16 = jnp.bfloat16
VMEM_BYTES = 24 * 1024 * 1024
GATES = 16


def dot(a, b, dims=((1,), (0,))):
    return lax.dot_general(a, b, (dims, ((), ())), preferred_element_type=F32)


def halves(x):
    high = x.astype(BF16)
    return high, (x - high.astype(F32)).astype(BF16)


def mm_right(a, b):
    return dot(jnp.concatenate([a, a], axis=1), jnp.concatenate(halves(b), axis=0))


def mm_parts(a, b):
    both = jnp.concatenate(a, axis=1)
    return dot(both, jnp.concatenate([b[0], b[0]], axis=0)) + dot(a[0], b[1])


def silu(x):
    half = 0.5 * x
    return half + half * jnp.tanh(half)


def unit(y, factor):
    scale = lax.rsqrt(jnp.sum(y * y, axis=-1, keepdims=True) + EPS)
    return (y * scale * factor).astype(BF16)


def iota(shape, dim):
    return lax.broadcasted_iota(jnp.int32, shape, dim)


def pack_kernel(
    heads_axis, q_in, k_in, v_in, at_in, bt_in, out_ref, q_ref, k_ref, v_ref, at_ref, bt_ref, sems
):
    peers, tokens = out_ref.shape[0], q_ref.shape[0]
    pairs = ((at_in, at_ref), (bt_in, bt_ref), (k_in, k_ref), (v_in, v_ref), (q_in, q_ref))
    copies = [pltpu.make_async_copy(a, b, sems.at[i]) for i, (a, b) in enumerate(pairs)]
    for copy in copies:
        copy.start()
    for copy in copies:
        copy.wait()
    subs = peers // heads_axis
    for dest in range(peers):
        key_head = (dest % heads_axis) * subs + dest // heads_axis
        lanes = slice(key_head * DK, (key_head + 1) * DK)
        out_ref[dest, GATES : GATES + tokens, :] = k_ref[:, lanes]
        for r in range(2):
            value_lanes = slice((2 * key_head + r) * DV, (2 * key_head + r + 1) * DV)
            out_ref[dest, GATES + (1 + r) * tokens : GATES + (2 + r) * tokens, :] = v_ref[
                :, value_lanes
            ]
        out_ref[dest, GATES + 3 * tokens :, :] = q_ref[:, lanes]
    value_heads = at_ref.shape[0]
    row, entry = iota((peers * GATES, value_heads), 0), iota((peers * GATES, value_heads), 1)
    dest, which = row // GATES, row % GATES
    first = 2 * ((dest % heads_axis) * subs + dest // heads_axis)
    pick_a = jnp.where((which < 2) & (entry == first + which), 1.0, 0.0).astype(BF16)
    pick_b = jnp.where(
        (which >= 2) & (which < 4) & (entry == first + which - 2), 1.0, 0.0
    ).astype(BF16)
    picked = (dot(pick_a, at_ref[...]) + dot(pick_b, bt_ref[...])).astype(BF16)
    lane_shift = tokens * lax.rem(lax.axis_index("head"), SPAN // tokens)
    place = jnp.where(
        iota((tokens, SPAN), 1) == iota((tokens, SPAN), 0) + lane_shift, 1.0, 0.0
    ).astype(BF16)
    gates = dot(picked, place).astype(BF16)
    for dest in range(peers):
        out_ref[dest, 0:GATES, :] = gates[GATES * dest : GATES * (dest + 1), :]


def invert(systems):
    size = systems[0].shape[0]
    blocks = size // SUB
    row, col = iota((size, size), 0), iota((size, size), 1)
    diagonal = (row // SUB) == (col // SUB)
    compact = jnp.concatenate(
        [
            jnp.sum(jnp.where(diagonal, n, 0.0).reshape(blocks, SUB, size), axis=0)
            for n in systems
        ],
        axis=0,
    )
    count = len(systems)
    lane, line = iota(compact.shape, 1), iota(compact.shape, 0)
    solved = jnp.where(lane % SUB == line % SUB, 1.0, 0.0).reshape(count, SUB, size)
    for m in range(SUB - 1):
        spread = jnp.take_along_axis(compact, (lane // SUB) * SUB + m, axis=1)
        solved = solved - spread.reshape(count, SUB, size) * solved[:, m : m + 1, :]
    inverses = [
        jnp.where(
            diagonal.reshape(blocks, SUB, size), solved[i : i + 1, :, :], 0.0
        ).reshape(size, size)
        for i in range(count)
    ]
    lows = [halves(n) for n in systems]
    parts = [halves(inv) for inv in inverses]
    width = SUB
    while width < size:
        odd = [(j, j + width) for j in range(width, size, 2 * width)]

        def rows_of(x):
            return jnp.concatenate([x[lo:hi] for lo, hi in odd], axis=0)

        def woven(even, x):
            pieces = []
            for j, (lo, hi) in enumerate(odd):
                pieces += [even[lo - width : lo], x[j * width : (j + 1) * width]]
            return jnp.concatenate(pieces, axis=0)

        below = ((row // (2 * width)) == (col // (2 * width))) & ((col // width) % 2 == 0)
        mask = rows_of(jnp.where(below, 1.0, 0.0).astype(BF16))
        blank = jnp.zeros((size, size), BF16)
        firsts = [
            mm_parts((rows_of(n[0]) * mask, rows_of(n[1]) * mask), t) for n, t in zip(lows, parts)
        ]
        spreads = [tuple(woven(blank, x) for x in halves(first)) for first in firsts]
        odds = [(rows_of(t[0]), rows_of(t[1])) for t in parts]
        seconds = [halves(-mm_parts(o, spread)) for o, spread in zip(odds, spreads)]
        parts = [
            tuple(woven(t[i], o[i] + second[i]) for i in range(2))
            for t, o, second in zip(parts, odds, seconds)
        ]
        width *= 2
    return parts


def gate_values(gates, sub, alog_ref, dt_ref):
    second = iota(gates.shape, 0) % GATES == 1
    a_log = jnp.where(second, alog_ref[2 * sub + 1], alog_ref[2 * sub])
    dt_bias = jnp.where(second, dt_ref[2 * sub + 1], dt_ref[2 * sub])
    shifted = gates + dt_bias
    soft = jnp.maximum(shifted, 0.0) + jnp.log1p(jnp.exp(-jnp.abs(shifted)))
    return -jnp.exp(a_log) * soft, 1.0 / (1.0 + jnp.exp(-gates))


def convolved(rows, at, count, lanes, tap):
    summed = tap[0:1] * rows[at : at + count, lanes]
    for j in range(1, CONV):
        summed = summed + tap[j : j + 1] * rows[at + j : at + j + count, lanes]
    return silu(summed)


def key_tap(sub, tap_ref):
    return tap_ref[:, pl.ds(pl.multiple_of(sub * DK, 128), DK)]


def value_taps(sub, cv_ref):
    lane = pl.multiple_of(sub * 2 * DV, 128)
    return [cv_ref[:, pl.ds(pl.multiple_of(lane + r * DV, 128), DV)] for r in range(2)]


def widened(rows, recv_ref, starts, tokens):
    rows[0:8, :] = jnp.zeros((8, rows.shape[1]), F32)
    for s in range(recv_ref.shape[0]):
        for g, start in enumerate(starts):
            rows[8 + s * tokens : 8 + (s + 1) * tokens, g * 128 : (g + 1) * 128] = recv_ref[
                s, start : start + tokens, :
            ].astype(F32)


def keys_kernel(
    recv_ref,
    ck_ref,
    alog_ref,
    dt_ref,
    keys_ref,
    keys_t_ref,
    t_ref,
    lin_ref,
    within_ref,
    cols_ref,
    rates_ref,
    early_ref,
    rows,
):
    sub = lax.axis_index("sub")
    later = lax.axis_index("half") > 0
    peers = recv_ref.shape[0]
    tokens = (recv_ref.shape[1] - GATES) // 4
    spans = peers * tokens // SPAN
    tap = key_tap(sub, ck_ref)
    widened(rows, recv_ref, [GATES], tokens)
    gates = jnp.concatenate(
        [
            sum(recv_ref[s, 0:GATES, :].astype(F32) for s in range(n, n + SPAN // tokens))
            for n in range(0, peers, SPAN // tokens)
        ],
        axis=0,
    )
    decay, rate = gate_values(gates, sub, alog_ref, dt_ref)
    early_ref[...] = jnp.where(iota((8, SPAN), 0) < 2, decay[0:8], rate[0:8])
    skipped = later & (iota(gates.shape, 0) < GATES) & (iota(gates.shape, 1) < EDGE)
    decay = jnp.where(skipped, 0.0, decay)
    rate = jnp.where(skipped, 0.0, rate)
    lane_r, lane_c = iota((SPAN, SPAN), 0), iota((SPAN, SPAN), 1)
    upto = jnp.where(lane_r <= lane_c, 1.0, 0.0).astype(BF16)
    d_high, _ = halves(decay)
    d_mid, d_low = halves(decay - d_high.astype(F32))
    cum = dot(d_high, upto) + (dot(d_mid, upto) + dot(d_low, upto))
    growth = jnp.exp(cum)
    here = pltpu.roll(rate, rate.shape[0] - 2, 0)
    rest = jnp.exp(cum[:, SPAN - 1 :] - cum) * here
    which = iota(gates.shape, 0) % GATES
    mixed = jnp.where(which < 2, cum, pltpu.roll(growth, 2, 0))
    columns = jnp.transpose(jnp.where(which < 4, mixed, pltpu.roll(rest, 4, 0)))
    cols_ref[...] = columns
    rates_ref[...] = here
    lower = lane_r >= lane_c
    strict = lane_r > lane_c
    both = [(n, r) for n in range(spans) for r in range(2)]
    keys = []
    for n in range(spans):
        k_n = unit(convolved(rows, n * SPAN + 8 - EDGE, SPAN, slice(0, DK), tap), 1.0)
        keys_ref[n * SPAN : (n + 1) * SPAN, :] = k_n
        keys.append(k_n)
    keys_t = []
    for n in range(spans):
        kt_n = jnp.transpose(keys[n].astype(F32)).astype(BF16)
        keys_t_ref[n] = kt_n
        keys_t.append(kt_n)
    grams = [dot(keys[n], keys_t[n]) for n in range(spans)]
    systems = []
    for n, r in both:
        at = GATES * n + r
        gap = columns[:, at : at + 1] - cum[at : at + 1, :]
        within = jnp.where(lower, jnp.exp(jnp.where(lower, gap, 0.0)), 0.0)
        within_ref[r, n * SPAN : (n + 1) * SPAN, :] = within.astype(BF16)
        systems.append(jnp.where(strict, within * grams[n], 0.0) * here[at : at + 1, :])
    inverses = invert(systems)
    for i, (n, r) in enumerate(both):
        t_ref[r, n] = jnp.concatenate(inverses[i], axis=1)
    scaled = []
    for n, r in both:
        at = GATES * n + r
        scaled.append(halves(columns[:, at + 2 : at + 3] * keys[n].astype(F32)))
    w_mats = [mm_parts(t, x) for t, x in zip(inverses, scaled)]
    weighed = []
    for (n, r), w_mat in zip(both, w_mats):
        at = GATES * n + r
        weighed.append(columns[:, at + 4 : at + 5] * w_mat)
    moved = [
        mm_right(keys_t[n], jnp.concatenate(weighed[2 * n : 2 * n + 2], axis=1))
        for n in range(spans)
    ]
    identity = jnp.where(lane_r == lane_c, 1.0, 0.0)
    for n, r in both:
        at = GATES * n + r
        lin = growth[at : at + 1, SPAN - 1 :] * identity - moved[n][:, r * DK : (r + 1) * DK]
        lin_ref[r, n] = jnp.concatenate(halves(lin), axis=1)


def step(lin, parts):
    high, low = parts
    return dot(lin, jnp.concatenate([high, high], axis=0)) + dot(lin[:, :DK], low)


def values_part(recv_ref, cv_ref, keys_t_ref, t_ref, cols_ref, rows, vs):
    sub = lax.axis_index("sub")
    tokens = (recv_ref.shape[1] - GATES) // 4
    spans = t_ref.shape[1]
    taps = value_taps(sub, cv_ref)
    widened(rows, recv_ref, [GATES + tokens, GATES + 2 * tokens], tokens)
    both = [(n, r) for n in range(spans) for r in range(2)]
    values = []
    for n, r in both:
        lanes = slice(r * DV, (r + 1) * DV)
        v_n = convolved(rows, n * SPAN + 8 - EDGE, SPAN, lanes, taps[r]).astype(BF16)
        vs[n * SPAN : (n + 1) * SPAN, lanes] = v_n
        values.append(jnp.concatenate([v_n, v_n], axis=0))
    solved = [dot(t_ref[r, n], v) for (n, r), v in zip(both, values)]
    weighed = []
    for (n, r), u_mat in zip(both, solved):
        at = GATES * n + r
        weighed.append(cols_ref[:, at + 4 : at + 5] * u_mat)
    moved = [
        mm_right(keys_t_ref[n], jnp.concatenate(weighed[2 * n : 2 * n + 2], axis=1))
        for n in range(spans)
    ]
    return [moved[n][:, r * DV : (r + 1) * DV] for n, r in both]


def opening_kernel(
    recv_ref, cv_ref, keys_t_ref, t_ref, lin_ref, cols_ref, hop_ref, vs_ref, xs_ref, rows
):
    first = lax.axis_index("half") == 0
    peers = recv_ref.shape[0]
    tokens = (recv_ref.shape[1] - GATES) // 4
    spans = t_ref.shape[1]
    for at, which in ((0, 3), (16, 0), (32, 1), (48, 2)):
        end = GATES + (which + 1) * tokens
        hop_ref[2 * DK + at : 2 * DK + at + 16, :] = recv_ref[peers - 1, end - 16 : end, :]

    @pl.when(first)
    def _():
        adds = values_part(recv_ref, cv_ref, keys_t_ref, t_ref, cols_ref, rows, vs_ref)
        states = [adds[0], adds[1]]
        for n in range(1, spans):
            for r in range(2):
                parts = halves(states[r])
                xs_ref[n, :, r * DV : (r + 1) * DV] = jnp.concatenate(parts, axis=0)
                states[r] = step(lin_ref[r, n], parts) + adds[2 * n + r]
        for r in range(2):
            hop_ref[r * DK : (r + 1) * DK, :] = states[r].astype(BF16)

    @pl.when(jnp.logical_not(first))
    def _():
        hop_ref[0 : 2 * DK, :] = jnp.zeros((2 * DK, DV), BF16)


def output_kernel(
    recv_ref,
    cq_ref,
    cv_ref,
    keys_ref,
    keys_t_ref,
    t_ref,
    lin_ref,
    within_ref,
    cols_ref,
    rates_ref,
    hop_ref,
    vs_ref,
    xs_ref,
    oa_ref,
    om_ref,
    last_ref,
    rows,
    query_rows,
    values,
    inner,
    readers,
    states_ref,
):
    sub = lax.axis_index("sub")
    first = lax.axis_index("half") == 0
    tokens = (recv_ref.shape[1] - GATES) // 4
    spans = t_ref.shape[1]
    both = [(n, r) for n in range(spans) for r in range(2)]
    tap = key_tap(sub, cq_ref)
    widened(query_rows, recv_ref, [GATES + 3 * tokens], tokens)

    def span_rows(n):
        return slice(n * SPAN, (n + 1) * SPAN)

    def growth(n, r):
        return cols_ref[:, GATES * n + 2 + r : GATES * n + 3 + r]

    def prepare():
        queries = []
        for n in range(spans):
            at = n * SPAN + 8 - EDGE
            q_n = unit(convolved(query_rows, at, SPAN, slice(0, DK), tap), DK**-0.5)
            queries.append(q_n)
            readers[n, 0:SPAN, :] = keys_ref[span_rows(n), :]
            readers[n, SPAN:, :] = q_n
        scores = [dot(queries[n], keys_t_ref[n]) for n in range(spans)]
        for n, r in both:
            at = GATES * n + r
            weight = within_ref[r, span_rows(n), :].astype(F32) * rates_ref[at : at + 1, :]
            inner[r, n] = (weight * scores[n]).astype(BF16)

    def twice(x, axis):
        return jnp.concatenate([x, x], axis=axis)

    @pl.when(first)
    def _():
        prepare()
        reads = [dot(twice(readers[n], 1), xs_ref[n]) for n in range(1, spans)]
        rests, seen = [], []
        for n, r in both:
            lanes = slice(r * DV, (r + 1) * DV)
            value = vs_ref[span_rows(n), lanes]
            if n == 0:
                rests.append(value)
                seen.append(None)
            else:
                read = growth(n, r) * reads[n - 1][:SPAN, lanes]
                rests.append((value.astype(F32) - read).astype(BF16))
                seen.append(growth(n, r) * reads[n - 1][SPAN:, lanes])
        fresh = [dot(t_ref[r, n], twice(x, 0)).astype(BF16) for (n, r), x in zip(both, rests)]
        spreads = [dot(inner[r, n], x) for (n, r), x in zip(both, fresh)]
        for (n, r), x, y in zip(both, spreads, seen):
            oa_ref[r, span_rows(n), :] = x if y is None else x + y
        for r in range(2):
            last_ref[r, :, 0:DV] = hop_ref[r * DK : (r + 1) * DK, :].astype(F32)
            last_ref[r, :, DV:] = jnp.zeros((DK, DV), F32)

    @pl.when(jnp.logical_not(first))
    def _():
        adds = values_part(recv_ref, cv_ref, keys_t_ref, t_ref, cols_ref, rows, values)
        zero_half = jnp.zeros((DK, DV), F32)
        states = [
            jnp.concatenate(
                [adds[r], lin_ref[r, 0, :, :DK].astype(F32) + lin_ref[r, 0, :, DK:].astype(F32)],
                axis=1,
            )
            for r in range(2)
        ]
        for n in range(1, spans):
            for r in range(2):
                parts = halves(states[r])
                states_ref[r, n] = jnp.concatenate(parts, axis=0)
                add = jnp.concatenate([adds[2 * n + r], zero_half], axis=1)
                states[r] = step(lin_ref[r, n], parts) + add
        for r in range(2):
            last_ref[r] = states[r]
        prepare()
        reads = [
            dot(twice(readers[n], 1), states_ref[r, n]) if n > 0 else None for n, r in both
        ]
        rests, seen = [], []
        for (n, r), read in zip(both, reads):
            value = values[span_rows(n), r * DV : (r + 1) * DV].astype(F32)
            if n == 0:
                known = growth(n, r) * readers[n].astype(F32)[:SPAN]
                asked = growth(n, r) * readers[n].astype(F32)[SPAN:]
                rest = jnp.concatenate([value, -known], axis=1)
                seen.append(jnp.concatenate([zero_half, asked], axis=1))
            else:
                rest = jnp.concatenate([value, zero_half], axis=1) - growth(n, r) * read[:SPAN]
                seen.append(growth(n, r) * read[SPAN:])
            rests.append(rest.astype(BF16))
        fresh = [dot(t_ref[r, n], twice(x, 0)).astype(BF16) for (n, r), x in zip(both, rests)]
        spreads = [dot(inner[r, n], x) for (n, r), x in zip(both, fresh)]
        for (n, r), x, y in zip(both, spreads, seen):
            out = x + y
            oa_ref[r, span_rows(n), :] = out[:, :DV]
            om_ref[r, span_rows(n), :] = out[:, DV:].astype(BF16)


def first_tokens(hop_ref, recv_ref, early_ref, cq_ref, ck_ref, cv_ref, rows):
    sub = lax.axis_index("sub")
    later = lax.axis_index("half") > 0
    tokens = (recv_ref.shape[1] - GATES) // 4
    taps = [key_tap(sub, cq_ref), key_tap(sub, ck_ref)] + value_taps(sub, cv_ref)
    results = []
    for g, first in enumerate((3, 0, 1, 2)):
        lanes = slice(g * 128, (g + 1) * 128)
        start = GATES + first * tokens
        rows[0:16, lanes] = hop_ref[2 * DK + 16 * g : 2 * DK + 16 * (g + 1), :].astype(F32)
        rows[16:32, lanes] = recv_ref[0, start : start + 16, :].astype(F32)
        results.append(convolved(rows, 16 - EDGE, 8, lanes, taps[g]))
    q_cols = jnp.transpose(unit(results[0], DK**-0.5).astype(F32))
    k_cols = jnp.transpose(unit(results[1], 1.0).astype(F32))
    gates = early_ref[...]
    line = iota((8, DV), 0)
    finals, outputs = [], []
    for r in range(2):
        values = results[2 + r].astype(BF16).astype(F32)
        entering = hop_ref[r * DK : (r + 1) * DK, :].astype(F32)
        state, out = entering, jnp.zeros((8, DV), F32)
        for t in range(EDGE):
            k_t, q_t = k_cols[:, t : t + 1], q_cols[:, t : t + 1]
            state = jnp.exp(gates[r : r + 1, t : t + 1]) * state
            held = jnp.sum(k_t * state, axis=0, keepdims=True)
            state = state + k_t * (
                gates[2 + r : 3 + r, t : t + 1] * (values[t : t + 1, :] - held)
            )
            out = jnp.where(line == t, jnp.sum(q_t * state, axis=0, keepdims=True), out)
        finals.append(jnp.where(later, state, entering))
        outputs.append(out)
    return finals, outputs, later


def finish_kernel(
    hop_ref, recv_ref, early_ref, cq_ref, ck_ref, cv_ref, gain_ref, oa_ref, om_ref, out_ref, rows
):
    peers, tokens = out_ref.shape[0], out_ref.shape[1]
    finals, outputs, later = first_tokens(
        hop_ref, recv_ref, early_ref, cq_ref, ck_ref, cv_ref, rows
    )
    states = [x.astype(BF16) for x in finals]
    gain = gain_ref[...]
    replaced = later & (iota((8, DV), 0) < EDGE)
    chunks = 4
    part, peer_part = peers * tokens // chunks, peers // chunks
    for c in range(chunks):
        at = c * part
        for r in range(2):
            passed = dot(om_ref[r, at : at + part, :], states[r])
            core = oa_ref[r, at : at + part, :] + jnp.where(later, passed, 0.0)
            if c == 0:
                core = jnp.concatenate(
                    [jnp.where(replaced, outputs[r], core[0:8]), core[8:]], axis=0
                )
            scale = lax.rsqrt(jnp.mean(core * core, axis=-1, keepdims=True) + EPS)
            normed = (core * scale * gain).astype(BF16)
            out_ref[c * peer_part : (c + 1) * peer_part, :, r * DV : (r + 1) * DV] = (
                normed.reshape(peer_part, tokens, DV)
            )


def advance_kernel(
    hop_ref, recv_ref, early_ref, cq_ref, ck_ref, cv_ref, hop_own, last_ref, next_ref, rows
):
    finals, _, _ = first_tokens(hop_ref, recv_ref, early_ref, cq_ref, ck_ref, cv_ref, rows)
    for r in range(2):
        last = last_ref[r]
        through = mm_parts(halves(last[:, DV:]), halves(finals[r]))
        next_ref[r * DK : (r + 1) * DK, :] = (through + last[:, :DV]).astype(BF16)
    next_ref[2 * DK :, :] = hop_own[2 * DK :, :]


def gate_kernel(heads_axis, normed_ref, z_ref, out_ref, made, sems):
    subs = normed_ref.shape[0] // heads_axis
    width = subs * 2 * DV
    copies = []
    for head in range(heads_axis):
        for sub in range(subs):
            at = (head * subs + sub) * 2 * DV
            gate = silu(z_ref[:, at : at + 2 * DV].astype(F32))
            value = normed_ref[sub * heads_axis + head].astype(F32)
            made[:, at : at + 2 * DV] = (value * gate).astype(BF16)
        lanes = pl.ds(head * width, width)
        copy = pltpu.make_async_copy(made.at[:, lanes], out_ref.at[:, lanes], sems.at[head])
        copy.start()
        copies.append(copy)
    for copy in copies:
        copy.wait()


VMEM = pl.BlockSpec(memory_space=pltpu.VMEM)
SMEM = pl.BlockSpec(memory_space=pltpu.SMEM)
ANY = pl.BlockSpec(memory_space=pl.ANY)


def near(x):
    return pltpu.with_memory_space_constraint(x, pltpu.VMEM)


def far(x):
    return pltpu.with_memory_space_constraint(x, pltpu.HBM)


def call(kernel, outs, in_specs, scratch=(), out_spec=VMEM, flops=1 << 26, moved=1 << 21):
    return pl.pallas_call(
        kernel,
        out_shape=outs,
        in_specs=in_specs,
        out_specs=jax.tree.map(lambda _: out_spec, outs),
        scratch_shapes=list(scratch),
        compiler_params=pltpu.CompilerParams(vmem_limit_bytes=VMEM_BYTES),
        cost_estimate=pl.CostEstimate(flops=flops, bytes_accessed=moved, transcendentals=0),
    )


def local(
    q_rows,
    k_rows,
    v_rows,
    z_rows,
    a_rows,
    b_rows,
    conv_q,
    conv_k,
    conv_v,
    a_log,
    dt_bias,
    norm_gain,
):
    shards, subs, heads_axis = (lax.axis_size(a) for a in ("half", "sub", "head"))
    peers, tokens = subs * heads_axis, q_rows.shape[0]
    total = peers * tokens
    spans = total // SPAN
    group = ("sub", "head")
    route = [(i, i + 1) for i in range(shards - 1)]
    inputs = [far(x) for x in (q_rows, k_rows, v_rows, a_rows.T, b_rows.T)]
    packed = call(
        functools.partial(pack_kernel, heads_axis),
        pltpu.VMEM((peers, GATES + 4 * tokens, 128), BF16),
        [ANY] * 5,
        [pltpu.VMEM(x.shape, BF16) for x in inputs] + [pltpu.SemaphoreType.DMA((5,))],
        flops=1 << 20,
    )(*inputs)
    blocks = near(lax.all_to_all(packed, group, 0, 0, tiled=True))
    keys, keys_t, inverses, lins, within, cols, rates, early = call(
        keys_kernel,
        (
            pltpu.VMEM((total, DK), BF16),
            pltpu.VMEM((spans, DK, SPAN), BF16),
            pltpu.VMEM((2, spans, SPAN, 2 * SPAN), BF16),
            pltpu.VMEM((2, spans, DK, 2 * DK), BF16),
            pltpu.VMEM((2, total, SPAN), BF16),
            pltpu.VMEM((SPAN, spans * GATES), F32),
            pltpu.VMEM((spans * GATES, SPAN), F32),
            pltpu.VMEM((8, SPAN), F32),
        ),
        [VMEM, VMEM, SMEM, SMEM],
        [pltpu.VMEM((8 + total, DK), F32)],
        flops=1 << 32,
    )(blocks, conv_k, a_log, dt_bias)
    keys, keys_t, inverses, lins, within, cols, rates, early = (
        near(x) for x in (keys, keys_t, inverses, lins, within, cols, rates, early)
    )
    hop, values, starts = call(
        opening_kernel,
        (
            pltpu.VMEM((2 * DK + 64, 128), BF16),
            pltpu.VMEM((total, 2 * DV), BF16),
            pltpu.VMEM((spans, 2 * DK, 2 * DV), BF16),
        ),
        [VMEM] * 6,
        [pltpu.VMEM((8 + total, 2 * DV), F32)],
        flops=1 << 32,
    )(blocks, conv_v, keys_t, inverses, lins, cols)
    entering = near(lax.ppermute(hop, "half", route))
    hop, values, starts = near(hop), near(values), near(starts)
    out_a, out_m, last = call(
        output_kernel,
        (
            pltpu.VMEM((2, total, DV), F32),
            pltpu.VMEM((2, total, DV), BF16),
            pltpu.VMEM((2, DK, 2 * DV), F32),
        ),
        [VMEM] * 13,
        [
            pltpu.VMEM((8 + total, 2 * DV), F32),
            pltpu.VMEM((8 + total, DK), F32),
            pltpu.VMEM((total, 2 * DV), BF16),
            pltpu.VMEM((2, spans, SPAN, SPAN), BF16),
            pltpu.VMEM((spans, 2 * SPAN, DK), BF16),
            pltpu.VMEM((2, spans, 2 * DK, 2 * DV), BF16),
        ],
        flops=1 << 32,
    )(
        blocks,
        conv_q,
        conv_v,
        keys,
        keys_t,
        inverses,
        lins,
        within,
        cols,
        rates,
        hop,
        values,
        starts,
    )
    for _ in range(shards - 2):
        moved = call(
            advance_kernel,
            pltpu.VMEM(hop.shape, BF16),
            [VMEM] * 8,
            [pltpu.VMEM((32, 512), F32)],
        )(entering, blocks, early, conv_q, conv_k, conv_v, hop, near(last))
        entering = near(lax.ppermute(moved, "half", route))
    normed = call(
        finish_kernel,
        pltpu.VMEM((peers, tokens, 2 * DV), BF16),
        [VMEM] * 9,
        [pltpu.VMEM((32, 512), F32)],
    )(
        entering,
        blocks,
        early,
        conv_q,
        conv_k,
        conv_v,
        norm_gain.reshape(1, DV),
        near(out_a),
        near(out_m),
    )
    returned = near(lax.all_to_all(normed, group, 0, 0, tiled=True))
    return call(
        functools.partial(gate_kernel, heads_axis),
        jax.ShapeDtypeStruct(z_rows.shape, BF16),
        [VMEM] * 2,
        [pltpu.VMEM(z_rows.shape, BF16), pltpu.SemaphoreType.DMA((heads_axis,))],
        ANY,
    )(returned, z_rows)


def solution(mesh):
    heads_axis = mesh.shape["head"]
    subs = KH // heads_axis
    regrouped = Mesh(
        mesh.devices.reshape(mesh.shape["ctx"] // subs, subs, heads_axis), ("half", "sub", "head")
    )
    row = P(("half", "sub", "head"), None)
    placed = (row,) * 6 + (P(None, "head"),) * 3 + (P("head"),) * 2 + (P(),)
    return jax.shard_map(local, mesh=regrouped, in_specs=placed, out_specs=row, check_vma=False)
```

```python
import functools

import jax
import jax.numpy as jnp
from jax import lax
from jax.experimental import pallas as pl
from jax.experimental.pallas import tpu as pltpu
from jax.sharding import Mesh, PartitionSpec as P

DK = 128
DV = 128
CONV = 4
KH = 16
SUB = 16
SPAN = 128
EDGE = CONV - 1
EPS = 1e-06
F32 = jnp.float32
BF16 = jnp.bfloat16
VMEM_BYTES = 24 * 1024 * 1024
GATES = 16


def dot(a, b, dims=((1,), (0,))):
    return lax.dot_general(a, b, (dims, ((), ())), preferred_element_type=F32)


def halves(x):
    high = x.astype(BF16)
    return high, (x - high.astype(F32)).astype(BF16)


def mm_right(a, b):
    return dot(jnp.concatenate([a, a], axis=1), jnp.concatenate(halves(b), axis=0))


def mm_parts(a, b):
    both = jnp.concatenate(a, axis=1)
    return dot(both, jnp.concatenate([b[0], b[0]], axis=0)) + dot(a[0], b[1])


def silu(x):
    half = 0.5 * x
    return half + half * jnp.tanh(half)


def unit(y, factor):
    scale = lax.rsqrt(jnp.sum(y * y, axis=-1, keepdims=True) + EPS)
    return (y * scale * factor).astype(BF16)


def iota(shape, dim):
    return lax.broadcasted_iota(jnp.int32, shape, dim)


def pack_kernel(
    heads_axis, q_in, k_in, v_in, at_in, bt_in, out_ref, q_ref, k_ref, v_ref, at_ref, bt_ref, sems
):
    peers, tokens = out_ref.shape[0], q_ref.shape[0]
    pairs = ((at_in, at_ref), (bt_in, bt_ref), (k_in, k_ref), (v_in, v_ref), (q_in, q_ref))
    copies = [pltpu.make_async_copy(a, b, sems.at[i]) for i, (a, b) in enumerate(pairs)]
    for copy in copies:
        copy.start()
    subs = peers // heads_axis
    key_heads = [(dest % heads_axis) * subs + dest // heads_axis for dest in range(peers)]
    for copy in copies[:2]:
        copy.wait()
    value_heads = at_ref.shape[0]
    row, entry = iota((peers * GATES, value_heads), 0), iota((peers * GATES, value_heads), 1)
    dest, which = row // GATES, row % GATES
    first = 2 * ((dest % heads_axis) * subs + dest // heads_axis)
    pick_a = jnp.where((which < 2) & (entry == first + which), 1.0, 0.0).astype(BF16)
    pick_b = jnp.where(
        (which >= 2) & (which < 4) & (entry == first + which - 2), 1.0, 0.0
    ).astype(BF16)
    picked = (dot(pick_a, at_ref[...]) + dot(pick_b, bt_ref[...])).astype(BF16)
    lane_shift = tokens * lax.rem(lax.axis_index("head"), SPAN // tokens)
    place = jnp.where(
        iota((tokens, SPAN), 1) == iota((tokens, SPAN), 0) + lane_shift, 1.0, 0.0
    ).astype(BF16)
    gates = dot(picked, place).astype(BF16)
    for dest in range(peers):
        out_ref[dest, 0:GATES, :] = gates[GATES * dest : GATES * (dest + 1), :]

    def laid(ref, lane, start):
        for dest, key_head in enumerate(key_heads):
            at = lane(key_head) * 128
            out_ref[dest, GATES + start * tokens : GATES + (start + 1) * tokens, :] = ref[
                :, at : at + 128
            ]

    copies[2].wait()
    laid(k_ref, lambda key_head: key_head, 0)
    copies[3].wait()
    laid(v_ref, lambda key_head: 2 * key_head, 1)
    laid(v_ref, lambda key_head: 2 * key_head + 1, 2)
    copies[4].wait()
    laid(q_ref, lambda key_head: key_head, 3)


def invert(systems):
    size = systems[0].shape[0]
    blocks = size // SUB
    row, col = iota((size, size), 0), iota((size, size), 1)
    diagonal = (row // SUB) == (col // SUB)
    compact = jnp.concatenate(
        [
            jnp.sum(jnp.where(diagonal, n, 0.0).reshape(blocks, SUB, size), axis=0)
            for n in systems
        ],
        axis=0,
    )
    count = len(systems)
    lane, line = iota(compact.shape, 1), iota(compact.shape, 0)
    solved = jnp.where(lane % SUB == line % SUB, 1.0, 0.0).reshape(count, SUB, size)
    for m in range(SUB - 1):
        spread = jnp.take_along_axis(compact, (lane // SUB) * SUB + m, axis=1)
        solved = solved - spread.reshape(count, SUB, size) * solved[:, m : m + 1, :]
    lows = [halves(n) for n in systems]
    placed = jnp.where(diagonal, 1.0, 0.0).astype(BF16)
    parts = [
        tuple(jnp.concatenate([x] * blocks, axis=0) * placed for x in halves(solved[i]))
        for i in range(count)
    ]
    width = SUB
    while width < size:
        odd = [(j, j + width) for j in range(width, size, 2 * width)]

        def rows_of(x):
            return jnp.concatenate([x[lo:hi] for lo, hi in odd], axis=0)

        def woven(even, x):
            pieces = []
            for j, (lo, hi) in enumerate(odd):
                pieces += [even[lo - width : lo], x[j * width : (j + 1) * width]]
            return jnp.concatenate(pieces, axis=0)

        below = ((row // (2 * width)) == (col // (2 * width))) & ((col // width) % 2 == 0)
        mask = rows_of(jnp.where(below, 1.0, 0.0).astype(BF16))
        blank = jnp.zeros((size, size), BF16)
        firsts = [
            mm_parts((rows_of(n[0]) * mask, rows_of(n[1]) * mask), t) for n, t in zip(lows, parts)
        ]
        spreads = [tuple(woven(blank, x) for x in halves(first)) for first in firsts]
        odds = [(rows_of(t[0]), rows_of(t[1])) for t in parts]
        seconds = [halves(-mm_parts(o, spread)) for o, spread in zip(odds, spreads)]
        parts = [
            tuple(woven(t[i], o[i] + second[i]) for i in range(2))
            for t, o, second in zip(parts, odds, seconds)
        ]
        width *= 2
    return parts


def gate_values(gates, sub, alog_ref, dt_ref):
    second = iota(gates.shape, 0) % GATES == 1
    a_log = jnp.where(second, alog_ref[2 * sub + 1], alog_ref[2 * sub])
    dt_bias = jnp.where(second, dt_ref[2 * sub + 1], dt_ref[2 * sub])
    shifted = gates + dt_bias
    soft = jnp.maximum(shifted, 0.0) + jnp.log1p(jnp.exp(-jnp.abs(shifted)))
    return -jnp.exp(a_log) * soft, 1.0 / (1.0 + jnp.exp(-gates))


def convolved(rows, at, count, lanes, tap):
    summed = tap[0:1] * rows[at : at + count, lanes]
    for j in range(1, CONV):
        summed = summed + tap[j : j + 1] * rows[at + j : at + j + count, lanes]
    return silu(summed)


def key_tap(sub, tap_ref):
    return tap_ref[:, pl.ds(pl.multiple_of(sub * DK, 128), DK)]


def value_taps(sub, cv_ref):
    lane = pl.multiple_of(sub * 2 * DV, 128)
    return [cv_ref[:, pl.ds(pl.multiple_of(lane + r * DV, 128), DV)] for r in range(2)]


def widened(rows, recv_ref, starts, tokens):
    rows[0:8, :] = jnp.zeros((8, rows.shape[1]), F32)
    for s in range(recv_ref.shape[0]):
        for g, start in enumerate(starts):
            rows[8 + s * tokens : 8 + (s + 1) * tokens, g * 128 : (g + 1) * 128] = recv_ref[
                s, start : start + tokens, :
            ].astype(F32)


def keys_kernel(
    recv_ref,
    ck_ref,
    alog_ref,
    dt_ref,
    keys_ref,
    keys_t_ref,
    t_ref,
    lin_ref,
    within_ref,
    cols_ref,
    early_ref,
    rows,
):
    sub = lax.axis_index("sub")
    later = lax.axis_index("half") > 0
    peers = recv_ref.shape[0]
    tokens = (recv_ref.shape[1] - GATES) // 4
    spans = peers * tokens // SPAN
    tap = key_tap(sub, ck_ref)
    widened(rows, recv_ref, [GATES], tokens)
    gates = jnp.concatenate(
        [
            sum(recv_ref[s, 0:GATES, :].astype(F32) for s in range(n, n + SPAN // tokens))
            for n in range(0, peers, SPAN // tokens)
        ],
        axis=0,
    )
    decay, rate = gate_values(gates, sub, alog_ref, dt_ref)
    early_ref[...] = jnp.where(iota((8, SPAN), 0) < 2, decay[0:8], rate[0:8])
    skipped = later & (iota(gates.shape, 0) < GATES) & (iota(gates.shape, 1) < EDGE)
    decay = jnp.where(skipped, 0.0, decay)
    rate = jnp.where(skipped, 0.0, rate)
    lane_r, lane_c = iota((SPAN, SPAN), 0), iota((SPAN, SPAN), 1)
    upto = jnp.where(lane_r <= lane_c, 1.0, 0.0).astype(BF16)
    d_high, _ = halves(decay)
    d_mid, d_low = halves(decay - d_high.astype(F32))
    cum = dot(d_high, upto) + (dot(d_mid, upto) + dot(d_low, upto))
    growth = jnp.exp(cum)
    here = pltpu.roll(rate, rate.shape[0] - 2, 0)
    rest = jnp.exp(cum[:, SPAN - 1 :] - cum) * here
    which = iota(gates.shape, 0) % GATES
    mixed = jnp.where(which < 2, cum, pltpu.roll(growth, 2, 0))
    columns = jnp.transpose(jnp.where(which < 4, mixed, pltpu.roll(rest, 4, 0)))
    cols_ref[...] = columns
    lower = lane_r >= lane_c
    strict = lane_r > lane_c
    both = [(n, r) for n in range(spans) for r in range(2)]
    keys = []
    for n in range(spans):
        k_n = unit(convolved(rows, n * SPAN + 8 - EDGE, SPAN, slice(0, DK), tap), 1.0)
        keys_ref[n * SPAN : (n + 1) * SPAN, :] = k_n
        keys.append(k_n)
    keys_t = []
    for n in range(spans):
        kt_n = jnp.transpose(keys[n].astype(F32)).astype(BF16)
        keys_t_ref[n] = kt_n
        keys_t.append(kt_n)
    grams = [dot(keys[n], keys_t[n]) for n in range(spans)]
    systems = []
    for n, r in both:
        at = GATES * n + r
        gap = columns[:, at : at + 1] - cum[at : at + 1, :]
        within = jnp.exp(jnp.where(lower, gap, 0.0)) * here[at : at + 1, :]
        within_ref[r, n * SPAN : (n + 1) * SPAN, :] = jnp.where(lower, within, 0.0).astype(BF16)
        systems.append(jnp.where(strict, within * grams[n], 0.0))
    inverses = invert(systems)
    for i, (n, r) in enumerate(both):
        t_ref[r, n] = jnp.concatenate(inverses[i], axis=1)
    scaled = []
    for n, r in both:
        at = GATES * n + r
        scaled.append(halves(columns[:, at + 2 : at + 3] * keys[n].astype(F32)))
    w_mats = [mm_parts(t, x) for t, x in zip(inverses, scaled)]
    weighed = []
    for (n, r), w_mat in zip(both, w_mats):
        at = GATES * n + r
        weighed.append(columns[:, at + 4 : at + 5] * w_mat)
    moved = [
        mm_right(keys_t[n], jnp.concatenate(weighed[2 * n : 2 * n + 2], axis=1))
        for n in range(spans)
    ]
    identity = jnp.where(lane_r == lane_c, 1.0, 0.0)
    for n, r in both:
        at = GATES * n + r
        lin = growth[at : at + 1, SPAN - 1 :] * identity - moved[n][:, r * DK : (r + 1) * DK]
        lin_ref[r, n] = jnp.concatenate(halves(lin), axis=1)


def step(lin, parts):
    high, low = parts
    return dot(lin, jnp.concatenate([high, high], axis=0)) + dot(lin[:, :DK], low)


def values_part(recv_ref, cv_ref, keys_t_ref, t_ref, cols_ref, rows, vs):
    sub = lax.axis_index("sub")
    tokens = (recv_ref.shape[1] - GATES) // 4
    spans = t_ref.shape[1]
    taps = value_taps(sub, cv_ref)
    widened(rows, recv_ref, [GATES + tokens, GATES + 2 * tokens], tokens)
    both = [(n, r) for n in range(spans) for r in range(2)]
    values = []
    for n, r in both:
        lanes = slice(r * DV, (r + 1) * DV)
        v_n = convolved(rows, n * SPAN + 8 - EDGE, SPAN, lanes, taps[r]).astype(BF16)
        vs[n * SPAN : (n + 1) * SPAN, lanes] = v_n
        values.append(jnp.concatenate([v_n, v_n], axis=0))
    solved = [dot(t_ref[r, n], v) for (n, r), v in zip(both, values)]
    weighed = []
    for (n, r), u_mat in zip(both, solved):
        at = GATES * n + r
        weighed.append(cols_ref[:, at + 4 : at + 5] * u_mat)
    moved = [
        mm_right(keys_t_ref[n], jnp.concatenate(weighed[2 * n : 2 * n + 2], axis=1))
        for n in range(spans)
    ]
    return [moved[n][:, r * DV : (r + 1) * DV] for n, r in both]


def opening_kernel(
    recv_ref, cv_ref, keys_t_ref, t_ref, lin_ref, cols_ref, hop_ref, vs_ref, xs_ref, rows
):
    first = lax.axis_index("half") == 0
    peers = recv_ref.shape[0]
    tokens = (recv_ref.shape[1] - GATES) // 4
    spans = t_ref.shape[1]
    edges = []
    for which in (3, 0, 1, 2):
        end = GATES + (which + 1) * tokens
        edges.append(recv_ref[peers - 1, end - 16 : end, :].astype(F32)[16 - EDGE :])
    edges.append(jnp.zeros((16 - 4 * EDGE, 128), F32))
    hop_ref[2 * DK :, :] = jnp.concatenate(edges, axis=0).astype(BF16)

    @pl.when(first)
    def _():
        adds = values_part(recv_ref, cv_ref, keys_t_ref, t_ref, cols_ref, rows, vs_ref)
        states = [adds[0], adds[1]]
        for n in range(1, spans):
            for r in range(2):
                parts = halves(states[r])
                xs_ref[n, :, r * DV : (r + 1) * DV] = jnp.concatenate(parts, axis=0)
                states[r] = step(lin_ref[r, n], parts) + adds[2 * n + r]
        for r in range(2):
            hop_ref[r * DK : (r + 1) * DK, :] = states[r].astype(BF16)

    @pl.when(jnp.logical_not(first))
    def _():
        hop_ref[0 : 2 * DK, :] = jnp.zeros((2 * DK, DV), BF16)


def output_kernel(
    recv_ref,
    cq_ref,
    cv_ref,
    keys_ref,
    keys_t_ref,
    t_ref,
    lin_ref,
    within_ref,
    cols_ref,
    hop_ref,
    vs_ref,
    xs_ref,
    oa_ref,
    om_ref,
    last_ref,
    rows,
    query_rows,
    values,
    inner,
    readers,
    states_ref,
):
    sub = lax.axis_index("sub")
    first = lax.axis_index("half") == 0
    tokens = (recv_ref.shape[1] - GATES) // 4
    spans = t_ref.shape[1]
    both = [(n, r) for n in range(spans) for r in range(2)]
    tap = key_tap(sub, cq_ref)
    widened(query_rows, recv_ref, [GATES + 3 * tokens], tokens)

    def span_rows(n):
        return slice(n * SPAN, (n + 1) * SPAN)

    def growth(n, r):
        return cols_ref[:, GATES * n + 2 + r : GATES * n + 3 + r]

    def prepare():
        queries = []
        for n in range(spans):
            at = n * SPAN + 8 - EDGE
            q_n = unit(convolved(query_rows, at, SPAN, slice(0, DK), tap), DK**-0.5)
            queries.append(q_n)
            readers[n, 0:SPAN, :] = keys_ref[span_rows(n), :]
            readers[n, SPAN:, :] = q_n
        scores = [dot(queries[n], keys_t_ref[n]) for n in range(spans)]
        for n, r in both:
            weight = within_ref[r, span_rows(n), :].astype(F32)
            inner[r, n] = (weight * scores[n]).astype(BF16)

    def twice(x, axis):
        return jnp.concatenate([x, x], axis=axis)

    @pl.when(first)
    def _():
        prepare()
        reads = [dot(twice(readers[n], 1), xs_ref[n]) for n in range(1, spans)]
        rests, seen = [], []
        for n, r in both:
            lanes = slice(r * DV, (r + 1) * DV)
            value = vs_ref[span_rows(n), lanes]
            if n == 0:
                rests.append(value)
                seen.append(None)
            else:
                read = growth(n, r) * reads[n - 1][:SPAN, lanes]
                rests.append((value.astype(F32) - read).astype(BF16))
                seen.append(growth(n, r) * reads[n - 1][SPAN:, lanes])
        fresh = [dot(t_ref[r, n], twice(x, 0)).astype(BF16) for (n, r), x in zip(both, rests)]
        spreads = [dot(inner[r, n], x) for (n, r), x in zip(both, fresh)]
        for (n, r), x, y in zip(both, spreads, seen):
            oa_ref[r, span_rows(n), :] = x if y is None else x + y
        for r in range(2):
            last_ref[r, :, 0:DV] = hop_ref[r * DK : (r + 1) * DK, :].astype(F32)
            last_ref[r, :, DV:] = jnp.zeros((DK, DV), F32)

    @pl.when(jnp.logical_not(first))
    def _():
        adds = values_part(recv_ref, cv_ref, keys_t_ref, t_ref, cols_ref, rows, values)
        zero_half = jnp.zeros((DK, DV), F32)
        states = [
            jnp.concatenate(
                [adds[r], lin_ref[r, 0, :, :DK].astype(F32) + lin_ref[r, 0, :, DK:].astype(F32)],
                axis=1,
            )
            for r in range(2)
        ]
        for n in range(1, spans):
            for r in range(2):
                parts = halves(states[r])
                states_ref[r, n] = jnp.concatenate(parts, axis=0)
                add = jnp.concatenate([adds[2 * n + r], zero_half], axis=1)
                states[r] = step(lin_ref[r, n], parts) + add
        for r in range(2):
            last_ref[r] = states[r]
        prepare()
        reads = [
            dot(twice(readers[n], 1), states_ref[r, n]) if n > 0 else None for n, r in both
        ]
        rests, seen = [], []
        for (n, r), read in zip(both, reads):
            value = values[span_rows(n), r * DV : (r + 1) * DV].astype(F32)
            if n == 0:
                known = growth(n, r) * readers[n].astype(F32)[:SPAN]
                asked = growth(n, r) * readers[n].astype(F32)[SPAN:]
                rest = jnp.concatenate([value, -known], axis=1)
                seen.append(jnp.concatenate([zero_half, asked], axis=1))
            else:
                rest = jnp.concatenate([value, zero_half], axis=1) - growth(n, r) * read[:SPAN]
                seen.append(growth(n, r) * read[SPAN:])
            rests.append(rest.astype(BF16))
        fresh = [dot(t_ref[r, n], twice(x, 0)).astype(BF16) for (n, r), x in zip(both, rests)]
        spreads = [dot(inner[r, n], x) for (n, r), x in zip(both, fresh)]
        for (n, r), x, y in zip(both, spreads, seen):
            out = x + y
            oa_ref[r, span_rows(n), :] = out[:, :DV]
            om_ref[r, span_rows(n), :] = out[:, DV:].astype(BF16)


def first_tokens(hop_ref, recv_ref, early_ref, cq_ref, ck_ref, cv_ref, rows):
    sub = lax.axis_index("sub")
    tokens = (recv_ref.shape[1] - GATES) // 4
    taps = [key_tap(sub, cq_ref), key_tap(sub, ck_ref)] + value_taps(sub, cv_ref)
    results = []
    edges = hop_ref[2 * DK :, :].astype(F32)
    for g, first in enumerate((3, 0, 1, 2)):
        lanes = slice(g * 128, (g + 1) * 128)
        start = GATES + first * tokens
        rows[16 - EDGE : 16, lanes] = edges[EDGE * g : EDGE * (g + 1)]
        rows[16:32, lanes] = recv_ref[0, start : start + 16, :].astype(F32)
        results.append(convolved(rows, 16 - EDGE, 8, lanes, taps[g]))
    q_cols = jnp.transpose(unit(results[0], DK**-0.5).astype(F32))
    k_cols = jnp.transpose(unit(results[1], 1.0).astype(F32))
    gates = early_ref[...]
    line = iota((8, DV), 0)
    finals, outputs = [], []
    for r in range(2):
        values = results[2 + r].astype(BF16).astype(F32)
        entering = hop_ref[r * DK : (r + 1) * DK, :].astype(F32)
        state, out = entering, jnp.zeros((8, DV), F32)
        for t in range(EDGE):
            k_t, q_t = k_cols[:, t : t + 1], q_cols[:, t : t + 1]
            state = jnp.exp(gates[r : r + 1, t : t + 1]) * state
            held = jnp.sum(k_t * state, axis=0, keepdims=True)
            state = state + k_t * (
                gates[2 + r : 3 + r, t : t + 1] * (values[t : t + 1, :] - held)
            )
            out = jnp.where(line == t, jnp.sum(q_t * state, axis=0, keepdims=True), out)
        finals.append(state)
        outputs.append(out)
    return finals, outputs


def finish_kernel(
    hop_ref, recv_ref, early_ref, cq_ref, ck_ref, cv_ref, gain_ref, oa_ref, om_ref, out_ref, rows
):
    peers, tokens = out_ref.shape[0], out_ref.shape[1]
    first = lax.axis_index("half") == 0
    gain = gain_ref[...]
    chunks = 4
    part, peer_part = peers * tokens // chunks, peers // chunks

    def put(c, r, core):
        scale = lax.rsqrt(jnp.mean(core * core, axis=-1, keepdims=True) + EPS)
        normed = (core * scale * gain).astype(BF16)
        out_ref[c * peer_part : (c + 1) * peer_part, :, r * DV : (r + 1) * DV] = normed.reshape(
            peer_part, tokens, DV
        )

    @pl.when(first)
    def _():
        for c in range(chunks):
            for r in range(2):
                put(c, r, oa_ref[r, c * part : (c + 1) * part, :])

    @pl.when(jnp.logical_not(first))
    def _():
        finals, outputs = first_tokens(hop_ref, recv_ref, early_ref, cq_ref, ck_ref, cv_ref, rows)
        replaced = iota((8, DV), 0) < EDGE
        passed = [dot(om_ref[r], finals[r].astype(BF16)) for r in range(2)]
        for c in range(chunks):
            at = c * part
            for r in range(2):
                core = oa_ref[r, at : at + part, :] + passed[r][at : at + part]
                if c == 0:
                    core = jnp.concatenate(
                        [jnp.where(replaced, outputs[r], core[0:8]), core[8:]], axis=0
                    )
                put(c, r, core)


def advance_kernel(
    hop_ref, recv_ref, early_ref, cq_ref, ck_ref, cv_ref, hop_own, last_ref, next_ref, rows
):
    finals, _ = first_tokens(hop_ref, recv_ref, early_ref, cq_ref, ck_ref, cv_ref, rows)
    first = lax.axis_index("half") == 0
    for r in range(2):
        last = last_ref[r]
        through = mm_parts(halves(last[:, DV:]), halves(finals[r]))
        moved = jnp.where(first, 0.0, through) + last[:, :DV]
        next_ref[r * DK : (r + 1) * DK, :] = moved.astype(BF16)
    next_ref[2 * DK :, :] = hop_own[2 * DK :, :]


def gate_kernel(heads_axis, normed_ref, z_ref, out_ref, made, sems):
    subs = normed_ref.shape[0] // heads_axis
    width = subs * 2 * DV
    copies = []
    for head in range(heads_axis):
        for sub in range(subs):
            at = (head * subs + sub) * 2 * DV
            gate = silu(z_ref[:, at : at + 2 * DV].astype(F32))
            value = normed_ref[sub * heads_axis + head].astype(F32)
            made[:, at : at + 2 * DV] = (value * gate).astype(BF16)
        lanes = pl.ds(head * width, width)
        copy = pltpu.make_async_copy(made.at[:, lanes], out_ref.at[:, lanes], sems.at[head])
        copy.start()
        copies.append(copy)
    for copy in copies:
        copy.wait()


VMEM = pl.BlockSpec(memory_space=pltpu.VMEM)
SMEM = pl.BlockSpec(memory_space=pltpu.SMEM)
ANY = pl.BlockSpec(memory_space=pl.ANY)


def near(x):
    return pltpu.with_memory_space_constraint(x, pltpu.VMEM)


def far(x):
    return pltpu.with_memory_space_constraint(x, pltpu.HBM)


def call(kernel, outs, in_specs, scratch=(), out_spec=VMEM, flops=1 << 26, moved=1 << 21):
    return pl.pallas_call(
        kernel,
        out_shape=outs,
        in_specs=in_specs,
        out_specs=jax.tree.map(lambda _: out_spec, outs),
        scratch_shapes=list(scratch),
        compiler_params=pltpu.CompilerParams(vmem_limit_bytes=VMEM_BYTES),
        cost_estimate=pl.CostEstimate(flops=flops, bytes_accessed=moved, transcendentals=0),
    )


def local(
    q_rows,
    k_rows,
    v_rows,
    z_rows,
    a_rows,
    b_rows,
    conv_q,
    conv_k,
    conv_v,
    a_log,
    dt_bias,
    norm_gain,
):
    shards, subs, heads_axis = (lax.axis_size(a) for a in ("half", "sub", "head"))
    peers, tokens = subs * heads_axis, q_rows.shape[0]
    total = peers * tokens
    spans = total // SPAN
    group = ("sub", "head")
    route = [(i, i + 1) for i in range(shards - 1)]
    inputs = [far(x) for x in (q_rows, k_rows, v_rows, a_rows.T, b_rows.T)]
    packed = call(
        functools.partial(pack_kernel, heads_axis),
        pltpu.VMEM((peers, GATES + 4 * tokens, 128), BF16),
        [ANY] * 5,
        [pltpu.VMEM(x.shape, BF16) for x in inputs] + [pltpu.SemaphoreType.DMA((5,))],
        flops=1 << 20,
    )(*inputs)
    blocks = near(lax.all_to_all(packed, group, 0, 0, tiled=True))
    keys, keys_t, inverses, lins, within, cols, early = call(
        keys_kernel,
        (
            pltpu.VMEM((total, DK), BF16),
            pltpu.VMEM((spans, DK, SPAN), BF16),
            pltpu.VMEM((2, spans, SPAN, 2 * SPAN), BF16),
            pltpu.VMEM((2, spans, DK, 2 * DK), BF16),
            pltpu.VMEM((2, total, SPAN), BF16),
            pltpu.VMEM((SPAN, spans * GATES), F32),
            pltpu.VMEM((8, SPAN), F32),
        ),
        [VMEM, VMEM, SMEM, SMEM],
        [pltpu.VMEM((8 + total, DK), F32)],
        flops=1 << 32,
    )(blocks, conv_k, a_log, dt_bias)
    keys, keys_t, inverses, lins, within, cols, early = (
        near(x) for x in (keys, keys_t, inverses, lins, within, cols, early)
    )
    hop, values, starts = call(
        opening_kernel,
        (
            pltpu.VMEM((2 * DK + 16, 128), BF16),
            pltpu.VMEM((total, 2 * DV), BF16),
            pltpu.VMEM((spans, 2 * DK, 2 * DV), BF16),
        ),
        [VMEM] * 6,
        [pltpu.VMEM((8 + total, 2 * DV), F32)],
        flops=1 << 32,
    )(blocks, conv_v, keys_t, inverses, lins, cols)
    entering = near(lax.ppermute(hop, "half", route))
    hop, values, starts = near(hop), near(values), near(starts)
    out_a, out_m, last = call(
        output_kernel,
        (
            pltpu.VMEM((2, total, DV), F32),
            pltpu.VMEM((2, total, DV), BF16),
            pltpu.VMEM((2, DK, 2 * DV), F32),
        ),
        [VMEM] * 12,
        [
            pltpu.VMEM((8 + total, 2 * DV), F32),
            pltpu.VMEM((8 + total, DK), F32),
            pltpu.VMEM((total, 2 * DV), BF16),
            pltpu.VMEM((2, spans, SPAN, SPAN), BF16),
            pltpu.VMEM((spans, 2 * SPAN, DK), BF16),
            pltpu.VMEM((2, spans, 2 * DK, 2 * DV), BF16),
        ],
        flops=1 << 32,
    )(
        blocks,
        conv_q,
        conv_v,
        keys,
        keys_t,
        inverses,
        lins,
        within,
        cols,
        hop,
        values,
        starts,
    )
    for _ in range(shards - 2):
        moved = call(
            advance_kernel,
            pltpu.VMEM(hop.shape, BF16),
            [VMEM] * 8,
            [pltpu.VMEM((32, 512), F32)],
        )(entering, blocks, early, conv_q, conv_k, conv_v, hop, near(last))
        entering = near(lax.ppermute(moved, "half", route))
    normed = call(
        finish_kernel,
        pltpu.VMEM((peers, tokens, 2 * DV), BF16),
        [VMEM] * 9,
        [pltpu.VMEM((32, 512), F32)],
    )(
        entering,
        blocks,
        early,
        conv_q,
        conv_k,
        conv_v,
        norm_gain.reshape(1, DV),
        near(out_a),
        near(out_m),
    )
    returned = near(lax.all_to_all(normed, group, 0, 0, tiled=True))
    return call(
        functools.partial(gate_kernel, heads_axis),
        jax.ShapeDtypeStruct(z_rows.shape, BF16),
        [VMEM] * 2,
        [pltpu.VMEM(z_rows.shape, BF16), pltpu.SemaphoreType.DMA((heads_axis,))],
        ANY,
    )(returned, z_rows)


def solution(mesh):
    heads_axis = mesh.shape["head"]
    subs = KH // heads_axis
    regrouped = Mesh(
        mesh.devices.reshape(mesh.shape["ctx"] // subs, subs, heads_axis), ("half", "sub", "head")
    )
    row = P(("half", "sub", "head"), None)
    placed = (row,) * 6 + (P(None, "head"),) * 3 + (P("head"),) * 2 + (P(),)
    return jax.shard_map(local, mesh=regrouped, in_specs=placed, out_specs=row, check_vma=False)
```

```python
import functools

import jax
import jax.numpy as jnp
from jax import lax
from jax.experimental import pallas as pl
from jax.experimental.pallas import tpu as pltpu
from jax.sharding import Mesh, PartitionSpec as P

DK = 128
DV = 128
CONV = 4
KH = 16
SUB = 16
SPAN = 128
EDGE = CONV - 1
EPS = 1e-06
F32 = jnp.float32
BF16 = jnp.bfloat16
VMEM_BYTES = 24 * 1024 * 1024
GATES = 8


def dot(a, b, dims=((1,), (0,))):
    return lax.dot_general(a, b, (dims, ((), ())), preferred_element_type=F32)


def halves(x):
    high = x.astype(BF16)
    return high, (x - high.astype(F32)).astype(BF16)


def mm_right(a, b):
    return dot(jnp.concatenate([a, a], axis=1), jnp.concatenate(halves(b), axis=0))


def mm_parts(a, b):
    rows, width = a[0].shape[0], b[0].shape[1]
    terms = dot(jnp.concatenate(a, axis=0), jnp.concatenate(b, axis=1))
    return terms[:rows, :width] + (terms[:rows, width:] + terms[rows:, :width])


def silu(x):
    half = 0.5 * x
    return half + half * jnp.tanh(half)


def unit(y, factor):
    scale = lax.rsqrt(jnp.sum(y * y, axis=-1, keepdims=True) + EPS)
    return (y * scale * factor).astype(BF16)


def iota(shape, dim):
    return lax.broadcasted_iota(jnp.int32, shape, dim)


def pack_kernel(
    heads_axis, q_in, k_in, v_in, at_in, bt_in, out_ref, q_ref, k_ref, v_ref, at_ref, bt_ref, sems
):
    peers, tokens = out_ref.shape[0], q_ref.shape[0]
    pairs = ((at_in, at_ref), (bt_in, bt_ref), (k_in, k_ref), (v_in, v_ref), (q_in, q_ref))
    copies = [pltpu.make_async_copy(a, b, sems.at[i]) for i, (a, b) in enumerate(pairs)]
    for copy in copies:
        copy.start()
    subs = peers // heads_axis
    key_heads = [(dest % heads_axis) * subs + dest // heads_axis for dest in range(peers)]
    for copy in copies[:2]:
        copy.wait()
    value_heads = at_ref.shape[0]
    row, entry = iota((peers * GATES, value_heads), 0), iota((peers * GATES, value_heads), 1)
    dest, which = row // GATES, row % GATES
    first = 2 * ((dest % heads_axis) * subs + dest // heads_axis)
    pick_a = jnp.where((which < 2) & (entry == first + which), 1.0, 0.0).astype(BF16)
    pick_b = jnp.where(
        (which >= 2) & (which < 4) & (entry == first + which - 2), 1.0, 0.0
    ).astype(BF16)
    picked = (dot(pick_a, at_ref[...]) + dot(pick_b, bt_ref[...])).astype(BF16)
    lane_shift = tokens * lax.rem(lax.axis_index("head"), SPAN // tokens)
    place = jnp.where(
        iota((tokens, SPAN), 1) == iota((tokens, SPAN), 0) + lane_shift, 1.0, 0.0
    ).astype(BF16)
    gates = dot(picked, place).astype(BF16)
    for dest in range(peers):
        out_ref[dest, 4 * tokens :, :] = gates[GATES * dest : GATES * (dest + 1), :]

    def laid(ref, lane, start):
        for dest, key_head in enumerate(key_heads):
            at = lane(key_head) * 128
            out_ref[dest, start * tokens : (start + 1) * tokens, :] = ref[
                :, at : at + 128
            ]

    copies[2].wait()
    laid(k_ref, lambda key_head: key_head, 0)
    copies[3].wait()
    laid(v_ref, lambda key_head: 2 * key_head, 1)
    laid(v_ref, lambda key_head: 2 * key_head + 1, 2)
    copies[4].wait()
    laid(q_ref, lambda key_head: key_head, 3)


def invert(systems, meanwhile):
    size = systems[0].shape[0]
    blocks = size // SUB
    row, col = iota((size, size), 0), iota((size, size), 1)
    diagonal = (row // SUB) == (col // SUB)
    compact = jnp.concatenate(
        [
            jnp.sum(jnp.where(diagonal, n, 0.0).reshape(blocks, SUB, size), axis=0)
            for n in systems
        ],
        axis=0,
    )
    count = len(systems)
    lane, line = iota(compact.shape, 1), iota(compact.shape, 0)
    solved = jnp.where(lane % SUB == line % SUB, 1.0, 0.0).reshape(count, SUB, size)
    for m in range(SUB - 1):
        spread = jnp.take_along_axis(compact, (lane // SUB) * SUB + m, axis=1)
        solved = solved - spread.reshape(count, SUB, size) * solved[:, m : m + 1, :]
    lows = [halves(n) for n in systems]
    placed = jnp.where(diagonal, 1.0, 0.0).astype(BF16)
    parts = [
        tuple(jnp.concatenate([x] * blocks, axis=0) * placed for x in halves(solved[i]))
        for i in range(count)
    ]
    width = SUB
    while width < size:
        odd = [(j, j + width) for j in range(width, size, 2 * width)]

        def rows_of(x):
            return jnp.concatenate([x[lo:hi] for lo, hi in odd], axis=0)

        def woven(even, x):
            pieces = []
            for j, (lo, hi) in enumerate(odd):
                pieces += [even[lo - width : lo], x[j * width : (j + 1) * width]]
            return jnp.concatenate(pieces, axis=0)

        below = ((row // (2 * width)) == (col // (2 * width))) & ((col // width) % 2 == 0)
        mask = rows_of(jnp.where(below, 1.0, 0.0).astype(BF16))
        blank = jnp.zeros((size, size), BF16)
        firsts = [
            mm_parts((rows_of(n[0]) * mask, rows_of(n[1]) * mask), t) for n, t in zip(lows, parts)
        ]
        meanwhile()
        spreads = [tuple(woven(blank, x) for x in halves(first)) for first in firsts]
        odds = [(rows_of(t[0]), rows_of(t[1])) for t in parts]
        seconds = [halves(-mm_parts(o, spread)) for o, spread in zip(odds, spreads)]
        meanwhile()
        parts = [
            tuple(woven(t[i], o[i] + second[i]) for i in range(2))
            for t, o, second in zip(parts, odds, seconds)
        ]
        width *= 2
    return parts


def gate_values(gates, sub, alog_ref, dt_ref):
    second = iota(gates.shape, 0) % GATES == 1
    a_log = jnp.where(second, alog_ref[2 * sub + 1], alog_ref[2 * sub])
    dt_bias = jnp.where(second, dt_ref[2 * sub + 1], dt_ref[2 * sub])
    shifted = gates + dt_bias
    soft = jnp.maximum(shifted, 0.0) + jnp.log1p(jnp.exp(-jnp.abs(shifted)))
    return -jnp.exp(a_log) * soft, 1.0 / (1.0 + jnp.exp(-gates))


def convolved(rows, at, count, lanes, tap):
    summed = tap[0:1] * rows[at : at + count, lanes]
    for j in range(1, CONV):
        summed = summed + tap[j : j + 1] * rows[at + j : at + j + count, lanes]
    return silu(summed)


def key_tap(sub, tap_ref):
    return tap_ref[:, pl.ds(pl.multiple_of(sub * DK, 128), DK)]


def value_taps(sub, cv_ref):
    lane = pl.multiple_of(sub * 2 * DV, 128)
    return [cv_ref[:, pl.ds(pl.multiple_of(lane + r * DV, 128), DV)] for r in range(2)]


def widened(rows, recv_ref, starts, tokens):
    rows[0:8, :] = jnp.zeros((8, rows.shape[1]), F32)
    for s in range(recv_ref.shape[0]):
        for g, start in enumerate(starts):
            rows[8 + s * tokens : 8 + (s + 1) * tokens, g * 128 : (g + 1) * 128] = recv_ref[
                s, start : start + tokens, :
            ].astype(F32)


def keys_kernel(
    recv_ref,
    ck_ref,
    cv_ref,
    alog_ref,
    dt_ref,
    keys_ref,
    keys_t_ref,
    t_ref,
    lin_ref,
    within_ref,
    cols_ref,
    early_ref,
    values_ref,
    rows,
):
    sub = lax.axis_index("sub")
    later = lax.axis_index("half") > 0
    peers = recv_ref.shape[0]
    tokens = (recv_ref.shape[1] - GATES) // 4
    spans = peers * tokens // SPAN
    taps = [key_tap(sub, ck_ref)] + value_taps(sub, cv_ref)
    widened(rows, recv_ref, [0, tokens, 2 * tokens], tokens)
    stacked = [
        sum(recv_ref[s, 4 * tokens :, :].astype(F32) for s in range(n, n + SPAN // tokens))
        for n in range(0, peers, SPAN // tokens)
    ]
    stacked.append(jnp.zeros((SPAN - spans * GATES, SPAN), F32))
    gates = jnp.concatenate(stacked, axis=0)
    decay, rate = gate_values(gates, sub, alog_ref, dt_ref)
    early_ref[...] = jnp.where(iota((8, SPAN), 0) < 2, decay[0:8], rate[0:8])
    skipped = later & (iota(gates.shape, 0) < GATES) & (iota(gates.shape, 1) < EDGE)
    decay = jnp.where(skipped, 0.0, decay)
    rate = jnp.where(skipped, 0.0, rate)
    lane_r, lane_c = iota((SPAN, SPAN), 0), iota((SPAN, SPAN), 1)
    upto = jnp.where(lane_r <= lane_c, 1.0, 0.0).astype(BF16)
    d_high, _ = halves(decay)
    d_mid, d_low = halves(decay - d_high.astype(F32))
    cum = dot(d_high, upto) + (dot(d_mid, upto) + dot(d_low, upto))
    growth = jnp.exp(cum)
    here = pltpu.roll(rate, rate.shape[0] - 2, 0)
    rest = jnp.exp(cum[:, SPAN - 1 :] - cum) * here
    which = iota(gates.shape, 0) % GATES
    mixed = jnp.where(which < 2, cum, pltpu.roll(growth, 2, 0))
    columns = jnp.transpose(jnp.where(which < 4, mixed, pltpu.roll(rest, 4, 0)))
    cols_ref[...] = columns
    lower = lane_r >= lane_c
    strict = lane_r > lane_c
    both = [(n, r) for n in range(spans) for r in range(2)]
    keys = []
    for n in range(spans):
        k_n = unit(convolved(rows, n * SPAN + 8 - EDGE, SPAN, slice(0, DK), taps[0]), 1.0)
        keys_ref[n * SPAN : (n + 1) * SPAN, :] = k_n
        keys.append(k_n)
    keys_t = []
    for n in range(spans):
        kt_n = jnp.transpose(keys[n].astype(F32)).astype(BF16)
        keys_t_ref[n] = kt_n
        keys_t.append(kt_n)
    grams = [dot(keys[n], keys_t[n]) for n in range(spans)]
    systems = []
    for n, r in both:
        at = GATES * n + r
        gap = columns[:, at : at + 1] - cum[at : at + 1, :]
        within = jnp.exp(jnp.where(lower, gap, 0.0)) * here[at : at + 1, :]
        within_ref[r, n * SPAN : (n + 1) * SPAN, :] = jnp.where(lower, within, 0.0).astype(BF16)
        systems.append(jnp.where(strict, within * grams[n], 0.0))
    waiting = list(both)

    def meanwhile():
        for n, r in waiting[: 2 * spans // 6 + 1]:
            lanes = slice((1 + r) * DV, (2 + r) * DV)
            value = convolved(rows, n * SPAN + 8 - EDGE, SPAN, lanes, taps[1 + r])
            values_ref[n * SPAN : (n + 1) * SPAN, r * DV : (r + 1) * DV] = value.astype(BF16)
        del waiting[: 2 * spans // 6 + 1]

    inverses = invert(systems, meanwhile)
    while waiting:
        meanwhile()
    for i, (n, r) in enumerate(both):
        t_ref[r, n] = jnp.concatenate(inverses[i], axis=1)
    scaled = []
    for n, r in both:
        at = GATES * n + r
        scaled.append(halves(columns[:, at + 2 : at + 3] * keys[n].astype(F32)))
    w_mats = [mm_parts(t, x) for t, x in zip(inverses, scaled)]
    weighed = []
    for (n, r), w_mat in zip(both, w_mats):
        at = GATES * n + r
        weighed.append(columns[:, at + 4 : at + 5] * w_mat)
    moved = [
        mm_right(keys_t[n], jnp.concatenate(weighed[2 * n : 2 * n + 2], axis=1))
        for n in range(spans)
    ]
    identity = jnp.where(lane_r == lane_c, 1.0, 0.0)
    for n, r in both:
        at = GATES * n + r
        lin = growth[at : at + 1, SPAN - 1 :] * identity - moved[n][:, r * DK : (r + 1) * DK]
        lin_ref[r, n] = jnp.concatenate(halves(lin), axis=1)


def step(lin, parts):
    high, low = parts
    return dot(lin, jnp.concatenate([high, high], axis=0)) + dot(lin[:, :DK], low)


def added(values_ref, keys_t_ref, t_ref, cols_ref):
    spans = t_ref.shape[1]
    both = [(n, r) for n in range(spans) for r in range(2)]
    values = []
    for n, r in both:
        v_n = values_ref[n * SPAN : (n + 1) * SPAN, r * DV : (r + 1) * DV]
        values.append(jnp.concatenate([v_n, v_n], axis=0))
    solved = [dot(t_ref[r, n], v) for (n, r), v in zip(both, values)]
    weighed = []
    for (n, r), u_mat in zip(both, solved):
        at = GATES * n + r
        weighed.append(cols_ref[:, at + 4 : at + 5] * u_mat)
    moved = [
        mm_right(keys_t_ref[n], jnp.concatenate(weighed[2 * n : 2 * n + 2], axis=1))
        for n in range(spans)
    ]
    return [moved[n][:, r * DV : (r + 1) * DV] for n, r in both]


def opening_kernel(
    recv_ref, values_ref, keys_t_ref, t_ref, lin_ref, cols_ref, hop_ref, xs_ref
):
    first = lax.axis_index("half") == 0
    peers = recv_ref.shape[0]
    tokens = (recv_ref.shape[1] - GATES) // 4
    spans = t_ref.shape[1]
    edges = []
    for which in (3, 0, 1, 2):
        end = (which + 1) * tokens
        edges.append(recv_ref[peers - 1, end - 16 : end, :].astype(F32)[16 - EDGE :])
    edges.append(jnp.zeros((16 - 4 * EDGE, 128), F32))
    hop_ref[2 * DK :, :] = jnp.concatenate(edges, axis=0).astype(BF16)

    @pl.when(first)
    def _():
        adds = added(values_ref, keys_t_ref, t_ref, cols_ref)
        states = [adds[0], adds[1]]
        for n in range(1, spans):
            for r in range(2):
                parts = halves(states[r])
                xs_ref[n, :, r * DV : (r + 1) * DV] = jnp.concatenate(parts, axis=0)
                states[r] = step(lin_ref[r, n], parts) + adds[2 * n + r]
        for r in range(2):
            hop_ref[r * DK : (r + 1) * DK, :] = states[r].astype(BF16)

    @pl.when(jnp.logical_not(first))
    def _():
        hop_ref[0 : 2 * DK, :] = jnp.zeros((2 * DK, DV), BF16)


def output_kernel(
    recv_ref,
    cq_ref,
    keys_ref,
    keys_t_ref,
    t_ref,
    lin_ref,
    within_ref,
    cols_ref,
    values_ref,
    hop_ref,
    xs_ref,
    oa_ref,
    om_ref,
    last_ref,
    query_rows,
    inner,
    readers,
    states_ref,
):
    sub = lax.axis_index("sub")
    first = lax.axis_index("half") == 0
    tokens = (recv_ref.shape[1] - GATES) // 4
    spans = t_ref.shape[1]
    both = [(n, r) for n in range(spans) for r in range(2)]
    tap = key_tap(sub, cq_ref)
    widened(query_rows, recv_ref, [3 * tokens], tokens)

    def span_rows(n):
        return slice(n * SPAN, (n + 1) * SPAN)

    def growth(n, r):
        return cols_ref[:, GATES * n + 2 + r : GATES * n + 3 + r]

    def prepare():
        queries = []
        for n in range(spans):
            at = n * SPAN + 8 - EDGE
            q_n = unit(convolved(query_rows, at, SPAN, slice(0, DK), tap), DK**-0.5)
            queries.append(q_n)
            readers[n, 0:SPAN, :] = keys_ref[span_rows(n), :]
            readers[n, SPAN:, :] = q_n
        scores = [dot(queries[n], keys_t_ref[n]) for n in range(spans)]
        for n, r in both:
            weight = within_ref[r, span_rows(n), :].astype(F32)
            inner[r, n] = (weight * scores[n]).astype(BF16)

    def twice(x, axis):
        return jnp.concatenate([x, x], axis=axis)

    @pl.when(first)
    def _():
        prepare()
        reads = [dot(twice(readers[n], 1), xs_ref[n]) for n in range(1, spans)]
        rests, seen = [], []
        for n, r in both:
            lanes = slice(r * DV, (r + 1) * DV)
            value = values_ref[span_rows(n), lanes]
            if n == 0:
                rests.append(value)
                seen.append(None)
            else:
                read = growth(n, r) * reads[n - 1][:SPAN, lanes]
                rests.append((value.astype(F32) - read).astype(BF16))
                seen.append(growth(n, r) * reads[n - 1][SPAN:, lanes])
        fresh = [dot(t_ref[r, n], twice(x, 0)).astype(BF16) for (n, r), x in zip(both, rests)]
        spreads = [dot(inner[r, n], x) for (n, r), x in zip(both, fresh)]
        for (n, r), x, y in zip(both, spreads, seen):
            oa_ref[r, span_rows(n), :] = x if y is None else x + y
        for r in range(2):
            last_ref[r, :, 0:DV] = hop_ref[r * DK : (r + 1) * DK, :].astype(F32)
            last_ref[r, :, DV:] = jnp.zeros((DK, DV), F32)

    @pl.when(jnp.logical_not(first))
    def _():
        adds = added(values_ref, keys_t_ref, t_ref, cols_ref)
        zero_half = jnp.zeros((DK, DV), F32)
        states = [
            jnp.concatenate(
                [adds[r], lin_ref[r, 0, :, :DK].astype(F32) + lin_ref[r, 0, :, DK:].astype(F32)],
                axis=1,
            )
            for r in range(2)
        ]
        for n in range(1, spans):
            for r in range(2):
                parts = halves(states[r])
                states_ref[r, n] = jnp.concatenate(parts, axis=0)
                add = jnp.concatenate([adds[2 * n + r], zero_half], axis=1)
                states[r] = step(lin_ref[r, n], parts) + add
        for r in range(2):
            last_ref[r] = states[r]
        prepare()
        reads = [
            dot(twice(readers[n], 1), states_ref[r, n]) if n > 0 else None for n, r in both
        ]
        rests, seen = [], []
        for (n, r), read in zip(both, reads):
            value = values_ref[span_rows(n), r * DV : (r + 1) * DV].astype(F32)
            if n == 0:
                known = growth(n, r) * readers[n].astype(F32)[:SPAN]
                asked = growth(n, r) * readers[n].astype(F32)[SPAN:]
                rest = jnp.concatenate([value, -known], axis=1)
                seen.append(jnp.concatenate([zero_half, asked], axis=1))
            else:
                rest = jnp.concatenate([value, zero_half], axis=1) - growth(n, r) * read[:SPAN]
                seen.append(growth(n, r) * read[SPAN:])
            rests.append(rest.astype(BF16))
        fresh = [dot(t_ref[r, n], twice(x, 0)).astype(BF16) for (n, r), x in zip(both, rests)]
        spreads = [dot(inner[r, n], x) for (n, r), x in zip(both, fresh)]
        for (n, r), x, y in zip(both, spreads, seen):
            out = x + y
            oa_ref[r, span_rows(n), :] = out[:, :DV]
            om_ref[r, span_rows(n), :] = out[:, DV:].astype(BF16)


def first_tokens(hop_ref, recv_ref, early_ref, cq_ref, ck_ref, cv_ref, rows):
    sub = lax.axis_index("sub")
    tokens = (recv_ref.shape[1] - GATES) // 4
    taps = [key_tap(sub, cq_ref), key_tap(sub, ck_ref)] + value_taps(sub, cv_ref)
    results = []
    edges = hop_ref[2 * DK :, :].astype(F32)
    for g, first in enumerate((3, 0, 1, 2)):
        lanes = slice(g * 128, (g + 1) * 128)
        start = first * tokens
        rows[16 - EDGE : 16, lanes] = edges[EDGE * g : EDGE * (g + 1)]
        rows[16:32, lanes] = recv_ref[0, start : start + 16, :].astype(F32)
        results.append(convolved(rows, 16 - EDGE, 8, lanes, taps[g]))
    q_cols = jnp.transpose(unit(results[0], DK**-0.5).astype(F32))
    k_cols = jnp.transpose(unit(results[1], 1.0).astype(F32))
    gates = early_ref[...]
    line = iota((8, DV), 0)
    finals, outputs = [], []
    for r in range(2):
        values = results[2 + r].astype(BF16).astype(F32)
        entering = hop_ref[r * DK : (r + 1) * DK, :].astype(F32)
        state, out = entering, jnp.zeros((8, DV), F32)
        for t in range(EDGE):
            k_t, q_t = k_cols[:, t : t + 1], q_cols[:, t : t + 1]
            state = jnp.exp(gates[r : r + 1, t : t + 1]) * state
            held = jnp.sum(k_t * state, axis=0, keepdims=True)
            state = state + k_t * (
                gates[2 + r : 3 + r, t : t + 1] * (values[t : t + 1, :] - held)
            )
            out = jnp.where(line == t, jnp.sum(q_t * state, axis=0, keepdims=True), out)
        finals.append(state)
        outputs.append(out)
    return finals, outputs


def finish_kernel(
    hop_ref, recv_ref, early_ref, cq_ref, ck_ref, cv_ref, gain_ref, oa_ref, om_ref, out_ref, rows
):
    peers, tokens = out_ref.shape[0], out_ref.shape[1]
    first = lax.axis_index("half") == 0
    gain = gain_ref[...]
    chunks = 4
    part, peer_part = peers * tokens // chunks, peers // chunks

    def put(c, r, core):
        scale = lax.rsqrt(jnp.mean(core * core, axis=-1, keepdims=True) + EPS)
        normed = (core * scale * gain).astype(BF16)
        out_ref[c * peer_part : (c + 1) * peer_part, :, r * DV : (r + 1) * DV] = normed.reshape(
            peer_part, tokens, DV
        )

    @pl.when(first)
    def _():
        for c in range(chunks):
            for r in range(2):
                put(c, r, oa_ref[r, c * part : (c + 1) * part, :])

    @pl.when(jnp.logical_not(first))
    def _():
        finals, outputs = first_tokens(hop_ref, recv_ref, early_ref, cq_ref, ck_ref, cv_ref, rows)
        replaced = iota((8, DV), 0) < EDGE
        passed = [dot(om_ref[r], finals[r].astype(BF16)) for r in range(2)]
        for c in range(chunks):
            at = c * part
            for r in range(2):
                core = oa_ref[r, at : at + part, :] + passed[r][at : at + part]
                if c == 0:
                    core = jnp.concatenate(
                        [jnp.where(replaced, outputs[r], core[0:8]), core[8:]], axis=0
                    )
                put(c, r, core)


def advance_kernel(
    hop_ref, recv_ref, early_ref, cq_ref, ck_ref, cv_ref, hop_own, last_ref, next_ref, rows
):
    finals, _ = first_tokens(hop_ref, recv_ref, early_ref, cq_ref, ck_ref, cv_ref, rows)
    first = lax.axis_index("half") == 0
    for r in range(2):
        last = last_ref[r]
        through = mm_parts(halves(last[:, DV:]), halves(finals[r]))
        moved = jnp.where(first, 0.0, through) + last[:, :DV]
        next_ref[r * DK : (r + 1) * DK, :] = moved.astype(BF16)
    next_ref[2 * DK :, :] = hop_own[2 * DK :, :]


def gate_kernel(heads_axis, normed_ref, z_ref, out_ref, made, sems):
    subs = normed_ref.shape[0] // heads_axis
    width = subs * 2 * DV
    copies = []
    for head in range(heads_axis):
        for sub in range(subs):
            at = (head * subs + sub) * 2 * DV
            gate = silu(z_ref[:, at : at + 2 * DV].astype(F32))
            value = normed_ref[sub * heads_axis + head].astype(F32)
            made[:, at : at + 2 * DV] = (value * gate).astype(BF16)
        lanes = pl.ds(head * width, width)
        copy = pltpu.make_async_copy(made.at[:, lanes], out_ref.at[:, lanes], sems.at[head])
        copy.start()
        copies.append(copy)
    for copy in copies:
        copy.wait()


VMEM = pl.BlockSpec(memory_space=pltpu.VMEM)
SMEM = pl.BlockSpec(memory_space=pltpu.SMEM)
ANY = pl.BlockSpec(memory_space=pl.ANY)


def near(x):
    return pltpu.with_memory_space_constraint(x, pltpu.VMEM)


def far(x):
    return pltpu.with_memory_space_constraint(x, pltpu.HBM)


def call(kernel, outs, in_specs, scratch=(), out_spec=VMEM, flops=1 << 26, moved=1 << 21):
    return pl.pallas_call(
        kernel,
        out_shape=outs,
        in_specs=in_specs,
        out_specs=jax.tree.map(lambda _: out_spec, outs),
        scratch_shapes=list(scratch),
        compiler_params=pltpu.CompilerParams(vmem_limit_bytes=VMEM_BYTES),
        cost_estimate=pl.CostEstimate(flops=flops, bytes_accessed=moved, transcendentals=0),
    )


def local(
    q_rows,
    k_rows,
    v_rows,
    z_rows,
    a_rows,
    b_rows,
    conv_q,
    conv_k,
    conv_v,
    a_log,
    dt_bias,
    norm_gain,
):
    shards, subs, heads_axis = (lax.axis_size(a) for a in ("half", "sub", "head"))
    peers, tokens = subs * heads_axis, q_rows.shape[0]
    total = peers * tokens
    spans = total // SPAN
    group = ("sub", "head")
    route = [(i, i + 1) for i in range(shards - 1)]
    inputs = [far(x) for x in (q_rows, k_rows, v_rows, a_rows.T, b_rows.T)]
    packed = call(
        functools.partial(pack_kernel, heads_axis),
        pltpu.VMEM((peers, GATES + 4 * tokens, 128), BF16),
        [ANY] * 5,
        [pltpu.VMEM(x.shape, BF16) for x in inputs] + [pltpu.SemaphoreType.DMA((5,))],
        flops=1 << 20,
    )(*inputs)
    blocks = near(lax.all_to_all(packed, group, 0, 0, tiled=True))
    made = call(
        keys_kernel,
        (
            pltpu.VMEM((total, DK), BF16),
            pltpu.VMEM((spans, DK, SPAN), BF16),
            pltpu.VMEM((2, spans, SPAN, 2 * SPAN), BF16),
            pltpu.VMEM((2, spans, DK, 2 * DK), BF16),
            pltpu.VMEM((2, total, SPAN), BF16),
            pltpu.VMEM((SPAN, SPAN), F32),
            pltpu.VMEM((8, SPAN), F32),
            pltpu.VMEM((total, 2 * DV), BF16),
        ),
        [VMEM, VMEM, VMEM, SMEM, SMEM],
        [pltpu.VMEM((8 + total, DK + 2 * DV), F32)],
        flops=1 << 32,
    )(blocks, conv_k, conv_v, a_log, dt_bias)
    keys, keys_t, inverses, lins, within, cols, early, values = (near(x) for x in made)
    hop, starts = call(
        opening_kernel,
        (
            pltpu.VMEM((2 * DK + 16, 128), BF16),
            pltpu.VMEM((spans, 2 * DK, 2 * DV), BF16),
        ),
        [VMEM] * 6,
        flops=1 << 32,
    )(blocks, values, keys_t, inverses, lins, cols)
    entering = near(lax.ppermute(hop, "half", route))
    hop, starts = near(hop), near(starts)
    out_a, out_m, last = call(
        output_kernel,
        (
            pltpu.VMEM((2, total, DV), F32),
            pltpu.VMEM((2, total, DV), BF16),
            pltpu.VMEM((2, DK, 2 * DV), F32),
        ),
        [VMEM] * 11,
        [
            pltpu.VMEM((8 + total, DK), F32),
            pltpu.VMEM((2, spans, SPAN, SPAN), BF16),
            pltpu.VMEM((spans, 2 * SPAN, DK), BF16),
            pltpu.VMEM((2, spans, 2 * DK, 2 * DV), BF16),
        ],
        flops=1 << 32,
    )(blocks, conv_q, keys, keys_t, inverses, lins, within, cols, values, hop, starts)
    for _ in range(shards - 2):
        moved = call(
            advance_kernel,
            pltpu.VMEM(hop.shape, BF16),
            [VMEM] * 8,
            [pltpu.VMEM((32, 512), F32)],
        )(entering, blocks, early, conv_q, conv_k, conv_v, hop, near(last))
        entering = near(lax.ppermute(moved, "half", route))
    normed = call(
        finish_kernel,
        pltpu.VMEM((peers, tokens, 2 * DV), BF16),
        [VMEM] * 9,
        [pltpu.VMEM((32, 512), F32)],
    )(
        entering,
        blocks,
        early,
        conv_q,
        conv_k,
        conv_v,
        norm_gain.reshape(1, DV),
        near(out_a),
        near(out_m),
    )
    returned = near(lax.all_to_all(normed, group, 0, 0, tiled=True))
    return call(
        functools.partial(gate_kernel, heads_axis),
        jax.ShapeDtypeStruct(z_rows.shape, BF16),
        [VMEM] * 2,
        [pltpu.VMEM(z_rows.shape, BF16), pltpu.SemaphoreType.DMA((heads_axis,))],
        ANY,
    )(returned, z_rows)


def solution(mesh):
    heads_axis = mesh.shape["head"]
    subs = KH // heads_axis
    regrouped = Mesh(
        mesh.devices.reshape(mesh.shape["ctx"] // subs, subs, heads_axis), ("half", "sub", "head")
    )
    row = P(("half", "sub", "head"), None)
    placed = (row,) * 6 + (P(None, "head"),) * 3 + (P("head"),) * 2 + (P(),)
    return jax.shard_map(local, mesh=regrouped, in_specs=placed, out_specs=row, check_vma=False)
```

```python
import functools

import jax
import jax.numpy as jnp
from jax import lax
from jax.experimental import pallas as pl
from jax.experimental.pallas import tpu as pltpu
from jax.sharding import Mesh, PartitionSpec as P

DK = 128
DV = 128
CONV = 4
KH = 16
SUB = 16
SPAN = 128
EDGE = CONV - 1
EPS = 1e-06
F32 = jnp.float32
BF16 = jnp.bfloat16
VMEM_BYTES = 24 * 1024 * 1024
GATES = 8


def dot(a, b, dims=((1,), (0,))):
    return lax.dot_general(a, b, (dims, ((), ())), preferred_element_type=F32)


def halves(x):
    high = x.astype(BF16)
    return high, (x - high.astype(F32)).astype(BF16)


def mm_parts(a, b):
    both = jnp.concatenate(a, axis=1)
    return dot(both, jnp.concatenate([b[0], b[0]], axis=0)) + dot(a[0], b[1])


def silu(x):
    half = 0.5 * x
    return half + half * jnp.tanh(half)


def unit(y, factor):
    scale = lax.rsqrt(jnp.sum(y * y, axis=-1, keepdims=True) + EPS)
    return (y * scale * factor).astype(BF16)


def iota(shape, dim):
    return lax.broadcasted_iota(jnp.int32, shape, dim)


def pack_kernel(
    heads_axis, q_in, k_in, v_in, at_in, bt_in, out_ref, q_ref, k_ref, v_ref, at_ref, bt_ref, sems
):
    peers, tokens = out_ref.shape[0], q_ref.shape[0]
    pairs = ((at_in, at_ref), (bt_in, bt_ref), (k_in, k_ref), (v_in, v_ref), (q_in, q_ref))
    copies = [pltpu.make_async_copy(a, b, sems.at[i]) for i, (a, b) in enumerate(pairs)]
    for copy in copies:
        copy.start()
    subs = peers // heads_axis
    key_heads = [(dest % heads_axis) * subs + dest // heads_axis for dest in range(peers)]
    for copy in copies[:2]:
        copy.wait()
    value_heads = at_ref.shape[0]
    row, entry = iota((peers * GATES, value_heads), 0), iota((peers * GATES, value_heads), 1)
    dest, which = row // GATES, row % GATES
    first = 2 * ((dest % heads_axis) * subs + dest // heads_axis)
    pick_a = jnp.where((which < 2) & (entry == first + which), 1.0, 0.0).astype(BF16)
    pick_b = jnp.where(
        (which >= 2) & (which < 4) & (entry == first + which - 2), 1.0, 0.0
    ).astype(BF16)
    picked = (dot(pick_a, at_ref[...]) + dot(pick_b, bt_ref[...])).astype(BF16)
    lane_shift = tokens * lax.rem(lax.axis_index("head"), SPAN // tokens)
    place = jnp.where(
        iota((tokens, SPAN), 1) == iota((tokens, SPAN), 0) + lane_shift, 1.0, 0.0
    ).astype(BF16)
    gates = dot(picked, place).astype(BF16)
    for dest in range(peers):
        out_ref[dest, 4 * tokens :, :] = gates[GATES * dest : GATES * (dest + 1), :]

    def laid(ref, lane, start):
        for dest, key_head in enumerate(key_heads):
            at = lane(key_head) * 128
            out_ref[dest, start * tokens : (start + 1) * tokens, :] = ref[
                :, at : at + 128
            ]

    copies[2].wait()
    laid(k_ref, lambda key_head: key_head, 0)
    copies[3].wait()
    laid(v_ref, lambda key_head: 2 * key_head, 1)
    laid(v_ref, lambda key_head: 2 * key_head + 1, 2)
    copies[4].wait()
    laid(q_ref, lambda key_head: key_head, 3)


def invert(systems):
    size = systems[0].shape[0]
    blocks = size // SUB
    row, col = iota((size, size), 0), iota((size, size), 1)
    diagonal = (row // SUB) == (col // SUB)
    compact = jnp.concatenate(
        [
            jnp.sum(jnp.where(diagonal, n, 0.0).reshape(blocks, SUB, size), axis=0)
            for n in systems
        ],
        axis=0,
    )
    count = len(systems)
    lane, line = iota(compact.shape, 1), iota(compact.shape, 0)
    solved = jnp.where(lane % SUB == line % SUB, 1.0, 0.0).reshape(count, SUB, size)
    for m in range(SUB - 1):
        spread = jnp.take_along_axis(compact, (lane // SUB) * SUB + m, axis=1)
        solved = solved - spread.reshape(count, SUB, size) * solved[:, m : m + 1, :]
    lows = [halves(n) for n in systems]
    placed = jnp.where(diagonal, 1.0, 0.0).astype(BF16)
    parts = [
        tuple(jnp.concatenate([x] * blocks, axis=0) * placed for x in halves(solved[i]))
        for i in range(count)
    ]
    width = SUB
    while width < size:
        odd = [(j, j + width) for j in range(width, size, 2 * width)]

        def rows_of(x):
            return jnp.concatenate([x[lo:hi] for lo, hi in odd], axis=0)

        def woven(even, x):
            pieces = []
            for j, (lo, hi) in enumerate(odd):
                pieces += [even[lo - width : lo], x[j * width : (j + 1) * width]]
            return jnp.concatenate(pieces, axis=0)

        below = ((row // (2 * width)) == (col // (2 * width))) & ((col // width) % 2 == 0)
        mask = rows_of(jnp.where(below, 1.0, 0.0).astype(BF16))
        blank = jnp.zeros((size, size), BF16)
        firsts = [
            mm_parts((rows_of(n[0]) * mask, rows_of(n[1]) * mask), t) for n, t in zip(lows, parts)
        ]
        spreads = [tuple(woven(blank, x) for x in halves(first)) for first in firsts]
        odds = [(rows_of(t[0]), rows_of(t[1])) for t in parts]
        seconds = [halves(-mm_parts(o, spread)) for o, spread in zip(odds, spreads)]
        parts = [
            tuple(woven(t[i], o[i] + second[i]) for i in range(2))
            for t, o, second in zip(parts, odds, seconds)
        ]
        width *= 2
    return parts


def gate_values(gates, sub, alog_ref, dt_ref):
    second = iota(gates.shape, 0) % GATES == 1
    a_log = jnp.where(second, alog_ref[2 * sub + 1], alog_ref[2 * sub])
    dt_bias = jnp.where(second, dt_ref[2 * sub + 1], dt_ref[2 * sub])
    shifted = gates + dt_bias
    soft = jnp.maximum(shifted, 0.0) + jnp.log1p(jnp.exp(-jnp.abs(shifted)))
    return -jnp.exp(a_log) * soft, 1.0 / (1.0 + jnp.exp(-gates))


def convolved(rows, at, count, lanes, tap):
    summed = tap[0:1] * rows[at : at + count, lanes]
    for j in range(1, CONV):
        summed = summed + tap[j : j + 1] * rows[at + j : at + j + count, lanes]
    return silu(summed)


def key_tap(sub, tap_ref):
    return tap_ref[:, pl.ds(pl.multiple_of(sub * DK, 128), DK)]


def value_taps(sub, cv_ref):
    lane = pl.multiple_of(sub * 2 * DV, 128)
    return [cv_ref[:, pl.ds(pl.multiple_of(lane + r * DV, 128), DV)] for r in range(2)]


def widened(rows, recv_ref, starts, tokens):
    rows[0:8, :] = jnp.zeros((8, rows.shape[1]), F32)
    for s in range(recv_ref.shape[0]):
        for g, start in enumerate(starts):
            rows[8 + s * tokens : 8 + (s + 1) * tokens, g * 128 : (g + 1) * 128] = recv_ref[
                s, start : start + tokens, :
            ].astype(F32)


def keys_kernel(
    recv_ref,
    ck_ref,
    alog_ref,
    dt_ref,
    keys_ref,
    keys_t_ref,
    t_ref,
    lin_ref,
    ends_ref,
    within_ref,
    cols_ref,
    early_ref,
    rows,
):
    sub = lax.axis_index("sub")
    later = lax.axis_index("half") > 0
    peers = recv_ref.shape[0]
    tokens = (recv_ref.shape[1] - GATES) // 4
    spans = peers * tokens // SPAN
    tap = key_tap(sub, ck_ref)
    widened(rows, recv_ref, [0], tokens)
    stacked = [
        sum(recv_ref[s, 4 * tokens :, :].astype(F32) for s in range(n, n + SPAN // tokens))
        for n in range(0, peers, SPAN // tokens)
    ]
    stacked.append(jnp.zeros((SPAN - spans * GATES, SPAN), F32))
    gates = jnp.concatenate(stacked, axis=0)
    decay, rate = gate_values(gates, sub, alog_ref, dt_ref)
    early_ref[...] = jnp.where(iota((8, SPAN), 0) < 2, decay[0:8], rate[0:8])
    skipped = later & (iota(gates.shape, 0) < GATES) & (iota(gates.shape, 1) < EDGE)
    decay = jnp.where(skipped, 0.0, decay)
    rate = jnp.where(skipped, 0.0, rate)
    lane_r, lane_c = iota((SPAN, SPAN), 0), iota((SPAN, SPAN), 1)
    upto = jnp.where(lane_r <= lane_c, 1.0, 0.0).astype(BF16)
    d_high, _ = halves(decay)
    d_mid, d_low = halves(decay - d_high.astype(F32))
    cum = dot(d_high, upto) + (dot(d_mid, upto) + dot(d_low, upto))
    growth = jnp.exp(cum)
    here = pltpu.roll(rate, rate.shape[0] - 2, 0)
    rest = jnp.exp(cum[:, SPAN - 1 :] - cum) * here
    which = iota(gates.shape, 0) % GATES
    mixed = jnp.where(which < 2, cum, pltpu.roll(growth, 2, 0))
    columns = jnp.transpose(jnp.where(which < 4, mixed, pltpu.roll(rest, 4, 0)))
    cols_ref[...] = columns
    lower = lane_r >= lane_c
    strict = lane_r > lane_c
    both = [(n, r) for n in range(spans) for r in range(2)]
    keys = []
    for n in range(spans):
        k_n = unit(convolved(rows, n * SPAN + 8 - EDGE, SPAN, slice(0, DK), tap), 1.0)
        keys_ref[n * SPAN : (n + 1) * SPAN, :] = k_n
        keys.append(k_n)
    keys_t = []
    for n in range(spans):
        kt_n = jnp.transpose(keys[n].astype(F32)).astype(BF16)
        keys_t_ref[n] = kt_n
        keys_t.append(kt_n)
    grams = [dot(keys[n], keys_t[n]) for n in range(spans)]
    systems = []
    for n, r in both:
        at = GATES * n + r
        gap = columns[:, at : at + 1] - cum[at : at + 1, :]
        within = jnp.exp(jnp.where(lower, gap, 0.0)) * here[at : at + 1, :]
        within_ref[r, n * SPAN : (n + 1) * SPAN, :] = jnp.where(lower, within, 0.0).astype(BF16)
        systems.append(jnp.where(strict, within * grams[n], 0.0))
    inverses = invert(systems)
    for i, (n, r) in enumerate(both):
        t_ref[r, n] = jnp.concatenate(inverses[i], axis=1)
    scaled = []
    for n, r in both:
        at = GATES * n + r
        right = (columns[:, at + 2 : at + 3] * keys[n].astype(F32)).astype(BF16)
        scaled.append(jnp.concatenate([right, right], axis=0))
    w_mats = [dot(jnp.concatenate(t, axis=1), x) for t, x in zip(inverses, scaled)]
    weighed = []
    for (n, r), w_mat in zip(both, w_mats):
        at = GATES * n + r
        weighed.append((columns[:, at + 4 : at + 5] * w_mat).astype(BF16))
    moved = [
        dot(keys_t[n], jnp.concatenate(weighed[2 * n : 2 * n + 2], axis=1)) for n in range(spans)
    ]
    ends_ref[...] = jnp.broadcast_to(growth[:, SPAN - 1 :], ends_ref.shape)
    for n, r in both:
        lin_ref[r, n] = moved[n][:, r * DK : (r + 1) * DK].astype(BF16)


def step(end, moved, state, parts):
    both = jnp.concatenate([moved, moved], axis=1)
    return end * state - dot(both, jnp.concatenate(parts, axis=0))


def values_part(recv_ref, cv_ref, keys_t_ref, t_ref, cols_ref, rows, vs):
    sub = lax.axis_index("sub")
    tokens = (recv_ref.shape[1] - GATES) // 4
    spans = t_ref.shape[1]
    taps = value_taps(sub, cv_ref)
    widened(rows, recv_ref, [tokens, 2 * tokens], tokens)
    both = [(n, r) for n in range(spans) for r in range(2)]
    values = []
    for n, r in both:
        lanes = slice(r * DV, (r + 1) * DV)
        v_n = convolved(rows, n * SPAN + 8 - EDGE, SPAN, lanes, taps[r]).astype(BF16)
        vs[n * SPAN : (n + 1) * SPAN, lanes] = v_n
        values.append(jnp.concatenate([v_n, v_n], axis=0))
    solved = [dot(t_ref[r, n], v) for (n, r), v in zip(both, values)]
    weighed = []
    for (n, r), u_mat in zip(both, solved):
        at = GATES * n + r
        weighed.append((cols_ref[:, at + 4 : at + 5] * u_mat).astype(BF16))
    moved = [
        dot(keys_t_ref[n], jnp.concatenate(weighed[2 * n : 2 * n + 2], axis=1))
        for n in range(spans)
    ]
    return [moved[n][:, r * DV : (r + 1) * DV] for n, r in both]


def opening_kernel(
    recv_ref, cv_ref, keys_t_ref, t_ref, lin_ref, ends_ref, cols_ref, hop_ref, vs_ref, xs_ref, rows
):
    first = lax.axis_index("half") == 0
    peers = recv_ref.shape[0]
    tokens = (recv_ref.shape[1] - GATES) // 4
    spans = t_ref.shape[1]
    edges = []
    for which in (3, 0, 1, 2):
        end = (which + 1) * tokens
        edges.append(recv_ref[peers - 1, end - 16 : end, :].astype(F32)[16 - EDGE :])
    edges.append(jnp.zeros((16 - 4 * EDGE, 128), F32))
    hop_ref[2 * DK :, :] = jnp.concatenate(edges, axis=0).astype(BF16)

    @pl.when(first)
    def _():
        adds = values_part(recv_ref, cv_ref, keys_t_ref, t_ref, cols_ref, rows, vs_ref)
        states = [adds[0], adds[1]]
        for n in range(1, spans):
            for r in range(2):
                parts = halves(states[r])
                xs_ref[n, :, r * DV : (r + 1) * DV] = jnp.concatenate(parts, axis=0)
                end = ends_ref[GATES * n + r : GATES * n + r + 1, :]
                states[r] = step(end, lin_ref[r, n], states[r], parts) + adds[2 * n + r]
        for r in range(2):
            hop_ref[r * DK : (r + 1) * DK, :] = states[r].astype(BF16)

    @pl.when(jnp.logical_not(first))
    def _():
        hop_ref[0 : 2 * DK, :] = jnp.zeros((2 * DK, DV), BF16)


def output_kernel(
    recv_ref,
    cq_ref,
    cv_ref,
    keys_ref,
    keys_t_ref,
    t_ref,
    lin_ref,
    ends_ref,
    within_ref,
    cols_ref,
    hop_ref,
    vs_ref,
    xs_ref,
    oa_ref,
    om_ref,
    last_ref,
    rows,
    query_rows,
    values,
    inner,
    readers,
    states_ref,
):
    sub = lax.axis_index("sub")
    first = lax.axis_index("half") == 0
    tokens = (recv_ref.shape[1] - GATES) // 4
    spans = t_ref.shape[1]
    both = [(n, r) for n in range(spans) for r in range(2)]
    tap = key_tap(sub, cq_ref)
    widened(query_rows, recv_ref, [3 * tokens], tokens)

    def span_rows(n):
        return slice(n * SPAN, (n + 1) * SPAN)

    def growth(n, r):
        return cols_ref[:, GATES * n + 2 + r : GATES * n + 3 + r]

    def prepare():
        queries = []
        for n in range(spans):
            at = n * SPAN + 8 - EDGE
            q_n = unit(convolved(query_rows, at, SPAN, slice(0, DK), tap), DK**-0.5)
            queries.append(q_n)
            readers[n, 0:SPAN, :] = keys_ref[span_rows(n), :]
            readers[n, SPAN:, :] = q_n
        scores = [dot(queries[n], keys_t_ref[n]) for n in range(spans)]
        for n, r in both:
            weight = within_ref[r, span_rows(n), :].astype(F32)
            inner[r, n] = (weight * scores[n]).astype(BF16)

    def twice(x, axis):
        return jnp.concatenate([x, x], axis=axis)

    @pl.when(first)
    def _():
        prepare()
        reads = [dot(twice(readers[n], 1), xs_ref[n]) for n in range(1, spans)]
        rests, seen = [], []
        for n, r in both:
            lanes = slice(r * DV, (r + 1) * DV)
            value = vs_ref[span_rows(n), lanes]
            if n == 0:
                rests.append(value)
                seen.append(None)
            else:
                read = growth(n, r) * reads[n - 1][:SPAN, lanes]
                rests.append((value.astype(F32) - read).astype(BF16))
                seen.append(growth(n, r) * reads[n - 1][SPAN:, lanes])
        fresh = [dot(t_ref[r, n], twice(x, 0)).astype(BF16) for (n, r), x in zip(both, rests)]
        spreads = [dot(inner[r, n], x) for (n, r), x in zip(both, fresh)]
        for (n, r), x, y in zip(both, spreads, seen):
            oa_ref[r, span_rows(n), :] = x if y is None else x + y
        for r in range(2):
            last_ref[r, :, 0:DV] = hop_ref[r * DK : (r + 1) * DK, :].astype(F32)
            last_ref[r, :, DV:] = jnp.zeros((DK, DV), F32)

    @pl.when(jnp.logical_not(first))
    def _():
        adds = values_part(recv_ref, cv_ref, keys_t_ref, t_ref, cols_ref, rows, values)
        zero_half = jnp.zeros((DK, DV), F32)
        identity = jnp.where(iota((DK, DK), 0) == iota((DK, DK), 1), 1.0, 0.0)
        states = [
            jnp.concatenate(
                [adds[r], ends_ref[r : r + 1, :] * identity - lin_ref[r, 0].astype(F32)], axis=1
            )
            for r in range(2)
        ]
        for n in range(1, spans):
            for r in range(2):
                parts = halves(states[r])
                states_ref[r, n] = jnp.concatenate(parts, axis=0)
                add = jnp.concatenate([adds[2 * n + r], zero_half], axis=1)
                end = ends_ref[GATES * n + r : GATES * n + r + 1, :]
                end = jnp.concatenate([end, end], axis=1)
                states[r] = step(end, lin_ref[r, n], states[r], parts) + add
        for r in range(2):
            last_ref[r] = states[r]
        prepare()
        reads = [
            dot(twice(readers[n], 1), states_ref[r, n]) if n > 0 else None for n, r in both
        ]
        rests, seen = [], []
        for (n, r), read in zip(both, reads):
            value = values[span_rows(n), r * DV : (r + 1) * DV].astype(F32)
            if n == 0:
                known = growth(n, r) * readers[n].astype(F32)[:SPAN]
                asked = growth(n, r) * readers[n].astype(F32)[SPAN:]
                rest = jnp.concatenate([value, -known], axis=1)
                seen.append(jnp.concatenate([zero_half, asked], axis=1))
            else:
                rest = jnp.concatenate([value, zero_half], axis=1) - growth(n, r) * read[:SPAN]
                seen.append(growth(n, r) * read[SPAN:])
            rests.append(rest.astype(BF16))
        fresh = [dot(t_ref[r, n], twice(x, 0)).astype(BF16) for (n, r), x in zip(both, rests)]
        spreads = [dot(inner[r, n], x) for (n, r), x in zip(both, fresh)]
        for (n, r), x, y in zip(both, spreads, seen):
            out = x + y
            oa_ref[r, span_rows(n), :] = out[:, :DV]
            om_ref[r, span_rows(n), :] = out[:, DV:].astype(BF16)


def first_tokens(hop_ref, recv_ref, early_ref, cq_ref, ck_ref, cv_ref, rows):
    sub = lax.axis_index("sub")
    tokens = (recv_ref.shape[1] - GATES) // 4
    taps = [key_tap(sub, cq_ref), key_tap(sub, ck_ref)] + value_taps(sub, cv_ref)
    results = []
    edges = hop_ref[2 * DK :, :].astype(F32)
    for g, first in enumerate((3, 0, 1, 2)):
        lanes = slice(g * 128, (g + 1) * 128)
        start = first * tokens
        rows[16 - EDGE : 16, lanes] = edges[EDGE * g : EDGE * (g + 1)]
        rows[16:32, lanes] = recv_ref[0, start : start + 16, :].astype(F32)
        results.append(convolved(rows, 16 - EDGE, 8, lanes, taps[g]))
    q_cols = jnp.transpose(unit(results[0], DK**-0.5).astype(F32))
    k_cols = jnp.transpose(unit(results[1], 1.0).astype(F32))
    gates = early_ref[...]
    line = iota((8, DV), 0)
    finals, outputs = [], []
    for r in range(2):
        values = results[2 + r].astype(BF16).astype(F32)
        entering = hop_ref[r * DK : (r + 1) * DK, :].astype(F32)
        state, out = entering, jnp.zeros((8, DV), F32)
        for t in range(EDGE):
            k_t, q_t = k_cols[:, t : t + 1], q_cols[:, t : t + 1]
            state = jnp.exp(gates[r : r + 1, t : t + 1]) * state
            held = jnp.sum(k_t * state, axis=0, keepdims=True)
            state = state + k_t * (
                gates[2 + r : 3 + r, t : t + 1] * (values[t : t + 1, :] - held)
            )
            out = jnp.where(line == t, jnp.sum(q_t * state, axis=0, keepdims=True), out)
        finals.append(state)
        outputs.append(out)
    return finals, outputs


def finish_kernel(
    hop_ref, recv_ref, early_ref, cq_ref, ck_ref, cv_ref, gain_ref, oa_ref, om_ref, out_ref, rows
):
    peers, tokens = out_ref.shape[0], out_ref.shape[1]
    first = lax.axis_index("half") == 0
    gain = gain_ref[...]
    chunks = 4
    part, peer_part = peers * tokens // chunks, peers // chunks

    def put(c, r, core):
        scale = lax.rsqrt(jnp.mean(core * core, axis=-1, keepdims=True) + EPS)
        normed = (core * scale * gain).astype(BF16)
        out_ref[c * peer_part : (c + 1) * peer_part, :, r * DV : (r + 1) * DV] = normed.reshape(
            peer_part, tokens, DV
        )

    @pl.when(first)
    def _():
        for c in range(chunks):
            for r in range(2):
                put(c, r, oa_ref[r, c * part : (c + 1) * part, :])

    @pl.when(jnp.logical_not(first))
    def _():
        finals, outputs = first_tokens(hop_ref, recv_ref, early_ref, cq_ref, ck_ref, cv_ref, rows)
        replaced = iota((8, DV), 0) < EDGE
        passed = [dot(om_ref[r], finals[r].astype(BF16)) for r in range(2)]
        for c in range(chunks):
            at = c * part
            for r in range(2):
                core = oa_ref[r, at : at + part, :] + passed[r][at : at + part]
                if c == 0:
                    core = jnp.concatenate(
                        [jnp.where(replaced, outputs[r], core[0:8]), core[8:]], axis=0
                    )
                put(c, r, core)


def advance_kernel(
    hop_ref, recv_ref, early_ref, cq_ref, ck_ref, cv_ref, hop_own, last_ref, next_ref, rows
):
    finals, _ = first_tokens(hop_ref, recv_ref, early_ref, cq_ref, ck_ref, cv_ref, rows)
    first = lax.axis_index("half") == 0
    for r in range(2):
        last = last_ref[r]
        through = mm_parts(halves(last[:, DV:]), halves(finals[r]))
        moved = jnp.where(first, 0.0, through) + last[:, :DV]
        next_ref[r * DK : (r + 1) * DK, :] = moved.astype(BF16)
    next_ref[2 * DK :, :] = hop_own[2 * DK :, :]


def gate_kernel(heads_axis, normed_ref, z_ref, out_ref, made, sems):
    subs = normed_ref.shape[0] // heads_axis
    width = subs * 2 * DV
    copies = []
    for head in range(heads_axis):
        for sub in range(subs):
            at = (head * subs + sub) * 2 * DV
            gate = silu(z_ref[:, at : at + 2 * DV].astype(F32))
            value = normed_ref[sub * heads_axis + head].astype(F32)
            made[:, at : at + 2 * DV] = (value * gate).astype(BF16)
        lanes = pl.ds(head * width, width)
        copy = pltpu.make_async_copy(made.at[:, lanes], out_ref.at[:, lanes], sems.at[head])
        copy.start()
        copies.append(copy)
    for copy in copies:
        copy.wait()


VMEM = pl.BlockSpec(memory_space=pltpu.VMEM)
SMEM = pl.BlockSpec(memory_space=pltpu.SMEM)
ANY = pl.BlockSpec(memory_space=pl.ANY)


def near(x):
    return pltpu.with_memory_space_constraint(x, pltpu.VMEM)


def far(x):
    return pltpu.with_memory_space_constraint(x, pltpu.HBM)


def call(kernel, outs, in_specs, scratch=(), out_spec=VMEM, flops=1 << 26, moved=1 << 21):
    return pl.pallas_call(
        kernel,
        out_shape=outs,
        in_specs=in_specs,
        out_specs=jax.tree.map(lambda _: out_spec, outs),
        scratch_shapes=list(scratch),
        compiler_params=pltpu.CompilerParams(vmem_limit_bytes=VMEM_BYTES),
        cost_estimate=pl.CostEstimate(flops=flops, bytes_accessed=moved, transcendentals=0),
    )


def local(
    q_rows,
    k_rows,
    v_rows,
    z_rows,
    a_rows,
    b_rows,
    conv_q,
    conv_k,
    conv_v,
    a_log,
    dt_bias,
    norm_gain,
):
    shards, subs, heads_axis = (lax.axis_size(a) for a in ("half", "sub", "head"))
    peers, tokens = subs * heads_axis, q_rows.shape[0]
    total = peers * tokens
    spans = total // SPAN
    group = ("sub", "head")
    route = [(i, i + 1) for i in range(shards - 1)]
    inputs = [far(x) for x in (q_rows, k_rows, v_rows, a_rows.T, b_rows.T)]
    packed = call(
        functools.partial(pack_kernel, heads_axis),
        pltpu.VMEM((peers, GATES + 4 * tokens, 128), BF16),
        [ANY] * 5,
        [pltpu.VMEM(x.shape, BF16) for x in inputs] + [pltpu.SemaphoreType.DMA((5,))],
        flops=1 << 20,
    )(*inputs)
    blocks = near(lax.all_to_all(packed, group, 0, 0, tiled=True))
    keys, keys_t, inverses, lins, ends, within, cols, early = call(
        keys_kernel,
        (
            pltpu.VMEM((total, DK), BF16),
            pltpu.VMEM((spans, DK, SPAN), BF16),
            pltpu.VMEM((2, spans, SPAN, 2 * SPAN), BF16),
            pltpu.VMEM((2, spans, DK, DK), BF16),
            pltpu.VMEM((SPAN, DK), F32),
            pltpu.VMEM((2, total, SPAN), BF16),
            pltpu.VMEM((SPAN, SPAN), F32),
            pltpu.VMEM((8, SPAN), F32),
        ),
        [VMEM, VMEM, SMEM, SMEM],
        [pltpu.VMEM((8 + total, DK), F32)],
        flops=1 << 32,
    )(blocks, conv_k, a_log, dt_bias)
    keys, keys_t, inverses, lins, ends, within, cols, early = (
        near(x) for x in (keys, keys_t, inverses, lins, ends, within, cols, early)
    )
    hop, values, starts = call(
        opening_kernel,
        (
            pltpu.VMEM((2 * DK + 16, 128), BF16),
            pltpu.VMEM((total, 2 * DV), BF16),
            pltpu.VMEM((spans, 2 * DK, 2 * DV), BF16),
        ),
        [VMEM] * 7,
        [pltpu.VMEM((8 + total, 2 * DV), F32)],
        flops=1 << 32,
    )(blocks, conv_v, keys_t, inverses, lins, ends, cols)
    entering = near(lax.ppermute(hop, "half", route))
    hop, values, starts = near(hop), near(values), near(starts)
    out_a, out_m, last = call(
        output_kernel,
        (
            pltpu.VMEM((2, total, DV), F32),
            pltpu.VMEM((2, total, DV), BF16),
            pltpu.VMEM((2, DK, 2 * DV), F32),
        ),
        [VMEM] * 13,
        [
            pltpu.VMEM((8 + total, 2 * DV), F32),
            pltpu.VMEM((8 + total, DK), F32),
            pltpu.VMEM((total, 2 * DV), BF16),
            pltpu.VMEM((2, spans, SPAN, SPAN), BF16),
            pltpu.VMEM((spans, 2 * SPAN, DK), BF16),
            pltpu.VMEM((2, spans, 2 * DK, 2 * DV), BF16),
        ],
        flops=1 << 32,
    )(
        blocks,
        conv_q,
        conv_v,
        keys,
        keys_t,
        inverses,
        lins,
        ends,
        within,
        cols,
        hop,
        values,
        starts,
    )
    for _ in range(shards - 2):
        moved = call(
            advance_kernel,
            pltpu.VMEM(hop.shape, BF16),
            [VMEM] * 8,
            [pltpu.VMEM((32, 512), F32)],
        )(entering, blocks, early, conv_q, conv_k, conv_v, hop, near(last))
        entering = near(lax.ppermute(moved, "half", route))
    normed = call(
        finish_kernel,
        pltpu.VMEM((peers, tokens, 2 * DV), BF16),
        [VMEM] * 9,
        [pltpu.VMEM((32, 512), F32)],
    )(
        entering,
        blocks,
        early,
        conv_q,
        conv_k,
        conv_v,
        norm_gain.reshape(1, DV),
        near(out_a),
        near(out_m),
    )
    returned = near(lax.all_to_all(normed, group, 0, 0, tiled=True))
    return call(
        functools.partial(gate_kernel, heads_axis),
        jax.ShapeDtypeStruct(z_rows.shape, BF16),
        [VMEM] * 2,
        [pltpu.VMEM(z_rows.shape, BF16), pltpu.SemaphoreType.DMA((heads_axis,))],
        ANY,
    )(returned, z_rows)


def solution(mesh):
    heads_axis = mesh.shape["head"]
    subs = KH // heads_axis
    regrouped = Mesh(
        mesh.devices.reshape(mesh.shape["ctx"] // subs, subs, heads_axis), ("half", "sub", "head")
    )
    row = P(("half", "sub", "head"), None)
    placed = (row,) * 6 + (P(None, "head"),) * 3 + (P("head"),) * 2 + (P(),)
    return jax.shard_map(local, mesh=regrouped, in_specs=placed, out_specs=row, check_vma=False)
```

```python
import functools

import jax
import jax.numpy as jnp
from jax import lax
from jax.experimental import pallas as pl
from jax.experimental.pallas import tpu as pltpu
from jax.sharding import Mesh, PartitionSpec as P

DK = 128
DV = 128
CONV = 4
KH = 16
SUB = 16
SPAN = 128
EDGE = CONV - 1
EPS = 1e-06
F32 = jnp.float32
BF16 = jnp.bfloat16
VMEM_BYTES = 24 * 1024 * 1024
GATES = 8


def dot(a, b, dims=((1,), (0,))):
    return lax.dot_general(a, b, (dims, ((), ())), preferred_element_type=F32)


def halves(x):
    high = x.astype(BF16)
    return high, (x - high.astype(F32)).astype(BF16)


def mm_parts(a, b):
    both = jnp.concatenate(a, axis=1)
    return dot(both, jnp.concatenate([b[0], b[0]], axis=0)) + dot(a[0], b[1])


def silu(x):
    half = 0.5 * x
    return half + half * jnp.tanh(half)


def unit(y, factor):
    scale = lax.rsqrt(jnp.sum(y * y, axis=-1, keepdims=True) + EPS)
    return (y * scale * factor).astype(BF16)


def iota(shape, dim):
    return lax.broadcasted_iota(jnp.int32, shape, dim)


def block_of(x, size):
    return lax.shift_right_logical(x, jnp.full(x.shape, size.bit_length() - 1, jnp.int32))


def place_in(x, size):
    return x & (size - 1)


def pack_kernel(
    heads_axis, q_in, k_in, v_in, at_in, bt_in, out_ref, q_ref, k_ref, v_ref, at_ref, bt_ref, sems
):
    peers, tokens = out_ref.shape[0], q_ref.shape[0]
    pairs = ((at_in, at_ref), (bt_in, bt_ref), (k_in, k_ref), (v_in, v_ref), (q_in, q_ref))
    copies = [pltpu.make_async_copy(a, b, sems.at[i]) for i, (a, b) in enumerate(pairs)]
    for copy in copies:
        copy.start()
    subs = peers // heads_axis
    key_heads = [(dest % heads_axis) * subs + dest // heads_axis for dest in range(peers)]
    for copy in copies[:2]:
        copy.wait()
    value_heads = at_ref.shape[0]
    row, entry = iota((peers * GATES, value_heads), 0), iota((peers * GATES, value_heads), 1)
    dest, which = block_of(row, GATES), place_in(row, GATES)
    first = 2 * (place_in(dest, heads_axis) * subs + block_of(dest, heads_axis))
    pick_a = jnp.where((which < 2) & (entry == first + which), 1.0, 0.0).astype(BF16)
    pick_b = jnp.where(
        (which >= 2) & (which < 4) & (entry == first + which - 2), 1.0, 0.0
    ).astype(BF16)
    picked = (dot(pick_a, at_ref[...]) + dot(pick_b, bt_ref[...])).astype(BF16)
    lane_shift = tokens * lax.rem(lax.axis_index("head"), SPAN // tokens)
    place = jnp.where(
        iota((tokens, SPAN), 1) == iota((tokens, SPAN), 0) + lane_shift, 1.0, 0.0
    ).astype(BF16)
    gates = dot(picked, place).astype(BF16)
    for dest in range(peers):
        out_ref[dest, 4 * tokens :, :] = gates[GATES * dest : GATES * (dest + 1), :]

    def laid(ref, lane, start):
        for dest, key_head in enumerate(key_heads):
            at = lane(key_head) * 128
            out_ref[dest, start * tokens : (start + 1) * tokens, :] = ref[
                :, at : at + 128
            ]

    copies[2].wait()
    laid(k_ref, lambda key_head: key_head, 0)
    copies[3].wait()
    laid(v_ref, lambda key_head: 2 * key_head, 1)
    laid(v_ref, lambda key_head: 2 * key_head + 1, 2)
    copies[4].wait()
    laid(q_ref, lambda key_head: key_head, 3)


def invert(systems):
    size = systems[0].shape[0]
    blocks = size // SUB
    row, col = iota((size, size), 0), iota((size, size), 1)
    diagonal = block_of(row, SUB) == block_of(col, SUB)
    compact = jnp.concatenate(
        [
            jnp.sum(jnp.where(diagonal, n, 0.0).reshape(blocks, SUB, size), axis=0)
            for n in systems
        ],
        axis=0,
    )
    count = len(systems)
    lane, line = iota(compact.shape, 1), iota(compact.shape, 0)
    solved = jnp.where(place_in(lane ^ line, SUB) == 0, 1.0, 0.0).reshape(count, SUB, size)
    for m in range(SUB - 1):
        source = (lane & ~(SUB - 1)) | m
        spread = jnp.take_along_axis(compact, source, axis=1, mode="promise_in_bounds")
        solved = solved - spread.reshape(count, SUB, size) * solved[:, m : m + 1, :]
    lows = [halves(n) for n in systems]
    placed = jnp.where(diagonal, 1.0, 0.0).astype(BF16)
    parts = [
        tuple(jnp.concatenate([x] * blocks, axis=0) * placed for x in halves(solved[i]))
        for i in range(count)
    ]
    width = SUB
    while width < size:
        odd = [(j, j + width) for j in range(width, size, 2 * width)]

        def rows_of(x):
            return jnp.concatenate([x[lo:hi] for lo, hi in odd], axis=0)

        def woven(even, x):
            pieces = []
            for j, (lo, hi) in enumerate(odd):
                pieces += [even[lo - width : lo], x[j * width : (j + 1) * width]]
            return jnp.concatenate(pieces, axis=0)

        below = (block_of(row ^ col, 2 * width) == 0) & ((col & width) == 0)
        mask = rows_of(jnp.where(below, 1.0, 0.0).astype(BF16))
        blank = jnp.zeros((size, size), BF16)
        firsts = [
            mm_parts((rows_of(n[0]) * mask, rows_of(n[1]) * mask), t) for n, t in zip(lows, parts)
        ]
        spreads = [tuple(woven(blank, x) for x in halves(first)) for first in firsts]
        odds = [(rows_of(t[0]), rows_of(t[1])) for t in parts]
        seconds = [halves(-mm_parts(o, spread)) for o, spread in zip(odds, spreads)]
        parts = [
            tuple(woven(t[i], o[i] + second[i]) for i in range(2))
            for t, o, second in zip(parts, odds, seconds)
        ]
        width *= 2
    return parts


def gate_values(gates, sub, alog_ref, dt_ref):
    second = place_in(iota(gates.shape, 0), GATES) == 1
    a_log = jnp.where(second, alog_ref[2 * sub + 1], alog_ref[2 * sub])
    dt_bias = jnp.where(second, dt_ref[2 * sub + 1], dt_ref[2 * sub])
    shifted = gates + dt_bias
    soft = jnp.maximum(shifted, 0.0) + jnp.log1p(jnp.exp(-jnp.abs(shifted)))
    return -jnp.exp(a_log) * soft, 1.0 / (1.0 + jnp.exp(-gates))


def convolved(rows, at, count, lanes, tap):
    summed = tap[0:1] * rows[at : at + count, lanes]
    for j in range(1, CONV):
        summed = summed + tap[j : j + 1] * rows[at + j : at + j + count, lanes]
    return silu(summed)


def key_tap(sub, tap_ref):
    return tap_ref[:, pl.ds(pl.multiple_of(sub * DK, 128), DK)]


def value_taps(sub, cv_ref):
    lane = pl.multiple_of(sub * 2 * DV, 128)
    return [cv_ref[:, pl.ds(pl.multiple_of(lane + r * DV, 128), DV)] for r in range(2)]


def widened(rows, recv_ref, starts, tokens):
    rows[0:8, :] = jnp.zeros((8, rows.shape[1]), F32)
    for s in range(recv_ref.shape[0]):
        for g, start in enumerate(starts):
            rows[8 + s * tokens : 8 + (s + 1) * tokens, g * 128 : (g + 1) * 128] = recv_ref[
                s, start : start + tokens, :
            ].astype(F32)


def keys_kernel(
    recv_ref,
    ck_ref,
    alog_ref,
    dt_ref,
    keys_ref,
    keys_t_ref,
    t_ref,
    lin_ref,
    ends_ref,
    within_ref,
    cols_ref,
    early_ref,
    rows,
):
    sub = lax.axis_index("sub")
    later = lax.axis_index("half") > 0
    peers = recv_ref.shape[0]
    tokens = (recv_ref.shape[1] - GATES) // 4
    spans = peers * tokens // SPAN
    tap = key_tap(sub, ck_ref)
    widened(rows, recv_ref, [0], tokens)
    stacked = [
        sum(recv_ref[s, 4 * tokens :, :].astype(F32) for s in range(n, n + SPAN // tokens))
        for n in range(0, peers, SPAN // tokens)
    ]
    stacked.append(jnp.zeros((SPAN - spans * GATES, SPAN), F32))
    gates = jnp.concatenate(stacked, axis=0)
    decay, rate = gate_values(gates, sub, alog_ref, dt_ref)
    early_ref[...] = jnp.where(iota((8, SPAN), 0) < 2, decay[0:8], rate[0:8])
    skipped = later & (iota(gates.shape, 0) < GATES) & (iota(gates.shape, 1) < EDGE)
    decay = jnp.where(skipped, 0.0, decay)
    rate = jnp.where(skipped, 0.0, rate)
    lane_r, lane_c = iota((SPAN, SPAN), 0), iota((SPAN, SPAN), 1)
    upto = jnp.where(lane_r <= lane_c, 1.0, 0.0).astype(BF16)
    d_high, _ = halves(decay)
    d_mid, d_low = halves(decay - d_high.astype(F32))
    cum = dot(d_high, upto) + (dot(d_mid, upto) + dot(d_low, upto))
    growth = jnp.exp(cum)
    here = pltpu.roll(rate, rate.shape[0] - 2, 0)
    rest = jnp.exp(cum[:, SPAN - 1 :] - cum) * here
    which = place_in(iota(gates.shape, 0), GATES)
    mixed = jnp.where(which < 2, cum, pltpu.roll(growth, 2, 0))
    columns = jnp.transpose(jnp.where(which < 4, mixed, pltpu.roll(rest, 4, 0)))
    cols_ref[...] = columns
    lower = lane_r >= lane_c
    strict = lane_r > lane_c
    both = [(n, r) for n in range(spans) for r in range(2)]
    keys = []
    for n in range(spans):
        k_n = unit(convolved(rows, n * SPAN + 8 - EDGE, SPAN, slice(0, DK), tap), 1.0)
        keys_ref[n * SPAN : (n + 1) * SPAN, :] = k_n
        keys.append(k_n)
    keys_t = []
    for n in range(spans):
        kt_n = jnp.transpose(keys[n].astype(F32)).astype(BF16)
        keys_t_ref[n] = kt_n
        keys_t.append(kt_n)
    grams = [dot(keys[n], keys_t[n]) for n in range(spans)]
    systems = []
    for n, r in both:
        at = GATES * n + r
        gap = columns[:, at : at + 1] - cum[at : at + 1, :]
        within = jnp.exp(jnp.where(lower, gap, 0.0)) * here[at : at + 1, :]
        within_ref[r, n * SPAN : (n + 1) * SPAN, :] = jnp.where(lower, within, 0.0).astype(BF16)
        systems.append(jnp.where(strict, within * grams[n], 0.0))
    inverses = invert(systems)
    for i, (n, r) in enumerate(both):
        t_ref[r, n] = jnp.concatenate(inverses[i], axis=1)
    scaled = []
    for n, r in both:
        at = GATES * n + r
        right = (columns[:, at + 2 : at + 3] * keys[n].astype(F32)).astype(BF16)
        scaled.append(jnp.concatenate([right, right], axis=0))
    w_mats = [dot(jnp.concatenate(t, axis=1), x) for t, x in zip(inverses, scaled)]
    weighed = []
    for (n, r), w_mat in zip(both, w_mats):
        at = GATES * n + r
        weighed.append((columns[:, at + 4 : at + 5] * w_mat).astype(BF16))
    moved = [
        dot(keys_t[n], jnp.concatenate(weighed[2 * n : 2 * n + 2], axis=1)) for n in range(spans)
    ]
    ends_ref[...] = jnp.broadcast_to(growth[:, SPAN - 1 :], ends_ref.shape)
    for n, r in both:
        lin_ref[r, n] = moved[n][:, r * DK : (r + 1) * DK].astype(BF16)


def step(end, moved, state, parts):
    both = jnp.concatenate([moved, moved], axis=1)
    return end * state - dot(both, jnp.concatenate(parts, axis=0))


def values_part(recv_ref, cv_ref, keys_t_ref, t_ref, cols_ref, rows, vs):
    sub = lax.axis_index("sub")
    tokens = (recv_ref.shape[1] - GATES) // 4
    spans = t_ref.shape[1]
    taps = value_taps(sub, cv_ref)
    widened(rows, recv_ref, [tokens, 2 * tokens], tokens)
    both = [(n, r) for n in range(spans) for r in range(2)]
    values = []
    for n, r in both:
        lanes = slice(r * DV, (r + 1) * DV)
        v_n = convolved(rows, n * SPAN + 8 - EDGE, SPAN, lanes, taps[r]).astype(BF16)
        vs[n * SPAN : (n + 1) * SPAN, lanes] = v_n
        values.append(jnp.concatenate([v_n, v_n], axis=0))
    solved = [dot(t_ref[r, n], v) for (n, r), v in zip(both, values)]
    weighed = []
    for (n, r), u_mat in zip(both, solved):
        at = GATES * n + r
        weighed.append((cols_ref[:, at + 4 : at + 5] * u_mat).astype(BF16))
    moved = [
        dot(keys_t_ref[n], jnp.concatenate(weighed[2 * n : 2 * n + 2], axis=1))
        for n in range(spans)
    ]
    return [moved[n][:, r * DV : (r + 1) * DV] for n, r in both]


def opening_kernel(
    recv_ref, cv_ref, keys_t_ref, t_ref, lin_ref, ends_ref, cols_ref, hop_ref, vs_ref, xs_ref, rows
):
    first = lax.axis_index("half") == 0
    peers = recv_ref.shape[0]
    tokens = (recv_ref.shape[1] - GATES) // 4
    spans = t_ref.shape[1]
    edges = []
    for which in (3, 0, 1, 2):
        end = (which + 1) * tokens
        edges.append(recv_ref[peers - 1, end - 16 : end, :].astype(F32)[16 - EDGE :])
    edges.append(jnp.zeros((16 - 4 * EDGE, 128), F32))
    hop_ref[2 * DK :, :] = jnp.concatenate(edges, axis=0).astype(BF16)

    @pl.when(first)
    def _():
        adds = values_part(recv_ref, cv_ref, keys_t_ref, t_ref, cols_ref, rows, vs_ref)
        states = [adds[0], adds[1]]
        for n in range(1, spans):
            for r in range(2):
                parts = halves(states[r])
                xs_ref[n, :, r * DV : (r + 1) * DV] = jnp.concatenate(parts, axis=0)
                end = ends_ref[GATES * n + r : GATES * n + r + 1, :]
                states[r] = step(end, lin_ref[r, n], states[r], parts) + adds[2 * n + r]
        for r in range(2):
            hop_ref[r * DK : (r + 1) * DK, :] = states[r].astype(BF16)

    @pl.when(jnp.logical_not(first))
    def _():
        hop_ref[0 : 2 * DK, :] = jnp.zeros((2 * DK, DV), BF16)


def output_kernel(
    recv_ref,
    cq_ref,
    cv_ref,
    keys_ref,
    keys_t_ref,
    t_ref,
    lin_ref,
    ends_ref,
    within_ref,
    cols_ref,
    hop_ref,
    vs_ref,
    xs_ref,
    oa_ref,
    om_ref,
    last_ref,
    rows,
    query_rows,
    values,
    inner,
    readers,
    states_ref,
):
    sub = lax.axis_index("sub")
    first = lax.axis_index("half") == 0
    tokens = (recv_ref.shape[1] - GATES) // 4
    spans = t_ref.shape[1]
    both = [(n, r) for n in range(spans) for r in range(2)]
    tap = key_tap(sub, cq_ref)
    widened(query_rows, recv_ref, [3 * tokens], tokens)

    def span_rows(n):
        return slice(n * SPAN, (n + 1) * SPAN)

    def growth(n, r):
        return cols_ref[:, GATES * n + 2 + r : GATES * n + 3 + r]

    def prepare():
        queries = []
        for n in range(spans):
            at = n * SPAN + 8 - EDGE
            q_n = unit(convolved(query_rows, at, SPAN, slice(0, DK), tap), DK**-0.5)
            queries.append(q_n)
            readers[n, 0:SPAN, :] = keys_ref[span_rows(n), :]
            readers[n, SPAN:, :] = q_n
        scores = [dot(queries[n], keys_t_ref[n]) for n in range(spans)]
        for n, r in both:
            weight = within_ref[r, span_rows(n), :].astype(F32)
            inner[r, n] = (weight * scores[n]).astype(BF16)

    def twice(x, axis):
        return jnp.concatenate([x, x], axis=axis)

    @pl.when(first)
    def _():
        prepare()
        reads = [dot(twice(readers[n], 1), xs_ref[n]) for n in range(1, spans)]
        rests, seen = [], []
        for n, r in both:
            lanes = slice(r * DV, (r + 1) * DV)
            value = vs_ref[span_rows(n), lanes]
            if n == 0:
                rests.append(value)
                seen.append(None)
            else:
                read = growth(n, r) * reads[n - 1][:SPAN, lanes]
                rests.append((value.astype(F32) - read).astype(BF16))
                seen.append(growth(n, r) * reads[n - 1][SPAN:, lanes])
        fresh = [dot(t_ref[r, n], twice(x, 0)).astype(BF16) for (n, r), x in zip(both, rests)]
        spreads = [dot(inner[r, n], x) for (n, r), x in zip(both, fresh)]
        for (n, r), x, y in zip(both, spreads, seen):
            oa_ref[r, span_rows(n), :] = x if y is None else x + y
        for r in range(2):
            last_ref[r, :, 0:DV] = hop_ref[r * DK : (r + 1) * DK, :].astype(F32)
            last_ref[r, :, DV:] = jnp.zeros((DK, DV), F32)

    @pl.when(jnp.logical_not(first))
    def _():
        adds = values_part(recv_ref, cv_ref, keys_t_ref, t_ref, cols_ref, rows, values)
        zero_half = jnp.zeros((DK, DV), F32)
        identity = jnp.where(iota((DK, DK), 0) == iota((DK, DK), 1), 1.0, 0.0)
        states = [
            jnp.concatenate(
                [adds[r], ends_ref[r : r + 1, :] * identity - lin_ref[r, 0].astype(F32)], axis=1
            )
            for r in range(2)
        ]
        for n in range(1, spans):
            for r in range(2):
                parts = halves(states[r])
                states_ref[r, n] = jnp.concatenate(parts, axis=0)
                add = jnp.concatenate([adds[2 * n + r], zero_half], axis=1)
                end = ends_ref[GATES * n + r : GATES * n + r + 1, :]
                end = jnp.concatenate([end, end], axis=1)
                states[r] = step(end, lin_ref[r, n], states[r], parts) + add
        for r in range(2):
            last_ref[r] = states[r]
        prepare()
        reads = [
            dot(twice(readers[n], 1), states_ref[r, n]) if n > 0 else None for n, r in both
        ]
        rests, seen = [], []
        for (n, r), read in zip(both, reads):
            value = values[span_rows(n), r * DV : (r + 1) * DV].astype(F32)
            if n == 0:
                known = growth(n, r) * readers[n].astype(F32)[:SPAN]
                asked = growth(n, r) * readers[n].astype(F32)[SPAN:]
                rest = jnp.concatenate([value, -known], axis=1)
                seen.append(jnp.concatenate([zero_half, asked], axis=1))
            else:
                rest = jnp.concatenate([value, zero_half], axis=1) - growth(n, r) * read[:SPAN]
                seen.append(growth(n, r) * read[SPAN:])
            rests.append(rest.astype(BF16))
        fresh = [dot(t_ref[r, n], twice(x, 0)).astype(BF16) for (n, r), x in zip(both, rests)]
        spreads = [dot(inner[r, n], x) for (n, r), x in zip(both, fresh)]
        for (n, r), x, y in zip(both, spreads, seen):
            out = x + y
            oa_ref[r, span_rows(n), :] = out[:, :DV]
            om_ref[r, span_rows(n), :] = out[:, DV:].astype(BF16)


def first_tokens(hop_ref, recv_ref, early_ref, cq_ref, ck_ref, cv_ref, rows):
    sub = lax.axis_index("sub")
    tokens = (recv_ref.shape[1] - GATES) // 4
    taps = [key_tap(sub, cq_ref), key_tap(sub, ck_ref)] + value_taps(sub, cv_ref)
    results = []
    edges = hop_ref[2 * DK :, :].astype(F32)
    for g, first in enumerate((3, 0, 1, 2)):
        lanes = slice(g * 128, (g + 1) * 128)
        start = first * tokens
        rows[16 - EDGE : 16, lanes] = edges[EDGE * g : EDGE * (g + 1)]
        rows[16:32, lanes] = recv_ref[0, start : start + 16, :].astype(F32)
        results.append(convolved(rows, 16 - EDGE, 8, lanes, taps[g]))
    q_cols = jnp.transpose(unit(results[0], DK**-0.5).astype(F32))
    k_cols = jnp.transpose(unit(results[1], 1.0).astype(F32))
    gates = early_ref[...]
    line = iota((8, DV), 0)
    finals, outputs = [], []
    for r in range(2):
        values = results[2 + r].astype(BF16).astype(F32)
        entering = hop_ref[r * DK : (r + 1) * DK, :].astype(F32)
        state, out = entering, jnp.zeros((8, DV), F32)
        for t in range(EDGE):
            k_t, q_t = k_cols[:, t : t + 1], q_cols[:, t : t + 1]
            state = jnp.exp(gates[r : r + 1, t : t + 1]) * state
            held = jnp.sum(k_t * state, axis=0, keepdims=True)
            state = state + k_t * (
                gates[2 + r : 3 + r, t : t + 1] * (values[t : t + 1, :] - held)
            )
            out = jnp.where(line == t, jnp.sum(q_t * state, axis=0, keepdims=True), out)
        finals.append(state)
        outputs.append(out)
    return finals, outputs


def finish_kernel(
    hop_ref, recv_ref, early_ref, cq_ref, ck_ref, cv_ref, gain_ref, oa_ref, om_ref, out_ref, rows
):
    peers, tokens = out_ref.shape[0], out_ref.shape[1]
    first = lax.axis_index("half") == 0
    gain = gain_ref[...]
    chunks = 4
    part, peer_part = peers * tokens // chunks, peers // chunks

    def put(c, r, core):
        scale = lax.rsqrt(jnp.mean(core * core, axis=-1, keepdims=True) + EPS)
        normed = (core * scale * gain).astype(BF16)
        out_ref[c * peer_part : (c + 1) * peer_part, :, r * DV : (r + 1) * DV] = normed.reshape(
            peer_part, tokens, DV
        )

    @pl.when(first)
    def _():
        for c in range(chunks):
            for r in range(2):
                put(c, r, oa_ref[r, c * part : (c + 1) * part, :])

    @pl.when(jnp.logical_not(first))
    def _():
        finals, outputs = first_tokens(hop_ref, recv_ref, early_ref, cq_ref, ck_ref, cv_ref, rows)
        replaced = iota((8, DV), 0) < EDGE
        passed = [dot(om_ref[r], finals[r].astype(BF16)) for r in range(2)]
        for c in range(chunks):
            at = c * part
            for r in range(2):
                core = oa_ref[r, at : at + part, :] + passed[r][at : at + part]
                if c == 0:
                    core = jnp.concatenate(
                        [jnp.where(replaced, outputs[r], core[0:8]), core[8:]], axis=0
                    )
                put(c, r, core)


def advance_kernel(
    hop_ref, recv_ref, early_ref, cq_ref, ck_ref, cv_ref, hop_own, last_ref, next_ref, rows
):
    finals, _ = first_tokens(hop_ref, recv_ref, early_ref, cq_ref, ck_ref, cv_ref, rows)
    first = lax.axis_index("half") == 0
    for r in range(2):
        last = last_ref[r]
        through = mm_parts(halves(last[:, DV:]), halves(finals[r]))
        moved = jnp.where(first, 0.0, through) + last[:, :DV]
        next_ref[r * DK : (r + 1) * DK, :] = moved.astype(BF16)
    next_ref[2 * DK :, :] = hop_own[2 * DK :, :]


def gate_kernel(heads_axis, normed_ref, z_ref, out_ref, made, sems):
    subs = normed_ref.shape[0] // heads_axis
    width = subs * 2 * DV
    copies = []
    for head in range(heads_axis):
        for sub in range(subs):
            at = (head * subs + sub) * 2 * DV
            gate = silu(z_ref[:, at : at + 2 * DV].astype(F32))
            value = normed_ref[sub * heads_axis + head].astype(F32)
            made[:, at : at + 2 * DV] = (value * gate).astype(BF16)
        lanes = pl.ds(head * width, width)
        copy = pltpu.make_async_copy(made.at[:, lanes], out_ref.at[:, lanes], sems.at[head])
        copy.start()
        copies.append(copy)
    for copy in copies:
        copy.wait()


VMEM = pl.BlockSpec(memory_space=pltpu.VMEM)
SMEM = pl.BlockSpec(memory_space=pltpu.SMEM)
ANY = pl.BlockSpec(memory_space=pl.ANY)


def near(x):
    return pltpu.with_memory_space_constraint(x, pltpu.VMEM)


def far(x):
    return pltpu.with_memory_space_constraint(x, pltpu.HBM)


def call(kernel, outs, in_specs, scratch=(), out_spec=VMEM, flops=1 << 26, moved=1 << 21):
    return pl.pallas_call(
        kernel,
        out_shape=outs,
        in_specs=in_specs,
        out_specs=jax.tree.map(lambda _: out_spec, outs),
        scratch_shapes=list(scratch),
        compiler_params=pltpu.CompilerParams(vmem_limit_bytes=VMEM_BYTES),
        cost_estimate=pl.CostEstimate(flops=flops, bytes_accessed=moved, transcendentals=0),
    )


def local(
    q_rows,
    k_rows,
    v_rows,
    z_rows,
    a_rows,
    b_rows,
    conv_q,
    conv_k,
    conv_v,
    a_log,
    dt_bias,
    norm_gain,
):
    shards, subs, heads_axis = (lax.axis_size(a) for a in ("half", "sub", "head"))
    peers, tokens = subs * heads_axis, q_rows.shape[0]
    total = peers * tokens
    spans = total // SPAN
    group = ("sub", "head")
    route = [(i, i + 1) for i in range(shards - 1)]
    inputs = [far(x) for x in (q_rows, k_rows, v_rows, a_rows.T, b_rows.T)]
    packed = call(
        functools.partial(pack_kernel, heads_axis),
        pltpu.VMEM((peers, GATES + 4 * tokens, 128), BF16),
        [ANY] * 5,
        [pltpu.VMEM(x.shape, BF16) for x in inputs] + [pltpu.SemaphoreType.DMA((5,))],
        flops=1 << 20,
    )(*inputs)
    blocks = near(lax.all_to_all(packed, group, 0, 0, tiled=True))
    keys, keys_t, inverses, lins, ends, within, cols, early = call(
        keys_kernel,
        (
            pltpu.VMEM((total, DK), BF16),
            pltpu.VMEM((spans, DK, SPAN), BF16),
            pltpu.VMEM((2, spans, SPAN, 2 * SPAN), BF16),
            pltpu.VMEM((2, spans, DK, DK), BF16),
            pltpu.VMEM((SPAN, DK), F32),
            pltpu.VMEM((2, total, SPAN), BF16),
            pltpu.VMEM((SPAN, SPAN), F32),
            pltpu.VMEM((8, SPAN), F32),
        ),
        [VMEM, VMEM, SMEM, SMEM],
        [pltpu.VMEM((8 + total, DK), F32)],
        flops=1 << 32,
    )(blocks, conv_k, a_log, dt_bias)
    keys, keys_t, inverses, lins, ends, within, cols, early = (
        near(x) for x in (keys, keys_t, inverses, lins, ends, within, cols, early)
    )
    hop, values, starts = call(
        opening_kernel,
        (
            pltpu.VMEM((2 * DK + 16, 128), BF16),
            pltpu.VMEM((total, 2 * DV), BF16),
            pltpu.VMEM((spans, 2 * DK, 2 * DV), BF16),
        ),
        [VMEM] * 7,
        [pltpu.VMEM((8 + total, 2 * DV), F32)],
        flops=1 << 32,
    )(blocks, conv_v, keys_t, inverses, lins, ends, cols)
    entering = near(lax.ppermute(hop, "half", route))
    hop, values, starts = near(hop), near(values), near(starts)
    out_a, out_m, last = call(
        output_kernel,
        (
            pltpu.VMEM((2, total, DV), F32),
            pltpu.VMEM((2, total, DV), BF16),
            pltpu.VMEM((2, DK, 2 * DV), F32),
        ),
        [VMEM] * 13,
        [
            pltpu.VMEM((8 + total, 2 * DV), F32),
            pltpu.VMEM((8 + total, DK), F32),
            pltpu.VMEM((total, 2 * DV), BF16),
            pltpu.VMEM((2, spans, SPAN, SPAN), BF16),
            pltpu.VMEM((spans, 2 * SPAN, DK), BF16),
            pltpu.VMEM((2, spans, 2 * DK, 2 * DV), BF16),
        ],
        flops=1 << 32,
    )(
        blocks,
        conv_q,
        conv_v,
        keys,
        keys_t,
        inverses,
        lins,
        ends,
        within,
        cols,
        hop,
        values,
        starts,
    )
    for _ in range(shards - 2):
        moved = call(
            advance_kernel,
            pltpu.VMEM(hop.shape, BF16),
            [VMEM] * 8,
            [pltpu.VMEM((32, 512), F32)],
        )(entering, blocks, early, conv_q, conv_k, conv_v, hop, near(last))
        entering = near(lax.ppermute(moved, "half", route))
    normed = call(
        finish_kernel,
        pltpu.VMEM((peers, tokens, 2 * DV), BF16),
        [VMEM] * 9,
        [pltpu.VMEM((32, 512), F32)],
    )(
        entering,
        blocks,
        early,
        conv_q,
        conv_k,
        conv_v,
        norm_gain.reshape(1, DV),
        near(out_a),
        near(out_m),
    )
    returned = near(lax.all_to_all(normed, group, 0, 0, tiled=True))
    return call(
        functools.partial(gate_kernel, heads_axis),
        jax.ShapeDtypeStruct(z_rows.shape, BF16),
        [VMEM] * 2,
        [pltpu.VMEM(z_rows.shape, BF16), pltpu.SemaphoreType.DMA((heads_axis,))],
        ANY,
    )(returned, z_rows)


def solution(mesh):
    heads_axis = mesh.shape["head"]
    subs = KH // heads_axis
    regrouped = Mesh(
        mesh.devices.reshape(mesh.shape["ctx"] // subs, subs, heads_axis), ("half", "sub", "head")
    )
    row = P(("half", "sub", "head"), None)
    placed = (row,) * 6 + (P(None, "head"),) * 3 + (P("head"),) * 2 + (P(),)
    return jax.shard_map(local, mesh=regrouped, in_specs=placed, out_specs=row, check_vma=False)
```

```python
import functools

import jax
import jax.numpy as jnp
from jax import lax
from jax.experimental import pallas as pl
from jax.experimental.pallas import tpu as pltpu
from jax.sharding import Mesh, PartitionSpec as P

DK = 128
DV = 128
CONV = 4
KH = 16
SUB = 16
SPAN = 128
GROUP = 4
EDGE = CONV - 1
EPS = 1e-06
F32 = jnp.float32
BF16 = jnp.bfloat16
VMEM_BYTES = 24 * 1024 * 1024
GATES = 8


def dot(a, b, dims=((1,), (0,))):
    return lax.dot_general(a, b, (dims, ((), ())), preferred_element_type=F32)


def halves(x):
    high = x.astype(BF16)
    return high, (x - high.astype(F32)).astype(BF16)


def mm_parts(a, b):
    both = jnp.concatenate(a, axis=1)
    return dot(both, jnp.concatenate([b[0], b[0]], axis=0)) + dot(a[0], b[1])


def silu(x):
    half = 0.5 * x
    return half + half * jnp.tanh(half)


def unit(y, factor):
    scale = lax.rsqrt(jnp.sum(y * y, axis=-1, keepdims=True) + EPS)
    return (y * scale * factor).astype(BF16)


def iota(shape, dim):
    return lax.broadcasted_iota(jnp.int32, shape, dim)


def block_of(x, size):
    return lax.shift_right_logical(x, jnp.full(x.shape, size.bit_length() - 1, jnp.int32))


def place_in(x, size):
    return x & (size - 1)


def pack_kernel(
    heads_axis, q_in, k_in, v_in, at_in, bt_in, out_ref, q_ref, k_ref, v_ref, at_ref, bt_ref, sems
):
    peers, tokens = out_ref.shape[0], q_ref.shape[0]
    pairs = ((at_in, at_ref), (bt_in, bt_ref), (k_in, k_ref), (v_in, v_ref), (q_in, q_ref))
    copies = [pltpu.make_async_copy(a, b, sems.at[i]) for i, (a, b) in enumerate(pairs)]
    for copy in copies:
        copy.start()
    subs = peers // heads_axis
    key_heads = [(dest % heads_axis) * subs + dest // heads_axis for dest in range(peers)]
    for copy in copies[:2]:
        copy.wait()
    value_heads = at_ref.shape[0]
    row, entry = iota((peers * GATES, value_heads), 0), iota((peers * GATES, value_heads), 1)
    dest, which = block_of(row, GATES), place_in(row, GATES)
    first = 2 * (place_in(dest, heads_axis) * subs + block_of(dest, heads_axis))
    pick_a = jnp.where((which < 2) & (entry == first + which), 1.0, 0.0).astype(BF16)
    pick_b = jnp.where(
        (which >= 2) & (which < 4) & (entry == first + which - 2), 1.0, 0.0
    ).astype(BF16)
    picked = (dot(pick_a, at_ref[...]) + dot(pick_b, bt_ref[...])).astype(BF16)
    lane_shift = tokens * lax.rem(lax.axis_index("head"), SPAN // tokens)
    place = jnp.where(
        iota((tokens, SPAN), 1) == iota((tokens, SPAN), 0) + lane_shift, 1.0, 0.0
    ).astype(BF16)
    gates = dot(picked, place).astype(BF16)
    for dest in range(peers):
        out_ref[dest, 4 * tokens :, :] = gates[GATES * dest : GATES * (dest + 1), :]

    def laid(ref, lane, start):
        for dest, key_head in enumerate(key_heads):
            at = lane(key_head) * 128
            out_ref[dest, start * tokens : (start + 1) * tokens, :] = ref[
                :, at : at + 128
            ]

    copies[2].wait()
    laid(k_ref, lambda key_head: key_head, 0)
    copies[3].wait()
    laid(v_ref, lambda key_head: 2 * key_head, 1)
    laid(v_ref, lambda key_head: 2 * key_head + 1, 2)
    copies[4].wait()
    laid(q_ref, lambda key_head: key_head, 3)


def invert(systems):
    size = systems[0].shape[0]
    blocks = size // SUB
    row, col = iota((size, size), 0), iota((size, size), 1)
    diagonal = block_of(row, SUB) == block_of(col, SUB)
    compact = jnp.concatenate(
        [
            jnp.sum(jnp.where(diagonal, n, 0.0).reshape(blocks, SUB, size), axis=0)
            for n in systems
        ],
        axis=0,
    )
    count = len(systems)
    lane, line = iota(compact.shape, 1), iota(compact.shape, 0)
    solved = jnp.where(place_in(lane ^ line, SUB) == 0, 1.0, 0.0).reshape(count, SUB, size)
    for m in range(SUB - 1):
        source = (lane & ~(SUB - 1)) | m
        spread = jnp.take_along_axis(compact, source, axis=1, mode="promise_in_bounds")
        solved = solved - spread.reshape(count, SUB, size) * solved[:, m : m + 1, :]
    lows = [halves(n) for n in systems]
    placed = jnp.where(diagonal, 1.0, 0.0).astype(BF16)
    parts = [
        tuple(jnp.concatenate([x] * blocks, axis=0) * placed for x in halves(solved[i]))
        for i in range(count)
    ]
    levels = []
    width = SUB
    while width < size:
        below = (block_of(row ^ col, 2 * width) == 0) & ((col & width) == 0)
        levels.append((width, jnp.where(below, 1.0, 0.0).astype(BF16)))
        width *= 2
    grown = []
    for i in range(0, count, GROUP):
        grown += doubled(lows[i : i + GROUP], parts[i : i + GROUP], levels)
    return grown


def doubled(lows, parts, levels):
    size = levels[0][1].shape[0]
    blank = jnp.zeros((size, size), BF16)
    for width, below in levels:
        odd = [(j, j + width) for j in range(width, size, 2 * width)]

        def rows_of(x):
            return jnp.concatenate([x[lo:hi] for lo, hi in odd], axis=0)

        def woven(even, x):
            pieces = []
            for j, (lo, hi) in enumerate(odd):
                pieces += [even[lo - width : lo], x[j * width : (j + 1) * width]]
            return jnp.concatenate(pieces, axis=0)

        mask = rows_of(below)
        firsts = [
            mm_parts((rows_of(n[0]) * mask, rows_of(n[1]) * mask), t) for n, t in zip(lows, parts)
        ]
        spreads = [tuple(woven(blank, x) for x in halves(first)) for first in firsts]
        odds = [(rows_of(t[0]), rows_of(t[1])) for t in parts]
        seconds = [halves(-mm_parts(o, spread)) for o, spread in zip(odds, spreads)]
        parts = [
            tuple(woven(t[i], o[i] + second[i]) for i in range(2))
            for t, o, second in zip(parts, odds, seconds)
        ]
    return parts


def gate_values(gates, sub, alog_ref, dt_ref):
    second = place_in(iota(gates.shape, 0), GATES) == 1
    a_log = jnp.where(second, alog_ref[2 * sub + 1], alog_ref[2 * sub])
    dt_bias = jnp.where(second, dt_ref[2 * sub + 1], dt_ref[2 * sub])
    shifted = gates + dt_bias
    soft = jnp.maximum(shifted, 0.0) + jnp.log1p(jnp.exp(-jnp.abs(shifted)))
    return -jnp.exp(a_log) * soft, 1.0 / (1.0 + jnp.exp(-gates))


def convolved(rows, at, count, lanes, tap):
    summed = tap[0:1] * rows[at : at + count, lanes]
    for j in range(1, CONV):
        summed = summed + tap[j : j + 1] * rows[at + j : at + j + count, lanes]
    return silu(summed)


def key_tap(sub, tap_ref):
    return tap_ref[:, pl.ds(pl.multiple_of(sub * DK, 128), DK)]


def value_taps(sub, cv_ref):
    lane = pl.multiple_of(sub * 2 * DV, 128)
    return [cv_ref[:, pl.ds(pl.multiple_of(lane + r * DV, 128), DV)] for r in range(2)]


def widened(rows, recv_ref, starts, tokens):
    rows[0:8, :] = jnp.zeros((8, rows.shape[1]), F32)
    for s in range(recv_ref.shape[0]):
        for g, start in enumerate(starts):
            rows[8 + s * tokens : 8 + (s + 1) * tokens, g * 128 : (g + 1) * 128] = recv_ref[
                s, start : start + tokens, :
            ].astype(F32)


def keys_kernel(
    recv_ref,
    ck_ref,
    alog_ref,
    dt_ref,
    keys_ref,
    keys_t_ref,
    t_ref,
    lin_ref,
    ends_ref,
    within_ref,
    cols_ref,
    early_ref,
    rows,
):
    sub = lax.axis_index("sub")
    later = lax.axis_index("half") > 0
    peers = recv_ref.shape[0]
    tokens = (recv_ref.shape[1] - GATES) // 4
    spans = peers * tokens // SPAN
    tap = key_tap(sub, ck_ref)
    widened(rows, recv_ref, [0], tokens)
    stacked = [
        sum(recv_ref[s, 4 * tokens :, :].astype(F32) for s in range(n, n + SPAN // tokens))
        for n in range(0, peers, SPAN // tokens)
    ]
    stacked.append(jnp.zeros((SPAN - spans * GATES, SPAN), F32))
    gates = jnp.concatenate(stacked, axis=0)
    decay, rate = gate_values(gates, sub, alog_ref, dt_ref)
    early_ref[...] = jnp.where(iota((8, SPAN), 0) < 2, decay[0:8], rate[0:8])
    skipped = later & (iota(gates.shape, 0) < GATES) & (iota(gates.shape, 1) < EDGE)
    decay = jnp.where(skipped, 0.0, decay)
    rate = jnp.where(skipped, 0.0, rate)
    lane_r, lane_c = iota((SPAN, SPAN), 0), iota((SPAN, SPAN), 1)
    upto = jnp.where(lane_r <= lane_c, 1.0, 0.0).astype(BF16)
    d_high, _ = halves(decay)
    d_mid, d_low = halves(decay - d_high.astype(F32))
    cum = dot(d_high, upto) + (dot(d_mid, upto) + dot(d_low, upto))
    growth = jnp.exp(cum)
    here = pltpu.roll(rate, rate.shape[0] - 2, 0)
    rest = jnp.exp(cum[:, SPAN - 1 :] - cum) * here
    which = place_in(iota(gates.shape, 0), GATES)
    mixed = jnp.where(which < 2, cum, pltpu.roll(growth, 2, 0))
    columns = jnp.transpose(jnp.where(which < 4, mixed, pltpu.roll(rest, 4, 0)))
    cols_ref[...] = columns
    lower = lane_r >= lane_c
    strict = lane_r > lane_c
    both = [(n, r) for n in range(spans) for r in range(2)]
    keys = []
    for n in range(spans):
        k_n = unit(convolved(rows, n * SPAN + 8 - EDGE, SPAN, slice(0, DK), tap), 1.0)
        keys_ref[n * SPAN : (n + 1) * SPAN, :] = k_n
        keys.append(k_n)
    keys_t = []
    for n in range(spans):
        kt_n = jnp.transpose(keys[n].astype(F32)).astype(BF16)
        keys_t_ref[n] = kt_n
        keys_t.append(kt_n)
    grams = [dot(keys[n], keys_t[n]) for n in range(spans)]
    systems = []
    for n, r in both:
        at = GATES * n + r
        gap = columns[:, at : at + 1] - cum[at : at + 1, :]
        within = jnp.exp(jnp.where(lower, gap, 0.0)) * here[at : at + 1, :]
        within_ref[r, n * SPAN : (n + 1) * SPAN, :] = jnp.where(lower, within, 0.0).astype(BF16)
        systems.append(jnp.where(strict, within * grams[n], 0.0))
    inverses = invert(systems)
    for i, (n, r) in enumerate(both):
        t_ref[r, n, 0], t_ref[r, n, 1] = inverses[i]
    scaled = []
    for n, r in both:
        at = GATES * n + r
        right = (columns[:, at + 2 : at + 3] * keys[n].astype(F32)).astype(BF16)
        scaled.append(jnp.concatenate([right, right], axis=0))
    w_mats = [dot(jnp.concatenate(t, axis=1), x) for t, x in zip(inverses, scaled)]
    weighed = []
    for (n, r), w_mat in zip(both, w_mats):
        at = GATES * n + r
        weighed.append((columns[:, at + 4 : at + 5] * w_mat).astype(BF16))
    moved = [
        dot(keys_t[n], jnp.concatenate(weighed[2 * n : 2 * n + 2], axis=1)) for n in range(spans)
    ]
    ends_ref[...] = jnp.broadcast_to(growth[:, SPAN - 1 :], ends_ref.shape)
    for n, r in both:
        lin_ref[r, n] = moved[n][:, r * DK : (r + 1) * DK].astype(BF16)


def unwound(t_ref, n, r, x):
    both = jnp.concatenate([t_ref[r, n, 0], t_ref[r, n, 1]], axis=1)
    return dot(both, jnp.concatenate([x, x], axis=0))


def end_of(ends_ref, n, r):
    return ends_ref[GATES * n + r : GATES * n + r + 1, :]


def followed(span_map, state):
    end, moved, add = span_map
    return step(end, moved, state, halves(state)) + add


def composed(maps):
    if len(maps) == 1:
        return maps[0]
    half = len(maps) // 2
    end_a, moved_a, add_a = composed(maps[:half])
    end_b, moved_b, add_b = composed(maps[half:])
    high, low = halves(add_a)
    rights = jnp.concatenate(
        [
            jnp.concatenate([moved_a, high], axis=1),
            jnp.concatenate([jnp.zeros_like(moved_a), low], axis=1),
        ],
        axis=0,
    )
    passed = dot(jnp.concatenate([moved_b, moved_b], axis=1), rights)
    moved = end_b * moved_a.astype(F32) + end_a * moved_b.astype(F32) - passed[:, :DK]
    add = end_b * add_a - passed[:, DK:] + add_b
    return end_a * end_b, moved.astype(BF16), add


def step(end, moved, state, parts):
    both = jnp.concatenate([moved, moved], axis=1)
    return end * state - dot(both, jnp.concatenate(parts, axis=0))


def values_part(recv_ref, cv_ref, keys_t_ref, t_ref, cols_ref, rows, vs):
    sub = lax.axis_index("sub")
    tokens = (recv_ref.shape[1] - GATES) // 4
    spans = t_ref.shape[1]
    taps = value_taps(sub, cv_ref)
    widened(rows, recv_ref, [tokens, 2 * tokens], tokens)
    both = [(n, r) for n in range(spans) for r in range(2)]
    values = []
    for n, r in both:
        lanes = slice(r * DV, (r + 1) * DV)
        v_n = convolved(rows, n * SPAN + 8 - EDGE, SPAN, lanes, taps[r]).astype(BF16)
        vs[r, n * SPAN : (n + 1) * SPAN, :] = v_n
        values.append(v_n)
    solved = [unwound(t_ref, n, r, v) for (n, r), v in zip(both, values)]
    weighed = []
    for (n, r), u_mat in zip(both, solved):
        at = GATES * n + r
        weighed.append((cols_ref[:, at + 4 : at + 5] * u_mat).astype(BF16))
    moved = [
        dot(keys_t_ref[n], jnp.concatenate(weighed[2 * n : 2 * n + 2], axis=1))
        for n in range(spans)
    ]
    return [moved[n][:, r * DV : (r + 1) * DV] for n, r in both]


def opening_kernel(
    recv_ref, cv_ref, keys_t_ref, t_ref, lin_ref, ends_ref, cols_ref, hop_ref, vs_ref, xs_ref, adds_ref, rows
):
    first = lax.axis_index("half") == 0
    peers = recv_ref.shape[0]
    tokens = (recv_ref.shape[1] - GATES) // 4
    spans = t_ref.shape[1]
    edges = []
    for which in (3, 0, 1, 2):
        end = (which + 1) * tokens
        edges.append(recv_ref[peers - 1, end - 16 : end, :].astype(F32)[16 - EDGE :])
    edges.append(jnp.zeros((16 - 4 * EDGE, 128), F32))
    hop_ref[2 * DK :, :] = jnp.concatenate(edges, axis=0).astype(BF16)

    @pl.when(first)
    def _():
        adds = values_part(recv_ref, cv_ref, keys_t_ref, t_ref, cols_ref, rows, vs_ref)
        for n in range(spans):
            for r in range(2):
                adds_ref[r, n] = adds[2 * n + r]
        maps = [
            [(end_of(ends_ref, n, r), lin_ref[r, n], adds[2 * n + r]) for n in range(spans)]
            for r in range(2)
        ]
        states = [m[0][2] for m in maps]
        done = 1
        while done < spans:
            for r in range(2):
                if done > 1:
                    xs_ref[r, done] = jnp.concatenate(halves(states[r]), axis=0)
            later = [composed(m[done : 2 * done]) for m in maps]
            states = [followed(m, x) for m, x in zip(later, states)]
            done *= 2
        for r in range(2):
            hop_ref[r * DK : (r + 1) * DK, :] = states[r].astype(BF16)

    @pl.when(jnp.logical_not(first))
    def _():
        hop_ref[0 : 2 * DK, :] = jnp.zeros((2 * DK, DV), BF16)


def output_kernel(
    recv_ref,
    cq_ref,
    cv_ref,
    keys_ref,
    keys_t_ref,
    t_ref,
    lin_ref,
    ends_ref,
    within_ref,
    cols_ref,
    hop_ref,
    vs_ref,
    xs_ref,
    adds_ref,
    oa_ref,
    om_ref,
    last_ref,
    rows,
    query_rows,
    values,
    inner,
    readers,
    states_ref,
):
    sub = lax.axis_index("sub")
    first = lax.axis_index("half") == 0
    tokens = (recv_ref.shape[1] - GATES) // 4
    spans = t_ref.shape[1]
    both = [(n, r) for n in range(spans) for r in range(2)]
    tap = key_tap(sub, cq_ref)
    widened(query_rows, recv_ref, [3 * tokens], tokens)

    def span_rows(n):
        return slice(n * SPAN, (n + 1) * SPAN)

    def growth(n, r):
        return cols_ref[:, GATES * n + 2 + r : GATES * n + 3 + r]

    def prepare():
        queries = []
        for n in range(spans):
            at = n * SPAN + 8 - EDGE
            q_n = unit(convolved(query_rows, at, SPAN, slice(0, DK), tap), DK**-0.5)
            queries.append(q_n)
            readers[n, 0:SPAN, :] = keys_ref[span_rows(n), :]
            readers[n, SPAN:, :] = q_n
        scores = [dot(queries[n], keys_t_ref[n]) for n in range(spans)]
        for n, r in both:
            weight = within_ref[r, span_rows(n), :].astype(F32)
            inner[r, n] = (weight * scores[n]).astype(BF16)

    def twice(x, axis):
        return jnp.concatenate([x, x], axis=axis)

    @pl.when(first)
    def _():
        prepare()
        stacks, states = [], []
        for n in range(1, spans):
            if n == 1:
                states = [adds_ref[r, 0] for r in range(2)]
                stack = [jnp.concatenate(halves(x), axis=0) for x in states]
            elif n & (n - 1) == 0:
                stack = [xs_ref[r, n] for r in range(2)]
                states = [x[:DK].astype(F32) + x[DK:].astype(F32) for x in stack]
            else:
                states = [
                    followed(
                        (end_of(ends_ref, n - 1, r), lin_ref[r, n - 1], adds_ref[r, n - 1]),
                        states[r],
                    )
                    for r in range(2)
                ]
                stack = [jnp.concatenate(halves(x), axis=0) for x in states]
            stacks.append(jnp.concatenate(stack, axis=1))
        reads = [dot(twice(readers[n], 1), stacks[n - 1]) for n in range(1, spans)]
        rests, seen = [], []
        for n, r in both:
            lanes = slice(r * DV, (r + 1) * DV)
            value = vs_ref[r, span_rows(n), :]
            if n == 0:
                rests.append(value)
                seen.append(None)
            else:
                read = growth(n, r) * reads[n - 1][:SPAN, lanes]
                rests.append((value.astype(F32) - read).astype(BF16))
                seen.append(growth(n, r) * reads[n - 1][SPAN:, lanes])
        fresh = [unwound(t_ref, n, r, x).astype(BF16) for (n, r), x in zip(both, rests)]
        spreads = [dot(inner[r, n], x) for (n, r), x in zip(both, fresh)]
        for (n, r), x, y in zip(both, spreads, seen):
            oa_ref[r, span_rows(n), :] = x if y is None else x + y
        for r in range(2):
            last_ref[r, :, 0:DV] = hop_ref[r * DK : (r + 1) * DK, :].astype(F32)
            last_ref[r, :, DV:] = jnp.zeros((DK, DV), F32)

    @pl.when(jnp.logical_not(first))
    def _():
        adds = values_part(recv_ref, cv_ref, keys_t_ref, t_ref, cols_ref, rows, values)
        zero_half = jnp.zeros((DK, DV), F32)
        identity = jnp.where(iota((DK, DK), 0) == iota((DK, DK), 1), 1.0, 0.0)
        states = [
            jnp.concatenate(
                [adds[r], ends_ref[r : r + 1, :] * identity - lin_ref[r, 0].astype(F32)], axis=1
            )
            for r in range(2)
        ]
        for n in range(1, spans):
            for r in range(2):
                parts = halves(states[r])
                for i in range(2):
                    both_parts = [x[:, i * DV : (i + 1) * DV] for x in parts]
                    states_ref[i, r, n] = jnp.concatenate(both_parts, axis=0)
                add = jnp.concatenate([adds[2 * n + r], zero_half], axis=1)
                end = jnp.concatenate([end_of(ends_ref, n, r)] * 2, axis=1)
                states[r] = step(end, lin_ref[r, n], states[r], parts) + add
        for r in range(2):
            last_ref[r] = states[r]
        prepare()
        reads = [
            dot(
                twice(readers[n], 1),
                jnp.concatenate([states_ref[0, r, n], states_ref[1, r, n]], axis=1),
            )
            if n > 0
            else None
            for n, r in both
        ]
        rests, seen = [], []
        for (n, r), read in zip(both, reads):
            value = values[r, span_rows(n), :].astype(F32)
            if n == 0:
                known = growth(n, r) * readers[n].astype(F32)[:SPAN]
                asked = growth(n, r) * readers[n].astype(F32)[SPAN:]
                rest = jnp.concatenate([value, -known], axis=1)
                seen.append(jnp.concatenate([zero_half, asked], axis=1))
            else:
                rest = jnp.concatenate([value, zero_half], axis=1) - growth(n, r) * read[:SPAN]
                seen.append(growth(n, r) * read[SPAN:])
            rests.append(rest.astype(BF16))
        fresh = [unwound(t_ref, n, r, x).astype(BF16) for (n, r), x in zip(both, rests)]
        spreads = [dot(inner[r, n], x) for (n, r), x in zip(both, fresh)]
        for (n, r), x, y in zip(both, spreads, seen):
            out = x + y
            oa_ref[r, span_rows(n), :] = out[:, :DV]
            om_ref[r, span_rows(n), :] = out[:, DV:].astype(BF16)


def first_tokens(hop_ref, recv_ref, early_ref, cq_ref, ck_ref, cv_ref, rows):
    sub = lax.axis_index("sub")
    tokens = (recv_ref.shape[1] - GATES) // 4
    taps = [key_tap(sub, cq_ref), key_tap(sub, ck_ref)] + value_taps(sub, cv_ref)
    results = []
    edges = hop_ref[2 * DK :, :].astype(F32)
    for g, first in enumerate((3, 0, 1, 2)):
        lanes = slice(g * 128, (g + 1) * 128)
        start = first * tokens
        rows[16 - EDGE : 16, lanes] = edges[EDGE * g : EDGE * (g + 1)]
        rows[16:32, lanes] = recv_ref[0, start : start + 16, :].astype(F32)
        results.append(convolved(rows, 16 - EDGE, 8, lanes, taps[g]))
    q_cols = jnp.transpose(unit(results[0], DK**-0.5).astype(F32))
    k_cols = jnp.transpose(unit(results[1], 1.0).astype(F32))
    gates = early_ref[...]
    line = iota((8, DV), 0)
    finals, outputs = [], []
    for r in range(2):
        values = results[2 + r].astype(BF16).astype(F32)
        entering = hop_ref[r * DK : (r + 1) * DK, :].astype(F32)
        state, out = entering, jnp.zeros((8, DV), F32)
        for t in range(EDGE):
            k_t, q_t = k_cols[:, t : t + 1], q_cols[:, t : t + 1]
            state = jnp.exp(gates[r : r + 1, t : t + 1]) * state
            held = jnp.sum(k_t * state, axis=0, keepdims=True)
            state = state + k_t * (
                gates[2 + r : 3 + r, t : t + 1] * (values[t : t + 1, :] - held)
            )
            out = jnp.where(line == t, jnp.sum(q_t * state, axis=0, keepdims=True), out)
        finals.append(state)
        outputs.append(out)
    return finals, outputs


def finish_kernel(
    hop_ref, recv_ref, early_ref, cq_ref, ck_ref, cv_ref, gain_ref, oa_ref, om_ref, out_ref, rows
):
    peers, tokens = out_ref.shape[0], out_ref.shape[1] // 2
    first = lax.axis_index("half") == 0
    gain = gain_ref[...]
    chunks = 4
    part, peer_part = peers * tokens // chunks, peers // chunks

    def put(c, r, core):
        scale = lax.rsqrt(jnp.mean(core * core, axis=-1, keepdims=True) + EPS)
        normed = (core * scale * gain).astype(BF16)
        here = slice(c * peer_part, (c + 1) * peer_part)
        out_ref[here, r * tokens : (r + 1) * tokens, :] = normed.reshape(peer_part, tokens, DV)

    @pl.when(first)
    def _():
        for c in range(chunks):
            for r in range(2):
                put(c, r, oa_ref[r, c * part : (c + 1) * part, :])

    @pl.when(jnp.logical_not(first))
    def _():
        finals, outputs = first_tokens(hop_ref, recv_ref, early_ref, cq_ref, ck_ref, cv_ref, rows)
        replaced = iota((8, DV), 0) < EDGE
        passed = [dot(om_ref[r], finals[r].astype(BF16)) for r in range(2)]
        for c in range(chunks):
            at = c * part
            for r in range(2):
                core = oa_ref[r, at : at + part, :] + passed[r][at : at + part]
                if c == 0:
                    core = jnp.concatenate(
                        [jnp.where(replaced, outputs[r], core[0:8]), core[8:]], axis=0
                    )
                put(c, r, core)


def advance_kernel(
    hop_ref, recv_ref, early_ref, cq_ref, ck_ref, cv_ref, hop_own, last_ref, next_ref, rows
):
    finals, _ = first_tokens(hop_ref, recv_ref, early_ref, cq_ref, ck_ref, cv_ref, rows)
    first = lax.axis_index("half") == 0
    for r in range(2):
        last = last_ref[r]
        through = mm_parts(halves(last[:, DV:]), halves(finals[r]))
        moved = jnp.where(first, 0.0, through) + last[:, :DV]
        next_ref[r * DK : (r + 1) * DK, :] = moved.astype(BF16)
    next_ref[2 * DK :, :] = hop_own[2 * DK :, :]


def gate_kernel(heads_axis, normed_ref, z_ref, out_ref, made, sems):
    subs, tokens = normed_ref.shape[0] // heads_axis, z_ref.shape[0]
    width = subs * 2 * DV
    copies = []
    for head in range(heads_axis):
        for sub in range(subs):
            for r in range(2):
                at = (2 * (head * subs + sub) + r) * DV
                gate = silu(z_ref[:, at : at + DV].astype(F32))
                here = slice(r * tokens, (r + 1) * tokens)
                value = normed_ref[sub * heads_axis + head, here, :].astype(F32)
                made[:, at : at + DV] = (value * gate).astype(BF16)
        lanes = pl.ds(head * width, width)
        copy = pltpu.make_async_copy(made.at[:, lanes], out_ref.at[:, lanes], sems.at[head])
        copy.start()
        copies.append(copy)
    for copy in copies:
        copy.wait()


VMEM = pl.BlockSpec(memory_space=pltpu.VMEM)
SMEM = pl.BlockSpec(memory_space=pltpu.SMEM)
ANY = pl.BlockSpec(memory_space=pl.ANY)


def near(x):
    return pltpu.with_memory_space_constraint(x, pltpu.VMEM)


def far(x):
    return pltpu.with_memory_space_constraint(x, pltpu.HBM)


def call(kernel, outs, in_specs, scratch=(), out_spec=VMEM, flops=1 << 26, moved=1 << 21):
    return pl.pallas_call(
        kernel,
        out_shape=outs,
        in_specs=in_specs,
        out_specs=jax.tree.map(lambda _: out_spec, outs),
        scratch_shapes=list(scratch),
        compiler_params=pltpu.CompilerParams(vmem_limit_bytes=VMEM_BYTES),
        cost_estimate=pl.CostEstimate(flops=flops, bytes_accessed=moved, transcendentals=0),
    )


def local(
    q_rows,
    k_rows,
    v_rows,
    z_rows,
    a_rows,
    b_rows,
    conv_q,
    conv_k,
    conv_v,
    a_log,
    dt_bias,
    norm_gain,
):
    shards, subs, heads_axis = (lax.axis_size(a) for a in ("half", "sub", "head"))
    peers, tokens = subs * heads_axis, q_rows.shape[0]
    total = peers * tokens
    spans = total // SPAN
    group = ("sub", "head")
    route = [(i, i + 1) for i in range(shards - 1)]
    inputs = [far(x) for x in (q_rows, k_rows, v_rows, a_rows.T, b_rows.T)]
    packed = call(
        functools.partial(pack_kernel, heads_axis),
        pltpu.VMEM((peers, GATES + 4 * tokens, 128), BF16),
        [ANY] * 5,
        [pltpu.VMEM(x.shape, BF16) for x in inputs] + [pltpu.SemaphoreType.DMA((5,))],
        flops=1 << 20,
    )(*inputs)
    blocks = near(lax.all_to_all(packed, group, 0, 0, tiled=True))
    keys, keys_t, inverses, lins, ends, within, cols, early = call(
        keys_kernel,
        (
            pltpu.VMEM((total, DK), BF16),
            pltpu.VMEM((spans, DK, SPAN), BF16),
            pltpu.VMEM((2, spans, 2, SPAN, SPAN), BF16),
            pltpu.VMEM((2, spans, DK, DK), BF16),
            pltpu.VMEM((SPAN, DK), F32),
            pltpu.VMEM((2, total, SPAN), BF16),
            pltpu.VMEM((SPAN, SPAN), F32),
            pltpu.VMEM((8, SPAN), F32),
        ),
        [VMEM, VMEM, SMEM, SMEM],
        [pltpu.VMEM((8 + total, DK), F32)],
        flops=1 << 32,
    )(blocks, conv_k, a_log, dt_bias)
    keys, keys_t, inverses, lins, ends, within, cols, early = (
        near(x) for x in (keys, keys_t, inverses, lins, ends, within, cols, early)
    )
    hop, values, starts, adds = call(
        opening_kernel,
        (
            pltpu.VMEM((2 * DK + 16, 128), BF16),
            pltpu.VMEM((2, total, DV), BF16),
            pltpu.VMEM((2, spans, 2 * DK, DV), BF16),
            pltpu.VMEM((2, spans, DK, DV), F32),
        ),
        [VMEM] * 7,
        [pltpu.VMEM((8 + total, 2 * DV), F32)],
        flops=1 << 32,
    )(blocks, conv_v, keys_t, inverses, lins, ends, cols)
    entering = near(lax.ppermute(hop, "half", route))
    hop, values, starts, adds = (near(x) for x in (hop, values, starts, adds))
    out_a, out_m, last = call(
        output_kernel,
        (
            pltpu.VMEM((2, total, DV), F32),
            pltpu.VMEM((2, total, DV), BF16),
            pltpu.VMEM((2, DK, 2 * DV), F32),
        ),
        [VMEM] * 14,
        [
            pltpu.VMEM((8 + total, 2 * DV), F32),
            pltpu.VMEM((8 + total, DK), F32),
            pltpu.VMEM((2, total, DV), BF16),
            pltpu.VMEM((2, spans, SPAN, SPAN), BF16),
            pltpu.VMEM((spans, 2 * SPAN, DK), BF16),
            pltpu.VMEM((2, 2, spans, 2 * DK, DV), BF16),
        ],
        flops=1 << 32,
    )(
        blocks,
        conv_q,
        conv_v,
        keys,
        keys_t,
        inverses,
        lins,
        ends,
        within,
        cols,
        hop,
        values,
        starts,
        adds,
    )
    for _ in range(shards - 2):
        moved = call(
            advance_kernel,
            pltpu.VMEM(hop.shape, BF16),
            [VMEM] * 8,
            [pltpu.VMEM((32, 512), F32)],
        )(entering, blocks, early, conv_q, conv_k, conv_v, hop, near(last))
        entering = near(lax.ppermute(moved, "half", route))
    normed = call(
        finish_kernel,
        pltpu.VMEM((peers, 2 * tokens, DV), BF16),
        [VMEM] * 9,
        [pltpu.VMEM((32, 512), F32)],
    )(
        entering,
        blocks,
        early,
        conv_q,
        conv_k,
        conv_v,
        norm_gain.reshape(1, DV),
        near(out_a),
        near(out_m),
    )
    returned = near(lax.all_to_all(normed, group, 0, 0, tiled=True))
    return call(
        functools.partial(gate_kernel, heads_axis),
        jax.ShapeDtypeStruct(z_rows.shape, BF16),
        [VMEM] * 2,
        [pltpu.VMEM(z_rows.shape, BF16), pltpu.SemaphoreType.DMA((heads_axis,))],
        ANY,
    )(returned, z_rows)


def solution(mesh):
    heads_axis = mesh.shape["head"]
    subs = KH // heads_axis
    regrouped = Mesh(
        mesh.devices.reshape(mesh.shape["ctx"] // subs, subs, heads_axis), ("half", "sub", "head")
    )
    row = P(("half", "sub", "head"), None)
    placed = (row,) * 6 + (P(None, "head"),) * 3 + (P("head"),) * 2 + (P(),)
    return jax.shard_map(local, mesh=regrouped, in_specs=placed, out_specs=row, check_vma=False)
```

```python
import functools

import jax
import jax.numpy as jnp
from jax import lax
from jax.experimental import pallas as pl
from jax.experimental.pallas import tpu as pltpu
from jax.sharding import Mesh, PartitionSpec as P

DK = 128
DV = 128
CONV = 4
KH = 16
SUB = 16
SPAN = 128
EDGE = CONV - 1
EPS = 1e-06
F32 = jnp.float32
BF16 = jnp.bfloat16
VMEM_BYTES = 24 * 1024 * 1024
GATES = 8


def dot(a, b, dims=((1,), (0,))):
    return lax.dot_general(a, b, (dims, ((), ())), preferred_element_type=F32)


def halves(x):
    high = x.astype(BF16)
    return high, (x - high.astype(F32)).astype(BF16)


def mm_parts(a, b):
    both = jnp.concatenate(a, axis=1)
    return dot(both, jnp.concatenate([b[0], b[0]], axis=0)) + dot(a[0], b[1])


def silu(x):
    half = 0.5 * x
    return half + half * jnp.tanh(half)


def unit(y, factor):
    scale = lax.rsqrt(jnp.sum(y * y, axis=-1, keepdims=True) + EPS)
    return (y * scale * factor).astype(BF16)


def iota(shape, dim):
    return lax.broadcasted_iota(jnp.int32, shape, dim)


def block_of(x, size):
    return lax.shift_right_logical(x, jnp.full(x.shape, size.bit_length() - 1, jnp.int32))


def place_in(x, size):
    return x & (size - 1)


def pack_kernel(
    heads_axis, q_in, k_in, v_in, at_in, bt_in, out_ref, q_ref, k_ref, v_ref, at_ref, bt_ref, sems
):
    peers, tokens = out_ref.shape[0], q_ref.shape[0]
    pairs = ((at_in, at_ref), (bt_in, bt_ref), (k_in, k_ref), (v_in, v_ref), (q_in, q_ref))
    copies = [pltpu.make_async_copy(a, b, sems.at[i]) for i, (a, b) in enumerate(pairs)]
    for copy in copies:
        copy.start()
    subs = peers // heads_axis
    key_heads = [(dest % heads_axis) * subs + dest // heads_axis for dest in range(peers)]
    for copy in copies[:2]:
        copy.wait()
    value_heads = at_ref.shape[0]
    row, entry = iota((peers * GATES, value_heads), 0), iota((peers * GATES, value_heads), 1)
    dest, which = block_of(row, GATES), place_in(row, GATES)
    first = 2 * (place_in(dest, heads_axis) * subs + block_of(dest, heads_axis))
    pick_a = jnp.where((which < 2) & (entry == first + which), 1.0, 0.0).astype(BF16)
    pick_b = jnp.where(
        (which >= 2) & (which < 4) & (entry == first + which - 2), 1.0, 0.0
    ).astype(BF16)
    picked = (dot(pick_a, at_ref[...]) + dot(pick_b, bt_ref[...])).astype(BF16)
    lane_shift = tokens * lax.rem(lax.axis_index("head"), SPAN // tokens)
    place = jnp.where(
        iota((tokens, SPAN), 1) == iota((tokens, SPAN), 0) + lane_shift, 1.0, 0.0
    ).astype(BF16)
    gates = dot(picked, place).astype(BF16)
    for dest in range(peers):
        out_ref[dest, 4 * tokens :, :] = gates[GATES * dest : GATES * (dest + 1), :]

    def laid(ref, lane, start):
        for dest, key_head in enumerate(key_heads):
            at = lane(key_head) * 128
            out_ref[dest, start * tokens : (start + 1) * tokens, :] = ref[
                :, at : at + 128
            ]

    copies[2].wait()
    laid(k_ref, lambda key_head: key_head, 0)
    copies[3].wait()
    laid(v_ref, lambda key_head: 2 * key_head, 1)
    laid(v_ref, lambda key_head: 2 * key_head + 1, 2)
    copies[4].wait()
    laid(q_ref, lambda key_head: key_head, 3)


def invert(systems):
    size = systems[0].shape[0]
    blocks = size // SUB
    row, col = iota((size, size), 0), iota((size, size), 1)
    diagonal = block_of(row, SUB) == block_of(col, SUB)
    compact = jnp.concatenate(
        [
            jnp.sum(jnp.where(diagonal, n, 0.0).reshape(blocks, SUB, size), axis=0)
            for n in systems
        ],
        axis=0,
    )
    count = len(systems)
    lane, line = iota(compact.shape, 1), iota(compact.shape, 0)
    solved = jnp.where(place_in(lane ^ line, SUB) == 0, 1.0, 0.0).reshape(count, SUB, size)
    for m in range(SUB - 1):
        source = (lane & ~(SUB - 1)) | m
        spread = jnp.take_along_axis(compact, source, axis=1, mode="promise_in_bounds")
        solved = solved - spread.reshape(count, SUB, size) * solved[:, m : m + 1, :]
    lows = [halves(n) for n in systems]
    placed = jnp.where(diagonal, 1.0, 0.0).astype(BF16)
    parts = [
        tuple(jnp.concatenate([x] * blocks, axis=0) * placed for x in halves(solved[i]))
        for i in range(count)
    ]
    levels = []
    width = SUB
    while width < size:
        below = (block_of(row ^ col, 2 * width) == 0) & ((col & width) == 0)
        levels.append((width, jnp.where(below, 1.0, 0.0).astype(BF16)))
        width *= 2
    return doubled(lows, parts, levels)


def doubled(lows, parts, levels):
    size = levels[0][1].shape[0]
    blank = jnp.zeros((size, size), BF16)
    for width, below in levels:
        odd = [(j, j + width) for j in range(width, size, 2 * width)]

        def rows_of(x):
            return jnp.concatenate([x[lo:hi] for lo, hi in odd], axis=0)

        def woven(even, x):
            pieces = []
            for j, (lo, hi) in enumerate(odd):
                pieces += [even[lo - width : lo], x[j * width : (j + 1) * width]]
            return jnp.concatenate(pieces, axis=0)

        mask = rows_of(below)
        firsts = [
            mm_parts((rows_of(n[0]) * mask, rows_of(n[1]) * mask), t) for n, t in zip(lows, parts)
        ]
        spreads = [tuple(woven(blank, x) for x in halves(first)) for first in firsts]
        odds = [(rows_of(t[0]), rows_of(t[1])) for t in parts]
        seconds = [halves(-mm_parts(o, spread)) for o, spread in zip(odds, spreads)]
        parts = [
            tuple(woven(t[i], o[i] + second[i]) for i in range(2))
            for t, o, second in zip(parts, odds, seconds)
        ]
    return parts


def gate_values(gates, sub, alog_ref, dt_ref):
    second = place_in(iota(gates.shape, 0), GATES) == 1
    a_log = jnp.where(second, alog_ref[2 * sub + 1], alog_ref[2 * sub])
    dt_bias = jnp.where(second, dt_ref[2 * sub + 1], dt_ref[2 * sub])
    shifted = gates + dt_bias
    soft = jnp.maximum(shifted, 0.0) + jnp.log1p(jnp.exp(-jnp.abs(shifted)))
    return -jnp.exp(a_log) * soft, 1.0 / (1.0 + jnp.exp(-gates))


def convolved(rows, at, count, lanes, tap):
    summed = tap[0:1] * rows[at : at + count, lanes]
    for j in range(1, CONV):
        summed = summed + tap[j : j + 1] * rows[at + j : at + j + count, lanes]
    return silu(summed)


def key_tap(sub, tap_ref):
    return tap_ref[:, pl.ds(pl.multiple_of(sub * DK, 128), DK)]


def value_taps(sub, cv_ref):
    lane = pl.multiple_of(sub * 2 * DV, 128)
    return [cv_ref[:, pl.ds(pl.multiple_of(lane + r * DV, 128), DV)] for r in range(2)]


def widened(rows, recv_ref, starts, tokens):
    rows[0:8, :] = jnp.zeros((8, rows.shape[1]), F32)
    for s in range(recv_ref.shape[0]):
        for g, start in enumerate(starts):
            rows[8 + s * tokens : 8 + (s + 1) * tokens, g * 128 : (g + 1) * 128] = recv_ref[
                s, start : start + tokens, :
            ].astype(F32)


def keys_part(
    recv_ref,
    ck_ref,
    alog_ref,
    dt_ref,
    keys_ref,
    keys_t_ref,
    t_ref,
    lin_ref,
    ends_ref,
    within_ref,
    cols_ref,
    early_ref,
    rows,
):
    sub = lax.axis_index("sub")
    later = lax.axis_index("half") > 0
    peers = recv_ref.shape[0]
    tokens = (recv_ref.shape[1] - GATES) // 4
    spans = peers * tokens // SPAN
    tap = key_tap(sub, ck_ref)
    widened(rows, recv_ref, [0], tokens)
    stacked = [
        sum(recv_ref[s, 4 * tokens :, :].astype(F32) for s in range(n, n + SPAN // tokens))
        for n in range(0, peers, SPAN // tokens)
    ]
    stacked.append(jnp.zeros((SPAN - spans * GATES, SPAN), F32))
    gates = jnp.concatenate(stacked, axis=0)
    decay, rate = gate_values(gates, sub, alog_ref, dt_ref)
    if early_ref is not None:
        early_ref[...] = jnp.where(iota((8, SPAN), 0) < 2, decay[0:8], rate[0:8])
    skipped = later & (iota(gates.shape, 0) < GATES) & (iota(gates.shape, 1) < EDGE)
    decay = jnp.where(skipped, 0.0, decay)
    rate = jnp.where(skipped, 0.0, rate)
    lane_r, lane_c = iota((SPAN, SPAN), 0), iota((SPAN, SPAN), 1)
    upto = jnp.where(lane_r <= lane_c, 1.0, 0.0).astype(BF16)
    d_high, _ = halves(decay)
    d_mid, d_low = halves(decay - d_high.astype(F32))
    cum = dot(d_high, upto) + (dot(d_mid, upto) + dot(d_low, upto))
    growth = jnp.exp(cum)
    here = pltpu.roll(rate, rate.shape[0] - 2, 0)
    rest = jnp.exp(cum[:, SPAN - 1 :] - cum) * here
    which = place_in(iota(gates.shape, 0), GATES)
    mixed = jnp.where(which < 2, cum, pltpu.roll(growth, 2, 0))
    columns = jnp.transpose(jnp.where(which < 4, mixed, pltpu.roll(rest, 4, 0)))
    cols_ref[...] = columns
    lower = lane_r >= lane_c
    strict = lane_r > lane_c
    both = [(n, r) for n in range(spans) for r in range(2)]
    keys = []
    for n in range(spans):
        k_n = unit(convolved(rows, n * SPAN + 8 - EDGE, SPAN, slice(0, DK), tap), 1.0)
        keys_ref[n * SPAN : (n + 1) * SPAN, :] = k_n
        keys.append(k_n)
    keys_t = []
    for n in range(spans):
        kt_n = jnp.transpose(keys[n].astype(F32)).astype(BF16)
        keys_t_ref[n] = kt_n
        keys_t.append(kt_n)
    grams = [dot(keys[n], keys_t[n]) for n in range(spans)]
    systems = []
    for n, r in both:
        at = GATES * n + r
        gap = columns[:, at : at + 1] - cum[at : at + 1, :]
        within = jnp.exp(jnp.where(lower, gap, 0.0)) * here[at : at + 1, :]
        within_ref[r, n * SPAN : (n + 1) * SPAN, :] = jnp.where(lower, within, 0.0).astype(BF16)
        systems.append(jnp.where(strict, within * grams[n], 0.0))
    inverses = invert(systems)
    for i, (n, r) in enumerate(both):
        t_ref[r, n, 0], t_ref[r, n, 1] = inverses[i]
    scaled = []
    for n, r in both:
        at = GATES * n + r
        right = (columns[:, at + 2 : at + 3] * keys[n].astype(F32)).astype(BF16)
        scaled.append(jnp.concatenate([right, right], axis=0))
    w_mats = [dot(jnp.concatenate(t, axis=1), x) for t, x in zip(inverses, scaled)]
    weighed = []
    for (n, r), w_mat in zip(both, w_mats):
        at = GATES * n + r
        weighed.append((columns[:, at + 4 : at + 5] * w_mat).astype(BF16))
    moved = [
        dot(keys_t[n], jnp.concatenate(weighed[2 * n : 2 * n + 2], axis=1)) for n in range(spans)
    ]
    ends_ref[...] = jnp.broadcast_to(growth[:, SPAN - 1 :], ends_ref.shape)
    for n, r in both:
        lin_ref[r, n] = moved[n][:, r * DK : (r + 1) * DK].astype(BF16)


def unwound(t_ref, n, r, x):
    both = jnp.concatenate([t_ref[r, n, 0], t_ref[r, n, 1]], axis=1)
    return dot(both, jnp.concatenate([x, x], axis=0))


def end_of(ends_ref, n, r):
    return ends_ref[GATES * n + r : GATES * n + r + 1, :]


def followed(span_map, state):
    end, moved, add = span_map
    return step(end, moved, state, halves(state)) + add


def composed(maps):
    if len(maps) == 1:
        return maps[0]
    half = len(maps) // 2
    end_a, moved_a, add_a = composed(maps[:half])
    end_b, moved_b, add_b = composed(maps[half:])
    high, low = halves(add_a)
    rights = jnp.concatenate(
        [
            jnp.concatenate([moved_a, high], axis=1),
            jnp.concatenate([jnp.zeros_like(moved_a), low], axis=1),
        ],
        axis=0,
    )
    passed = dot(jnp.concatenate([moved_b, moved_b], axis=1), rights)
    moved = end_b * moved_a.astype(F32) + end_a * moved_b.astype(F32) - passed[:, :DK]
    add = end_b * add_a - passed[:, DK:] + add_b
    return end_a * end_b, moved.astype(BF16), add


def step(end, moved, state, parts):
    both = jnp.concatenate([moved, moved], axis=1)
    return end * state - dot(both, jnp.concatenate(parts, axis=0))


def values_part(recv_ref, cv_ref, keys_t_ref, t_ref, cols_ref, rows, vs):
    sub = lax.axis_index("sub")
    tokens = (recv_ref.shape[1] - GATES) // 4
    spans = t_ref.shape[1]
    taps = value_taps(sub, cv_ref)
    widened(rows, recv_ref, [tokens, 2 * tokens], tokens)
    both = [(n, r) for n in range(spans) for r in range(2)]
    values = []
    for n, r in both:
        lanes = slice(r * DV, (r + 1) * DV)
        v_n = convolved(rows, n * SPAN + 8 - EDGE, SPAN, lanes, taps[r]).astype(BF16)
        vs[r, n * SPAN : (n + 1) * SPAN, :] = v_n
        values.append(v_n)
    solved = [unwound(t_ref, n, r, v) for (n, r), v in zip(both, values)]
    weighed = []
    for (n, r), u_mat in zip(both, solved):
        at = GATES * n + r
        weighed.append((cols_ref[:, at + 4 : at + 5] * u_mat).astype(BF16))
    moved = [
        dot(keys_t_ref[n], jnp.concatenate(weighed[2 * n : 2 * n + 2], axis=1))
        for n in range(spans)
    ]
    return [moved[n][:, r * DV : (r + 1) * DV] for n, r in both]


def opening_kernel(
    recv_ref,
    ck_ref,
    cv_ref,
    alog_ref,
    dt_ref,
    hop_ref,
    keys_ref,
    keys_t_ref,
    t_ref,
    lin_ref,
    ends_ref,
    within_ref,
    cols_ref,
    vs_ref,
    xs_ref,
    adds_ref,
    key_rows,
    rows,
):
    first = lax.axis_index("half") == 0
    peers = recv_ref.shape[0]
    tokens = (recv_ref.shape[1] - GATES) // 4
    spans = t_ref.shape[1]
    edges = []
    for which in (3, 0, 1, 2):
        end = (which + 1) * tokens
        edges.append(recv_ref[peers - 1, end - 16 : end, :].astype(F32)[16 - EDGE :])
    edges.append(jnp.zeros((16 - 4 * EDGE, 128), F32))
    hop_ref[2 * DK :, :] = jnp.concatenate(edges, axis=0).astype(BF16)

    @pl.when(first)
    def _():
        keys_part(
            recv_ref,
            ck_ref,
            alog_ref,
            dt_ref,
            keys_ref,
            keys_t_ref,
            t_ref,
            lin_ref,
            ends_ref,
            within_ref,
            cols_ref,
            None,
            key_rows,
        )
        adds = values_part(recv_ref, cv_ref, keys_t_ref, t_ref, cols_ref, rows, vs_ref)
        for n in range(spans):
            for r in range(2):
                adds_ref[r, n] = adds[2 * n + r]
        maps = [
            [(end_of(ends_ref, n, r), lin_ref[r, n], adds[2 * n + r]) for n in range(spans)]
            for r in range(2)
        ]
        states = [m[0][2] for m in maps]
        done = 1
        while done < spans:
            for r in range(2):
                if done > 1:
                    xs_ref[r, done] = jnp.concatenate(halves(states[r]), axis=0)
            later = [composed(m[done : 2 * done]) for m in maps]
            states = [followed(m, x) for m, x in zip(later, states)]
            done *= 2
        for r in range(2):
            hop_ref[r * DK : (r + 1) * DK, :] = states[r].astype(BF16)

    @pl.when(jnp.logical_not(first))
    def _():
        hop_ref[0 : 2 * DK, :] = jnp.zeros((2 * DK, DV), BF16)


def output_kernel(
    recv_ref,
    cq_ref,
    ck_ref,
    cv_ref,
    alog_ref,
    dt_ref,
    hop_ref,
    first_keys,
    first_keys_t,
    first_t,
    first_lin,
    first_ends,
    first_within,
    first_cols,
    vs_ref,
    xs_ref,
    adds_ref,
    oa_ref,
    om_ref,
    last_ref,
    early_ref,
    own_keys,
    own_keys_t,
    own_t,
    own_lin,
    own_ends,
    own_within,
    own_cols,
    key_rows,
    rows,
    query_rows,
    values,
    inner,
    readers,
    states_ref,
):
    sub = lax.axis_index("sub")
    first = lax.axis_index("half") == 0
    tokens = (recv_ref.shape[1] - GATES) // 4
    spans = own_t.shape[1]
    both = [(n, r) for n in range(spans) for r in range(2)]
    tap = key_tap(sub, cq_ref)
    widened(query_rows, recv_ref, [3 * tokens], tokens)

    def span_rows(n):
        return slice(n * SPAN, (n + 1) * SPAN)

    def growing(cols_ref):
        return lambda n, r: cols_ref[:, GATES * n + 2 + r : GATES * n + 3 + r]

    def prepare(keys_ref, keys_t_ref, within_ref):
        queries = []
        for n in range(spans):
            at = n * SPAN + 8 - EDGE
            q_n = unit(convolved(query_rows, at, SPAN, slice(0, DK), tap), DK**-0.5)
            queries.append(q_n)
            readers[n, 0:SPAN, :] = keys_ref[span_rows(n), :]
            readers[n, SPAN:, :] = q_n
        scores = [dot(queries[n], keys_t_ref[n]) for n in range(spans)]
        for n, r in both:
            weight = within_ref[r, span_rows(n), :].astype(F32)
            inner[r, n] = (weight * scores[n]).astype(BF16)

    def twice(x, axis):
        return jnp.concatenate([x, x], axis=axis)

    @pl.when(first)
    def _():
        t_ref, lin_ref, ends_ref = first_t, first_lin, first_ends
        growth = growing(first_cols)
        prepare(first_keys, first_keys_t, first_within)
        stacks, states = [], []
        for n in range(1, spans):
            if n == 1:
                states = [adds_ref[r, 0] for r in range(2)]
                stack = [jnp.concatenate(halves(x), axis=0) for x in states]
            elif n & (n - 1) == 0:
                stack = [xs_ref[r, n] for r in range(2)]
                states = [x[:DK].astype(F32) + x[DK:].astype(F32) for x in stack]
            else:
                states = [
                    followed(
                        (end_of(ends_ref, n - 1, r), lin_ref[r, n - 1], adds_ref[r, n - 1]),
                        states[r],
                    )
                    for r in range(2)
                ]
                stack = [jnp.concatenate(halves(x), axis=0) for x in states]
            stacks.append(jnp.concatenate(stack, axis=1))
        reads = [dot(twice(readers[n], 1), stacks[n - 1]) for n in range(1, spans)]
        rests, seen = [], []
        for n, r in both:
            lanes = slice(r * DV, (r + 1) * DV)
            value = vs_ref[r, span_rows(n), :]
            if n == 0:
                rests.append(value)
                seen.append(None)
            else:
                read = growth(n, r) * reads[n - 1][:SPAN, lanes]
                rests.append((value.astype(F32) - read).astype(BF16))
                seen.append(growth(n, r) * reads[n - 1][SPAN:, lanes])
        fresh = [unwound(t_ref, n, r, x).astype(BF16) for (n, r), x in zip(both, rests)]
        spreads = [dot(inner[r, n], x) for (n, r), x in zip(both, fresh)]
        for (n, r), x, y in zip(both, spreads, seen):
            oa_ref[r, span_rows(n), :] = x if y is None else x + y
        for r in range(2):
            last_ref[r, :, 0:DV] = hop_ref[r * DK : (r + 1) * DK, :].astype(F32)
            last_ref[r, :, DV:] = jnp.zeros((DK, DV), F32)

    @pl.when(jnp.logical_not(first))
    def _():
        t_ref, lin_ref, ends_ref = own_t, own_lin, own_ends
        growth = growing(own_cols)
        keys_part(
            recv_ref,
            ck_ref,
            alog_ref,
            dt_ref,
            own_keys,
            own_keys_t,
            own_t,
            own_lin,
            own_ends,
            own_within,
            own_cols,
            early_ref,
            key_rows,
        )
        adds = values_part(recv_ref, cv_ref, own_keys_t, own_t, own_cols, rows, values)
        zero_half = jnp.zeros((DK, DV), F32)
        identity = jnp.where(iota((DK, DK), 0) == iota((DK, DK), 1), 1.0, 0.0)
        states = [
            jnp.concatenate(
                [adds[r], ends_ref[r : r + 1, :] * identity - lin_ref[r, 0].astype(F32)], axis=1
            )
            for r in range(2)
        ]
        for n in range(1, spans):
            for r in range(2):
                parts = halves(states[r])
                for i in range(2):
                    both_parts = [x[:, i * DV : (i + 1) * DV] for x in parts]
                    states_ref[i, r, n] = jnp.concatenate(both_parts, axis=0)
                add = jnp.concatenate([adds[2 * n + r], zero_half], axis=1)
                end = jnp.concatenate([end_of(ends_ref, n, r)] * 2, axis=1)
                states[r] = step(end, lin_ref[r, n], states[r], parts) + add
        for r in range(2):
            last_ref[r] = states[r]
        prepare(own_keys, own_keys_t, own_within)
        reads = [
            dot(
                twice(readers[n], 1),
                jnp.concatenate([states_ref[0, r, n], states_ref[1, r, n]], axis=1),
            )
            if n > 0
            else None
            for n, r in both
        ]
        rests, seen = [], []
        for (n, r), read in zip(both, reads):
            value = values[r, span_rows(n), :].astype(F32)
            if n == 0:
                known = growth(n, r) * readers[n].astype(F32)[:SPAN]
                asked = growth(n, r) * readers[n].astype(F32)[SPAN:]
                rest = jnp.concatenate([value, -known], axis=1)
                seen.append(jnp.concatenate([zero_half, asked], axis=1))
            else:
                rest = jnp.concatenate([value, zero_half], axis=1) - growth(n, r) * read[:SPAN]
                seen.append(growth(n, r) * read[SPAN:])
            rests.append(rest.astype(BF16))
        fresh = [unwound(t_ref, n, r, x).astype(BF16) for (n, r), x in zip(both, rests)]
        spreads = [dot(inner[r, n], x) for (n, r), x in zip(both, fresh)]
        for (n, r), x, y in zip(both, spreads, seen):
            out = x + y
            oa_ref[r, span_rows(n), :] = out[:, :DV]
            om_ref[r, span_rows(n), :] = out[:, DV:].astype(BF16)


def first_tokens(hop_ref, recv_ref, early_ref, cq_ref, ck_ref, cv_ref, rows):
    sub = lax.axis_index("sub")
    tokens = (recv_ref.shape[1] - GATES) // 4
    taps = [key_tap(sub, cq_ref), key_tap(sub, ck_ref)] + value_taps(sub, cv_ref)
    results = []
    edges = hop_ref[2 * DK :, :].astype(F32)
    for g, first in enumerate((3, 0, 1, 2)):
        lanes = slice(g * 128, (g + 1) * 128)
        start = first * tokens
        rows[16 - EDGE : 16, lanes] = edges[EDGE * g : EDGE * (g + 1)]
        rows[16:32, lanes] = recv_ref[0, start : start + 16, :].astype(F32)
        results.append(convolved(rows, 16 - EDGE, 8, lanes, taps[g]))
    q_cols = jnp.transpose(unit(results[0], DK**-0.5).astype(F32))
    k_cols = jnp.transpose(unit(results[1], 1.0).astype(F32))
    gates = early_ref[...]
    line = iota((8, DV), 0)
    finals, outputs = [], []
    for r in range(2):
        values = results[2 + r].astype(BF16).astype(F32)
        entering = hop_ref[r * DK : (r + 1) * DK, :].astype(F32)
        state, out = entering, jnp.zeros((8, DV), F32)
        for t in range(EDGE):
            k_t, q_t = k_cols[:, t : t + 1], q_cols[:, t : t + 1]
            state = jnp.exp(gates[r : r + 1, t : t + 1]) * state
            held = jnp.sum(k_t * state, axis=0, keepdims=True)
            state = state + k_t * (
                gates[2 + r : 3 + r, t : t + 1] * (values[t : t + 1, :] - held)
            )
            out = jnp.where(line == t, jnp.sum(q_t * state, axis=0, keepdims=True), out)
        finals.append(state)
        outputs.append(out)
    return finals, outputs


def finish_kernel(
    hop_ref, recv_ref, early_ref, cq_ref, ck_ref, cv_ref, gain_ref, oa_ref, om_ref, out_ref, rows
):
    peers, tokens = out_ref.shape[0], out_ref.shape[1] // 2
    first = lax.axis_index("half") == 0
    gain = gain_ref[...]
    chunks = 4
    part, peer_part = peers * tokens // chunks, peers // chunks

    def put(c, r, core):
        scale = lax.rsqrt(jnp.mean(core * core, axis=-1, keepdims=True) + EPS)
        normed = (core * scale * gain).astype(BF16)
        here = slice(c * peer_part, (c + 1) * peer_part)
        out_ref[here, r * tokens : (r + 1) * tokens, :] = normed.reshape(peer_part, tokens, DV)

    @pl.when(first)
    def _():
        for c in range(chunks):
            for r in range(2):
                put(c, r, oa_ref[r, c * part : (c + 1) * part, :])

    @pl.when(jnp.logical_not(first))
    def _():
        finals, outputs = first_tokens(hop_ref, recv_ref, early_ref, cq_ref, ck_ref, cv_ref, rows)
        replaced = iota((8, DV), 0) < EDGE
        passed = [dot(om_ref[r], finals[r].astype(BF16)) for r in range(2)]
        for c in range(chunks):
            at = c * part
            for r in range(2):
                core = oa_ref[r, at : at + part, :] + passed[r][at : at + part]
                if c == 0:
                    core = jnp.concatenate(
                        [jnp.where(replaced, outputs[r], core[0:8]), core[8:]], axis=0
                    )
                put(c, r, core)


def advance_kernel(
    hop_ref, recv_ref, early_ref, cq_ref, ck_ref, cv_ref, hop_own, last_ref, next_ref, rows
):
    finals, _ = first_tokens(hop_ref, recv_ref, early_ref, cq_ref, ck_ref, cv_ref, rows)
    first = lax.axis_index("half") == 0
    for r in range(2):
        last = last_ref[r]
        through = mm_parts(halves(last[:, DV:]), halves(finals[r]))
        moved = jnp.where(first, 0.0, through) + last[:, :DV]
        next_ref[r * DK : (r + 1) * DK, :] = moved.astype(BF16)
    next_ref[2 * DK :, :] = hop_own[2 * DK :, :]


def gate_kernel(heads_axis, normed_ref, z_ref, out_ref, made, sems):
    subs, tokens = normed_ref.shape[0] // heads_axis, z_ref.shape[0]
    width = subs * 2 * DV
    copies = []
    for head in range(heads_axis):
        for sub in range(subs):
            for r in range(2):
                at = (2 * (head * subs + sub) + r) * DV
                gate = silu(z_ref[:, at : at + DV].astype(F32))
                here = slice(r * tokens, (r + 1) * tokens)
                value = normed_ref[sub * heads_axis + head, here, :].astype(F32)
                made[:, at : at + DV] = (value * gate).astype(BF16)
        lanes = pl.ds(head * width, width)
        copy = pltpu.make_async_copy(made.at[:, lanes], out_ref.at[:, lanes], sems.at[head])
        copy.start()
        copies.append(copy)
    for copy in copies:
        copy.wait()


VMEM = pl.BlockSpec(memory_space=pltpu.VMEM)
SMEM = pl.BlockSpec(memory_space=pltpu.SMEM)
ANY = pl.BlockSpec(memory_space=pl.ANY)


def near(x):
    return pltpu.with_memory_space_constraint(x, pltpu.VMEM)


def far(x):
    return pltpu.with_memory_space_constraint(x, pltpu.HBM)


def call(kernel, outs, in_specs, scratch=(), out_spec=VMEM, flops=1 << 26, moved=1 << 21):
    return pl.pallas_call(
        kernel,
        out_shape=outs,
        in_specs=in_specs,
        out_specs=jax.tree.map(lambda _: out_spec, outs),
        scratch_shapes=list(scratch),
        compiler_params=pltpu.CompilerParams(vmem_limit_bytes=VMEM_BYTES),
        cost_estimate=pl.CostEstimate(flops=flops, bytes_accessed=moved, transcendentals=0),
    )


def local(
    q_rows,
    k_rows,
    v_rows,
    z_rows,
    a_rows,
    b_rows,
    conv_q,
    conv_k,
    conv_v,
    a_log,
    dt_bias,
    norm_gain,
):
    shards, subs, heads_axis = (lax.axis_size(a) for a in ("half", "sub", "head"))
    peers, tokens = subs * heads_axis, q_rows.shape[0]
    total = peers * tokens
    spans = total // SPAN
    group = ("sub", "head")
    route = [(i, i + 1) for i in range(shards - 1)]
    inputs = [far(x) for x in (q_rows, k_rows, v_rows, a_rows.T, b_rows.T)]
    packed = call(
        functools.partial(pack_kernel, heads_axis),
        pltpu.VMEM((peers, GATES + 4 * tokens, 128), BF16),
        [ANY] * 5,
        [pltpu.VMEM(x.shape, BF16) for x in inputs] + [pltpu.SemaphoreType.DMA((5,))],
        flops=1 << 20,
    )(*inputs)
    blocks = near(lax.all_to_all(packed, group, 0, 0, tiled=True))
    made = (
        pltpu.VMEM((total, DK), BF16),
        pltpu.VMEM((spans, DK, SPAN), BF16),
        pltpu.VMEM((2, spans, 2, SPAN, SPAN), BF16),
        pltpu.VMEM((2, spans, DK, DK), BF16),
        pltpu.VMEM((SPAN, DK), F32),
        pltpu.VMEM((2, total, SPAN), BF16),
        pltpu.VMEM((SPAN, SPAN), F32),
    )
    long_rows = [pltpu.VMEM((8 + total, DK), F32), pltpu.VMEM((8 + total, 2 * DV), F32)]
    params = (conv_k, conv_v, a_log, dt_bias)
    hop, *opened = call(
        opening_kernel,
        (
            pltpu.VMEM((2 * DK + 16, 128), BF16),
            *made,
            pltpu.VMEM((2, total, DV), BF16),
            pltpu.VMEM((2, spans, 2 * DK, DV), BF16),
            pltpu.VMEM((2, spans, DK, DV), F32),
        ),
        [VMEM] * 3 + [SMEM] * 2,
        long_rows,
        flops=1 << 32,
    )(blocks, *params)
    entering = near(lax.ppermute(hop, "half", route))
    hop = near(hop)
    opened = [near(x) for x in opened]
    out_a, out_m, last, early = call(
        output_kernel,
        (
            pltpu.VMEM((2, total, DV), F32),
            pltpu.VMEM((2, total, DV), BF16),
            pltpu.VMEM((2, DK, 2 * DV), F32),
            pltpu.VMEM((8, SPAN), F32),
        ),
        [VMEM] * 4 + [SMEM] * 2 + [VMEM] * (1 + len(opened)),
        [
            *made,
            *long_rows,
            pltpu.VMEM((8 + total, DK), F32),
            pltpu.VMEM((2, total, DV), BF16),
            pltpu.VMEM((2, spans, SPAN, SPAN), BF16),
            pltpu.VMEM((spans, 2 * SPAN, DK), BF16),
            pltpu.VMEM((2, 2, spans, 2 * DK, DV), BF16),
        ],
        flops=1 << 32,
    )(blocks, conv_q, *params, hop, *opened)
    early = near(early)
    for _ in range(shards - 2):
        moved = call(
            advance_kernel,
            pltpu.VMEM(hop.shape, BF16),
            [VMEM] * 8,
            [pltpu.VMEM((32, 512), F32)],
        )(entering, blocks, early, conv_q, conv_k, conv_v, hop, near(last))
        entering = near(lax.ppermute(moved, "half", route))
    normed = call(
        finish_kernel,
        pltpu.VMEM((peers, 2 * tokens, DV), BF16),
        [VMEM] * 9,
        [pltpu.VMEM((32, 512), F32)],
    )(
        entering,
        blocks,
        early,
        conv_q,
        conv_k,
        conv_v,
        norm_gain.reshape(1, DV),
        near(out_a),
        near(out_m),
    )
    returned = near(lax.all_to_all(normed, group, 0, 0, tiled=True))
    return call(
        functools.partial(gate_kernel, heads_axis),
        jax.ShapeDtypeStruct(z_rows.shape, BF16),
        [VMEM] * 2,
        [pltpu.VMEM(z_rows.shape, BF16), pltpu.SemaphoreType.DMA((heads_axis,))],
        ANY,
    )(returned, z_rows)


def solution(mesh):
    heads_axis = mesh.shape["head"]
    subs = KH // heads_axis
    regrouped = Mesh(
        mesh.devices.reshape(mesh.shape["ctx"] // subs, subs, heads_axis), ("half", "sub", "head")
    )
    row = P(("half", "sub", "head"), None)
    placed = (row,) * 6 + (P(None, "head"),) * 3 + (P("head"),) * 2 + (P(),)
    return jax.shard_map(local, mesh=regrouped, in_specs=placed, out_specs=row, check_vma=False)
```

```python
import functools

import jax
import jax.numpy as jnp
from jax import lax
from jax.experimental import pallas as pl
from jax.experimental.pallas import tpu as pltpu
from jax.sharding import Mesh, PartitionSpec as P

DK = 128
DV = 128
CONV = 4
KH = 16
SUB = 16
SPAN = 128
PASSES = 2
EDGE = CONV - 1
EPS = 1e-06
F32 = jnp.float32
BF16 = jnp.bfloat16
VMEM_BYTES = 24 * 1024 * 1024
GATES = 8


def dot(a, b, dims=((1,), (0,))):
    return lax.dot_general(a, b, (dims, ((), ())), preferred_element_type=F32)


def halves(x):
    high = x.astype(BF16)
    return high, (x - high.astype(F32)).astype(BF16)


def mm_parts(a, b):
    both = jnp.concatenate(a, axis=1)
    return dot(both, jnp.concatenate([b[0], b[0]], axis=0)) + dot(a[0], b[1])


def silu(x):
    half = 0.5 * x
    return half + half * jnp.tanh(half)


def unit(y, factor):
    scale = lax.rsqrt(jnp.sum(y * y, axis=-1, keepdims=True) + EPS)
    return (y * scale * factor).astype(BF16)


def iota(shape, dim):
    return lax.broadcasted_iota(jnp.int32, shape, dim)


def block_of(x, size):
    return lax.shift_right_logical(x, jnp.full(x.shape, size.bit_length() - 1, jnp.int32))


def place_in(x, size):
    return x & (size - 1)


def pack_kernel(
    heads_axis, q_in, k_in, v_in, at_in, bt_in, out_ref, q_ref, k_ref, v_ref, at_ref, bt_ref, sems
):
    peers, tokens = out_ref.shape[0], q_ref.shape[0]
    pairs = ((at_in, at_ref), (bt_in, bt_ref), (k_in, k_ref), (v_in, v_ref), (q_in, q_ref))
    copies = [pltpu.make_async_copy(a, b, sems.at[i]) for i, (a, b) in enumerate(pairs)]
    for copy in copies:
        copy.start()
    subs = peers // heads_axis
    key_heads = [(dest % heads_axis) * subs + dest // heads_axis for dest in range(peers)]
    for copy in copies[:2]:
        copy.wait()
    value_heads = at_ref.shape[0]
    row, entry = iota((peers * GATES, value_heads), 0), iota((peers * GATES, value_heads), 1)
    dest, which = block_of(row, GATES), place_in(row, GATES)
    first = 2 * (place_in(dest, heads_axis) * subs + block_of(dest, heads_axis))
    pick_a = jnp.where((which < 2) & (entry == first + which), 1.0, 0.0).astype(BF16)
    pick_b = jnp.where(
        (which >= 2) & (which < 4) & (entry == first + which - 2), 1.0, 0.0
    ).astype(BF16)
    picked = (dot(pick_a, at_ref[...]) + dot(pick_b, bt_ref[...])).astype(BF16)
    lane_shift = tokens * lax.rem(lax.axis_index("head"), SPAN // tokens)
    place = jnp.where(
        iota((tokens, SPAN), 1) == iota((tokens, SPAN), 0) + lane_shift, 1.0, 0.0
    ).astype(BF16)
    gates = dot(picked, place).astype(BF16)
    for dest in range(peers):
        out_ref[dest, 4 * tokens :, :] = gates[GATES * dest : GATES * (dest + 1), :]

    def laid(ref, lane, start):
        for dest, key_head in enumerate(key_heads):
            at = lane(key_head) * 128
            out_ref[dest, start * tokens : (start + 1) * tokens, :] = ref[
                :, at : at + 128
            ]

    copies[2].wait()
    laid(k_ref, lambda key_head: key_head, 0)
    copies[3].wait()
    laid(v_ref, lambda key_head: 2 * key_head, 1)
    laid(v_ref, lambda key_head: 2 * key_head + 1, 2)
    copies[4].wait()
    laid(q_ref, lambda key_head: key_head, 3)


def compacted(system):
    size = system.shape[0]
    diagonal = block_of(iota((size, size), 0), SUB) == block_of(iota((size, size), 1), SUB)
    return jnp.sum(jnp.where(diagonal, system, 0.0).reshape(size // SUB, SUB, size), axis=0)


def substituted(compact):
    count, _, size = compact.shape
    flat = compact.reshape(count * SUB, size)
    lane, line = iota(flat.shape, 1), iota(flat.shape, 0)
    solved = jnp.where(place_in(lane ^ line, SUB) == 0, 1.0, 0.0).reshape(count, SUB, size)
    for m in range(SUB - 1):
        source = (lane & ~(SUB - 1)) | m
        spread = jnp.take_along_axis(flat, source, axis=1, mode="promise_in_bounds")
        solved = solved - spread.reshape(count, SUB, size) * solved[:, m : m + 1, :]
    return solved


def inverted(lows, small):
    size = lows[0][0].shape[0]
    row, col = iota((size, size), 0), iota((size, size), 1)
    placed = jnp.where(block_of(row, SUB) == block_of(col, SUB), 1.0, 0.0).astype(BF16)
    parts = [
        tuple(jnp.concatenate([x] * (size // SUB), axis=0) * placed for x in halves(block))
        for block in small
    ]
    levels = []
    width = SUB
    while width < size:
        below = (block_of(row ^ col, 2 * width) == 0) & ((col & width) == 0)
        levels.append((width, jnp.where(below, 1.0, 0.0).astype(BF16)))
        width *= 2
    return doubled(lows, parts, levels)


def doubled(lows, parts, levels):
    size = levels[0][1].shape[0]
    blank = jnp.zeros((size, size), BF16)
    for width, below in levels:
        odd = [(j, j + width) for j in range(width, size, 2 * width)]

        def rows_of(x):
            return jnp.concatenate([x[lo:hi] for lo, hi in odd], axis=0)

        def woven(even, x):
            pieces = []
            for j, (lo, hi) in enumerate(odd):
                pieces += [even[lo - width : lo], x[j * width : (j + 1) * width]]
            return jnp.concatenate(pieces, axis=0)

        mask = rows_of(below)
        firsts = [
            mm_parts((rows_of(n[0]) * mask, rows_of(n[1]) * mask), t) for n, t in zip(lows, parts)
        ]
        spreads = [tuple(woven(blank, x) for x in halves(first)) for first in firsts]
        odds = [(rows_of(t[0]), rows_of(t[1])) for t in parts]
        seconds = [halves(-mm_parts(o, spread)) for o, spread in zip(odds, spreads)]
        parts = [
            tuple(woven(t[i], o[i] + second[i]) for i in range(2))
            for t, o, second in zip(parts, odds, seconds)
        ]
    return parts


def gate_values(gates, sub, alog_ref, dt_ref):
    second = place_in(iota(gates.shape, 0), GATES) == 1
    a_log = jnp.where(second, alog_ref[2 * sub + 1], alog_ref[2 * sub])
    dt_bias = jnp.where(second, dt_ref[2 * sub + 1], dt_ref[2 * sub])
    shifted = gates + dt_bias
    soft = jnp.maximum(shifted, 0.0) + jnp.log1p(jnp.exp(-jnp.abs(shifted)))
    return -jnp.exp(a_log) * soft, 1.0 / (1.0 + jnp.exp(-gates))


def convolved(rows, at, count, lanes, tap):
    summed = tap[0:1] * rows[at : at + count, lanes]
    for j in range(1, CONV):
        summed = summed + tap[j : j + 1] * rows[at + j : at + j + count, lanes]
    return silu(summed)


def key_tap(sub, tap_ref):
    return tap_ref[:, pl.ds(pl.multiple_of(sub * DK, 128), DK)]


def value_taps(sub, cv_ref):
    lane = pl.multiple_of(sub * 2 * DV, 128)
    return [cv_ref[:, pl.ds(pl.multiple_of(lane + r * DV, 128), DV)] for r in range(2)]


def widened(rows, recv_ref, starts, tokens):
    rows[0:8, :] = jnp.zeros((8, rows.shape[1]), F32)
    for s in range(recv_ref.shape[0]):
        for g, start in enumerate(starts):
            rows[8 + s * tokens : 8 + (s + 1) * tokens, g * 128 : (g + 1) * 128] = recv_ref[
                s, start : start + tokens, :
            ].astype(F32)


def keys_kernel(
    recv_ref,
    ck_ref,
    alog_ref,
    dt_ref,
    keys_ref,
    keys_t_ref,
    t_ref,
    lin_ref,
    ends_ref,
    within_ref,
    cols_ref,
    early_ref,
    rows,
    col_parts,
    cum_parts,
    here_parts,
    systems_ref,
    small_ref,
):
    sub = lax.axis_index("sub")
    later = lax.axis_index("half") > 0
    peers = recv_ref.shape[0]
    tokens = (recv_ref.shape[1] - GATES) // 4
    spans = peers * tokens // SPAN
    tap = key_tap(sub, ck_ref)
    part = spans // PASSES
    part_rows = part * SPAN
    rows[0, 0:8, :] = jnp.zeros((8, DK), F32)
    for s in range(peers):
        p, at = divmod(s * tokens, part_rows)
        rows[p, 8 + at : 8 + at + tokens, :] = recv_ref[s, 0:tokens, :].astype(F32)
        if at + tokens == part_rows and p + 1 < PASSES:
            rows[p + 1, 0:8, :] = recv_ref[s, tokens - 16 : tokens, :].astype(F32)[8:]
    stacked = [
        sum(recv_ref[s, 4 * tokens :, :].astype(F32) for s in range(n, n + SPAN // tokens))
        for n in range(0, peers, SPAN // tokens)
    ]
    stacked.append(jnp.zeros((SPAN - spans * GATES, SPAN), F32))
    gates = jnp.concatenate(stacked, axis=0)
    decay, rate = gate_values(gates, sub, alog_ref, dt_ref)
    early_ref[...] = jnp.where(iota((8, SPAN), 0) < 2, decay[0:8], rate[0:8])
    skipped = later & (iota(gates.shape, 0) < GATES) & (iota(gates.shape, 1) < EDGE)
    decay = jnp.where(skipped, 0.0, decay)
    rate = jnp.where(skipped, 0.0, rate)
    lane_r, lane_c = iota((SPAN, SPAN), 0), iota((SPAN, SPAN), 1)
    upto = jnp.where(lane_r <= lane_c, 1.0, 0.0).astype(BF16)
    d_high, _ = halves(decay)
    d_mid, d_low = halves(decay - d_high.astype(F32))
    cum = dot(d_high, upto) + (dot(d_mid, upto) + dot(d_low, upto))
    growth = jnp.exp(cum)
    here = pltpu.roll(rate, rate.shape[0] - 2, 0)
    rest = jnp.exp(cum[:, SPAN - 1 :] - cum) * here
    which = place_in(iota(gates.shape, 0), GATES)
    mixed = jnp.where(which < 2, cum, pltpu.roll(growth, 2, 0))
    columns = jnp.transpose(jnp.where(which < 4, mixed, pltpu.roll(rest, 4, 0)))
    cols_ref[...] = columns
    ends_ref[...] = jnp.broadcast_to(growth[:, SPAN - 1 :], ends_ref.shape)
    lines = part * GATES
    for p in range(PASSES):
        cum_parts[p] = cum[p * lines : (p + 1) * lines]
        here_parts[p] = here[p * lines : (p + 1) * lines]
        shift = (SPAN - p * lines) % SPAN
        col_parts[p] = pltpu.roll(columns, shift, 1) if shift else columns
    lower = lane_r >= lane_c
    strict = lane_r > lane_c
    both = [(n, r) for n in range(part) for r in range(2)]

    def first_pass(p, carry):
        columns, cum, here = col_parts[p], cum_parts[p], here_parts[p]
        keys = [
            unit(convolved(rows.at[p], n * SPAN + 8 - EDGE, SPAN, slice(0, DK), tap), 1.0)
            for n in range(part)
        ]
        keys_t = [jnp.transpose(k_n.astype(F32)).astype(BF16) for k_n in keys]
        for n in range(part):
            keys_ref[pl.ds(pl.multiple_of((p * part + n) * SPAN, SPAN), SPAN), :] = keys[n]
            keys_t_ref[p * part + n] = keys_t[n]
        grams = [dot(keys[n], keys_t[n]) for n in range(part)]
        for i, (n, r) in enumerate(both):
            at = GATES * n + r
            gap = columns[:, at : at + 1] - cum[at : at + 1, :]
            within = jnp.exp(jnp.where(lower, gap, 0.0)) * here[at : at + 1, :]
            here_rows = pl.ds(pl.multiple_of((p * part + n) * SPAN, SPAN), SPAN)
            within_ref[r, here_rows, :] = jnp.where(lower, within, 0.0).astype(BF16)
            system = jnp.where(strict, within * grams[n], 0.0)
            systems_ref[p, i, 0], systems_ref[p, i, 1] = halves(system)
            small_ref[p, i] = compacted(system)
        return carry

    lax.fori_loop(0, PASSES, first_pass, 0)
    count = PASSES * len(both)
    small = substituted(small_ref[...].reshape(count, SUB, SPAN))
    small_ref[...] = small.reshape(small_ref.shape)

    def second_pass(p, carry):
        columns = col_parts[p]
        lows = [(systems_ref[p, i, 0], systems_ref[p, i, 1]) for i in range(len(both))]
        inverses = inverted(lows, [small_ref[p, i] for i in range(len(both))])
        scaled = []
        for i, (n, r) in enumerate(both):
            t_ref[r, p * part + n, 0], t_ref[r, p * part + n, 1] = inverses[i]
            at = GATES * n + r
            here_rows = pl.ds(pl.multiple_of((p * part + n) * SPAN, SPAN), SPAN)
            right = columns[:, at + 2 : at + 3] * keys_ref[here_rows, :].astype(F32)
            scaled.append(jnp.concatenate([right.astype(BF16)] * 2, axis=0))
        w_mats = [dot(jnp.concatenate(t, axis=1), x) for t, x in zip(inverses, scaled)]
        weighed = []
        for (n, r), w_mat in zip(both, w_mats):
            at = GATES * n + r
            weighed.append((columns[:, at + 4 : at + 5] * w_mat).astype(BF16))
        moved = [
            dot(keys_t_ref[p * part + n], jnp.concatenate(weighed[2 * n : 2 * n + 2], axis=1))
            for n in range(part)
        ]
        for n, r in both:
            lin_ref[r, p * part + n] = moved[n][:, r * DK : (r + 1) * DK].astype(BF16)
        return carry

    lax.fori_loop(0, PASSES, second_pass, 0)


def unwound(t_ref, n, r, x):
    both = jnp.concatenate([t_ref[r, n, 0], t_ref[r, n, 1]], axis=1)
    return dot(both, jnp.concatenate([x, x], axis=0))


def end_of(ends_ref, n, r):
    return ends_ref[GATES * n + r : GATES * n + r + 1, :]


def followed(span_map, state):
    end, moved, add = span_map
    return step(end, moved, state, halves(state)) + add


def composed(maps):
    if len(maps) == 1:
        return maps[0]
    half = len(maps) // 2
    end_a, moved_a, add_a = composed(maps[:half])
    end_b, moved_b, add_b = composed(maps[half:])
    high, low = halves(add_a)
    rights = jnp.concatenate(
        [
            jnp.concatenate([moved_a, high], axis=1),
            jnp.concatenate([jnp.zeros_like(moved_a), low], axis=1),
        ],
        axis=0,
    )
    passed = dot(jnp.concatenate([moved_b, moved_b], axis=1), rights)
    moved = end_b * moved_a.astype(F32) + end_a * moved_b.astype(F32) - passed[:, :DK]
    add = end_b * add_a - passed[:, DK:] + add_b
    return end_a * end_b, moved.astype(BF16), add


def step(end, moved, state, parts):
    both = jnp.concatenate([moved, moved], axis=1)
    return end * state - dot(both, jnp.concatenate(parts, axis=0))


def values_part(recv_ref, cv_ref, keys_t_ref, t_ref, cols_ref, rows, vs):
    sub = lax.axis_index("sub")
    tokens = (recv_ref.shape[1] - GATES) // 4
    spans = t_ref.shape[1]
    taps = value_taps(sub, cv_ref)
    widened(rows, recv_ref, [tokens, 2 * tokens], tokens)
    both = [(n, r) for n in range(spans) for r in range(2)]
    values = []
    for n, r in both:
        lanes = slice(r * DV, (r + 1) * DV)
        v_n = convolved(rows, n * SPAN + 8 - EDGE, SPAN, lanes, taps[r]).astype(BF16)
        vs[r, n * SPAN : (n + 1) * SPAN, :] = v_n
        values.append(v_n)
    solved = [unwound(t_ref, n, r, v) for (n, r), v in zip(both, values)]
    weighed = []
    for (n, r), u_mat in zip(both, solved):
        at = GATES * n + r
        weighed.append((cols_ref[:, at + 4 : at + 5] * u_mat).astype(BF16))
    moved = [
        dot(keys_t_ref[n], jnp.concatenate(weighed[2 * n : 2 * n + 2], axis=1))
        for n in range(spans)
    ]
    return [moved[n][:, r * DV : (r + 1) * DV] for n, r in both]


def opening_kernel(
    recv_ref, cv_ref, keys_t_ref, t_ref, lin_ref, ends_ref, cols_ref, hop_ref, vs_ref, xs_ref, adds_ref, rows
):
    first = lax.axis_index("half") == 0
    peers = recv_ref.shape[0]
    tokens = (recv_ref.shape[1] - GATES) // 4
    spans = t_ref.shape[1]
    edges = []
    for which in (3, 0, 1, 2):
        end = (which + 1) * tokens
        edges.append(recv_ref[peers - 1, end - 16 : end, :].astype(F32)[16 - EDGE :])
    edges.append(jnp.zeros((16 - 4 * EDGE, 128), F32))
    hop_ref[2 * DK :, :] = jnp.concatenate(edges, axis=0).astype(BF16)

    @pl.when(first)
    def _():
        adds = values_part(recv_ref, cv_ref, keys_t_ref, t_ref, cols_ref, rows, vs_ref)
        for n in range(spans):
            for r in range(2):
                adds_ref[r, n] = adds[2 * n + r]
        maps = [
            [(end_of(ends_ref, n, r), lin_ref[r, n], adds[2 * n + r]) for n in range(spans)]
            for r in range(2)
        ]
        states = [m[0][2] for m in maps]
        done = 1
        while done < spans:
            for r in range(2):
                if done > 1:
                    xs_ref[r, done] = jnp.concatenate(halves(states[r]), axis=0)
            later = [composed(m[done : 2 * done]) for m in maps]
            states = [followed(m, x) for m, x in zip(later, states)]
            done *= 2
        for r in range(2):
            hop_ref[r * DK : (r + 1) * DK, :] = states[r].astype(BF16)

    @pl.when(jnp.logical_not(first))
    def _():
        hop_ref[0 : 2 * DK, :] = jnp.zeros((2 * DK, DV), BF16)


def output_kernel(
    recv_ref,
    cq_ref,
    cv_ref,
    keys_ref,
    keys_t_ref,
    t_ref,
    lin_ref,
    ends_ref,
    within_ref,
    cols_ref,
    hop_ref,
    vs_ref,
    xs_ref,
    adds_ref,
    oa_ref,
    om_ref,
    last_ref,
    rows,
    query_rows,
    values,
    inner,
    readers,
    states_ref,
):
    sub = lax.axis_index("sub")
    first = lax.axis_index("half") == 0
    tokens = (recv_ref.shape[1] - GATES) // 4
    spans = t_ref.shape[1]
    both = [(n, r) for n in range(spans) for r in range(2)]
    tap = key_tap(sub, cq_ref)
    widened(query_rows, recv_ref, [3 * tokens], tokens)

    def span_rows(n):
        return slice(n * SPAN, (n + 1) * SPAN)

    def growth(n, r):
        return cols_ref[:, GATES * n + 2 + r : GATES * n + 3 + r]

    def prepare():
        queries = []
        for n in range(spans):
            at = n * SPAN + 8 - EDGE
            q_n = unit(convolved(query_rows, at, SPAN, slice(0, DK), tap), DK**-0.5)
            queries.append(q_n)
            readers[n, 0:SPAN, :] = keys_ref[span_rows(n), :]
            readers[n, SPAN:, :] = q_n
        scores = [dot(queries[n], keys_t_ref[n]) for n in range(spans)]
        for n, r in both:
            weight = within_ref[r, span_rows(n), :].astype(F32)
            inner[r, n] = (weight * scores[n]).astype(BF16)

    def twice(x, axis):
        return jnp.concatenate([x, x], axis=axis)

    @pl.when(first)
    def _():
        prepare()
        stacks, states = [], []
        for n in range(1, spans):
            if n == 1:
                states = [adds_ref[r, 0] for r in range(2)]
                stack = [jnp.concatenate(halves(x), axis=0) for x in states]
            elif n & (n - 1) == 0:
                stack = [xs_ref[r, n] for r in range(2)]
                states = [x[:DK].astype(F32) + x[DK:].astype(F32) for x in stack]
            else:
                states = [
                    followed(
                        (end_of(ends_ref, n - 1, r), lin_ref[r, n - 1], adds_ref[r, n - 1]),
                        states[r],
                    )
                    for r in range(2)
                ]
                stack = [jnp.concatenate(halves(x), axis=0) for x in states]
            stacks.append(jnp.concatenate(stack, axis=1))
        reads = [dot(twice(readers[n], 1), stacks[n - 1]) for n in range(1, spans)]
        rests, seen = [], []
        for n, r in both:
            lanes = slice(r * DV, (r + 1) * DV)
            value = vs_ref[r, span_rows(n), :]
            if n == 0:
                rests.append(value)
                seen.append(None)
            else:
                read = growth(n, r) * reads[n - 1][:SPAN, lanes]
                rests.append((value.astype(F32) - read).astype(BF16))
                seen.append(growth(n, r) * reads[n - 1][SPAN:, lanes])
        fresh = [unwound(t_ref, n, r, x).astype(BF16) for (n, r), x in zip(both, rests)]
        spreads = [dot(inner[r, n], x) for (n, r), x in zip(both, fresh)]
        for (n, r), x, y in zip(both, spreads, seen):
            oa_ref[r, span_rows(n), :] = x if y is None else x + y
        for r in range(2):
            last_ref[r, :, 0:DV] = hop_ref[r * DK : (r + 1) * DK, :].astype(F32)
            last_ref[r, :, DV:] = jnp.zeros((DK, DV), F32)

    @pl.when(jnp.logical_not(first))
    def _():
        adds = values_part(recv_ref, cv_ref, keys_t_ref, t_ref, cols_ref, rows, values)
        zero_half = jnp.zeros((DK, DV), F32)
        identity = jnp.where(iota((DK, DK), 0) == iota((DK, DK), 1), 1.0, 0.0)
        states = [
            jnp.concatenate(
                [adds[r], ends_ref[r : r + 1, :] * identity - lin_ref[r, 0].astype(F32)], axis=1
            )
            for r in range(2)
        ]
        for n in range(1, spans):
            for r in range(2):
                parts = halves(states[r])
                for i in range(2):
                    both_parts = [x[:, i * DV : (i + 1) * DV] for x in parts]
                    states_ref[i, r, n] = jnp.concatenate(both_parts, axis=0)
                add = jnp.concatenate([adds[2 * n + r], zero_half], axis=1)
                end = jnp.concatenate([end_of(ends_ref, n, r)] * 2, axis=1)
                states[r] = step(end, lin_ref[r, n], states[r], parts) + add
        for r in range(2):
            last_ref[r] = states[r]
        prepare()
        reads = [
            dot(
                twice(readers[n], 1),
                jnp.concatenate([states_ref[0, r, n], states_ref[1, r, n]], axis=1),
            )
            if n > 0
            else None
            for n, r in both
        ]
        rests, seen = [], []
        for (n, r), read in zip(both, reads):
            value = values[r, span_rows(n), :].astype(F32)
            if n == 0:
                known = growth(n, r) * readers[n].astype(F32)[:SPAN]
                asked = growth(n, r) * readers[n].astype(F32)[SPAN:]
                rest = jnp.concatenate([value, -known], axis=1)
                seen.append(jnp.concatenate([zero_half, asked], axis=1))
            else:
                rest = jnp.concatenate([value, zero_half], axis=1) - growth(n, r) * read[:SPAN]
                seen.append(growth(n, r) * read[SPAN:])
            rests.append(rest.astype(BF16))
        fresh = [unwound(t_ref, n, r, x).astype(BF16) for (n, r), x in zip(both, rests)]
        spreads = [dot(inner[r, n], x) for (n, r), x in zip(both, fresh)]
        for (n, r), x, y in zip(both, spreads, seen):
            out = x + y
            oa_ref[r, span_rows(n), :] = out[:, :DV]
            om_ref[r, span_rows(n), :] = out[:, DV:].astype(BF16)


def first_tokens(hop_ref, recv_ref, early_ref, cq_ref, ck_ref, cv_ref, rows):
    sub = lax.axis_index("sub")
    tokens = (recv_ref.shape[1] - GATES) // 4
    taps = [key_tap(sub, cq_ref), key_tap(sub, ck_ref)] + value_taps(sub, cv_ref)
    results = []
    edges = hop_ref[2 * DK :, :].astype(F32)
    for g, first in enumerate((3, 0, 1, 2)):
        lanes = slice(g * 128, (g + 1) * 128)
        start = first * tokens
        rows[16 - EDGE : 16, lanes] = edges[EDGE * g : EDGE * (g + 1)]
        rows[16:32, lanes] = recv_ref[0, start : start + 16, :].astype(F32)
        results.append(convolved(rows, 16 - EDGE, 8, lanes, taps[g]))
    q_cols = jnp.transpose(unit(results[0], DK**-0.5).astype(F32))
    k_cols = jnp.transpose(unit(results[1], 1.0).astype(F32))
    gates = early_ref[...]
    line = iota((8, DV), 0)
    finals, outputs = [], []
    for r in range(2):
        values = results[2 + r].astype(BF16).astype(F32)
        entering = hop_ref[r * DK : (r + 1) * DK, :].astype(F32)
        state, out = entering, jnp.zeros((8, DV), F32)
        for t in range(EDGE):
            k_t, q_t = k_cols[:, t : t + 1], q_cols[:, t : t + 1]
            state = jnp.exp(gates[r : r + 1, t : t + 1]) * state
            held = jnp.sum(k_t * state, axis=0, keepdims=True)
            state = state + k_t * (
                gates[2 + r : 3 + r, t : t + 1] * (values[t : t + 1, :] - held)
            )
            out = jnp.where(line == t, jnp.sum(q_t * state, axis=0, keepdims=True), out)
        finals.append(state)
        outputs.append(out)
    return finals, outputs


def finish_kernel(
    hop_ref, recv_ref, early_ref, cq_ref, ck_ref, cv_ref, gain_ref, oa_ref, om_ref, out_ref, rows
):
    peers, tokens = out_ref.shape[0], out_ref.shape[1] // 2
    first = lax.axis_index("half") == 0
    gain = gain_ref[...]
    chunks = 4
    part, peer_part = peers * tokens // chunks, peers // chunks

    def put(c, r, core):
        scale = lax.rsqrt(jnp.mean(core * core, axis=-1, keepdims=True) + EPS)
        normed = (core * scale * gain).astype(BF16)
        here = slice(c * peer_part, (c + 1) * peer_part)
        out_ref[here, r * tokens : (r + 1) * tokens, :] = normed.reshape(peer_part, tokens, DV)

    @pl.when(first)
    def _():
        for c in range(chunks):
            for r in range(2):
                put(c, r, oa_ref[r, c * part : (c + 1) * part, :])

    @pl.when(jnp.logical_not(first))
    def _():
        finals, outputs = first_tokens(hop_ref, recv_ref, early_ref, cq_ref, ck_ref, cv_ref, rows)
        replaced = iota((8, DV), 0) < EDGE
        passed = [dot(om_ref[r], finals[r].astype(BF16)) for r in range(2)]
        for c in range(chunks):
            at = c * part
            for r in range(2):
                core = oa_ref[r, at : at + part, :] + passed[r][at : at + part]
                if c == 0:
                    core = jnp.concatenate(
                        [jnp.where(replaced, outputs[r], core[0:8]), core[8:]], axis=0
                    )
                put(c, r, core)


def advance_kernel(
    hop_ref, recv_ref, early_ref, cq_ref, ck_ref, cv_ref, hop_own, last_ref, next_ref, rows
):
    finals, _ = first_tokens(hop_ref, recv_ref, early_ref, cq_ref, ck_ref, cv_ref, rows)
    first = lax.axis_index("half") == 0
    for r in range(2):
        last = last_ref[r]
        through = mm_parts(halves(last[:, DV:]), halves(finals[r]))
        moved = jnp.where(first, 0.0, through) + last[:, :DV]
        next_ref[r * DK : (r + 1) * DK, :] = moved.astype(BF16)
    next_ref[2 * DK :, :] = hop_own[2 * DK :, :]


def gate_kernel(heads_axis, normed_ref, z_ref, out_ref, made, sems):
    subs, tokens = normed_ref.shape[0] // heads_axis, z_ref.shape[0]
    width = subs * 2 * DV
    copies = []
    for head in range(heads_axis):
        for sub in range(subs):
            for r in range(2):
                at = (2 * (head * subs + sub) + r) * DV
                gate = silu(z_ref[:, at : at + DV].astype(F32))
                here = slice(r * tokens, (r + 1) * tokens)
                value = normed_ref[sub * heads_axis + head, here, :].astype(F32)
                made[:, at : at + DV] = (value * gate).astype(BF16)
        lanes = pl.ds(head * width, width)
        copy = pltpu.make_async_copy(made.at[:, lanes], out_ref.at[:, lanes], sems.at[head])
        copy.start()
        copies.append(copy)
    for copy in copies:
        copy.wait()


VMEM = pl.BlockSpec(memory_space=pltpu.VMEM)
SMEM = pl.BlockSpec(memory_space=pltpu.SMEM)
ANY = pl.BlockSpec(memory_space=pl.ANY)


def near(x):
    return pltpu.with_memory_space_constraint(x, pltpu.VMEM)


def far(x):
    return pltpu.with_memory_space_constraint(x, pltpu.HBM)


def call(kernel, outs, in_specs, scratch=(), out_spec=VMEM, flops=1 << 26, moved=1 << 21):
    return pl.pallas_call(
        kernel,
        out_shape=outs,
        in_specs=in_specs,
        out_specs=jax.tree.map(lambda _: out_spec, outs),
        scratch_shapes=list(scratch),
        compiler_params=pltpu.CompilerParams(vmem_limit_bytes=VMEM_BYTES),
        cost_estimate=pl.CostEstimate(flops=flops, bytes_accessed=moved, transcendentals=0),
    )


def local(
    q_rows,
    k_rows,
    v_rows,
    z_rows,
    a_rows,
    b_rows,
    conv_q,
    conv_k,
    conv_v,
    a_log,
    dt_bias,
    norm_gain,
):
    shards, subs, heads_axis = (lax.axis_size(a) for a in ("half", "sub", "head"))
    peers, tokens = subs * heads_axis, q_rows.shape[0]
    total = peers * tokens
    spans = total // SPAN
    group = ("sub", "head")
    route = [(i, i + 1) for i in range(shards - 1)]
    inputs = [far(x) for x in (q_rows, k_rows, v_rows, a_rows.T, b_rows.T)]
    packed = call(
        functools.partial(pack_kernel, heads_axis),
        pltpu.VMEM((peers, GATES + 4 * tokens, 128), BF16),
        [ANY] * 5,
        [pltpu.VMEM(x.shape, BF16) for x in inputs] + [pltpu.SemaphoreType.DMA((5,))],
        flops=1 << 20,
    )(*inputs)
    blocks = near(lax.all_to_all(packed, group, 0, 0, tiled=True))
    keys, keys_t, inverses, lins, ends, within, cols, early = call(
        keys_kernel,
        (
            pltpu.VMEM((total, DK), BF16),
            pltpu.VMEM((spans, DK, SPAN), BF16),
            pltpu.VMEM((2, spans, 2, SPAN, SPAN), BF16),
            pltpu.VMEM((2, spans, DK, DK), BF16),
            pltpu.VMEM((SPAN, DK), F32),
            pltpu.VMEM((2, total, SPAN), BF16),
            pltpu.VMEM((SPAN, SPAN), F32),
            pltpu.VMEM((8, SPAN), F32),
        ),
        [VMEM, VMEM, SMEM, SMEM],
        [
            pltpu.VMEM((PASSES, 8 + total // PASSES, DK), F32),
            pltpu.VMEM((PASSES, SPAN, SPAN), F32),
            pltpu.VMEM((PASSES, spans // PASSES * GATES, SPAN), F32),
            pltpu.VMEM((PASSES, spans // PASSES * GATES, SPAN), F32),
            pltpu.VMEM((PASSES, 2 * spans // PASSES, 2, SPAN, SPAN), BF16),
            pltpu.VMEM((PASSES, 2 * spans // PASSES, SUB, SPAN), F32),
        ],
        flops=1 << 32,
    )(blocks, conv_k, a_log, dt_bias)
    keys, keys_t, inverses, lins, ends, within, cols, early = (
        near(x) for x in (keys, keys_t, inverses, lins, ends, within, cols, early)
    )
    hop, values, starts, adds = call(
        opening_kernel,
        (
            pltpu.VMEM((2 * DK + 16, 128), BF16),
            pltpu.VMEM((2, total, DV), BF16),
            pltpu.VMEM((2, spans, 2 * DK, DV), BF16),
            pltpu.VMEM((2, spans, DK, DV), F32),
        ),
        [VMEM] * 7,
        [pltpu.VMEM((8 + total, 2 * DV), F32)],
        flops=1 << 32,
    )(blocks, conv_v, keys_t, inverses, lins, ends, cols)
    entering = near(lax.ppermute(hop, "half", route))
    hop, values, starts, adds = (near(x) for x in (hop, values, starts, adds))
    out_a, out_m, last = call(
        output_kernel,
        (
            pltpu.VMEM((2, total, DV), F32),
            pltpu.VMEM((2, total, DV), BF16),
            pltpu.VMEM((2, DK, 2 * DV), F32),
        ),
        [VMEM] * 14,
        [
            pltpu.VMEM((8 + total, 2 * DV), F32),
            pltpu.VMEM((8 + total, DK), F32),
            pltpu.VMEM((2, total, DV), BF16),
            pltpu.VMEM((2, spans, SPAN, SPAN), BF16),
            pltpu.VMEM((spans, 2 * SPAN, DK), BF16),
            pltpu.VMEM((2, 2, spans, 2 * DK, DV), BF16),
        ],
        flops=1 << 32,
    )(
        blocks,
        conv_q,
        conv_v,
        keys,
        keys_t,
        inverses,
        lins,
        ends,
        within,
        cols,
        hop,
        values,
        starts,
        adds,
    )
    for _ in range(shards - 2):
        moved = call(
            advance_kernel,
            pltpu.VMEM(hop.shape, BF16),
            [VMEM] * 8,
            [pltpu.VMEM((32, 512), F32)],
        )(entering, blocks, early, conv_q, conv_k, conv_v, hop, near(last))
        entering = near(lax.ppermute(moved, "half", route))
    normed = call(
        finish_kernel,
        pltpu.VMEM((peers, 2 * tokens, DV), BF16),
        [VMEM] * 9,
        [pltpu.VMEM((32, 512), F32)],
    )(
        entering,
        blocks,
        early,
        conv_q,
        conv_k,
        conv_v,
        norm_gain.reshape(1, DV),
        near(out_a),
        near(out_m),
    )
    returned = near(lax.all_to_all(normed, group, 0, 0, tiled=True))
    return call(
        functools.partial(gate_kernel, heads_axis),
        jax.ShapeDtypeStruct(z_rows.shape, BF16),
        [VMEM] * 2,
        [pltpu.VMEM(z_rows.shape, BF16), pltpu.SemaphoreType.DMA((heads_axis,))],
        ANY,
    )(returned, z_rows)


def solution(mesh):
    heads_axis = mesh.shape["head"]
    subs = KH // heads_axis
    regrouped = Mesh(
        mesh.devices.reshape(mesh.shape["ctx"] // subs, subs, heads_axis), ("half", "sub", "head")
    )
    row = P(("half", "sub", "head"), None)
    placed = (row,) * 6 + (P(None, "head"),) * 3 + (P("head"),) * 2 + (P(),)
    return jax.shard_map(local, mesh=regrouped, in_specs=placed, out_specs=row, check_vma=False)
```

```python
import functools

import jax
import jax.numpy as jnp
from jax import lax
from jax.experimental import pallas as pl
from jax.experimental.pallas import tpu as pltpu
from jax.sharding import Mesh, PartitionSpec as P

DK = 128
DV = 128
CONV = 4
KH = 16
SUB = 16
SPAN = 128
EDGE = CONV - 1
EPS = 1e-06
F32 = jnp.float32
BF16 = jnp.bfloat16
VMEM_BYTES = 24 * 1024 * 1024
GATES = 8


def dot(a, b, dims=((1,), (0,))):
    return lax.dot_general(a, b, (dims, ((), ())), preferred_element_type=F32)


def halves(x):
    high = x.astype(BF16)
    return high, (x - high.astype(F32)).astype(BF16)


def mm_parts(a, b):
    both = jnp.concatenate(a, axis=1)
    return dot(both, jnp.concatenate([b[0], b[0]], axis=0)) + dot(a[0], b[1])


def silu(x):
    half = 0.5 * x
    return half + half * jnp.tanh(half)


def unit(y, factor):
    scale = lax.rsqrt(jnp.sum(y * y, axis=-1, keepdims=True) + EPS)
    return (y * scale * factor).astype(BF16)


def iota(shape, dim):
    return lax.broadcasted_iota(jnp.int32, shape, dim)


def block_of(x, size):
    return lax.shift_right_logical(x, jnp.full(x.shape, size.bit_length() - 1, jnp.int32))


def place_in(x, size):
    return x & (size - 1)


def pack_kernel(
    heads_axis, q_in, k_in, v_in, at_in, bt_in, out_ref, q_ref, k_ref, v_ref, at_ref, bt_ref, sems
):
    peers, tokens = out_ref.shape[0], q_ref.shape[0]
    pairs = ((at_in, at_ref), (bt_in, bt_ref), (k_in, k_ref), (v_in, v_ref), (q_in, q_ref))
    copies = [pltpu.make_async_copy(a, b, sems.at[i]) for i, (a, b) in enumerate(pairs)]
    for copy in copies:
        copy.start()
    subs = peers // heads_axis
    key_heads = [(dest % heads_axis) * subs + dest // heads_axis for dest in range(peers)]
    for copy in copies[:2]:
        copy.wait()
    value_heads = at_ref.shape[0]
    row, entry = iota((peers * GATES, value_heads), 0), iota((peers * GATES, value_heads), 1)
    dest, which = block_of(row, GATES), place_in(row, GATES)
    first = 2 * (place_in(dest, heads_axis) * subs + block_of(dest, heads_axis))
    pick_a = jnp.where((which < 2) & (entry == first + which), 1.0, 0.0).astype(BF16)
    pick_b = jnp.where(
        (which >= 2) & (which < 4) & (entry == first + which - 2), 1.0, 0.0
    ).astype(BF16)
    picked = (dot(pick_a, at_ref[...]) + dot(pick_b, bt_ref[...])).astype(BF16)
    lane_shift = tokens * lax.rem(lax.axis_index("head"), SPAN // tokens)
    place = jnp.where(
        iota((tokens, SPAN), 1) == iota((tokens, SPAN), 0) + lane_shift, 1.0, 0.0
    ).astype(BF16)
    gates = dot(picked, place).astype(BF16)
    for dest in range(peers):
        out_ref[dest, 4 * tokens :, :] = gates[GATES * dest : GATES * (dest + 1), :]

    def laid(ref, lane, start):
        for dest, key_head in enumerate(key_heads):
            at = lane(key_head) * 128
            out_ref[dest, start * tokens : (start + 1) * tokens, :] = ref[
                :, at : at + 128
            ]

    copies[2].wait()
    laid(k_ref, lambda key_head: key_head, 0)
    copies[3].wait()
    laid(v_ref, lambda key_head: 2 * key_head, 1)
    laid(v_ref, lambda key_head: 2 * key_head + 1, 2)
    copies[4].wait()
    laid(q_ref, lambda key_head: key_head, 3)


def compacted(system):
    size = system.shape[0]
    diagonal = block_of(iota((size, size), 0), SUB) == block_of(iota((size, size), 1), SUB)
    return jnp.sum(jnp.where(diagonal, system, 0.0).reshape(size // SUB, SUB, size), axis=0)


def substituted(compact):
    count, _, size = compact.shape
    flat = compact.reshape(count * SUB, size)
    lane, line = iota(flat.shape, 1), iota(flat.shape, 0)
    solved = jnp.where(place_in(lane ^ line, SUB) == 0, 1.0, 0.0).reshape(count, SUB, size)
    for m in range(SUB - 1):
        source = (lane & ~(SUB - 1)) | m
        spread = jnp.take_along_axis(flat, source, axis=1, mode="promise_in_bounds")
        solved = solved + spread.reshape(count, SUB, size) * solved[:, m : m + 1, :]
    return solved


def inverted(systems, small):
    size = systems[0][0].shape[0]
    row, col = iota((size, size), 0), iota((size, size), 1)
    placed = jnp.where(block_of(row, SUB) == block_of(col, SUB), 1.0, 0.0).astype(BF16)
    parts = [
        tuple(jnp.concatenate([x] * (size // SUB), axis=0) * placed for x in halves(block))
        for block in small
    ]
    blank = jnp.zeros((size, size), BF16)
    width = SUB
    while width < size:
        odd = [(j, j + width) for j in range(width, size, 2 * width)]

        def rows_of(x):
            return jnp.concatenate([x[lo:hi] for lo, hi in odd], axis=0)

        def woven(even, x):
            pieces = []
            for j, (lo, hi) in enumerate(odd):
                pieces += [even[lo - width : lo], x[j * width : (j + 1) * width]]
            return jnp.concatenate(pieces, axis=0)

        below = rows_of(block_of(row ^ col, 2 * width)) + rows_of(col & width) == 0
        identity = rows_of(jnp.where(row == col, 1.0, 0.0))
        firsts = [
            mm_parts((rows_of(n[0]), rows_of(n[1])), t) for n, t in zip(systems, parts)
        ]
        rights = [
            tuple(woven(blank, x) for x in halves(jnp.where(below, first, identity)))
            for first in firsts
        ]
        odds = [(rows_of(t[0]), rows_of(t[1])) for t in parts]
        grown = [halves(mm_parts(o, right)) for o, right in zip(odds, rights)]
        parts = [tuple(woven(t[i], g[i]) for i in range(2)) for t, g in zip(parts, grown)]
        width *= 2
    return parts


def gate_values(gates, sub, alog_ref, dt_ref):
    second = place_in(iota(gates.shape, 0), GATES) == 1
    a_log = jnp.where(second, alog_ref[2 * sub + 1], alog_ref[2 * sub])
    dt_bias = jnp.where(second, dt_ref[2 * sub + 1], dt_ref[2 * sub])
    shifted = gates + dt_bias
    soft = jnp.maximum(shifted, 0.0) + jnp.log1p(jnp.exp(-jnp.abs(shifted)))
    return -jnp.exp(a_log) * soft, 1.0 / (1.0 + jnp.exp(-gates))


def convolved(rows, at, count, lanes, tap):
    summed = tap[0:1] * rows[at : at + count, lanes]
    for j in range(1, CONV):
        summed = summed + tap[j : j + 1] * rows[at + j : at + j + count, lanes]
    return silu(summed)


def key_tap(sub, tap_ref):
    return tap_ref[:, pl.ds(pl.multiple_of(sub * DK, 128), DK)]


def value_taps(sub, cv_ref):
    lane = pl.multiple_of(sub * 2 * DV, 128)
    return [cv_ref[:, pl.ds(pl.multiple_of(lane + r * DV, 128), DV)] for r in range(2)]


def widened(rows, recv_ref, starts, tokens):
    rows[0:8, :] = jnp.zeros((8, rows.shape[1]), F32)
    for s in range(recv_ref.shape[0]):
        for g, start in enumerate(starts):
            rows[8 + s * tokens : 8 + (s + 1) * tokens, g * 128 : (g + 1) * 128] = recv_ref[
                s, start : start + tokens, :
            ].astype(F32)


def systems_kernel(
    recv_ref,
    ck_ref,
    alog_ref,
    dt_ref,
    keys_ref,
    keys_t_ref,
    systems_ref,
    small_ref,
    ends_ref,
    within_ref,
    cols_ref,
    early_ref,
    rows,
):
    sub = lax.axis_index("sub")
    later = lax.axis_index("half") > 0
    peers = recv_ref.shape[0]
    tokens = (recv_ref.shape[1] - GATES) // 4
    spans = peers * tokens // SPAN
    tap = key_tap(sub, ck_ref)
    widened(rows, recv_ref, [0], tokens)
    stacked = [
        sum(recv_ref[s, 4 * tokens :, :].astype(F32) for s in range(n, n + SPAN // tokens))
        for n in range(0, peers, SPAN // tokens)
    ]
    stacked.append(jnp.zeros((SPAN - spans * GATES, SPAN), F32))
    gates = jnp.concatenate(stacked, axis=0)
    decay, rate = gate_values(gates, sub, alog_ref, dt_ref)
    early_ref[...] = jnp.where(iota((8, SPAN), 0) < 2, decay[0:8], rate[0:8])
    skipped = later & (iota(gates.shape, 0) < GATES) & (iota(gates.shape, 1) < EDGE)
    decay = jnp.where(skipped, 0.0, decay)
    rate = jnp.where(skipped, 0.0, rate)
    lane_r, lane_c = iota((SPAN, SPAN), 0), iota((SPAN, SPAN), 1)
    upto = jnp.where(lane_r <= lane_c, 1.0, 0.0).astype(BF16)
    d_high, _ = halves(decay)
    d_mid, d_low = halves(decay - d_high.astype(F32))
    cum = dot(d_high, upto) + (dot(d_mid, upto) + dot(d_low, upto))
    growth = jnp.exp(cum)
    here = pltpu.roll(rate, rate.shape[0] - 2, 0)
    rest = jnp.exp(cum[:, SPAN - 1 :] - cum) * here
    which = place_in(iota(gates.shape, 0), GATES)
    mixed = jnp.where(which < 2, cum, pltpu.roll(growth, 2, 0))
    columns = jnp.transpose(jnp.where(which < 4, mixed, pltpu.roll(rest, 4, 0)))
    cols_ref[...] = columns
    lower = lane_r >= lane_c
    strict = lane_r > lane_c
    both = [(n, r) for n in range(spans) for r in range(2)]
    keys = []
    for n in range(spans):
        k_n = unit(convolved(rows, n * SPAN + 8 - EDGE, SPAN, slice(0, DK), tap), 1.0)
        keys_ref[n * SPAN : (n + 1) * SPAN, :] = k_n
        keys.append(k_n)
    keys_t = []
    for n in range(spans):
        kt_n = jnp.transpose(keys[n].astype(F32)).astype(BF16)
        keys_t_ref[n] = kt_n
        keys_t.append(kt_n)
    grams = [dot(keys[n], keys_t[n]) for n in range(spans)]
    for n, r in both:
        at = GATES * n + r
        gap = columns[:, at : at + 1] - cum[at : at + 1, :]
        within = jnp.exp(jnp.where(lower, gap, 0.0)) * here[at : at + 1, :]
        within_ref[r, n * SPAN : (n + 1) * SPAN, :] = jnp.where(lower, within, 0.0).astype(BF16)
        system = jnp.where(strict, within * -grams[n], 0.0)
        systems_ref[r, n, 0], systems_ref[r, n, 1] = halves(system)
        small_ref[r, n] = compacted(system)
    ends_ref[...] = jnp.broadcast_to(growth[:, SPAN - 1 :], ends_ref.shape)


def inverse_kernel(
    on_first, hop_ref, keys_ref, keys_t_ref, systems_ref, small_ref, cols_ref, t_ref, lin_ref
):
    del hop_ref
    spans = keys_t_ref.shape[0]
    both = [(n, r) for n in range(spans) for r in range(2)]

    @pl.when((lax.axis_index("half") == 0) == on_first)
    def _():
        compact = jnp.concatenate([small_ref[r, n] for n, r in both], axis=0)
        small = substituted(compact.reshape(len(both), SUB, SPAN))
        systems = [(systems_ref[r, n, 0], systems_ref[r, n, 1]) for n, r in both]
        inverses = inverted(systems, [small[i] for i in range(len(both))])
        scaled = []
        for i, (n, r) in enumerate(both):
            t_ref[r, n, 0], t_ref[r, n, 1] = inverses[i]
            at = GATES * n + r
            key = keys_ref[n * SPAN : (n + 1) * SPAN, :].astype(F32)
            right = (cols_ref[:, at + 2 : at + 3] * key).astype(BF16)
            scaled.append(jnp.concatenate([right, right], axis=0))
        w_mats = [dot(jnp.concatenate(t, axis=1), x) for t, x in zip(inverses, scaled)]
        weighed = []
        for (n, r), w_mat in zip(both, w_mats):
            at = GATES * n + r
            weighed.append((cols_ref[:, at + 4 : at + 5] * w_mat).astype(BF16))
        moved = [
            dot(keys_t_ref[n], jnp.concatenate(weighed[2 * n : 2 * n + 2], axis=1))
            for n in range(spans)
        ]
        for n, r in both:
            lin_ref[r, n] = moved[n][:, r * DK : (r + 1) * DK].astype(BF16)


def unwound(t_ref, n, r, x):
    both = jnp.concatenate([t_ref[r, n, 0], t_ref[r, n, 1]], axis=1)
    return dot(both, jnp.concatenate([x, x], axis=0))


def end_of(ends_ref, n, r):
    return ends_ref[GATES * n + r : GATES * n + r + 1, :]


def followed(span_map, state):
    end, moved, add = span_map
    return step(end, moved, state, halves(state)) + add


def composed(maps):
    if len(maps) == 1:
        return maps[0]
    half = len(maps) // 2
    end_a, moved_a, add_a = composed(maps[:half])
    end_b, moved_b, add_b = composed(maps[half:])
    high, low = halves(add_a)
    rights = jnp.concatenate(
        [
            jnp.concatenate([moved_a, high], axis=1),
            jnp.concatenate([jnp.zeros_like(moved_a), low], axis=1),
        ],
        axis=0,
    )
    passed = dot(jnp.concatenate([moved_b, moved_b], axis=1), rights)
    moved = end_b * moved_a.astype(F32) + end_a * moved_b.astype(F32) - passed[:, :DK]
    add = end_b * add_a - passed[:, DK:] + add_b
    return end_a * end_b, moved.astype(BF16), add


def step(end, moved, state, parts):
    both = jnp.concatenate([moved, moved], axis=1)
    return end * state - dot(both, jnp.concatenate(parts, axis=0))


def values_part(recv_ref, cv_ref, keys_t_ref, t_ref, cols_ref, rows, vs):
    sub = lax.axis_index("sub")
    tokens = (recv_ref.shape[1] - GATES) // 4
    spans = t_ref.shape[1]
    taps = value_taps(sub, cv_ref)
    widened(rows, recv_ref, [tokens, 2 * tokens], tokens)
    both = [(n, r) for n in range(spans) for r in range(2)]
    values = []
    for n, r in both:
        lanes = slice(r * DV, (r + 1) * DV)
        v_n = convolved(rows, n * SPAN + 8 - EDGE, SPAN, lanes, taps[r]).astype(BF16)
        vs[r, n * SPAN : (n + 1) * SPAN, :] = v_n
        values.append(v_n)
    solved = [unwound(t_ref, n, r, v) for (n, r), v in zip(both, values)]
    weighed = []
    for (n, r), u_mat in zip(both, solved):
        at = GATES * n + r
        weighed.append((cols_ref[:, at + 4 : at + 5] * u_mat).astype(BF16))
    moved = [
        dot(keys_t_ref[n], jnp.concatenate(weighed[2 * n : 2 * n + 2], axis=1))
        for n in range(spans)
    ]
    return [moved[n][:, r * DV : (r + 1) * DV] for n, r in both]


def opening_kernel(
    recv_ref, cv_ref, keys_t_ref, t_ref, lin_ref, ends_ref, cols_ref, hop_ref, vs_ref, xs_ref, adds_ref, rows
):
    first = lax.axis_index("half") == 0
    peers = recv_ref.shape[0]
    tokens = (recv_ref.shape[1] - GATES) // 4
    spans = t_ref.shape[1]
    edges = []
    for which in (3, 0, 1, 2):
        end = (which + 1) * tokens
        edges.append(recv_ref[peers - 1, end - 16 : end, :].astype(F32)[16 - EDGE :])
    edges.append(jnp.zeros((16 - 4 * EDGE, 128), F32))
    hop_ref[2 * DK :, :] = jnp.concatenate(edges, axis=0).astype(BF16)

    @pl.when(first)
    def _():
        adds = values_part(recv_ref, cv_ref, keys_t_ref, t_ref, cols_ref, rows, vs_ref)
        for n in range(spans):
            for r in range(2):
                adds_ref[r, n] = adds[2 * n + r]
        maps = [
            [(end_of(ends_ref, n, r), lin_ref[r, n], adds[2 * n + r]) for n in range(spans)]
            for r in range(2)
        ]
        states = [m[0][2] for m in maps]
        done = 1
        while done < spans:
            for r in range(2):
                if done > 1:
                    xs_ref[r, done] = jnp.concatenate(halves(states[r]), axis=0)
            later = [composed(m[done : 2 * done]) for m in maps]
            states = [followed(m, x) for m, x in zip(later, states)]
            done *= 2
        for r in range(2):
            hop_ref[r * DK : (r + 1) * DK, :] = states[r].astype(BF16)

    @pl.when(jnp.logical_not(first))
    def _():
        hop_ref[0 : 2 * DK, :] = jnp.zeros((2 * DK, DV), BF16)


def states_kernel(
    recv_ref,
    cv_ref,
    keys_t_ref,
    t_ref,
    lin_ref,
    ends_ref,
    cols_ref,
    values_ref,
    states_ref,
    last_ref,
    rows,
):
    @pl.when(lax.axis_index("half") > 0)
    def _():
        spans = t_ref.shape[1]
        adds = values_part(recv_ref, cv_ref, keys_t_ref, t_ref, cols_ref, rows, values_ref)
        zero_half = jnp.zeros((DK, DV), F32)
        identity = jnp.where(iota((DK, DK), 0) == iota((DK, DK), 1), 1.0, 0.0)
        states = [
            jnp.concatenate(
                [adds[r], ends_ref[r : r + 1, :] * identity - lin_ref[r, 0].astype(F32)], axis=1
            )
            for r in range(2)
        ]
        for n in range(1, spans):
            for r in range(2):
                parts = halves(states[r])
                for i in range(2):
                    both_parts = [x[:, i * DV : (i + 1) * DV] for x in parts]
                    states_ref[i, r, n] = jnp.concatenate(both_parts, axis=0)
                add = jnp.concatenate([adds[2 * n + r], zero_half], axis=1)
                end = jnp.concatenate([end_of(ends_ref, n, r)] * 2, axis=1)
                states[r] = step(end, lin_ref[r, n], states[r], parts) + add
        for r in range(2):
            last_ref[r] = states[r]


def span_rows(n):
    return slice(n * SPAN, (n + 1) * SPAN)


def twice(x, axis):
    return jnp.concatenate([x, x], axis=axis)


def asked(recv_ref, cq_ref, keys_ref, keys_t_ref, within_ref, query_rows):
    tokens = (recv_ref.shape[1] - GATES) // 4
    spans = keys_t_ref.shape[0]
    tap = key_tap(lax.axis_index("sub"), cq_ref)
    widened(query_rows, recv_ref, [3 * tokens], tokens)
    queries = [
        unit(convolved(query_rows, n * SPAN + 8 - EDGE, SPAN, slice(0, DK), tap), DK**-0.5)
        for n in range(spans)
    ]
    readers = [
        jnp.concatenate([keys_ref[span_rows(n), :], queries[n]], axis=0) for n in range(spans)
    ]
    scores = [dot(queries[n], keys_t_ref[n]) for n in range(spans)]
    inner = [
        (within_ref[r, span_rows(n), :].astype(F32) * scores[n]).astype(BF16)
        for n in range(spans)
        for r in range(2)
    ]
    return readers, inner


def first_outputs_kernel(
    recv_ref,
    cq_ref,
    keys_ref,
    keys_t_ref,
    t_ref,
    lin_ref,
    ends_ref,
    within_ref,
    cols_ref,
    values_ref,
    xs_ref,
    adds_ref,
    oa_ref,
    query_rows,
):
    @pl.when(lax.axis_index("half") == 0)
    def _():
        spans = t_ref.shape[1]
        both = [(n, r) for n in range(spans) for r in range(2)]
        readers, inner = asked(recv_ref, cq_ref, keys_ref, keys_t_ref, within_ref, query_rows)
        stacks, states = [], []
        for n in range(1, spans):
            if n == 1:
                states = [adds_ref[r, 0] for r in range(2)]
                stack = [jnp.concatenate(halves(x), axis=0) for x in states]
            elif n & (n - 1) == 0:
                stack = [xs_ref[r, n] for r in range(2)]
                states = [x[:DK].astype(F32) + x[DK:].astype(F32) for x in stack]
            else:
                states = [
                    followed(
                        (end_of(ends_ref, n - 1, r), lin_ref[r, n - 1], adds_ref[r, n - 1]),
                        states[r],
                    )
                    for r in range(2)
                ]
                stack = [jnp.concatenate(halves(x), axis=0) for x in states]
            stacks.append(jnp.concatenate(stack, axis=1))
        reads = [dot(twice(readers[n], 1), stacks[n - 1]) for n in range(1, spans)]
        rests, seen = [], []
        for n, r in both:
            lanes = slice(r * DV, (r + 1) * DV)
            value = values_ref[r, span_rows(n), :]
            if n == 0:
                rests.append(value)
                seen.append(None)
            else:
                growth = cols_ref[:, GATES * n + 2 + r : GATES * n + 3 + r]
                read = growth * reads[n - 1][:SPAN, lanes]
                rests.append((value.astype(F32) - read).astype(BF16))
                seen.append(growth * reads[n - 1][SPAN:, lanes])
        fresh = [unwound(t_ref, n, r, x).astype(BF16) for (n, r), x in zip(both, rests)]
        spreads = [dot(w, x) for w, x in zip(inner, fresh)]
        for (n, r), x, y in zip(both, spreads, seen):
            oa_ref[r, span_rows(n), :] = x if y is None else x + y


def later_outputs_kernel(
    recv_ref,
    cq_ref,
    keys_ref,
    keys_t_ref,
    t_ref,
    within_ref,
    cols_ref,
    values_ref,
    states_ref,
    oa_ref,
    om_ref,
    query_rows,
):
    @pl.when(lax.axis_index("half") > 0)
    def _():
        spans = t_ref.shape[1]
        both = [(n, r) for n in range(spans) for r in range(2)]
        readers, inner = asked(recv_ref, cq_ref, keys_ref, keys_t_ref, within_ref, query_rows)
        zero_half = jnp.zeros((SPAN, DV), F32)
        reads = [
            dot(
                twice(readers[n], 1),
                jnp.concatenate([states_ref[0, r, n], states_ref[1, r, n]], axis=1),
            )
            if n > 0
            else None
            for n, r in both
        ]
        rests, seen = [], []
        for (n, r), read in zip(both, reads):
            value = values_ref[r, span_rows(n), :].astype(F32)
            growth = cols_ref[:, GATES * n + 2 + r : GATES * n + 3 + r]
            if n == 0:
                reader = readers[n].astype(F32)
                rest = jnp.concatenate([value, -(growth * reader[:SPAN])], axis=1)
                seen.append(jnp.concatenate([zero_half, growth * reader[SPAN:]], axis=1))
            else:
                rest = jnp.concatenate([value, zero_half], axis=1) - growth * read[:SPAN]
                seen.append(growth * read[SPAN:])
            rests.append(rest.astype(BF16))
        fresh = [unwound(t_ref, n, r, x).astype(BF16) for (n, r), x in zip(both, rests)]
        spreads = [dot(w, x) for w, x in zip(inner, fresh)]
        for (n, r), x, y in zip(both, spreads, seen):
            out = x + y
            oa_ref[r, span_rows(n), :] = out[:, :DV]
            om_ref[r, span_rows(n), :] = out[:, DV:].astype(BF16)


def first_tokens(hop_ref, recv_ref, early_ref, cq_ref, ck_ref, cv_ref, rows):
    sub = lax.axis_index("sub")
    tokens = (recv_ref.shape[1] - GATES) // 4
    taps = [key_tap(sub, cq_ref), key_tap(sub, ck_ref)] + value_taps(sub, cv_ref)
    results = []
    edges = hop_ref[2 * DK :, :].astype(F32)
    for g, first in enumerate((3, 0, 1, 2)):
        lanes = slice(g * 128, (g + 1) * 128)
        start = first * tokens
        rows[16 - EDGE : 16, lanes] = edges[EDGE * g : EDGE * (g + 1)]
        rows[16:32, lanes] = recv_ref[0, start : start + 16, :].astype(F32)
        results.append(convolved(rows, 16 - EDGE, 8, lanes, taps[g]))
    q_cols = jnp.transpose(unit(results[0], DK**-0.5).astype(F32))
    k_cols = jnp.transpose(unit(results[1], 1.0).astype(F32))
    gates = early_ref[...]
    line = iota((8, DV), 0)
    finals, outputs = [], []
    for r in range(2):
        values = results[2 + r].astype(BF16).astype(F32)
        entering = hop_ref[r * DK : (r + 1) * DK, :].astype(F32)
        state, out = entering, jnp.zeros((8, DV), F32)
        for t in range(EDGE):
            k_t, q_t = k_cols[:, t : t + 1], q_cols[:, t : t + 1]
            state = jnp.exp(gates[r : r + 1, t : t + 1]) * state
            held = jnp.sum(k_t * state, axis=0, keepdims=True)
            state = state + k_t * (
                gates[2 + r : 3 + r, t : t + 1] * (values[t : t + 1, :] - held)
            )
            out = jnp.where(line == t, jnp.sum(q_t * state, axis=0, keepdims=True), out)
        finals.append(state)
        outputs.append(out)
    return finals, outputs


def finish_kernel(
    hop_ref,
    recv_ref,
    early_ref,
    cq_ref,
    ck_ref,
    cv_ref,
    gain_ref,
    first_oa,
    oa_ref,
    om_ref,
    out_ref,
    rows,
):
    peers, tokens = out_ref.shape[0], out_ref.shape[1] // 2
    first = lax.axis_index("half") == 0
    gain = gain_ref[...]
    chunks = 4
    part, peer_part = peers * tokens // chunks, peers // chunks

    def put(c, r, core):
        scale = lax.rsqrt(jnp.mean(core * core, axis=-1, keepdims=True) + EPS)
        normed = (core * scale * gain).astype(BF16)
        here = slice(c * peer_part, (c + 1) * peer_part)
        out_ref[here, r * tokens : (r + 1) * tokens, :] = normed.reshape(peer_part, tokens, DV)

    @pl.when(first)
    def _():
        for c in range(chunks):
            for r in range(2):
                put(c, r, first_oa[r, c * part : (c + 1) * part, :])

    @pl.when(jnp.logical_not(first))
    def _():
        finals, outputs = first_tokens(hop_ref, recv_ref, early_ref, cq_ref, ck_ref, cv_ref, rows)
        replaced = iota((8, DV), 0) < EDGE
        passed = [dot(om_ref[r], finals[r].astype(BF16)) for r in range(2)]
        for c in range(chunks):
            at = c * part
            for r in range(2):
                core = oa_ref[r, at : at + part, :] + passed[r][at : at + part]
                if c == 0:
                    core = jnp.concatenate(
                        [jnp.where(replaced, outputs[r], core[0:8]), core[8:]], axis=0
                    )
                put(c, r, core)


def advance_kernel(
    hop_ref, recv_ref, early_ref, cq_ref, ck_ref, cv_ref, hop_own, last_ref, next_ref, rows
):
    finals, _ = first_tokens(hop_ref, recv_ref, early_ref, cq_ref, ck_ref, cv_ref, rows)
    first = lax.axis_index("half") == 0
    for r in range(2):
        last = last_ref[r]
        through = mm_parts(halves(last[:, DV:]), halves(finals[r]))
        own = hop_own[r * DK : (r + 1) * DK, :].astype(F32)
        moved = jnp.where(first, own, through + last[:, :DV])
        next_ref[r * DK : (r + 1) * DK, :] = moved.astype(BF16)
    next_ref[2 * DK :, :] = hop_own[2 * DK :, :]


def gate_kernel(heads_axis, normed_ref, z_ref, out_ref, made, sems):
    subs, tokens = normed_ref.shape[0] // heads_axis, z_ref.shape[0]
    width = subs * 2 * DV
    copies = []
    for head in range(heads_axis):
        for sub in range(subs):
            for r in range(2):
                at = (2 * (head * subs + sub) + r) * DV
                gate = silu(z_ref[:, at : at + DV].astype(F32))
                here = slice(r * tokens, (r + 1) * tokens)
                value = normed_ref[sub * heads_axis + head, here, :].astype(F32)
                made[:, at : at + DV] = (value * gate).astype(BF16)
        lanes = pl.ds(head * width, width)
        copy = pltpu.make_async_copy(made.at[:, lanes], out_ref.at[:, lanes], sems.at[head])
        copy.start()
        copies.append(copy)
    for copy in copies:
        copy.wait()


VMEM = pl.BlockSpec(memory_space=pltpu.VMEM)
SMEM = pl.BlockSpec(memory_space=pltpu.SMEM)
ANY = pl.BlockSpec(memory_space=pl.ANY)


def near(x):
    return pltpu.with_memory_space_constraint(x, pltpu.VMEM)


def far(x):
    return pltpu.with_memory_space_constraint(x, pltpu.HBM)


def call(kernel, outs, in_specs, scratch=(), out_spec=VMEM, flops=1 << 26, moved=1 << 21):
    return pl.pallas_call(
        kernel,
        out_shape=outs,
        in_specs=in_specs,
        out_specs=jax.tree.map(lambda _: out_spec, outs),
        scratch_shapes=list(scratch),
        compiler_params=pltpu.CompilerParams(vmem_limit_bytes=VMEM_BYTES),
        cost_estimate=pl.CostEstimate(flops=flops, bytes_accessed=moved, transcendentals=0),
    )


def local(
    q_rows,
    k_rows,
    v_rows,
    z_rows,
    a_rows,
    b_rows,
    conv_q,
    conv_k,
    conv_v,
    a_log,
    dt_bias,
    norm_gain,
):
    shards, subs, heads_axis = (lax.axis_size(a) for a in ("half", "sub", "head"))
    peers, tokens = subs * heads_axis, q_rows.shape[0]
    total = peers * tokens
    spans = total // SPAN
    group = ("sub", "head")
    route = [(i, i + 1) for i in range(shards - 1)]
    inputs = [far(x) for x in (q_rows, k_rows, v_rows, a_rows.T, b_rows.T)]
    packed = call(
        functools.partial(pack_kernel, heads_axis),
        pltpu.VMEM((peers, GATES + 4 * tokens, 128), BF16),
        [ANY] * 5,
        [pltpu.VMEM(x.shape, BF16) for x in inputs] + [pltpu.SemaphoreType.DMA((5,))],
        flops=1 << 20,
    )(*inputs)
    blocks = near(lax.all_to_all(packed, group, 0, 0, tiled=True))
    made = call(
        systems_kernel,
        (
            pltpu.VMEM((total, DK), BF16),
            pltpu.VMEM((spans, DK, SPAN), BF16),
            pltpu.VMEM((2, spans, 2, SPAN, SPAN), BF16),
            pltpu.VMEM((2, spans, SUB, SPAN), F32),
            pltpu.VMEM((SPAN, DK), F32),
            pltpu.VMEM((2, total, SPAN), BF16),
            pltpu.VMEM((SPAN, SPAN), F32),
            pltpu.VMEM((8, SPAN), F32),
        ),
        [VMEM, VMEM, SMEM, SMEM],
        [pltpu.VMEM((8 + total, DK), F32)],
        flops=1 << 32,
    )(blocks, conv_k, a_log, dt_bias)
    keys, keys_t, systems, small, ends, within, cols, early = (near(x) for x in made)
    map_shapes = (
        pltpu.VMEM((2, spans, 2, SPAN, SPAN), BF16),
        pltpu.VMEM((2, spans, DK, DK), BF16),
    )

    def inverses_of(on_first, after):
        solved = call(
            functools.partial(inverse_kernel, on_first), map_shapes, [VMEM] * 6, flops=1 << 32
        )(after, keys, keys_t, systems, small, cols)
        return [near(x) for x in solved]

    inverses, lins = inverses_of(True, early)
    hop, values, starts, adds = call(
        opening_kernel,
        (
            pltpu.VMEM((2 * DK + 16, 128), BF16),
            pltpu.VMEM((2, total, DV), BF16),
            pltpu.VMEM((2, spans, 2 * DK, DV), BF16),
            pltpu.VMEM((2, spans, DK, DV), F32),
        ),
        [VMEM] * 7,
        [pltpu.VMEM((8 + total, 2 * DV), F32)],
        flops=1 << 32,
    )(blocks, conv_v, keys_t, inverses, lins, ends, cols)
    entering = near(lax.ppermute(hop, "half", route))
    hop, values, starts, adds = (near(x) for x in (hop, values, starts, adds))
    first_out = call(
        first_outputs_kernel,
        pltpu.VMEM((2, total, DV), F32),
        [VMEM] * 12,
        [pltpu.VMEM((8 + total, DK), F32)],
        flops=1 << 32,
    )(
        blocks,
        conv_q,
        keys,
        keys_t,
        inverses,
        lins,
        ends,
        within,
        cols,
        values,
        starts,
        adds,
    )
    later_inverses, later_lins = inverses_of(False, hop)
    later_values, states, last = call(
        states_kernel,
        (
            pltpu.VMEM((2, total, DV), BF16),
            pltpu.VMEM((2, 2, spans, 2 * DK, DV), BF16),
            pltpu.VMEM((2, DK, 2 * DV), F32),
        ),
        [VMEM] * 7,
        [pltpu.VMEM((8 + total, 2 * DV), F32)],
        flops=1 << 32,
    )(blocks, conv_v, keys_t, later_inverses, later_lins, ends, cols)
    out_a, out_m = call(
        later_outputs_kernel,
        (pltpu.VMEM((2, total, DV), F32), pltpu.VMEM((2, total, DV), BF16)),
        [VMEM] * 9,
        [pltpu.VMEM((8 + total, DK), F32)],
        flops=1 << 32,
    )(
        blocks,
        conv_q,
        keys,
        keys_t,
        later_inverses,
        within,
        cols,
        near(later_values),
        near(states),
    )
    for _ in range(shards - 2):
        moved = call(
            advance_kernel,
            pltpu.VMEM(hop.shape, BF16),
            [VMEM] * 8,
            [pltpu.VMEM((32, 512), F32)],
        )(entering, blocks, early, conv_q, conv_k, conv_v, hop, near(last))
        entering = near(lax.ppermute(moved, "half", route))
    normed = call(
        finish_kernel,
        pltpu.VMEM((peers, 2 * tokens, DV), BF16),
        [VMEM] * 10,
        [pltpu.VMEM((32, 512), F32)],
    )(
        entering,
        blocks,
        early,
        conv_q,
        conv_k,
        conv_v,
        norm_gain.reshape(1, DV),
        near(first_out),
        near(out_a),
        near(out_m),
    )
    returned = near(lax.all_to_all(normed, group, 0, 0, tiled=True))
    return call(
        functools.partial(gate_kernel, heads_axis),
        jax.ShapeDtypeStruct(z_rows.shape, BF16),
        [VMEM] * 2,
        [pltpu.VMEM(z_rows.shape, BF16), pltpu.SemaphoreType.DMA((heads_axis,))],
        ANY,
    )(returned, z_rows)


def solution(mesh):
    heads_axis = mesh.shape["head"]
    subs = KH // heads_axis
    regrouped = Mesh(
        mesh.devices.reshape(mesh.shape["ctx"] // subs, subs, heads_axis), ("half", "sub", "head")
    )
    row = P(("half", "sub", "head"), None)
    placed = (row,) * 6 + (P(None, "head"),) * 3 + (P("head"),) * 2 + (P(),)
    return jax.shard_map(local, mesh=regrouped, in_specs=placed, out_specs=row, check_vma=False)
```

```python
import functools

import jax
import jax.numpy as jnp
from jax import lax
from jax.experimental import pallas as pl
from jax.experimental.pallas import tpu as pltpu
from jax.sharding import Mesh, PartitionSpec as P

DK = 128
DV = 128
CONV = 4
KH = 16
SUB = 16
SPAN = 128
EDGE = CONV - 1
EPS = 1e-06
F32 = jnp.float32
BF16 = jnp.bfloat16
VMEM_BYTES = 24 * 1024 * 1024
GATES = 8


def dot(a, b, dims=((1,), (0,))):
    return lax.dot_general(a, b, (dims, ((), ())), preferred_element_type=F32)


def halves(x):
    high = x.astype(BF16)
    return high, (x - high.astype(F32)).astype(BF16)


def mm_parts(a, b):
    left = jnp.concatenate([a[0], a[1], a[0]], axis=1)
    return dot(left, jnp.concatenate([b[0], b[0], b[1]], axis=0))


def silu(x):
    half = 0.5 * x
    return half + half * jnp.tanh(half)


def unit(y, factor):
    scale = lax.rsqrt(jnp.sum(y * y, axis=-1, keepdims=True) + EPS)
    return (y * scale * factor).astype(BF16)


def iota(shape, dim):
    return lax.broadcasted_iota(jnp.int32, shape, dim)


def block_of(x, size):
    return lax.shift_right_logical(x, jnp.full(x.shape, size.bit_length() - 1, jnp.int32))


def place_in(x, size):
    return x & (size - 1)


def pack_kernel(
    heads_axis, q_in, k_in, v_in, at_in, bt_in, out_ref, q_ref, k_ref, v_ref, at_ref, bt_ref, sems
):
    peers, tokens = out_ref.shape[0], q_ref.shape[0]
    pairs = ((at_in, at_ref), (bt_in, bt_ref), (k_in, k_ref), (v_in, v_ref), (q_in, q_ref))
    copies = [pltpu.make_async_copy(a, b, sems.at[i]) for i, (a, b) in enumerate(pairs)]
    for copy in copies:
        copy.start()
    subs = peers // heads_axis
    key_heads = [(dest % heads_axis) * subs + dest // heads_axis for dest in range(peers)]
    for copy in copies[:2]:
        copy.wait()
    value_heads = at_ref.shape[0]
    row, entry = iota((peers * GATES, value_heads), 0), iota((peers * GATES, value_heads), 1)
    dest, which = block_of(row, GATES), place_in(row, GATES)
    first = 2 * (place_in(dest, heads_axis) * subs + block_of(dest, heads_axis))
    pick_a = jnp.where((which < 2) & (entry == first + which), 1.0, 0.0).astype(BF16)
    pick_b = jnp.where(
        (which >= 2) & (which < 4) & (entry == first + which - 2), 1.0, 0.0
    ).astype(BF16)
    picked = (dot(pick_a, at_ref[...]) + dot(pick_b, bt_ref[...])).astype(BF16)
    lane_shift = tokens * lax.rem(lax.axis_index("head"), SPAN // tokens)
    place = jnp.where(
        iota((tokens, SPAN), 1) == iota((tokens, SPAN), 0) + lane_shift, 1.0, 0.0
    ).astype(BF16)
    gates = dot(picked, place).astype(BF16)
    for dest in range(peers):
        out_ref[dest, 4 * tokens :, :] = gates[GATES * dest : GATES * (dest + 1), :]

    def laid(ref, lane, start):
        for dest, key_head in enumerate(key_heads):
            at = lane(key_head) * 128
            out_ref[dest, start * tokens : (start + 1) * tokens, :] = ref[
                :, at : at + 128
            ]

    copies[2].wait()
    laid(k_ref, lambda key_head: key_head, 0)
    copies[3].wait()
    laid(v_ref, lambda key_head: 2 * key_head, 1)
    laid(v_ref, lambda key_head: 2 * key_head + 1, 2)
    copies[4].wait()
    laid(q_ref, lambda key_head: key_head, 3)


def compacted(system):
    size = system.shape[0]
    diagonal = block_of(iota((size, size), 0), SUB) == block_of(iota((size, size), 1), SUB)
    return jnp.sum(jnp.where(diagonal, system, 0.0).reshape(size // SUB, SUB, size), axis=0)


def substituted(compact):
    count, _, size = compact.shape
    flat = compact.reshape(count * SUB, size)
    lane, line = iota(flat.shape, 1), iota(flat.shape, 0)
    solved = jnp.where(place_in(lane ^ line, SUB) == 0, 1.0, 0.0).reshape(count, SUB, size)
    for m in range(SUB - 1):
        source = (lane & ~(SUB - 1)) | m
        spread = jnp.take_along_axis(flat, source, axis=1, mode="promise_in_bounds")
        solved = solved + spread.reshape(count, SUB, size) * solved[:, m : m + 1, :]
    return solved


def inverted(systems, small):
    size = systems[0][0].shape[0]
    row, col = iota((size, size), 0), iota((size, size), 1)
    placed = jnp.where(block_of(row, SUB) == block_of(col, SUB), 1.0, 0.0).astype(BF16)
    parts = [
        tuple(jnp.concatenate([x] * (size // SUB), axis=0) * placed for x in halves(block))
        for block in small
    ]
    blank = jnp.zeros((size, size), BF16)
    width = SUB
    while width < size:
        odd = [(j, j + width) for j in range(width, size, 2 * width)]

        def rows_of(x):
            return jnp.concatenate([x[lo:hi] for lo, hi in odd], axis=0)

        def woven(even, x):
            pieces = []
            for j, (lo, hi) in enumerate(odd):
                pieces += [even[lo - width : lo], x[j * width : (j + 1) * width]]
            return jnp.concatenate(pieces, axis=0)

        below = rows_of(block_of(row ^ col, 2 * width)) + rows_of(col & width) == 0
        identity = rows_of(jnp.where(row == col, 1.0, 0.0))
        firsts = [
            mm_parts((rows_of(n[0]), rows_of(n[1])), t) for n, t in zip(systems, parts)
        ]
        rights = [
            tuple(woven(blank, x) for x in halves(jnp.where(below, first, identity)))
            for first in firsts
        ]
        odds = [(rows_of(t[0]), rows_of(t[1])) for t in parts]
        grown = [halves(mm_parts(o, right)) for o, right in zip(odds, rights)]
        parts = [tuple(woven(t[i], g[i]) for i in range(2)) for t, g in zip(parts, grown)]
        width *= 2
    return parts


def gate_values(gates, sub, alog_ref, dt_ref):
    second = place_in(iota(gates.shape, 0), GATES) == 1
    a_log = jnp.where(second, alog_ref[2 * sub + 1], alog_ref[2 * sub])
    dt_bias = jnp.where(second, dt_ref[2 * sub + 1], dt_ref[2 * sub])
    shifted = gates + dt_bias
    soft = jnp.maximum(shifted, 0.0) + jnp.log1p(jnp.exp(-jnp.abs(shifted)))
    return -jnp.exp(a_log) * soft, 1.0 / (1.0 + jnp.exp(-gates))


def convolved(rows, at, count, lanes, tap):
    summed = tap[0:1] * rows[at : at + count, lanes]
    for j in range(1, CONV):
        summed = summed + tap[j : j + 1] * rows[at + j : at + j + count, lanes]
    return silu(summed)


def key_tap(sub, tap_ref):
    return tap_ref[:, pl.ds(pl.multiple_of(sub * DK, 128), DK)]


def value_taps(sub, cv_ref):
    lane = pl.multiple_of(sub * 2 * DV, 128)
    return [cv_ref[:, pl.ds(pl.multiple_of(lane + r * DV, 128), DV)] for r in range(2)]


def widened(rows, recv_ref, starts, tokens):
    rows[0:8, :] = jnp.zeros((8, rows.shape[1]), F32)
    for s in range(recv_ref.shape[0]):
        for g, start in enumerate(starts):
            rows[8 + s * tokens : 8 + (s + 1) * tokens, g * 128 : (g + 1) * 128] = recv_ref[
                s, start : start + tokens, :
            ].astype(F32)


def systems_kernel(
    recv_ref,
    ck_ref,
    alog_ref,
    dt_ref,
    *refs,
):
    systems_of(recv_ref, ck_ref, alog_ref, dt_ref, *refs[3:])


def systems_of(
    recv_ref,
    ck_ref,
    alog_ref,
    dt_ref,
    keys_ref,
    keys_t_ref,
    systems_ref,
    small_ref,
    ends_ref,
    within_ref,
    cols_ref,
    early_ref,
    rows,
):
    sub = lax.axis_index("sub")
    later = lax.axis_index("half") > 0
    peers = recv_ref.shape[0]
    tokens = (recv_ref.shape[1] - GATES) // 4
    spans = peers * tokens // SPAN
    tap = key_tap(sub, ck_ref)
    widened(rows, recv_ref, [0], tokens)
    stacked = [
        sum(recv_ref[s, 4 * tokens :, :].astype(F32) for s in range(n, n + SPAN // tokens))
        for n in range(0, peers, SPAN // tokens)
    ]
    stacked.append(jnp.zeros((SPAN - spans * GATES, SPAN), F32))
    gates = jnp.concatenate(stacked, axis=0)
    decay, rate = gate_values(gates, sub, alog_ref, dt_ref)
    early_ref[...] = jnp.where(iota((8, SPAN), 0) < 2, decay[0:8], rate[0:8])
    skipped = later & (iota(gates.shape, 0) < GATES) & (iota(gates.shape, 1) < EDGE)
    decay = jnp.where(skipped, 0.0, decay)
    rate = jnp.where(skipped, 0.0, rate)
    lane_r, lane_c = iota((SPAN, SPAN), 0), iota((SPAN, SPAN), 1)
    upto = jnp.where(lane_r <= lane_c, 1.0, 0.0).astype(BF16)
    d_high, _ = halves(decay)
    d_mid, d_low = halves(decay - d_high.astype(F32))
    cum = dot(d_high, upto) + (dot(d_mid, upto) + dot(d_low, upto))
    growth = jnp.exp(cum)
    here = pltpu.roll(rate, rate.shape[0] - 2, 0)
    rest = jnp.exp(cum[:, SPAN - 1 :] - cum) * here
    which = place_in(iota(gates.shape, 0), GATES)
    mixed = jnp.where(which < 2, cum, pltpu.roll(growth, 2, 0))
    columns = jnp.transpose(jnp.where(which < 4, mixed, pltpu.roll(rest, 4, 0)))
    cols_ref[...] = columns
    lower = lane_r >= lane_c
    strict = lane_r > lane_c
    both = [(n, r) for n in range(spans) for r in range(2)]
    keys = []
    for n in range(spans):
        k_n = unit(convolved(rows, n * SPAN + 8 - EDGE, SPAN, slice(0, DK), tap), 1.0)
        keys_ref[n * SPAN : (n + 1) * SPAN, :] = k_n
        keys.append(k_n)
    keys_t = []
    for n in range(spans):
        kt_n = jnp.transpose(keys[n].astype(F32)).astype(BF16)
        keys_t_ref[n] = kt_n
        keys_t.append(kt_n)
    grams = [dot(keys[n], keys_t[n]) for n in range(spans)]
    for n, r in both:
        at = GATES * n + r
        gap = columns[:, at : at + 1] - cum[at : at + 1, :]
        within = jnp.exp(jnp.where(lower, gap, 0.0)) * here[at : at + 1, :]
        within_ref[r, n * SPAN : (n + 1) * SPAN, :] = jnp.where(lower, within, 0.0).astype(BF16)
        system = jnp.where(strict, within * -grams[n], 0.0)
        systems_ref[r, n, 0], systems_ref[r, n, 1] = halves(system)
        small_ref[r, n] = compacted(system)
    ends_ref[...] = jnp.broadcast_to(growth[:, SPAN - 1 :], ends_ref.shape)


def inverse_kernel(
    on_first, hop_ref, keys_ref, keys_t_ref, systems_ref, small_ref, cols_ref, t_ref, lin_ref
):
    del hop_ref
    spans = keys_t_ref.shape[0]
    both = [(n, r) for n in range(spans) for r in range(2)]

    @pl.when((lax.axis_index("half") == 0) == on_first)
    def _():
        compact = jnp.concatenate([small_ref[r, n] for n, r in both], axis=0)
        small = substituted(compact.reshape(len(both), SUB, SPAN))
        systems = [(systems_ref[r, n, 0], systems_ref[r, n, 1]) for n, r in both]
        inverses = inverted(systems, [small[i] for i in range(len(both))])
        scaled = []
        for i, (n, r) in enumerate(both):
            t_ref[r, n, 0], t_ref[r, n, 1] = inverses[i]
            at = GATES * n + r
            key = keys_ref[n * SPAN : (n + 1) * SPAN, :].astype(F32)
            right = (cols_ref[:, at + 2 : at + 3] * key).astype(BF16)
            scaled.append(jnp.concatenate([right, right], axis=0))
        w_mats = [dot(jnp.concatenate(t, axis=1), x) for t, x in zip(inverses, scaled)]
        weighed = []
        for (n, r), w_mat in zip(both, w_mats):
            at = GATES * n + r
            weighed.append((cols_ref[:, at + 4 : at + 5] * w_mat).astype(BF16))
        moved = [
            dot(keys_t_ref[n], jnp.concatenate(weighed[2 * n : 2 * n + 2], axis=1))
            for n in range(spans)
        ]
        for n, r in both:
            lin_ref[r, n] = moved[n][:, r * DK : (r + 1) * DK].astype(BF16)


def unwound(t_ref, n, r, x):
    both = jnp.concatenate([t_ref[r, n, 0], t_ref[r, n, 1]], axis=1)
    return dot(both, jnp.concatenate([x, x], axis=0))


def end_of(ends_ref, n, r):
    return ends_ref[GATES * n + r : GATES * n + r + 1, :]


def followed(span_map, state):
    end, moved, add = span_map
    return step(end, moved, state, halves(state)) + add


def composed(maps):
    if len(maps) == 1:
        return maps[0]
    half = len(maps) // 2
    end_a, moved_a, add_a = composed(maps[:half])
    end_b, moved_b, add_b = composed(maps[half:])
    high, low = halves(add_a)
    rights = jnp.concatenate(
        [
            jnp.concatenate([moved_a, high], axis=1),
            jnp.concatenate([jnp.zeros_like(moved_a), low], axis=1),
        ],
        axis=0,
    )
    passed = dot(jnp.concatenate([moved_b, moved_b], axis=1), rights)
    moved = end_b * moved_a.astype(F32) + end_a * moved_b.astype(F32) - passed[:, :DK]
    add = end_b * add_a - passed[:, DK:] + add_b
    return end_a * end_b, moved.astype(BF16), add


def step(end, moved, state, parts):
    both = jnp.concatenate([moved, moved], axis=1)
    return end * state - dot(both, jnp.concatenate(parts, axis=0))


def values_part(recv_ref, cv_ref, keys_t_ref, t_ref, cols_ref, rows, vs):
    sub = lax.axis_index("sub")
    tokens = (recv_ref.shape[1] - GATES) // 4
    spans = t_ref.shape[1]
    taps = value_taps(sub, cv_ref)
    widened(rows, recv_ref, [tokens, 2 * tokens], tokens)
    both = [(n, r) for n in range(spans) for r in range(2)]
    values = []
    for n, r in both:
        lanes = slice(r * DV, (r + 1) * DV)
        v_n = convolved(rows, n * SPAN + 8 - EDGE, SPAN, lanes, taps[r]).astype(BF16)
        vs[r, n * SPAN : (n + 1) * SPAN, :] = v_n
        values.append(v_n)
    solved = [unwound(t_ref, n, r, v) for (n, r), v in zip(both, values)]
    weighed = []
    for (n, r), u_mat in zip(both, solved):
        at = GATES * n + r
        weighed.append((cols_ref[:, at + 4 : at + 5] * u_mat).astype(BF16))
    moved = [
        dot(keys_t_ref[n], jnp.concatenate(weighed[2 * n : 2 * n + 2], axis=1))
        for n in range(spans)
    ]
    return [moved[n][:, r * DV : (r + 1) * DV] for n, r in both]


def opening_kernel(
    recv_ref, cv_ref, keys_t_ref, t_ref, lin_ref, ends_ref, cols_ref, hop_ref, vs_ref, xs_ref, adds_ref, rows
):
    first = lax.axis_index("half") == 0
    peers = recv_ref.shape[0]
    tokens = (recv_ref.shape[1] - GATES) // 4
    spans = t_ref.shape[1]
    edges = []
    for which in (3, 0, 1, 2):
        end = (which + 1) * tokens
        edges.append(recv_ref[peers - 1, end - 16 : end, :].astype(F32)[16 - EDGE :])
    edges.append(jnp.zeros((16 - 4 * EDGE, 128), F32))
    hop_ref[2 * DK :, :] = jnp.concatenate(edges, axis=0).astype(BF16)

    @pl.when(first)
    def _():
        adds = values_part(recv_ref, cv_ref, keys_t_ref, t_ref, cols_ref, rows, vs_ref)
        for n in range(spans):
            for r in range(2):
                adds_ref[r, n] = adds[2 * n + r]
        maps = [
            [(end_of(ends_ref, n, r), lin_ref[r, n], adds[2 * n + r]) for n in range(spans)]
            for r in range(2)
        ]
        states = [m[0][2] for m in maps]
        done = 1
        while done < spans:
            for r in range(2):
                if done > 1:
                    xs_ref[r, done] = jnp.concatenate(halves(states[r]), axis=0)
            later = [composed(m[done : 2 * done]) for m in maps]
            states = [followed(m, x) for m, x in zip(later, states)]
            done *= 2
        for r in range(2):
            hop_ref[r * DK : (r + 1) * DK, :] = states[r].astype(BF16)

    @pl.when(jnp.logical_not(first))
    def _():
        hop_ref[0 : 2 * DK, :] = jnp.zeros((2 * DK, DV), BF16)


def states_kernel(
    recv_ref,
    cv_ref,
    keys_t_ref,
    t_ref,
    lin_ref,
    ends_ref,
    cols_ref,
    values_ref,
    states_ref,
    *rest,
):
    *last_ref, rows = rest

    @pl.when(lax.axis_index("half") > 0)
    def _():
        spans = t_ref.shape[1]
        adds = values_part(recv_ref, cv_ref, keys_t_ref, t_ref, cols_ref, rows, values_ref)
        zero_half = jnp.zeros((DK, DV), F32)
        identity = jnp.where(iota((DK, DK), 0) == iota((DK, DK), 1), 1.0, 0.0)
        states = [
            jnp.concatenate(
                [adds[r], ends_ref[r : r + 1, :] * identity - lin_ref[r, 0].astype(F32)], axis=1
            )
            for r in range(2)
        ]
        for n in range(1, spans):
            for r in range(2):
                parts = halves(states[r])
                for i in range(2):
                    both_parts = [x[:, i * DV : (i + 1) * DV] for x in parts]
                    states_ref[i, r, n] = jnp.concatenate(both_parts, axis=0)
                add = jnp.concatenate([adds[2 * n + r], zero_half], axis=1)
                end = jnp.concatenate([end_of(ends_ref, n, r)] * 2, axis=1)
                states[r] = step(end, lin_ref[r, n], states[r], parts) + add
        for ref in last_ref:
            for r in range(2):
                ref[r] = states[r]


def span_rows(n):
    return slice(n * SPAN, (n + 1) * SPAN)


def twice(x, axis):
    return jnp.concatenate([x, x], axis=axis)


def asked(recv_ref, cq_ref, keys_ref, keys_t_ref, within_ref, query_rows):
    tokens = (recv_ref.shape[1] - GATES) // 4
    spans = keys_t_ref.shape[0]
    tap = key_tap(lax.axis_index("sub"), cq_ref)
    widened(query_rows, recv_ref, [3 * tokens], tokens)
    queries = [
        unit(convolved(query_rows, n * SPAN + 8 - EDGE, SPAN, slice(0, DK), tap), DK**-0.5)
        for n in range(spans)
    ]
    readers = [
        jnp.concatenate([keys_ref[span_rows(n), :], queries[n]], axis=0) for n in range(spans)
    ]
    scores = [dot(queries[n], keys_t_ref[n]) for n in range(spans)]
    inner = [
        (within_ref[r, span_rows(n), :].astype(F32) * scores[n]).astype(BF16)
        for n in range(spans)
        for r in range(2)
    ]
    return readers, inner


def first_outputs_kernel(
    recv_ref,
    cq_ref,
    keys_ref,
    keys_t_ref,
    t_ref,
    lin_ref,
    ends_ref,
    within_ref,
    cols_ref,
    values_ref,
    xs_ref,
    adds_ref,
    oa_ref,
    query_rows,
):
    @pl.when(lax.axis_index("half") == 0)
    def _():
        spans = t_ref.shape[1]
        both = [(n, r) for n in range(spans) for r in range(2)]
        readers, inner = asked(recv_ref, cq_ref, keys_ref, keys_t_ref, within_ref, query_rows)
        stacks, states = [], []
        for n in range(1, spans):
            if n == 1:
                states = [adds_ref[r, 0] for r in range(2)]
                stack = [jnp.concatenate(halves(x), axis=0) for x in states]
            elif n & (n - 1) == 0:
                stack = [xs_ref[r, n] for r in range(2)]
                states = [x[:DK].astype(F32) + x[DK:].astype(F32) for x in stack]
            else:
                states = [
                    followed(
                        (end_of(ends_ref, n - 1, r), lin_ref[r, n - 1], adds_ref[r, n - 1]),
                        states[r],
                    )
                    for r in range(2)
                ]
                stack = [jnp.concatenate(halves(x), axis=0) for x in states]
            stacks.append(jnp.concatenate(stack, axis=1))
        reads = [dot(twice(readers[n], 1), stacks[n - 1]) for n in range(1, spans)]
        rests, seen = [], []
        for n, r in both:
            lanes = slice(r * DV, (r + 1) * DV)
            value = values_ref[r, span_rows(n), :]
            if n == 0:
                rests.append(value)
                seen.append(None)
            else:
                growth = cols_ref[:, GATES * n + 2 + r : GATES * n + 3 + r]
                read = growth * reads[n - 1][:SPAN, lanes]
                rests.append((value.astype(F32) - read).astype(BF16))
                seen.append(growth * reads[n - 1][SPAN:, lanes])
        fresh = [unwound(t_ref, n, r, x).astype(BF16) for (n, r), x in zip(both, rests)]
        spreads = [dot(w, x) for w, x in zip(inner, fresh)]
        for (n, r), x, y in zip(both, spreads, seen):
            oa_ref[r, span_rows(n), :] = x if y is None else x + y


def later_outputs_kernel(
    recv_ref,
    cq_ref,
    keys_ref,
    keys_t_ref,
    t_ref,
    within_ref,
    cols_ref,
    values_ref,
    states_ref,
    oa_ref,
    om_ref,
    query_rows,
):
    @pl.when(lax.axis_index("half") > 0)
    def _():
        spans = t_ref.shape[1]
        both = [(n, r) for n in range(spans) for r in range(2)]
        readers, inner = asked(recv_ref, cq_ref, keys_ref, keys_t_ref, within_ref, query_rows)
        zero_half = jnp.zeros((SPAN, DV), F32)
        reads = [
            dot(
                twice(readers[n], 1),
                jnp.concatenate([states_ref[0, r, n], states_ref[1, r, n]], axis=1),
            )
            if n > 0
            else None
            for n, r in both
        ]
        rests, seen = [], []
        for (n, r), read in zip(both, reads):
            value = values_ref[r, span_rows(n), :].astype(F32)
            growth = cols_ref[:, GATES * n + 2 + r : GATES * n + 3 + r]
            if n == 0:
                reader = readers[n].astype(F32)
                rest = jnp.concatenate([value, -(growth * reader[:SPAN])], axis=1)
                seen.append(jnp.concatenate([zero_half, growth * reader[SPAN:]], axis=1))
            else:
                rest = jnp.concatenate([value, zero_half], axis=1) - growth * read[:SPAN]
                seen.append(growth * read[SPAN:])
            rests.append(rest.astype(BF16))
        fresh = [unwound(t_ref, n, r, x).astype(BF16) for (n, r), x in zip(both, rests)]
        spreads = [dot(w, x) for w, x in zip(inner, fresh)]
        for (n, r), x, y in zip(both, spreads, seen):
            out = x + y
            oa_ref[r, span_rows(n), :] = out[:, :DV]
            om_ref[r, span_rows(n), :] = out[:, DV:].astype(BF16)


def first_tokens(hop_ref, recv_ref, early_ref, cq_ref, ck_ref, cv_ref, rows):
    sub = lax.axis_index("sub")
    tokens = (recv_ref.shape[1] - GATES) // 4
    taps = [key_tap(sub, cq_ref), key_tap(sub, ck_ref)] + value_taps(sub, cv_ref)
    results = []
    edges = hop_ref[2 * DK :, :].astype(F32)
    for g, first in enumerate((3, 0, 1, 2)):
        lanes = slice(g * 128, (g + 1) * 128)
        start = first * tokens
        rows[16 - EDGE : 16, lanes] = edges[EDGE * g : EDGE * (g + 1)]
        rows[16:32, lanes] = recv_ref[0, start : start + 16, :].astype(F32)
        results.append(convolved(rows, 16 - EDGE, 8, lanes, taps[g]))
    q_cols = jnp.transpose(unit(results[0], DK**-0.5).astype(F32))
    k_cols = jnp.transpose(unit(results[1], 1.0).astype(F32))
    gates = early_ref[...]
    line = iota((8, DV), 0)
    finals, outputs = [], []
    for r in range(2):
        values = results[2 + r].astype(BF16).astype(F32)
        entering = hop_ref[r * DK : (r + 1) * DK, :].astype(F32)
        state, out = entering, jnp.zeros((8, DV), F32)
        for t in range(EDGE):
            k_t, q_t = k_cols[:, t : t + 1], q_cols[:, t : t + 1]
            state = jnp.exp(gates[r : r + 1, t : t + 1]) * state
            held = jnp.sum(k_t * state, axis=0, keepdims=True)
            state = state + k_t * (
                gates[2 + r : 3 + r, t : t + 1] * (values[t : t + 1, :] - held)
            )
            out = jnp.where(line == t, jnp.sum(q_t * state, axis=0, keepdims=True), out)
        finals.append(state)
        outputs.append(out)
    return finals, outputs


def finish_kernel(
    hop_ref,
    recv_ref,
    early_ref,
    cq_ref,
    ck_ref,
    cv_ref,
    gain_ref,
    first_oa,
    oa_ref,
    om_ref,
    out_ref,
    rows,
):
    peers, tokens = out_ref.shape[0], out_ref.shape[1] // 2
    first = lax.axis_index("half") == 0
    gain = gain_ref[...]
    chunks = 4
    part, peer_part = peers * tokens // chunks, peers // chunks

    def put(c, r, core):
        scale = lax.rsqrt(jnp.mean(core * core, axis=-1, keepdims=True) + EPS)
        normed = (core * scale * gain).astype(BF16)
        here = slice(c * peer_part, (c + 1) * peer_part)
        out_ref[here, r * tokens : (r + 1) * tokens, :] = normed.reshape(peer_part, tokens, DV)

    @pl.when(first)
    def _():
        for c in range(chunks):
            for r in range(2):
                put(c, r, first_oa[r, c * part : (c + 1) * part, :])

    @pl.when(jnp.logical_not(first))
    def _():
        finals, outputs = first_tokens(hop_ref, recv_ref, early_ref, cq_ref, ck_ref, cv_ref, rows)
        replaced = iota((8, DV), 0) < EDGE
        passed = [dot(om_ref[r], finals[r].astype(BF16)) for r in range(2)]
        for c in range(chunks):
            at = c * part
            for r in range(2):
                core = oa_ref[r, at : at + part, :] + passed[r][at : at + part]
                if c == 0:
                    core = jnp.concatenate(
                        [jnp.where(replaced, outputs[r], core[0:8]), core[8:]], axis=0
                    )
                put(c, r, core)


def advance_kernel(
    hop_ref, recv_ref, early_ref, cq_ref, ck_ref, cv_ref, hop_own, last_ref, next_ref, rows
):
    finals, _ = first_tokens(hop_ref, recv_ref, early_ref, cq_ref, ck_ref, cv_ref, rows)
    first = lax.axis_index("half") == 0
    for r in range(2):
        last = last_ref[r]
        through = mm_parts(halves(last[:, DV:]), halves(finals[r]))
        own = hop_own[r * DK : (r + 1) * DK, :].astype(F32)
        moved = jnp.where(first, own, through + last[:, :DV])
        next_ref[r * DK : (r + 1) * DK, :] = moved.astype(BF16)
    next_ref[2 * DK :, :] = hop_own[2 * DK :, :]


def gate_kernel(heads_axis, normed_ref, z_ref, out_ref, made, sems):
    subs, tokens = normed_ref.shape[0] // heads_axis, z_ref.shape[0]
    width = subs * 2 * DV
    copies = []
    for head in range(heads_axis):
        for sub in range(subs):
            for r in range(2):
                at = (2 * (head * subs + sub) + r) * DV
                gate = silu(z_ref[:, at : at + DV].astype(F32))
                here = slice(r * tokens, (r + 1) * tokens)
                value = normed_ref[sub * heads_axis + head, here, :].astype(F32)
                made[:, at : at + DV] = (value * gate).astype(BF16)
        lanes = pl.ds(head * width, width)
        copy = pltpu.make_async_copy(made.at[:, lanes], out_ref.at[:, lanes], sems.at[head])
        copy.start()
        copies.append(copy)
    for copy in copies:
        copy.wait()


VMEM = pl.BlockSpec(memory_space=pltpu.VMEM)
SMEM = pl.BlockSpec(memory_space=pltpu.SMEM)
ANY = pl.BlockSpec(memory_space=pl.ANY)


def near(x):
    return pltpu.with_memory_space_constraint(x, pltpu.VMEM)


def far(x):
    return pltpu.with_memory_space_constraint(x, pltpu.HBM)


def call(kernel, outs, in_specs, scratch=(), out_spec=VMEM, flops=1 << 26, moved=1 << 21):
    return pl.pallas_call(
        kernel,
        out_shape=outs,
        in_specs=in_specs,
        out_specs=jax.tree.map(lambda _: out_spec, outs),
        scratch_shapes=list(scratch),
        compiler_params=pltpu.CompilerParams(vmem_limit_bytes=VMEM_BYTES),
        cost_estimate=pl.CostEstimate(flops=flops, bytes_accessed=moved, transcendentals=0),
    )


def local(
    q_rows,
    k_rows,
    v_rows,
    z_rows,
    a_rows,
    b_rows,
    conv_q,
    conv_k,
    conv_v,
    a_log,
    dt_bias,
    norm_gain,
):
    shards, subs, heads_axis = (lax.axis_size(a) for a in ("half", "sub", "head"))
    peers, tokens = subs * heads_axis, q_rows.shape[0]
    total = peers * tokens
    spans = total // SPAN
    group = ("sub", "head")
    route = [(i, i + 1) for i in range(shards - 1)]
    conv_q, conv_k, conv_v = near(conv_q), near(conv_k), near(conv_v)
    gain = near(norm_gain.reshape(1, DV))
    inputs = [far(x) for x in (q_rows, k_rows, v_rows, a_rows.T, b_rows.T)]
    packed = call(
        functools.partial(pack_kernel, heads_axis),
        pltpu.VMEM((peers, GATES + 4 * tokens, 128), BF16),
        [ANY] * 5,
        [pltpu.VMEM(x.shape, BF16) for x in inputs] + [pltpu.SemaphoreType.DMA((5,))],
        flops=1 << 20,
    )(*inputs)
    blocks = near(lax.all_to_all(packed, group, 0, 0, tiled=True))
    made = call(
        systems_kernel,
        (
            pltpu.VMEM((total, DK), BF16),
            pltpu.VMEM((spans, DK, SPAN), BF16),
            pltpu.VMEM((2, spans, 2, SPAN, SPAN), BF16),
            pltpu.VMEM((2, spans, SUB, SPAN), F32),
            pltpu.VMEM((SPAN, DK), F32),
            pltpu.VMEM((2, total, SPAN), BF16),
            pltpu.VMEM((SPAN, SPAN), F32),
            pltpu.VMEM((8, SPAN), F32),
        ),
        [VMEM, VMEM, SMEM, SMEM, VMEM, VMEM, VMEM],
        [pltpu.VMEM((8 + total, DK), F32)],
        flops=1 << 32,
    )(blocks, conv_k, a_log, dt_bias, conv_q, conv_v, gain)
    keys, keys_t, systems, small, ends, within, cols, early = (near(x) for x in made)
    map_shapes = (
        pltpu.VMEM((2, spans, 2, SPAN, SPAN), BF16),
        pltpu.VMEM((2, spans, DK, DK), BF16),
    )

    def inverses_of(on_first, after):
        solved = call(
            functools.partial(inverse_kernel, on_first), map_shapes, [VMEM] * 6, flops=1 << 32
        )(after, keys, keys_t, systems, small, cols)
        return [near(x) for x in solved]

    inverses, lins = inverses_of(True, early)
    hop, values, starts, adds = call(
        opening_kernel,
        (
            pltpu.VMEM((2 * DK + 16, 128), BF16),
            pltpu.VMEM((2, total, DV), BF16),
            pltpu.VMEM((2, spans, 2 * DK, DV), BF16),
            pltpu.VMEM((2, spans, DK, DV), F32),
        ),
        [VMEM] * 7,
        [pltpu.VMEM((8 + total, 2 * DV), F32)],
        flops=1 << 32,
    )(blocks, conv_v, keys_t, inverses, lins, ends, cols)
    entering = near(lax.ppermute(hop, "half", route))
    hop, values, starts, adds = (near(x) for x in (hop, values, starts, adds))
    first_out = call(
        first_outputs_kernel,
        pltpu.VMEM((2, total, DV), F32),
        [VMEM] * 12,
        [pltpu.VMEM((8 + total, DK), F32)],
        flops=1 << 32,
    )(
        blocks,
        conv_q,
        keys,
        keys_t,
        inverses,
        lins,
        ends,
        within,
        cols,
        values,
        starts,
        adds,
    )
    later_inverses, later_lins = inverses_of(False, hop)
    read_on = [pltpu.VMEM((2, DK, 2 * DV), F32)] if shards > 2 else []
    later_values, states, *last = call(
        states_kernel,
        (
            pltpu.VMEM((2, total, DV), BF16),
            pltpu.VMEM((2, 2, spans, 2 * DK, DV), BF16),
            *read_on,
        ),
        [VMEM] * 7,
        [pltpu.VMEM((8 + total, 2 * DV), F32)],
        flops=1 << 32,
    )(blocks, conv_v, keys_t, later_inverses, later_lins, ends, cols)
    out_a, out_m = call(
        later_outputs_kernel,
        (pltpu.VMEM((2, total, DV), F32), pltpu.VMEM((2, total, DV), BF16)),
        [VMEM] * 9,
        [pltpu.VMEM((8 + total, DK), F32)],
        flops=1 << 32,
    )(
        blocks,
        conv_q,
        keys,
        keys_t,
        later_inverses,
        within,
        cols,
        near(later_values),
        near(states),
    )
    for _ in range(shards - 2):
        moved = call(
            advance_kernel,
            pltpu.VMEM(hop.shape, BF16),
            [VMEM] * 8,
            [pltpu.VMEM((32, 512), F32)],
        )(entering, blocks, early, conv_q, conv_k, conv_v, hop, near(last[0]))
        entering = near(lax.ppermute(moved, "half", route))
    normed = call(
        finish_kernel,
        pltpu.VMEM((peers, 2 * tokens, DV), BF16),
        [VMEM] * 10,
        [pltpu.VMEM((32, 512), F32)],
    )(
        entering,
        blocks,
        early,
        conv_q,
        conv_k,
        conv_v,
        gain,
        near(first_out),
        near(out_a),
        near(out_m),
    )
    returned = near(lax.all_to_all(normed, group, 0, 0, tiled=True))
    return call(
        functools.partial(gate_kernel, heads_axis),
        jax.ShapeDtypeStruct(z_rows.shape, BF16),
        [VMEM] * 2,
        [pltpu.VMEM(z_rows.shape, BF16), pltpu.SemaphoreType.DMA((heads_axis,))],
        ANY,
    )(returned, z_rows)


def solution(mesh):
    heads_axis = mesh.shape["head"]
    subs = KH // heads_axis
    regrouped = Mesh(
        mesh.devices.reshape(mesh.shape["ctx"] // subs, subs, heads_axis), ("half", "sub", "head")
    )
    row = P(("half", "sub", "head"), None)
    placed = (row,) * 6 + (P(None, "head"),) * 3 + (P("head"),) * 2 + (P(),)
    return jax.shard_map(local, mesh=regrouped, in_specs=placed, out_specs=row, check_vma=False)
```

```python
import functools

import jax
import jax.numpy as jnp
from jax import lax
from jax.experimental import pallas as pl
from jax.experimental.pallas import tpu as pltpu
from jax.sharding import Mesh, PartitionSpec as P

DK = 128
DV = 128
CONV = 4
KH = 16
SUB = 16
SPAN = 128
EDGE = CONV - 1
EPS = 1e-06
F32 = jnp.float32
BF16 = jnp.bfloat16
VMEM_BYTES = 24 * 1024 * 1024
GATES = 8


def dot(a, b, dims=((1,), (0,))):
    return lax.dot_general(a, b, (dims, ((), ())), preferred_element_type=F32)


def halves(x):
    high = x.astype(BF16)
    return high, (x - high.astype(F32)).astype(BF16)


def mm_parts(a, b):
    left = jnp.concatenate([a[0], a[1], a[0]], axis=1)
    return dot(left, jnp.concatenate([b[0], b[0], b[1]], axis=0))


def silu(x):
    half = 0.5 * x
    return half + half * jnp.tanh(half)


def unit(y, factor):
    scale = lax.rsqrt(jnp.sum(y * y, axis=-1, keepdims=True) + EPS)
    return (y * scale * factor).astype(BF16)


def iota(shape, dim):
    return lax.broadcasted_iota(jnp.int32, shape, dim)


def block_of(x, size):
    return lax.shift_right_logical(x, jnp.full(x.shape, size.bit_length() - 1, jnp.int32))


def place_in(x, size):
    return x & (size - 1)


def pack_kernel(
    heads_axis, q_in, k_in, v_in, at_in, bt_in, out_ref, q_ref, k_ref, v_ref, at_ref, bt_ref, sems
):
    peers, tokens = out_ref.shape[0], q_ref.shape[0]
    pairs = ((at_in, at_ref), (bt_in, bt_ref), (k_in, k_ref), (v_in, v_ref), (q_in, q_ref))
    copies = [pltpu.make_async_copy(a, b, sems.at[i]) for i, (a, b) in enumerate(pairs)]
    for copy in copies:
        copy.start()
    subs = peers // heads_axis
    key_heads = [(dest % heads_axis) * subs + dest // heads_axis for dest in range(peers)]
    for copy in copies[:2]:
        copy.wait()
    value_heads = at_ref.shape[0]
    row, entry = iota((peers * GATES, value_heads), 0), iota((peers * GATES, value_heads), 1)
    dest, which = block_of(row, GATES), place_in(row, GATES)
    first = 2 * (place_in(dest, heads_axis) * subs + block_of(dest, heads_axis))
    pick_a = jnp.where((which < 2) & (entry == first + which), 1.0, 0.0).astype(BF16)
    pick_b = jnp.where(
        (which >= 2) & (which < 4) & (entry == first + which - 2), 1.0, 0.0
    ).astype(BF16)
    picked = (dot(pick_a, at_ref[...]) + dot(pick_b, bt_ref[...])).astype(BF16)
    lane_shift = tokens * lax.rem(lax.axis_index("head"), SPAN // tokens)
    place = jnp.where(
        iota((tokens, SPAN), 1) == iota((tokens, SPAN), 0) + lane_shift, 1.0, 0.0
    ).astype(BF16)
    gates = dot(picked, place).astype(BF16)
    for dest in range(peers):
        out_ref[dest, 4 * tokens :, :] = gates[GATES * dest : GATES * (dest + 1), :]

    def laid(ref, lane, start):
        for dest, key_head in enumerate(key_heads):
            at = lane(key_head) * 128
            out_ref[dest, start * tokens : (start + 1) * tokens, :] = ref[
                :, at : at + 128
            ]

    copies[2].wait()
    laid(k_ref, lambda key_head: key_head, 0)
    copies[3].wait()
    laid(v_ref, lambda key_head: 2 * key_head, 1)
    laid(v_ref, lambda key_head: 2 * key_head + 1, 2)
    copies[4].wait()
    laid(q_ref, lambda key_head: key_head, 3)


def compacted(system):
    size = system.shape[0]
    diagonal = block_of(iota((size, size), 0), SUB) == block_of(iota((size, size), 1), SUB)
    return jnp.sum(jnp.where(diagonal, system, 0.0).reshape(size // SUB, SUB, size), axis=0)


def substituted(compact):
    count, _, size = compact.shape
    flat = compact.reshape(count * SUB, size)
    lane, line = iota(flat.shape, 1), iota(flat.shape, 0)
    solved = jnp.where(place_in(lane ^ line, SUB) == 0, 1.0, 0.0).reshape(count, SUB, size)
    for m in range(SUB - 1):
        source = (lane & ~(SUB - 1)) | m
        spread = jnp.take_along_axis(flat, source, axis=1, mode="promise_in_bounds")
        solved = solved + spread.reshape(count, SUB, size) * solved[:, m : m + 1, :]
    return solved


def inverted(systems, small):
    size = systems[0][0].shape[0]
    row, col = iota((size, size), 0), iota((size, size), 1)
    placed = jnp.where(block_of(row, SUB) == block_of(col, SUB), 1.0, 0.0).astype(BF16)
    identity = jnp.where(row == col, 1.0, 0.0)
    rough = [
        jnp.concatenate([block.astype(BF16)] * (size // SUB), axis=0) * placed for block in small
    ]
    blank = jnp.zeros((size, size), BF16)
    width = SUB
    while width < size:
        odd = [(j, j + width) for j in range(width, size, 2 * width)]

        def rows_of(x):
            return jnp.concatenate([x[lo:hi] for lo, hi in odd], axis=0)

        def woven(even, x):
            pieces = []
            for j, (lo, hi) in enumerate(odd):
                pieces += [even[lo - width : lo], x[j * width : (j + 1) * width]]
            return jnp.concatenate(pieces, axis=0)

        below = rows_of(block_of(row ^ col, 2 * width)) + rows_of(col & width) == 0
        own = rows_of(identity)
        firsts = [dot(rows_of(n[0]), t) for n, t in zip(systems, rough)]
        rights = [
            woven(blank, jnp.where(below, first, own).astype(BF16)) for first in firsts
        ]
        grown = [dot(rows_of(t), right).astype(BF16) for t, right in zip(rough, rights)]
        rough = [woven(t, g) for t, g in zip(rough, grown)]
        width *= 2
    products = [
        dot(jnp.concatenate(n, axis=1), jnp.concatenate([t, t], axis=0))
        for n, t in zip(systems, rough)
    ]
    rests = [
        (identity - t.astype(F32) + product).astype(BF16) for t, product in zip(rough, products)
    ]
    return [halves(t.astype(F32) + dot(t, rest)) for t, rest in zip(rough, rests)]


def gate_values(gates, sub, alog_ref, dt_ref):
    second = place_in(iota(gates.shape, 0), GATES) == 1
    a_log = jnp.where(second, alog_ref[2 * sub + 1], alog_ref[2 * sub])
    dt_bias = jnp.where(second, dt_ref[2 * sub + 1], dt_ref[2 * sub])
    shifted = gates + dt_bias
    soft = jnp.maximum(shifted, 0.0) + jnp.log1p(jnp.exp(-jnp.abs(shifted)))
    return -jnp.exp(a_log) * soft, 1.0 / (1.0 + jnp.exp(-gates))


def convolved(rows, at, count, lanes, tap):
    summed = tap[0:1] * rows[at : at + count, lanes]
    for j in range(1, CONV):
        summed = summed + tap[j : j + 1] * rows[at + j : at + j + count, lanes]
    return silu(summed)


def key_tap(sub, tap_ref):
    return tap_ref[:, pl.ds(pl.multiple_of(sub * DK, 128), DK)]


def value_taps(sub, cv_ref):
    lane = pl.multiple_of(sub * 2 * DV, 128)
    return [cv_ref[:, pl.ds(pl.multiple_of(lane + r * DV, 128), DV)] for r in range(2)]


def widened(rows, recv_ref, starts, tokens):
    rows[0:8, :] = jnp.zeros((8, rows.shape[1]), F32)
    for s in range(recv_ref.shape[0]):
        for g, start in enumerate(starts):
            rows[8 + s * tokens : 8 + (s + 1) * tokens, g * 128 : (g + 1) * 128] = recv_ref[
                s, start : start + tokens, :
            ].astype(F32)


def systems_kernel(
    recv_ref,
    ck_ref,
    alog_ref,
    dt_ref,
    *refs,
):
    systems_of(recv_ref, ck_ref, alog_ref, dt_ref, *refs[3:])


def systems_of(
    recv_ref,
    ck_ref,
    alog_ref,
    dt_ref,
    keys_ref,
    keys_t_ref,
    systems_ref,
    small_ref,
    ends_ref,
    within_ref,
    cols_ref,
    early_ref,
    rows,
):
    sub = lax.axis_index("sub")
    later = lax.axis_index("half") > 0
    peers = recv_ref.shape[0]
    tokens = (recv_ref.shape[1] - GATES) // 4
    spans = peers * tokens // SPAN
    tap = key_tap(sub, ck_ref)
    widened(rows, recv_ref, [0], tokens)
    stacked = [
        sum(recv_ref[s, 4 * tokens :, :].astype(F32) for s in range(n, n + SPAN // tokens))
        for n in range(0, peers, SPAN // tokens)
    ]
    stacked.append(jnp.zeros((SPAN - spans * GATES, SPAN), F32))
    gates = jnp.concatenate(stacked, axis=0)
    decay, rate = gate_values(gates, sub, alog_ref, dt_ref)
    early_ref[...] = jnp.where(iota((8, SPAN), 0) < 2, decay[0:8], rate[0:8])
    skipped = later & (iota(gates.shape, 0) < GATES) & (iota(gates.shape, 1) < EDGE)
    decay = jnp.where(skipped, 0.0, decay)
    rate = jnp.where(skipped, 0.0, rate)
    lane_r, lane_c = iota((SPAN, SPAN), 0), iota((SPAN, SPAN), 1)
    upto = jnp.where(lane_r <= lane_c, 1.0, 0.0).astype(BF16)
    d_high, _ = halves(decay)
    d_mid, d_low = halves(decay - d_high.astype(F32))
    cum = dot(d_high, upto) + (dot(d_mid, upto) + dot(d_low, upto))
    growth = jnp.exp(cum)
    here = pltpu.roll(rate, rate.shape[0] - 2, 0)
    rest = jnp.exp(cum[:, SPAN - 1 :] - cum) * here
    which = place_in(iota(gates.shape, 0), GATES)
    mixed = jnp.where(which < 2, cum, pltpu.roll(growth, 2, 0))
    columns = jnp.transpose(jnp.where(which < 4, mixed, pltpu.roll(rest, 4, 0)))
    cols_ref[...] = columns
    lower = lane_r >= lane_c
    strict = lane_r > lane_c
    both = [(n, r) for n in range(spans) for r in range(2)]
    keys = []
    for n in range(spans):
        k_n = unit(convolved(rows, n * SPAN + 8 - EDGE, SPAN, slice(0, DK), tap), 1.0)
        keys_ref[n * SPAN : (n + 1) * SPAN, :] = k_n
        keys.append(k_n)
    keys_t = []
    for n in range(spans):
        kt_n = jnp.transpose(keys[n].astype(F32)).astype(BF16)
        keys_t_ref[n] = kt_n
        keys_t.append(kt_n)
    grams = [dot(keys[n], keys_t[n]) for n in range(spans)]
    for n, r in both:
        at = GATES * n + r
        gap = columns[:, at : at + 1] - cum[at : at + 1, :]
        within = jnp.exp(jnp.where(lower, gap, 0.0)) * here[at : at + 1, :]
        within_ref[r, n * SPAN : (n + 1) * SPAN, :] = jnp.where(lower, within, 0.0).astype(BF16)
        system = jnp.where(strict, within * -grams[n], 0.0)
        systems_ref[r, n, 0], systems_ref[r, n, 1] = halves(system)
        small_ref[r, n] = compacted(system)
    ends_ref[...] = jnp.broadcast_to(growth[:, SPAN - 1 :], ends_ref.shape)


def inverse_kernel(
    on_first, hop_ref, keys_ref, keys_t_ref, systems_ref, small_ref, cols_ref, t_ref, lin_ref
):
    del hop_ref
    spans = keys_t_ref.shape[0]
    both = [(n, r) for n in range(spans) for r in range(2)]

    @pl.when((lax.axis_index("half") == 0) == on_first)
    def _():
        compact = jnp.concatenate([small_ref[r, n] for n, r in both], axis=0)
        small = substituted(compact.reshape(len(both), SUB, SPAN))
        systems = [(systems_ref[r, n, 0], systems_ref[r, n, 1]) for n, r in both]
        inverses = inverted(systems, [small[i] for i in range(len(both))])
        scaled = []
        for i, (n, r) in enumerate(both):
            t_ref[r, n, 0], t_ref[r, n, 1] = inverses[i]
            at = GATES * n + r
            key = keys_ref[n * SPAN : (n + 1) * SPAN, :].astype(F32)
            right = (cols_ref[:, at + 2 : at + 3] * key).astype(BF16)
            scaled.append(jnp.concatenate([right, right], axis=0))
        w_mats = [dot(jnp.concatenate(t, axis=1), x) for t, x in zip(inverses, scaled)]
        weighed = []
        for (n, r), w_mat in zip(both, w_mats):
            at = GATES * n + r
            weighed.append((cols_ref[:, at + 4 : at + 5] * w_mat).astype(BF16))
        moved = [
            dot(keys_t_ref[n], jnp.concatenate(weighed[2 * n : 2 * n + 2], axis=1))
            for n in range(spans)
        ]
        for n, r in both:
            lin_ref[r, n] = moved[n][:, r * DK : (r + 1) * DK].astype(BF16)


def unwound(t_ref, n, r, x):
    both = jnp.concatenate([t_ref[r, n, 0], t_ref[r, n, 1]], axis=1)
    return dot(both, jnp.concatenate([x, x], axis=0))


def end_of(ends_ref, n, r):
    return ends_ref[GATES * n + r : GATES * n + r + 1, :]


def followed(span_map, state):
    end, moved, add = span_map
    return step(end, moved, state, halves(state)) + add


def composed(maps):
    if len(maps) == 1:
        return maps[0]
    half = len(maps) // 2
    end_a, moved_a, add_a = composed(maps[:half])
    end_b, moved_b, add_b = composed(maps[half:])
    high, low = halves(add_a)
    rights = jnp.concatenate(
        [
            jnp.concatenate([moved_a, high], axis=1),
            jnp.concatenate([jnp.zeros_like(moved_a), low], axis=1),
        ],
        axis=0,
    )
    passed = dot(jnp.concatenate([moved_b, moved_b], axis=1), rights)
    moved = end_b * moved_a.astype(F32) + end_a * moved_b.astype(F32) - passed[:, :DK]
    add = end_b * add_a - passed[:, DK:] + add_b
    return end_a * end_b, moved.astype(BF16), add


def step(end, moved, state, parts):
    both = jnp.concatenate([moved, moved], axis=1)
    return end * state - dot(both, jnp.concatenate(parts, axis=0))


def values_part(recv_ref, cv_ref, keys_t_ref, t_ref, cols_ref, rows, vs):
    sub = lax.axis_index("sub")
    tokens = (recv_ref.shape[1] - GATES) // 4
    spans = t_ref.shape[1]
    taps = value_taps(sub, cv_ref)
    widened(rows, recv_ref, [tokens, 2 * tokens], tokens)
    both = [(n, r) for n in range(spans) for r in range(2)]
    values = []
    for n, r in both:
        lanes = slice(r * DV, (r + 1) * DV)
        v_n = convolved(rows, n * SPAN + 8 - EDGE, SPAN, lanes, taps[r]).astype(BF16)
        vs[r, n * SPAN : (n + 1) * SPAN, :] = v_n
        values.append(v_n)
    solved = [unwound(t_ref, n, r, v) for (n, r), v in zip(both, values)]
    weighed = []
    for (n, r), u_mat in zip(both, solved):
        at = GATES * n + r
        weighed.append((cols_ref[:, at + 4 : at + 5] * u_mat).astype(BF16))
    moved = [
        dot(keys_t_ref[n], jnp.concatenate(weighed[2 * n : 2 * n + 2], axis=1))
        for n in range(spans)
    ]
    return [moved[n][:, r * DV : (r + 1) * DV] for n, r in both]


def opening_kernel(
    recv_ref, cv_ref, keys_t_ref, t_ref, lin_ref, ends_ref, cols_ref, hop_ref, vs_ref, xs_ref, adds_ref, rows
):
    first = lax.axis_index("half") == 0
    peers = recv_ref.shape[0]
    tokens = (recv_ref.shape[1] - GATES) // 4
    spans = t_ref.shape[1]
    edges = []
    for which in (3, 0, 1, 2):
        end = (which + 1) * tokens
        edges.append(recv_ref[peers - 1, end - 16 : end, :].astype(F32)[16 - EDGE :])
    edges.append(jnp.zeros((16 - 4 * EDGE, 128), F32))
    hop_ref[2 * DK :, :] = jnp.concatenate(edges, axis=0).astype(BF16)

    @pl.when(first)
    def _():
        adds = values_part(recv_ref, cv_ref, keys_t_ref, t_ref, cols_ref, rows, vs_ref)
        for n in range(spans):
            for r in range(2):
                adds_ref[r, n] = adds[2 * n + r]
        maps = [
            [(end_of(ends_ref, n, r), lin_ref[r, n], adds[2 * n + r]) for n in range(spans)]
            for r in range(2)
        ]
        states = [m[0][2] for m in maps]
        done = 1
        while done < spans:
            for r in range(2):
                if done > 1:
                    xs_ref[r, done] = jnp.concatenate(halves(states[r]), axis=0)
            later = [composed(m[done : 2 * done]) for m in maps]
            states = [followed(m, x) for m, x in zip(later, states)]
            done *= 2
        for r in range(2):
            hop_ref[r * DK : (r + 1) * DK, :] = states[r].astype(BF16)

    @pl.when(jnp.logical_not(first))
    def _():
        hop_ref[0 : 2 * DK, :] = jnp.zeros((2 * DK, DV), BF16)


def states_kernel(
    recv_ref,
    cv_ref,
    keys_t_ref,
    t_ref,
    lin_ref,
    ends_ref,
    cols_ref,
    values_ref,
    states_ref,
    *rest,
):
    *last_ref, rows = rest

    @pl.when(lax.axis_index("half") > 0)
    def _():
        spans = t_ref.shape[1]
        adds = values_part(recv_ref, cv_ref, keys_t_ref, t_ref, cols_ref, rows, values_ref)
        zero_half = jnp.zeros((DK, DV), F32)
        identity = jnp.where(iota((DK, DK), 0) == iota((DK, DK), 1), 1.0, 0.0)
        states = [
            jnp.concatenate(
                [adds[r], ends_ref[r : r + 1, :] * identity - lin_ref[r, 0].astype(F32)], axis=1
            )
            for r in range(2)
        ]
        for n in range(1, spans):
            for r in range(2):
                parts = halves(states[r])
                for i in range(2):
                    both_parts = [x[:, i * DV : (i + 1) * DV] for x in parts]
                    states_ref[i, r, n] = jnp.concatenate(both_parts, axis=0)
                add = jnp.concatenate([adds[2 * n + r], zero_half], axis=1)
                end = jnp.concatenate([end_of(ends_ref, n, r)] * 2, axis=1)
                states[r] = step(end, lin_ref[r, n], states[r], parts) + add
        for ref in last_ref:
            for r in range(2):
                ref[r] = states[r]


def span_rows(n):
    return slice(n * SPAN, (n + 1) * SPAN)


def twice(x, axis):
    return jnp.concatenate([x, x], axis=axis)


def asked(recv_ref, cq_ref, keys_ref, keys_t_ref, within_ref, query_rows):
    tokens = (recv_ref.shape[1] - GATES) // 4
    spans = keys_t_ref.shape[0]
    tap = key_tap(lax.axis_index("sub"), cq_ref)
    widened(query_rows, recv_ref, [3 * tokens], tokens)
    queries = [
        unit(convolved(query_rows, n * SPAN + 8 - EDGE, SPAN, slice(0, DK), tap), DK**-0.5)
        for n in range(spans)
    ]
    readers = [
        jnp.concatenate([keys_ref[span_rows(n), :], queries[n]], axis=0) for n in range(spans)
    ]
    scores = [dot(queries[n], keys_t_ref[n]) for n in range(spans)]
    inner = [
        (within_ref[r, span_rows(n), :].astype(F32) * scores[n]).astype(BF16)
        for n in range(spans)
        for r in range(2)
    ]
    return readers, inner


def first_outputs_kernel(
    recv_ref,
    cq_ref,
    keys_ref,
    keys_t_ref,
    t_ref,
    lin_ref,
    ends_ref,
    within_ref,
    cols_ref,
    values_ref,
    xs_ref,
    adds_ref,
    oa_ref,
    query_rows,
):
    @pl.when(lax.axis_index("half") == 0)
    def _():
        spans = t_ref.shape[1]
        both = [(n, r) for n in range(spans) for r in range(2)]
        readers, inner = asked(recv_ref, cq_ref, keys_ref, keys_t_ref, within_ref, query_rows)
        stacks, states = [], []
        for n in range(1, spans):
            if n == 1:
                states = [adds_ref[r, 0] for r in range(2)]
                stack = [jnp.concatenate(halves(x), axis=0) for x in states]
            elif n & (n - 1) == 0:
                stack = [xs_ref[r, n] for r in range(2)]
                states = [x[:DK].astype(F32) + x[DK:].astype(F32) for x in stack]
            else:
                states = [
                    followed(
                        (end_of(ends_ref, n - 1, r), lin_ref[r, n - 1], adds_ref[r, n - 1]),
                        states[r],
                    )
                    for r in range(2)
                ]
                stack = [jnp.concatenate(halves(x), axis=0) for x in states]
            stacks.append(jnp.concatenate(stack, axis=1))
        reads = [dot(twice(readers[n], 1), stacks[n - 1]) for n in range(1, spans)]
        rests, seen = [], []
        for n, r in both:
            lanes = slice(r * DV, (r + 1) * DV)
            value = values_ref[r, span_rows(n), :]
            if n == 0:
                rests.append(value)
                seen.append(None)
            else:
                growth = cols_ref[:, GATES * n + 2 + r : GATES * n + 3 + r]
                read = growth * reads[n - 1][:SPAN, lanes]
                rests.append((value.astype(F32) - read).astype(BF16))
                seen.append(growth * reads[n - 1][SPAN:, lanes])
        fresh = [unwound(t_ref, n, r, x).astype(BF16) for (n, r), x in zip(both, rests)]
        spreads = [dot(w, x) for w, x in zip(inner, fresh)]
        for (n, r), x, y in zip(both, spreads, seen):
            oa_ref[r, span_rows(n), :] = x if y is None else x + y


def later_outputs_kernel(
    recv_ref,
    cq_ref,
    keys_ref,
    keys_t_ref,
    t_ref,
    within_ref,
    cols_ref,
    values_ref,
    states_ref,
    oa_ref,
    om_ref,
    query_rows,
):
    @pl.when(lax.axis_index("half") > 0)
    def _():
        spans = t_ref.shape[1]
        both = [(n, r) for n in range(spans) for r in range(2)]
        readers, inner = asked(recv_ref, cq_ref, keys_ref, keys_t_ref, within_ref, query_rows)
        zero_half = jnp.zeros((SPAN, DV), F32)
        reads = [
            dot(
                twice(readers[n], 1),
                jnp.concatenate([states_ref[0, r, n], states_ref[1, r, n]], axis=1),
            )
            if n > 0
            else None
            for n, r in both
        ]
        rests, seen = [], []
        for (n, r), read in zip(both, reads):
            value = values_ref[r, span_rows(n), :].astype(F32)
            growth = cols_ref[:, GATES * n + 2 + r : GATES * n + 3 + r]
            if n == 0:
                reader = readers[n].astype(F32)
                rest = jnp.concatenate([value, -(growth * reader[:SPAN])], axis=1)
                seen.append(jnp.concatenate([zero_half, growth * reader[SPAN:]], axis=1))
            else:
                rest = jnp.concatenate([value, zero_half], axis=1) - growth * read[:SPAN]
                seen.append(growth * read[SPAN:])
            rests.append(rest.astype(BF16))
        fresh = [unwound(t_ref, n, r, x).astype(BF16) for (n, r), x in zip(both, rests)]
        spreads = [dot(w, x) for w, x in zip(inner, fresh)]
        for (n, r), x, y in zip(both, spreads, seen):
            out = x + y
            oa_ref[r, span_rows(n), :] = out[:, :DV]
            om_ref[r, span_rows(n), :] = out[:, DV:].astype(BF16)


def first_tokens(hop_ref, recv_ref, early_ref, cq_ref, ck_ref, cv_ref, rows):
    sub = lax.axis_index("sub")
    tokens = (recv_ref.shape[1] - GATES) // 4
    taps = [key_tap(sub, cq_ref), key_tap(sub, ck_ref)] + value_taps(sub, cv_ref)
    results = []
    edges = hop_ref[2 * DK :, :].astype(F32)
    for g, first in enumerate((3, 0, 1, 2)):
        lanes = slice(g * 128, (g + 1) * 128)
        start = first * tokens
        rows[16 - EDGE : 16, lanes] = edges[EDGE * g : EDGE * (g + 1)]
        rows[16:32, lanes] = recv_ref[0, start : start + 16, :].astype(F32)
        results.append(convolved(rows, 16 - EDGE, 8, lanes, taps[g]))
    q_cols = jnp.transpose(unit(results[0], DK**-0.5).astype(F32))
    k_cols = jnp.transpose(unit(results[1], 1.0).astype(F32))
    gates = early_ref[...]
    line = iota((8, DV), 0)
    finals, outputs = [], []
    for r in range(2):
        values = results[2 + r].astype(BF16).astype(F32)
        entering = hop_ref[r * DK : (r + 1) * DK, :].astype(F32)
        state, out = entering, jnp.zeros((8, DV), F32)
        for t in range(EDGE):
            k_t, q_t = k_cols[:, t : t + 1], q_cols[:, t : t + 1]
            state = jnp.exp(gates[r : r + 1, t : t + 1]) * state
            held = jnp.sum(k_t * state, axis=0, keepdims=True)
            state = state + k_t * (
                gates[2 + r : 3 + r, t : t + 1] * (values[t : t + 1, :] - held)
            )
            out = jnp.where(line == t, jnp.sum(q_t * state, axis=0, keepdims=True), out)
        finals.append(state)
        outputs.append(out)
    return finals, outputs


def finish_kernel(
    hop_ref,
    recv_ref,
    early_ref,
    cq_ref,
    ck_ref,
    cv_ref,
    gain_ref,
    first_oa,
    oa_ref,
    om_ref,
    out_ref,
    rows,
):
    peers, tokens = out_ref.shape[0], out_ref.shape[1] // 2
    first = lax.axis_index("half") == 0
    gain = gain_ref[...]
    chunks = 4
    part, peer_part = peers * tokens // chunks, peers // chunks

    def put(c, r, core):
        scale = lax.rsqrt(jnp.mean(core * core, axis=-1, keepdims=True) + EPS)
        normed = (core * scale * gain).astype(BF16)
        here = slice(c * peer_part, (c + 1) * peer_part)
        out_ref[here, r * tokens : (r + 1) * tokens, :] = normed.reshape(peer_part, tokens, DV)

    @pl.when(first)
    def _():
        for c in range(chunks):
            for r in range(2):
                put(c, r, first_oa[r, c * part : (c + 1) * part, :])

    @pl.when(jnp.logical_not(first))
    def _():
        finals, outputs = first_tokens(hop_ref, recv_ref, early_ref, cq_ref, ck_ref, cv_ref, rows)
        replaced = iota((8, DV), 0) < EDGE
        passed = [dot(om_ref[r], finals[r].astype(BF16)) for r in range(2)]
        for c in range(chunks):
            at = c * part
            for r in range(2):
                core = oa_ref[r, at : at + part, :] + passed[r][at : at + part]
                if c == 0:
                    core = jnp.concatenate(
                        [jnp.where(replaced, outputs[r], core[0:8]), core[8:]], axis=0
                    )
                put(c, r, core)


def advance_kernel(
    hop_ref, recv_ref, early_ref, cq_ref, ck_ref, cv_ref, hop_own, last_ref, next_ref, rows
):
    finals, _ = first_tokens(hop_ref, recv_ref, early_ref, cq_ref, ck_ref, cv_ref, rows)
    first = lax.axis_index("half") == 0
    for r in range(2):
        last = last_ref[r]
        through = mm_parts(halves(last[:, DV:]), halves(finals[r]))
        own = hop_own[r * DK : (r + 1) * DK, :].astype(F32)
        moved = jnp.where(first, own, through + last[:, :DV])
        next_ref[r * DK : (r + 1) * DK, :] = moved.astype(BF16)
    next_ref[2 * DK :, :] = hop_own[2 * DK :, :]


def gate_kernel(heads_axis, normed_ref, z_ref, out_ref, made, sems):
    subs, tokens = normed_ref.shape[0] // heads_axis, z_ref.shape[0]
    width = subs * 2 * DV
    copies = []
    for head in range(heads_axis):
        for sub in range(subs):
            for r in range(2):
                at = (2 * (head * subs + sub) + r) * DV
                gate = silu(z_ref[:, at : at + DV].astype(F32))
                here = slice(r * tokens, (r + 1) * tokens)
                value = normed_ref[sub * heads_axis + head, here, :].astype(F32)
                made[:, at : at + DV] = (value * gate).astype(BF16)
        lanes = pl.ds(head * width, width)
        copy = pltpu.make_async_copy(made.at[:, lanes], out_ref.at[:, lanes], sems.at[head])
        copy.start()
        copies.append(copy)
    for copy in copies:
        copy.wait()


VMEM = pl.BlockSpec(memory_space=pltpu.VMEM)
SMEM = pl.BlockSpec(memory_space=pltpu.SMEM)
ANY = pl.BlockSpec(memory_space=pl.ANY)


def near(x):
    return pltpu.with_memory_space_constraint(x, pltpu.VMEM)


def far(x):
    return pltpu.with_memory_space_constraint(x, pltpu.HBM)


def call(kernel, outs, in_specs, scratch=(), out_spec=VMEM, flops=1 << 26, moved=1 << 21):
    return pl.pallas_call(
        kernel,
        out_shape=outs,
        in_specs=in_specs,
        out_specs=jax.tree.map(lambda _: out_spec, outs),
        scratch_shapes=list(scratch),
        compiler_params=pltpu.CompilerParams(vmem_limit_bytes=VMEM_BYTES),
        cost_estimate=pl.CostEstimate(flops=flops, bytes_accessed=moved, transcendentals=0),
    )


def local(
    q_rows,
    k_rows,
    v_rows,
    z_rows,
    a_rows,
    b_rows,
    conv_q,
    conv_k,
    conv_v,
    a_log,
    dt_bias,
    norm_gain,
):
    shards, subs, heads_axis = (lax.axis_size(a) for a in ("half", "sub", "head"))
    peers, tokens = subs * heads_axis, q_rows.shape[0]
    total = peers * tokens
    spans = total // SPAN
    group = ("sub", "head")
    route = [(i, i + 1) for i in range(shards - 1)]
    conv_q, conv_k, conv_v = near(conv_q), near(conv_k), near(conv_v)
    gain = near(norm_gain.reshape(1, DV))
    inputs = [far(x) for x in (q_rows, k_rows, v_rows, a_rows.T, b_rows.T)]
    packed = call(
        functools.partial(pack_kernel, heads_axis),
        pltpu.VMEM((peers, GATES + 4 * tokens, 128), BF16),
        [ANY] * 5,
        [pltpu.VMEM(x.shape, BF16) for x in inputs] + [pltpu.SemaphoreType.DMA((5,))],
        flops=1 << 20,
    )(*inputs)
    blocks = near(lax.all_to_all(packed, group, 0, 0, tiled=True))
    made = call(
        systems_kernel,
        (
            pltpu.VMEM((total, DK), BF16),
            pltpu.VMEM((spans, DK, SPAN), BF16),
            pltpu.VMEM((2, spans, 2, SPAN, SPAN), BF16),
            pltpu.VMEM((2, spans, SUB, SPAN), F32),
            pltpu.VMEM((SPAN, DK), F32),
            pltpu.VMEM((2, total, SPAN), BF16),
            pltpu.VMEM((SPAN, SPAN), F32),
            pltpu.VMEM((8, SPAN), F32),
        ),
        [VMEM, VMEM, SMEM, SMEM, VMEM, VMEM, VMEM],
        [pltpu.VMEM((8 + total, DK), F32)],
        flops=1 << 32,
    )(blocks, conv_k, a_log, dt_bias, conv_q, conv_v, gain)
    keys, keys_t, systems, small, ends, within, cols, early = (near(x) for x in made)
    map_shapes = (
        pltpu.VMEM((2, spans, 2, SPAN, SPAN), BF16),
        pltpu.VMEM((2, spans, DK, DK), BF16),
    )

    def inverses_of(on_first, after):
        solved = call(
            functools.partial(inverse_kernel, on_first), map_shapes, [VMEM] * 6, flops=1 << 32
        )(after, keys, keys_t, systems, small, cols)
        return [near(x) for x in solved]

    inverses, lins = inverses_of(True, early)
    hop, values, starts, adds = call(
        opening_kernel,
        (
            pltpu.VMEM((2 * DK + 16, 128), BF16),
            pltpu.VMEM((2, total, DV), BF16),
            pltpu.VMEM((2, spans, 2 * DK, DV), BF16),
            pltpu.VMEM((2, spans, DK, DV), F32),
        ),
        [VMEM] * 7,
        [pltpu.VMEM((8 + total, 2 * DV), F32)],
        flops=1 << 32,
    )(blocks, conv_v, keys_t, inverses, lins, ends, cols)
    entering = near(lax.ppermute(hop, "half", route))
    hop, values, starts, adds = (near(x) for x in (hop, values, starts, adds))
    first_out = call(
        first_outputs_kernel,
        pltpu.VMEM((2, total, DV), F32),
        [VMEM] * 12,
        [pltpu.VMEM((8 + total, DK), F32)],
        flops=1 << 32,
    )(
        blocks,
        conv_q,
        keys,
        keys_t,
        inverses,
        lins,
        ends,
        within,
        cols,
        values,
        starts,
        adds,
    )
    later_inverses, later_lins = inverses_of(False, hop)
    read_on = [pltpu.VMEM((2, DK, 2 * DV), F32)] if shards > 2 else []
    later_values, states, *last = call(
        states_kernel,
        (
            pltpu.VMEM((2, total, DV), BF16),
            pltpu.VMEM((2, 2, spans, 2 * DK, DV), BF16),
            *read_on,
        ),
        [VMEM] * 7,
        [pltpu.VMEM((8 + total, 2 * DV), F32)],
        flops=1 << 32,
    )(blocks, conv_v, keys_t, later_inverses, later_lins, ends, cols)
    out_a, out_m = call(
        later_outputs_kernel,
        (pltpu.VMEM((2, total, DV), F32), pltpu.VMEM((2, total, DV), BF16)),
        [VMEM] * 9,
        [pltpu.VMEM((8 + total, DK), F32)],
        flops=1 << 32,
    )(
        blocks,
        conv_q,
        keys,
        keys_t,
        later_inverses,
        within,
        cols,
        near(later_values),
        near(states),
    )
    for _ in range(shards - 2):
        moved = call(
            advance_kernel,
            pltpu.VMEM(hop.shape, BF16),
            [VMEM] * 8,
            [pltpu.VMEM((32, 512), F32)],
        )(entering, blocks, early, conv_q, conv_k, conv_v, hop, near(last[0]))
        entering = near(lax.ppermute(moved, "half", route))
    normed = call(
        finish_kernel,
        pltpu.VMEM((peers, 2 * tokens, DV), BF16),
        [VMEM] * 10,
        [pltpu.VMEM((32, 512), F32)],
    )(
        entering,
        blocks,
        early,
        conv_q,
        conv_k,
        conv_v,
        gain,
        near(first_out),
        near(out_a),
        near(out_m),
    )
    returned = near(lax.all_to_all(normed, group, 0, 0, tiled=True))
    return call(
        functools.partial(gate_kernel, heads_axis),
        jax.ShapeDtypeStruct(z_rows.shape, BF16),
        [VMEM] * 2,
        [pltpu.VMEM(z_rows.shape, BF16), pltpu.SemaphoreType.DMA((heads_axis,))],
        ANY,
    )(returned, z_rows)


def solution(mesh):
    heads_axis = mesh.shape["head"]
    subs = KH // heads_axis
    regrouped = Mesh(
        mesh.devices.reshape(mesh.shape["ctx"] // subs, subs, heads_axis), ("half", "sub", "head")
    )
    row = P(("half", "sub", "head"), None)
    placed = (row,) * 6 + (P(None, "head"),) * 3 + (P("head"),) * 2 + (P(),)
    return jax.shard_map(local, mesh=regrouped, in_specs=placed, out_specs=row, check_vma=False)
```

```python
import functools

import jax
import jax.numpy as jnp
from jax import lax
from jax.experimental import pallas as pl
from jax.experimental.pallas import tpu as pltpu
from jax.sharding import Mesh, PartitionSpec as P

DK = 128
DV = 128
CONV = 4
KH = 16
SUB = 16
SPAN = 128
EDGE = CONV - 1
EPS = 1e-06
F32 = jnp.float32
BF16 = jnp.bfloat16
VMEM_BYTES = 24 * 1024 * 1024
GATES = 8


def dot(a, b, dims=((1,), (0,))):
    return lax.dot_general(a, b, (dims, ((), ())), preferred_element_type=F32)


def halves(x):
    high = x.astype(BF16)
    return high, (x - high.astype(F32)).astype(BF16)


def mm_parts(a, b):
    left = jnp.concatenate([a[0], a[1], a[0]], axis=1)
    return dot(left, jnp.concatenate([b[0], b[0], b[1]], axis=0))


def silu(x):
    half = 0.5 * x
    return half + half * jnp.tanh(half)


def unit(y, factor):
    scale = lax.rsqrt(jnp.sum(y * y, axis=-1, keepdims=True) + EPS)
    return (y * scale * factor).astype(BF16)


def iota(shape, dim):
    return lax.broadcasted_iota(jnp.int32, shape, dim)


def block_of(x, size):
    return lax.shift_right_logical(x, jnp.full(x.shape, size.bit_length() - 1, jnp.int32))


def place_in(x, size):
    return x & (size - 1)


def pack_kernel(
    heads_axis, q_in, k_in, v_in, at_in, bt_in, out_ref, q_ref, k_ref, v_ref, at_ref, bt_ref, sems
):
    peers, tokens = out_ref.shape[0], q_ref.shape[0]
    pairs = ((at_in, at_ref), (bt_in, bt_ref), (k_in, k_ref), (v_in, v_ref), (q_in, q_ref))
    copies = [pltpu.make_async_copy(a, b, sems.at[i]) for i, (a, b) in enumerate(pairs)]
    for copy in copies:
        copy.start()
    subs = peers // heads_axis
    key_heads = [(dest % heads_axis) * subs + dest // heads_axis for dest in range(peers)]
    for copy in copies[:2]:
        copy.wait()
    value_heads = at_ref.shape[0]
    row, entry = iota((peers * GATES, value_heads), 0), iota((peers * GATES, value_heads), 1)
    dest, which = block_of(row, GATES), place_in(row, GATES)
    first = 2 * (place_in(dest, heads_axis) * subs + block_of(dest, heads_axis))
    pick_a = jnp.where((which < 2) & (entry == first + which), 1.0, 0.0).astype(BF16)
    pick_b = jnp.where(
        (which >= 2) & (which < 4) & (entry == first + which - 2), 1.0, 0.0
    ).astype(BF16)
    picked = (dot(pick_a, at_ref[...]) + dot(pick_b, bt_ref[...])).astype(BF16)
    lane_shift = tokens * lax.rem(lax.axis_index("head"), SPAN // tokens)
    place = jnp.where(
        iota((tokens, SPAN), 1) == iota((tokens, SPAN), 0) + lane_shift, 1.0, 0.0
    ).astype(BF16)
    gates = dot(picked, place).astype(BF16)
    for dest in range(peers):
        out_ref[dest, 4 * tokens :, :] = gates[GATES * dest : GATES * (dest + 1), :]

    def laid(ref, lane, start):
        for dest, key_head in enumerate(key_heads):
            at = lane(key_head) * 128
            out_ref[dest, start * tokens : (start + 1) * tokens, :] = ref[
                :, at : at + 128
            ]

    copies[2].wait()
    laid(k_ref, lambda key_head: key_head, 0)
    copies[3].wait()
    laid(v_ref, lambda key_head: 2 * key_head, 1)
    laid(v_ref, lambda key_head: 2 * key_head + 1, 2)
    copies[4].wait()
    laid(q_ref, lambda key_head: key_head, 3)


def compacted(system):
    size = system.shape[0]
    diagonal = block_of(iota((size, size), 0), SUB) == block_of(iota((size, size), 1), SUB)
    return jnp.sum(jnp.where(diagonal, system, 0.0).reshape(size // SUB, SUB, size), axis=0)


def substituted(compact):
    count, _, size = compact.shape
    flat = compact.reshape(count * SUB, size)
    lane, line = iota(flat.shape, 1), iota(flat.shape, 0)
    solved = jnp.where(place_in(lane ^ line, SUB) == 0, 1.0, 0.0).reshape(count, SUB, size)
    for m in range(SUB - 1):
        source = (lane & ~(SUB - 1)) | m
        spread = jnp.take_along_axis(flat, source, axis=1, mode="promise_in_bounds")
        solved = solved + spread.reshape(count, SUB, size) * solved[:, m : m + 1, :]
    return solved


def inverted(systems, small, meanwhile=lambda: None):
    size = systems[0][0].shape[0]
    row, col = iota((size, size), 0), iota((size, size), 1)
    placed = jnp.where(block_of(row, SUB) == block_of(col, SUB), 1.0, 0.0).astype(BF16)
    identity = jnp.where(row == col, 1.0, 0.0)
    rough = [
        jnp.concatenate([block.astype(BF16)] * (size // SUB), axis=0) * placed for block in small
    ]
    blank = jnp.zeros((size, size), BF16)
    width = SUB
    while width < size:
        odd = [(j, j + width) for j in range(width, size, 2 * width)]

        def rows_of(x):
            return jnp.concatenate([x[lo:hi] for lo, hi in odd], axis=0)

        def woven(even, x):
            pieces = []
            for j, (lo, hi) in enumerate(odd):
                pieces += [even[lo - width : lo], x[j * width : (j + 1) * width]]
            return jnp.concatenate(pieces, axis=0)

        below = rows_of(block_of(row ^ col, 2 * width)) + rows_of(col & width) == 0
        own = rows_of(identity)
        firsts = [dot(rows_of(n[0]), t) for n, t in zip(systems, rough)]
        meanwhile()
        rights = [
            woven(blank, jnp.where(below, first, own).astype(BF16)) for first in firsts
        ]
        grown = [dot(rows_of(t), right).astype(BF16) for t, right in zip(rough, rights)]
        rough = [woven(t, g) for t, g in zip(rough, grown)]
        width *= 2
    products = [
        dot(jnp.concatenate(n, axis=1), jnp.concatenate([t, t], axis=0))
        for n, t in zip(systems, rough)
    ]
    rests = [
        (identity - t.astype(F32) + product).astype(BF16) for t, product in zip(rough, products)
    ]
    return [halves(t.astype(F32) + dot(t, rest)) for t, rest in zip(rough, rests)]


def gate_values(gates, sub, alog_ref, dt_ref):
    second = place_in(iota(gates.shape, 0), GATES) == 1
    a_log = jnp.where(second, alog_ref[2 * sub + 1], alog_ref[2 * sub])
    dt_bias = jnp.where(second, dt_ref[2 * sub + 1], dt_ref[2 * sub])
    shifted = gates + dt_bias
    soft = jnp.maximum(shifted, 0.0) + jnp.log1p(jnp.exp(-jnp.abs(shifted)))
    return -jnp.exp(a_log) * soft, 1.0 / (1.0 + jnp.exp(-gates))


def convolved(rows, at, count, lanes, tap):
    summed = tap[0:1] * rows[at : at + count, lanes]
    for j in range(1, CONV):
        summed = summed + tap[j : j + 1] * rows[at + j : at + j + count, lanes]
    return silu(summed)


def key_tap(sub, tap_ref):
    return tap_ref[:, pl.ds(pl.multiple_of(sub * DK, 128), DK)]


def value_taps(sub, cv_ref):
    lane = pl.multiple_of(sub * 2 * DV, 128)
    return [cv_ref[:, pl.ds(pl.multiple_of(lane + r * DV, 128), DV)] for r in range(2)]


def widened(rows, recv_ref, starts, tokens):
    rows[0:8, :] = jnp.zeros((8, rows.shape[1]), F32)
    for s in range(recv_ref.shape[0]):
        for g, start in enumerate(starts):
            rows[8 + s * tokens : 8 + (s + 1) * tokens, g * 128 : (g + 1) * 128] = recv_ref[
                s, start : start + tokens, :
            ].astype(F32)


def systems_kernel(
    recv_ref,
    ck_ref,
    alog_ref,
    dt_ref,
    *refs,
):
    systems_of(recv_ref, ck_ref, alog_ref, dt_ref, *refs[3:])


def systems_of(
    recv_ref,
    ck_ref,
    alog_ref,
    dt_ref,
    keys_ref,
    keys_t_ref,
    systems_ref,
    small_ref,
    ends_ref,
    within_ref,
    cols_ref,
    early_ref,
    rows,
):
    sub = lax.axis_index("sub")
    later = lax.axis_index("half") > 0
    peers = recv_ref.shape[0]
    tokens = (recv_ref.shape[1] - GATES) // 4
    spans = peers * tokens // SPAN
    tap = key_tap(sub, ck_ref)
    widened(rows, recv_ref, [0], tokens)
    stacked = [
        sum(recv_ref[s, 4 * tokens :, :].astype(F32) for s in range(n, n + SPAN // tokens))
        for n in range(0, peers, SPAN // tokens)
    ]
    stacked.append(jnp.zeros((SPAN - spans * GATES, SPAN), F32))
    gates = jnp.concatenate(stacked, axis=0)
    decay, rate = gate_values(gates, sub, alog_ref, dt_ref)
    early_ref[...] = jnp.where(iota((8, SPAN), 0) < 2, decay[0:8], rate[0:8])
    skipped = later & (iota(gates.shape, 0) < GATES) & (iota(gates.shape, 1) < EDGE)
    decay = jnp.where(skipped, 0.0, decay)
    rate = jnp.where(skipped, 0.0, rate)
    lane_r, lane_c = iota((SPAN, SPAN), 0), iota((SPAN, SPAN), 1)
    upto = jnp.where(lane_r <= lane_c, 1.0, 0.0).astype(BF16)
    d_high, _ = halves(decay)
    d_mid, d_low = halves(decay - d_high.astype(F32))
    cum = dot(d_high, upto) + (dot(d_mid, upto) + dot(d_low, upto))
    growth = jnp.exp(cum)
    here = pltpu.roll(rate, rate.shape[0] - 2, 0)
    rest = jnp.exp(cum[:, SPAN - 1 :] - cum) * here
    which = place_in(iota(gates.shape, 0), GATES)
    mixed = jnp.where(which < 2, cum, pltpu.roll(growth, 2, 0))
    columns = jnp.transpose(jnp.where(which < 4, mixed, pltpu.roll(rest, 4, 0)))
    cols_ref[...] = columns
    lower = lane_r >= lane_c
    strict = lane_r > lane_c
    both = [(n, r) for n in range(spans) for r in range(2)]
    keys = []
    for n in range(spans):
        k_n = unit(convolved(rows, n * SPAN + 8 - EDGE, SPAN, slice(0, DK), tap), 1.0)
        keys_ref[n * SPAN : (n + 1) * SPAN, :] = k_n
        keys.append(k_n)
    keys_t = []
    for n in range(spans):
        kt_n = jnp.transpose(keys[n].astype(F32)).astype(BF16)
        keys_t_ref[n] = kt_n
        keys_t.append(kt_n)
    grams = [dot(keys[n], keys_t[n]) for n in range(spans)]
    for n, r in both:
        at = GATES * n + r
        gap = columns[:, at : at + 1] - cum[at : at + 1, :]
        within = jnp.exp(jnp.where(lower, gap, 0.0)) * here[at : at + 1, :]
        within_ref[r, n * SPAN : (n + 1) * SPAN, :] = jnp.where(lower, within, 0.0).astype(BF16)
        system = jnp.where(strict, within * -grams[n], 0.0)
        systems_ref[r, n, 0], systems_ref[r, n, 1] = halves(system)
        small_ref[r, n] = compacted(system)
    ends_ref[...] = jnp.broadcast_to(growth[:, SPAN - 1 :], ends_ref.shape)


def inverse_kernel(
    hop_ref, keys_ref, keys_t_ref, systems_ref, small_ref, cols_ref, t_ref, lin_ref
):
    del hop_ref
    spans = keys_t_ref.shape[0]
    both = [(n, r) for n in range(spans) for r in range(2)]

    @pl.when(lax.axis_index("half") > 0)
    def _():
        compact = jnp.concatenate([small_ref[r, n] for n, r in both], axis=0)
        small = substituted(compact.reshape(len(both), SUB, SPAN))
        systems = [(systems_ref[r, n, 0], systems_ref[r, n, 1]) for n, r in both]
        inverses = inverted(systems, [small[i] for i in range(len(both))])
        scaled = []
        for i, (n, r) in enumerate(both):
            t_ref[r, n, 0], t_ref[r, n, 1] = inverses[i]
            at = GATES * n + r
            key = keys_ref[n * SPAN : (n + 1) * SPAN, :].astype(F32)
            right = (cols_ref[:, at + 2 : at + 3] * key).astype(BF16)
            scaled.append(jnp.concatenate([right, right], axis=0))
        w_mats = [dot(jnp.concatenate(t, axis=1), x) for t, x in zip(inverses, scaled)]
        weighed = []
        for (n, r), w_mat in zip(both, w_mats):
            at = GATES * n + r
            weighed.append((cols_ref[:, at + 4 : at + 5] * w_mat).astype(BF16))
        moved = [
            dot(keys_t_ref[n], jnp.concatenate(weighed[2 * n : 2 * n + 2], axis=1))
            for n in range(spans)
        ]
        for n, r in both:
            lin_ref[r, n] = moved[n][:, r * DK : (r + 1) * DK].astype(BF16)


def unwound(t_ref, n, r, x):
    both = jnp.concatenate([t_ref[r, n, 0], t_ref[r, n, 1]], axis=1)
    return dot(both, jnp.concatenate([x, x], axis=0))


def end_of(ends_ref, n, r):
    return ends_ref[GATES * n + r : GATES * n + r + 1, :]


def followed(span_map, state):
    end, moved, add = span_map
    return step(end, moved, state, halves(state)) + add


def composed(maps):
    if len(maps) == 1:
        return maps[0]
    half = len(maps) // 2
    end_a, moved_a, add_a = composed(maps[:half])
    end_b, moved_b, add_b = composed(maps[half:])
    high, low = halves(add_a)
    rights = jnp.concatenate(
        [
            jnp.concatenate([moved_a, high], axis=1),
            jnp.concatenate([jnp.zeros_like(moved_a), low], axis=1),
        ],
        axis=0,
    )
    passed = dot(jnp.concatenate([moved_b, moved_b], axis=1), rights)
    moved = end_b * moved_a.astype(F32) + end_a * moved_b.astype(F32) - passed[:, :DK]
    add = end_b * add_a - passed[:, DK:] + add_b
    return end_a * end_b, moved.astype(BF16), add


def step(end, moved, state, parts):
    both = jnp.concatenate([moved, moved], axis=1)
    return end * state - dot(both, jnp.concatenate(parts, axis=0))


def values_part(recv_ref, cv_ref, keys_t_ref, t_ref, cols_ref, rows, vs):
    sub = lax.axis_index("sub")
    tokens = (recv_ref.shape[1] - GATES) // 4
    spans = t_ref.shape[1]
    taps = value_taps(sub, cv_ref)
    widened(rows, recv_ref, [tokens, 2 * tokens], tokens)
    both = [(n, r) for n in range(spans) for r in range(2)]
    values = []
    for n, r in both:
        lanes = slice(r * DV, (r + 1) * DV)
        v_n = convolved(rows, n * SPAN + 8 - EDGE, SPAN, lanes, taps[r]).astype(BF16)
        vs[r, n * SPAN : (n + 1) * SPAN, :] = v_n
        values.append(v_n)
    solved = [unwound(t_ref, n, r, v) for (n, r), v in zip(both, values)]
    weighed = []
    for (n, r), u_mat in zip(both, solved):
        at = GATES * n + r
        weighed.append((cols_ref[:, at + 4 : at + 5] * u_mat).astype(BF16))
    moved = [
        dot(keys_t_ref[n], jnp.concatenate(weighed[2 * n : 2 * n + 2], axis=1))
        for n in range(spans)
    ]
    return [moved[n][:, r * DV : (r + 1) * DV] for n, r in both]


def opening_kernel(
    recv_ref,
    cv_ref,
    keys_ref,
    keys_t_ref,
    systems_ref,
    small_ref,
    ends_ref,
    cols_ref,
    hop_ref,
    t_ref,
    lin_ref,
    vs_ref,
    xs_ref,
    adds_ref,
    rows,
):
    first = lax.axis_index("half") == 0
    peers = recv_ref.shape[0]
    tokens = (recv_ref.shape[1] - GATES) // 4
    spans = keys_t_ref.shape[0]
    edges = []
    for which in (3, 0, 1, 2):
        end = (which + 1) * tokens
        edges.append(recv_ref[peers - 1, end - 16 : end, :].astype(F32)[16 - EDGE :])
    edges.append(jnp.zeros((16 - 4 * EDGE, 128), F32))
    hop_ref[2 * DK :, :] = jnp.concatenate(edges, axis=0).astype(BF16)

    @pl.when(first)
    def _():
        both = [(n, r) for n in range(spans) for r in range(2)]
        taps = value_taps(lax.axis_index("sub"), cv_ref)
        widened(rows, recv_ref, [tokens, 2 * tokens], tokens)
        waiting = list(both)

        def meanwhile():
            for n, r in waiting[:6]:
                lanes = slice(r * DV, (r + 1) * DV)
                value = convolved(rows, n * SPAN + 8 - EDGE, SPAN, lanes, taps[r])
                vs_ref[r, n * SPAN : (n + 1) * SPAN, :] = value.astype(BF16)
            del waiting[:6]

        compact = jnp.concatenate([small_ref[r, n] for n, r in both], axis=0)
        small = substituted(compact.reshape(len(both), SUB, SPAN))
        systems = [(systems_ref[r, n, 0], systems_ref[r, n, 1]) for n, r in both]
        inverses = inverted(systems, [small[i] for i in range(len(both))], meanwhile)
        while waiting:
            meanwhile()
        rights = []
        for i, (n, r) in enumerate(both):
            t_ref[r, n, 0], t_ref[r, n, 1] = inverses[i]
            at = GATES * n + r
            here = slice(n * SPAN, (n + 1) * SPAN)
            key = (cols_ref[:, at + 2 : at + 3] * keys_ref[here, :].astype(F32)).astype(BF16)
            right = jnp.concatenate([key, vs_ref[r, here, :]], axis=1)
            rights.append(jnp.concatenate([right, right], axis=0))
        solved = [dot(jnp.concatenate(t, axis=1), x) for t, x in zip(inverses, rights)]
        weighed = []
        for (n, r), x in zip(both, solved):
            at = GATES * n + r
            weighed.append((cols_ref[:, at + 4 : at + 5] * x).astype(BF16))
        moved = [
            dot(keys_t_ref[n], jnp.concatenate(weighed[2 * n : 2 * n + 2], axis=1))
            for n in range(spans)
        ]
        adds = []
        for n, r in both:
            at = 2 * r * DK
            lin_ref[r, n] = moved[n][:, at : at + DK].astype(BF16)
            adds.append(moved[n][:, at + DK : at + 2 * DK])
            adds_ref[r, n] = adds[-1]
        maps = [
            [(end_of(ends_ref, n, r), lin_ref[r, n], adds[2 * n + r]) for n in range(spans)]
            for r in range(2)
        ]
        states = [m[0][2] for m in maps]
        done = 1
        while done < spans:
            for r in range(2):
                if done > 1:
                    xs_ref[r, done] = jnp.concatenate(halves(states[r]), axis=0)
            later = [composed(m[done : 2 * done]) for m in maps]
            states = [followed(m, x) for m, x in zip(later, states)]
            done *= 2
        for r in range(2):
            hop_ref[r * DK : (r + 1) * DK, :] = states[r].astype(BF16)

    @pl.when(jnp.logical_not(first))
    def _():
        hop_ref[0 : 2 * DK, :] = jnp.zeros((2 * DK, DV), BF16)


def states_kernel(
    recv_ref,
    cv_ref,
    keys_t_ref,
    t_ref,
    lin_ref,
    ends_ref,
    cols_ref,
    values_ref,
    states_ref,
    *rest,
):
    *last_ref, rows = rest

    @pl.when(lax.axis_index("half") > 0)
    def _():
        spans = t_ref.shape[1]
        adds = values_part(recv_ref, cv_ref, keys_t_ref, t_ref, cols_ref, rows, values_ref)
        zero_half = jnp.zeros((DK, DV), F32)
        identity = jnp.where(iota((DK, DK), 0) == iota((DK, DK), 1), 1.0, 0.0)
        states = [
            jnp.concatenate(
                [adds[r], ends_ref[r : r + 1, :] * identity - lin_ref[r, 0].astype(F32)], axis=1
            )
            for r in range(2)
        ]
        for n in range(1, spans):
            for r in range(2):
                parts = halves(states[r])
                for i in range(2):
                    both_parts = [x[:, i * DV : (i + 1) * DV] for x in parts]
                    states_ref[i, r, n] = jnp.concatenate(both_parts, axis=0)
                add = jnp.concatenate([adds[2 * n + r], zero_half], axis=1)
                end = jnp.concatenate([end_of(ends_ref, n, r)] * 2, axis=1)
                states[r] = step(end, lin_ref[r, n], states[r], parts) + add
        for ref in last_ref:
            for r in range(2):
                ref[r] = states[r]


def span_rows(n):
    return slice(n * SPAN, (n + 1) * SPAN)


def twice(x, axis):
    return jnp.concatenate([x, x], axis=axis)


def asked(recv_ref, cq_ref, keys_ref, keys_t_ref, within_ref, query_rows):
    tokens = (recv_ref.shape[1] - GATES) // 4
    spans = keys_t_ref.shape[0]
    tap = key_tap(lax.axis_index("sub"), cq_ref)
    widened(query_rows, recv_ref, [3 * tokens], tokens)
    queries = [
        unit(convolved(query_rows, n * SPAN + 8 - EDGE, SPAN, slice(0, DK), tap), DK**-0.5)
        for n in range(spans)
    ]
    readers = [
        jnp.concatenate([keys_ref[span_rows(n), :], queries[n]], axis=0) for n in range(spans)
    ]
    scores = [dot(queries[n], keys_t_ref[n]) for n in range(spans)]
    inner = [
        (within_ref[r, span_rows(n), :].astype(F32) * scores[n]).astype(BF16)
        for n in range(spans)
        for r in range(2)
    ]
    return readers, inner


def first_outputs_kernel(
    recv_ref,
    cq_ref,
    keys_ref,
    keys_t_ref,
    t_ref,
    lin_ref,
    ends_ref,
    within_ref,
    cols_ref,
    values_ref,
    xs_ref,
    adds_ref,
    oa_ref,
    query_rows,
):
    @pl.when(lax.axis_index("half") == 0)
    def _():
        spans = t_ref.shape[1]
        both = [(n, r) for n in range(spans) for r in range(2)]
        readers, inner = asked(recv_ref, cq_ref, keys_ref, keys_t_ref, within_ref, query_rows)
        stacks, states = [], []
        for n in range(1, spans):
            if n == 1:
                states = [adds_ref[r, 0] for r in range(2)]
                stack = [jnp.concatenate(halves(x), axis=0) for x in states]
            elif n & (n - 1) == 0:
                stack = [xs_ref[r, n] for r in range(2)]
                states = [x[:DK].astype(F32) + x[DK:].astype(F32) for x in stack]
            else:
                states = [
                    followed(
                        (end_of(ends_ref, n - 1, r), lin_ref[r, n - 1], adds_ref[r, n - 1]),
                        states[r],
                    )
                    for r in range(2)
                ]
                stack = [jnp.concatenate(halves(x), axis=0) for x in states]
            stacks.append(jnp.concatenate(stack, axis=1))
        reads = [dot(twice(readers[n], 1), stacks[n - 1]) for n in range(1, spans)]
        rests, seen = [], []
        for n, r in both:
            lanes = slice(r * DV, (r + 1) * DV)
            value = values_ref[r, span_rows(n), :]
            if n == 0:
                rests.append(value)
                seen.append(None)
            else:
                growth = cols_ref[:, GATES * n + 2 + r : GATES * n + 3 + r]
                read = growth * reads[n - 1][:SPAN, lanes]
                rests.append((value.astype(F32) - read).astype(BF16))
                seen.append(growth * reads[n - 1][SPAN:, lanes])
        fresh = [unwound(t_ref, n, r, x).astype(BF16) for (n, r), x in zip(both, rests)]
        spreads = [dot(w, x) for w, x in zip(inner, fresh)]
        for (n, r), x, y in zip(both, spreads, seen):
            oa_ref[r, span_rows(n), :] = x if y is None else x + y


def later_outputs_kernel(
    recv_ref,
    cq_ref,
    keys_ref,
    keys_t_ref,
    t_ref,
    within_ref,
    cols_ref,
    values_ref,
    states_ref,
    oa_ref,
    om_ref,
    query_rows,
):
    @pl.when(lax.axis_index("half") > 0)
    def _():
        spans = t_ref.shape[1]
        both = [(n, r) for n in range(spans) for r in range(2)]
        readers, inner = asked(recv_ref, cq_ref, keys_ref, keys_t_ref, within_ref, query_rows)
        zero_half = jnp.zeros((SPAN, DV), F32)
        reads = [
            dot(
                twice(readers[n], 1),
                jnp.concatenate([states_ref[0, r, n], states_ref[1, r, n]], axis=1),
            )
            if n > 0
            else None
            for n, r in both
        ]
        rests, seen = [], []
        for (n, r), read in zip(both, reads):
            value = values_ref[r, span_rows(n), :].astype(F32)
            growth = cols_ref[:, GATES * n + 2 + r : GATES * n + 3 + r]
            if n == 0:
                reader = readers[n].astype(F32)
                rest = jnp.concatenate([value, -(growth * reader[:SPAN])], axis=1)
                seen.append(jnp.concatenate([zero_half, growth * reader[SPAN:]], axis=1))
            else:
                rest = jnp.concatenate([value, zero_half], axis=1) - growth * read[:SPAN]
                seen.append(growth * read[SPAN:])
            rests.append(rest.astype(BF16))
        fresh = [unwound(t_ref, n, r, x).astype(BF16) for (n, r), x in zip(both, rests)]
        spreads = [dot(w, x) for w, x in zip(inner, fresh)]
        for (n, r), x, y in zip(both, spreads, seen):
            out = x + y
            oa_ref[r, span_rows(n), :] = out[:, :DV]
            om_ref[r, span_rows(n), :] = out[:, DV:].astype(BF16)


def first_tokens(hop_ref, recv_ref, early_ref, cq_ref, ck_ref, cv_ref, rows):
    sub = lax.axis_index("sub")
    tokens = (recv_ref.shape[1] - GATES) // 4
    taps = [key_tap(sub, cq_ref), key_tap(sub, ck_ref)] + value_taps(sub, cv_ref)
    results = []
    edges = hop_ref[2 * DK :, :].astype(F32)
    for g, first in enumerate((3, 0, 1, 2)):
        lanes = slice(g * 128, (g + 1) * 128)
        start = first * tokens
        rows[16 - EDGE : 16, lanes] = edges[EDGE * g : EDGE * (g + 1)]
        rows[16:32, lanes] = recv_ref[0, start : start + 16, :].astype(F32)
        results.append(convolved(rows, 16 - EDGE, 8, lanes, taps[g]))
    q_cols = jnp.transpose(unit(results[0], DK**-0.5).astype(F32))
    k_cols = jnp.transpose(unit(results[1], 1.0).astype(F32))
    gates = early_ref[...]
    line = iota((8, DV), 0)
    finals, outputs = [], []
    for r in range(2):
        values = results[2 + r].astype(BF16).astype(F32)
        entering = hop_ref[r * DK : (r + 1) * DK, :].astype(F32)
        state, out = entering, jnp.zeros((8, DV), F32)
        for t in range(EDGE):
            k_t, q_t = k_cols[:, t : t + 1], q_cols[:, t : t + 1]
            state = jnp.exp(gates[r : r + 1, t : t + 1]) * state
            held = jnp.sum(k_t * state, axis=0, keepdims=True)
            state = state + k_t * (
                gates[2 + r : 3 + r, t : t + 1] * (values[t : t + 1, :] - held)
            )
            out = jnp.where(line == t, jnp.sum(q_t * state, axis=0, keepdims=True), out)
        finals.append(state)
        outputs.append(out)
    return finals, outputs


def finish_kernel(
    hop_ref,
    recv_ref,
    early_ref,
    cq_ref,
    ck_ref,
    cv_ref,
    gain_ref,
    first_oa,
    oa_ref,
    om_ref,
    out_ref,
    rows,
):
    peers, tokens = out_ref.shape[0], out_ref.shape[1] // 2
    first = lax.axis_index("half") == 0
    gain = gain_ref[...]
    chunks = 4
    part, peer_part = peers * tokens // chunks, peers // chunks

    def put(c, r, core):
        scale = lax.rsqrt(jnp.mean(core * core, axis=-1, keepdims=True) + EPS)
        normed = (core * scale * gain).astype(BF16)
        here = slice(c * peer_part, (c + 1) * peer_part)
        out_ref[here, r * tokens : (r + 1) * tokens, :] = normed.reshape(peer_part, tokens, DV)

    @pl.when(first)
    def _():
        for c in range(chunks):
            for r in range(2):
                put(c, r, first_oa[r, c * part : (c + 1) * part, :])

    @pl.when(jnp.logical_not(first))
    def _():
        finals, outputs = first_tokens(hop_ref, recv_ref, early_ref, cq_ref, ck_ref, cv_ref, rows)
        replaced = iota((8, DV), 0) < EDGE
        passed = [dot(om_ref[r], finals[r].astype(BF16)) for r in range(2)]
        for c in range(chunks):
            at = c * part
            for r in range(2):
                core = oa_ref[r, at : at + part, :] + passed[r][at : at + part]
                if c == 0:
                    core = jnp.concatenate(
                        [jnp.where(replaced, outputs[r], core[0:8]), core[8:]], axis=0
                    )
                put(c, r, core)


def advance_kernel(
    hop_ref, recv_ref, early_ref, cq_ref, ck_ref, cv_ref, hop_own, last_ref, next_ref, rows
):
    finals, _ = first_tokens(hop_ref, recv_ref, early_ref, cq_ref, ck_ref, cv_ref, rows)
    first = lax.axis_index("half") == 0
    for r in range(2):
        last = last_ref[r]
        through = mm_parts(halves(last[:, DV:]), halves(finals[r]))
        own = hop_own[r * DK : (r + 1) * DK, :].astype(F32)
        moved = jnp.where(first, own, through + last[:, :DV])
        next_ref[r * DK : (r + 1) * DK, :] = moved.astype(BF16)
    next_ref[2 * DK :, :] = hop_own[2 * DK :, :]


def gate_kernel(heads_axis, normed_ref, z_ref, out_ref, made, sems):
    subs, tokens = normed_ref.shape[0] // heads_axis, z_ref.shape[0]
    width = subs * 2 * DV
    copies = []
    for head in range(heads_axis):
        for sub in range(subs):
            for r in range(2):
                at = (2 * (head * subs + sub) + r) * DV
                gate = silu(z_ref[:, at : at + DV].astype(F32))
                here = slice(r * tokens, (r + 1) * tokens)
                value = normed_ref[sub * heads_axis + head, here, :].astype(F32)
                made[:, at : at + DV] = (value * gate).astype(BF16)
        lanes = pl.ds(head * width, width)
        copy = pltpu.make_async_copy(made.at[:, lanes], out_ref.at[:, lanes], sems.at[head])
        copy.start()
        copies.append(copy)
    for copy in copies:
        copy.wait()


VMEM = pl.BlockSpec(memory_space=pltpu.VMEM)
SMEM = pl.BlockSpec(memory_space=pltpu.SMEM)
ANY = pl.BlockSpec(memory_space=pl.ANY)


def near(x):
    return pltpu.with_memory_space_constraint(x, pltpu.VMEM)


def far(x):
    return pltpu.with_memory_space_constraint(x, pltpu.HBM)


def call(kernel, outs, in_specs, scratch=(), out_spec=VMEM, flops=1 << 26, moved=1 << 21):
    return pl.pallas_call(
        kernel,
        out_shape=outs,
        in_specs=in_specs,
        out_specs=jax.tree.map(lambda _: out_spec, outs),
        scratch_shapes=list(scratch),
        compiler_params=pltpu.CompilerParams(vmem_limit_bytes=VMEM_BYTES),
        cost_estimate=pl.CostEstimate(flops=flops, bytes_accessed=moved, transcendentals=0),
    )


def local(
    q_rows,
    k_rows,
    v_rows,
    z_rows,
    a_rows,
    b_rows,
    conv_q,
    conv_k,
    conv_v,
    a_log,
    dt_bias,
    norm_gain,
):
    shards, subs, heads_axis = (lax.axis_size(a) for a in ("half", "sub", "head"))
    peers, tokens = subs * heads_axis, q_rows.shape[0]
    total = peers * tokens
    spans = total // SPAN
    group = ("sub", "head")
    route = [(i, i + 1) for i in range(shards - 1)]
    conv_q, conv_k, conv_v = near(conv_q), near(conv_k), near(conv_v)
    gain = near(norm_gain.reshape(1, DV))
    inputs = [far(x) for x in (q_rows, k_rows, v_rows, a_rows.T, b_rows.T)]
    packed = call(
        functools.partial(pack_kernel, heads_axis),
        pltpu.VMEM((peers, GATES + 4 * tokens, 128), BF16),
        [ANY] * 5,
        [pltpu.VMEM(x.shape, BF16) for x in inputs] + [pltpu.SemaphoreType.DMA((5,))],
        flops=1 << 20,
    )(*inputs)
    blocks = near(lax.all_to_all(packed, group, 0, 0, tiled=True))
    made = call(
        systems_kernel,
        (
            pltpu.VMEM((total, DK), BF16),
            pltpu.VMEM((spans, DK, SPAN), BF16),
            pltpu.VMEM((2, spans, 2, SPAN, SPAN), BF16),
            pltpu.VMEM((2, spans, SUB, SPAN), F32),
            pltpu.VMEM((SPAN, DK), F32),
            pltpu.VMEM((2, total, SPAN), BF16),
            pltpu.VMEM((SPAN, SPAN), F32),
            pltpu.VMEM((8, SPAN), F32),
        ),
        [VMEM, VMEM, SMEM, SMEM, VMEM, VMEM, VMEM],
        [pltpu.VMEM((8 + total, DK), F32)],
        flops=1 << 32,
    )(blocks, conv_k, a_log, dt_bias, conv_q, conv_v, gain)
    keys, keys_t, systems, small, ends, within, cols, early = (near(x) for x in made)
    map_shapes = (
        pltpu.VMEM((2, spans, 2, SPAN, SPAN), BF16),
        pltpu.VMEM((2, spans, DK, DK), BF16),
    )

    hop, inverses, lins, values, starts, adds = call(
        opening_kernel,
        (
            pltpu.VMEM((2 * DK + 16, 128), BF16),
            *map_shapes,
            pltpu.VMEM((2, total, DV), BF16),
            pltpu.VMEM((2, spans, 2 * DK, DV), BF16),
            pltpu.VMEM((2, spans, DK, DV), F32),
        ),
        [VMEM] * 8,
        [pltpu.VMEM((8 + total, 2 * DV), F32)],
        flops=1 << 32,
    )(blocks, conv_v, keys, keys_t, systems, small, ends, cols)
    entering = near(lax.ppermute(hop, "half", route))
    hop, inverses, lins, values, starts, adds = (
        near(x) for x in (hop, inverses, lins, values, starts, adds)
    )
    first_out = call(
        first_outputs_kernel,
        pltpu.VMEM((2, total, DV), F32),
        [VMEM] * 12,
        [pltpu.VMEM((8 + total, DK), F32)],
        flops=1 << 32,
    )(
        blocks,
        conv_q,
        keys,
        keys_t,
        inverses,
        lins,
        ends,
        within,
        cols,
        values,
        starts,
        adds,
    )
    later_solved = call(inverse_kernel, map_shapes, [VMEM] * 6, flops=1 << 32)(
        hop, keys, keys_t, systems, small, cols
    )
    later_inverses, later_lins = (near(x) for x in later_solved)
    read_on = [pltpu.VMEM((2, DK, 2 * DV), F32)] if shards > 2 else []
    later_values, states, *last = call(
        states_kernel,
        (
            pltpu.VMEM((2, total, DV), BF16),
            pltpu.VMEM((2, 2, spans, 2 * DK, DV), BF16),
            *read_on,
        ),
        [VMEM] * 7,
        [pltpu.VMEM((8 + total, 2 * DV), F32)],
        flops=1 << 32,
    )(blocks, conv_v, keys_t, later_inverses, later_lins, ends, cols)
    out_a, out_m = call(
        later_outputs_kernel,
        (pltpu.VMEM((2, total, DV), F32), pltpu.VMEM((2, total, DV), BF16)),
        [VMEM] * 9,
        [pltpu.VMEM((8 + total, DK), F32)],
        flops=1 << 32,
    )(
        blocks,
        conv_q,
        keys,
        keys_t,
        later_inverses,
        within,
        cols,
        near(later_values),
        near(states),
    )
    for _ in range(shards - 2):
        moved = call(
            advance_kernel,
            pltpu.VMEM(hop.shape, BF16),
            [VMEM] * 8,
            [pltpu.VMEM((32, 512), F32)],
        )(entering, blocks, early, conv_q, conv_k, conv_v, hop, near(last[0]))
        entering = near(lax.ppermute(moved, "half", route))
    normed = call(
        finish_kernel,
        pltpu.VMEM((peers, 2 * tokens, DV), BF16),
        [VMEM] * 10,
        [pltpu.VMEM((32, 512), F32)],
    )(
        entering,
        blocks,
        early,
        conv_q,
        conv_k,
        conv_v,
        gain,
        near(first_out),
        near(out_a),
        near(out_m),
    )
    returned = near(lax.all_to_all(normed, group, 0, 0, tiled=True))
    return call(
        functools.partial(gate_kernel, heads_axis),
        jax.ShapeDtypeStruct(z_rows.shape, BF16),
        [VMEM] * 2,
        [pltpu.VMEM(z_rows.shape, BF16), pltpu.SemaphoreType.DMA((heads_axis,))],
        ANY,
    )(returned, z_rows)


def solution(mesh):
    heads_axis = mesh.shape["head"]
    subs = KH // heads_axis
    regrouped = Mesh(
        mesh.devices.reshape(mesh.shape["ctx"] // subs, subs, heads_axis), ("half", "sub", "head")
    )
    row = P(("half", "sub", "head"), None)
    placed = (row,) * 6 + (P(None, "head"),) * 3 + (P("head"),) * 2 + (P(),)
    return jax.shard_map(local, mesh=regrouped, in_specs=placed, out_specs=row, check_vma=False)
```

```python
import functools

import jax
import jax.numpy as jnp
from jax import lax
from jax.experimental import pallas as pl
from jax.experimental.pallas import tpu as pltpu
from jax.sharding import Mesh, PartitionSpec as P

DK = 128
DV = 128
CONV = 4
KH = 16
SUB = 16
SPAN = 128
EDGE = CONV - 1
EPS = 1e-06
F32 = jnp.float32
BF16 = jnp.bfloat16
VMEM_BYTES = 24 * 1024 * 1024
GATES = 8


def dot(a, b, dims=((1,), (0,))):
    return lax.dot_general(a, b, (dims, ((), ())), preferred_element_type=F32)


def halves(x):
    high = x.astype(BF16)
    return high, (x - high.astype(F32)).astype(BF16)


def mm_parts(a, b):
    left = jnp.concatenate([a[0], a[1], a[0]], axis=1)
    return dot(left, jnp.concatenate([b[0], b[0], b[1]], axis=0))


def silu(x):
    half = 0.5 * x
    return half + half * jnp.tanh(half)


def unit(y, factor):
    scale = lax.rsqrt(jnp.sum(y * y, axis=-1, keepdims=True) + EPS)
    return (y * scale * factor).astype(BF16)


def iota(shape, dim):
    return lax.broadcasted_iota(jnp.int32, shape, dim)


def block_of(x, size):
    return lax.shift_right_logical(x, jnp.full(x.shape, size.bit_length() - 1, jnp.int32))


def place_in(x, size):
    return x & (size - 1)


def pack_kernel(
    heads_axis, q_in, k_in, v_in, at_in, bt_in, out_ref, q_ref, k_ref, v_ref, at_ref, bt_ref, sems
):
    peers, tokens = out_ref.shape[0], q_ref.shape[0]
    pairs = ((at_in, at_ref), (bt_in, bt_ref), (k_in, k_ref), (v_in, v_ref), (q_in, q_ref))
    copies = [pltpu.make_async_copy(a, b, sems.at[i]) for i, (a, b) in enumerate(pairs)]
    for copy in copies:
        copy.start()
    subs = peers // heads_axis
    key_heads = [(dest % heads_axis) * subs + dest // heads_axis for dest in range(peers)]
    for copy in copies[:2]:
        copy.wait()
    value_heads = at_ref.shape[0]
    row, entry = iota((peers * GATES, value_heads), 0), iota((peers * GATES, value_heads), 1)
    dest, which = block_of(row, GATES), place_in(row, GATES)
    first = 2 * (place_in(dest, heads_axis) * subs + block_of(dest, heads_axis))
    pick_a = jnp.where((which < 2) & (entry == first + which), 1.0, 0.0).astype(BF16)
    pick_b = jnp.where(
        (which >= 2) & (which < 4) & (entry == first + which - 2), 1.0, 0.0
    ).astype(BF16)
    picked = (dot(pick_a, at_ref[...]) + dot(pick_b, bt_ref[...])).astype(BF16)
    lane_shift = tokens * lax.rem(lax.axis_index("head"), SPAN // tokens)
    place = jnp.where(
        iota((tokens, SPAN), 1) == iota((tokens, SPAN), 0) + lane_shift, 1.0, 0.0
    ).astype(BF16)
    gates = dot(picked, place).astype(BF16)
    for dest in range(peers):
        out_ref[dest, 4 * tokens :, :] = gates[GATES * dest : GATES * (dest + 1), :]

    def laid(ref, lane, start):
        for dest, key_head in enumerate(key_heads):
            at = lane(key_head) * 128
            out_ref[dest, start * tokens : (start + 1) * tokens, :] = ref[
                :, at : at + 128
            ]

    copies[2].wait()
    laid(k_ref, lambda key_head: key_head, 0)
    copies[3].wait()
    laid(v_ref, lambda key_head: 2 * key_head, 1)
    laid(v_ref, lambda key_head: 2 * key_head + 1, 2)
    copies[4].wait()
    laid(q_ref, lambda key_head: key_head, 3)


def compacted(system):
    size = system.shape[0]
    diagonal = block_of(iota((size, size), 0), SUB) == block_of(iota((size, size), 1), SUB)
    return jnp.sum(jnp.where(diagonal, system, 0.0).reshape(size // SUB, SUB, size), axis=0)


def substituted(compact):
    count, _, size = compact.shape
    flat = compact.reshape(count * SUB, size)
    lane, line = iota(flat.shape, 1), iota(flat.shape, 0)
    solved = jnp.where(place_in(lane ^ line, SUB) == 0, 1.0, 0.0).reshape(count, SUB, size)
    for m in range(SUB - 1):
        source = (lane & ~(SUB - 1)) | m
        spread = jnp.take_along_axis(flat, source, axis=1, mode="promise_in_bounds")
        solved = solved + spread.reshape(count, SUB, size) * solved[:, m : m + 1, :]
    return solved


def inverted(systems, small, meanwhile=lambda: None):
    size = systems[0][0].shape[0]
    row, col = iota((size, size), 0), iota((size, size), 1)
    placed = jnp.where(block_of(row, SUB) == block_of(col, SUB), 1.0, 0.0).astype(BF16)
    identity = jnp.where(row == col, 1.0, 0.0)
    rough = [
        jnp.concatenate([block.astype(BF16)] * (size // SUB), axis=0) * placed for block in small
    ]
    blank = jnp.zeros((size, size), BF16)
    width = SUB
    while width < size:
        odd = [(j, j + width) for j in range(width, size, 2 * width)]

        def rows_of(x):
            return jnp.concatenate([x[lo:hi] for lo, hi in odd], axis=0)

        def woven(even, x):
            pieces = []
            for j, (lo, hi) in enumerate(odd):
                pieces += [even[lo - width : lo], x[j * width : (j + 1) * width]]
            return jnp.concatenate(pieces, axis=0)

        below = rows_of(block_of(row ^ col, 2 * width)) + rows_of(col & width) == 0
        own = rows_of(identity)
        firsts = [dot(rows_of(n[0]), t) for n, t in zip(systems, rough)]
        meanwhile()
        rights = [
            woven(blank, jnp.where(below, first, own).astype(BF16)) for first in firsts
        ]
        grown = [dot(rows_of(t), right).astype(BF16) for t, right in zip(rough, rights)]
        rough = [woven(t, g) for t, g in zip(rough, grown)]
        width *= 2
    products = [
        dot(jnp.concatenate(n, axis=1), jnp.concatenate([t, t], axis=0))
        for n, t in zip(systems, rough)
    ]
    rests = [
        (identity - t.astype(F32) + product).astype(BF16) for t, product in zip(rough, products)
    ]
    return [halves(t.astype(F32) + dot(t, rest)) for t, rest in zip(rough, rests)]


def gate_values(gates, sub, alog_ref, dt_ref):
    second = place_in(iota(gates.shape, 0), GATES) == 1
    a_log = jnp.where(second, alog_ref[2 * sub + 1], alog_ref[2 * sub])
    dt_bias = jnp.where(second, dt_ref[2 * sub + 1], dt_ref[2 * sub])
    shifted = gates + dt_bias
    soft = jnp.maximum(shifted, 0.0) + jnp.log1p(jnp.exp(-jnp.abs(shifted)))
    return -jnp.exp(a_log) * soft, 1.0 / (1.0 + jnp.exp(-gates))


def convolved(rows, at, count, lanes, tap):
    summed = tap[0:1] * rows[at : at + count, lanes]
    for j in range(1, CONV):
        summed = summed + tap[j : j + 1] * rows[at + j : at + j + count, lanes]
    return silu(summed)


def key_tap(sub, tap_ref):
    return tap_ref[:, pl.ds(pl.multiple_of(sub * DK, 128), DK)]


def value_taps(sub, cv_ref):
    lane = pl.multiple_of(sub * 2 * DV, 128)
    return [cv_ref[:, pl.ds(pl.multiple_of(lane + r * DV, 128), DV)] for r in range(2)]


def widened(rows, recv_ref, starts, tokens):
    rows[0:8, :] = jnp.zeros((8, rows.shape[1]), F32)
    for s in range(recv_ref.shape[0]):
        for g, start in enumerate(starts):
            rows[8 + s * tokens : 8 + (s + 1) * tokens, g * 128 : (g + 1) * 128] = recv_ref[
                s, start : start + tokens, :
            ].astype(F32)


def systems_kernel(hop_ref, recv_ref, ck_ref, alog_ref, dt_ref, *refs):
    del hop_ref

    @pl.when(lax.axis_index("half") > 0)
    def _():
        systems_of(recv_ref, ck_ref, alog_ref, dt_ref, *refs)


def systems_of(
    recv_ref,
    ck_ref,
    alog_ref,
    dt_ref,
    keys_ref,
    keys_t_ref,
    systems_ref,
    small_ref,
    ends_ref,
    within_ref,
    cols_ref,
    early_ref,
    rows,
):
    sub = lax.axis_index("sub")
    later = lax.axis_index("half") > 0
    peers = recv_ref.shape[0]
    tokens = (recv_ref.shape[1] - GATES) // 4
    spans = peers * tokens // SPAN
    tap = key_tap(sub, ck_ref)
    widened(rows, recv_ref, [0], tokens)
    stacked = [
        sum(recv_ref[s, 4 * tokens :, :].astype(F32) for s in range(n, n + SPAN // tokens))
        for n in range(0, peers, SPAN // tokens)
    ]
    stacked.append(jnp.zeros((SPAN - spans * GATES, SPAN), F32))
    gates = jnp.concatenate(stacked, axis=0)
    decay, rate = gate_values(gates, sub, alog_ref, dt_ref)
    if early_ref is not None:
        early_ref[...] = jnp.where(iota((8, SPAN), 0) < 2, decay[0:8], rate[0:8])
    skipped = later & (iota(gates.shape, 0) < GATES) & (iota(gates.shape, 1) < EDGE)
    decay = jnp.where(skipped, 0.0, decay)
    rate = jnp.where(skipped, 0.0, rate)
    lane_r, lane_c = iota((SPAN, SPAN), 0), iota((SPAN, SPAN), 1)
    upto = jnp.where(lane_r <= lane_c, 1.0, 0.0).astype(BF16)
    d_high, _ = halves(decay)
    d_mid, d_low = halves(decay - d_high.astype(F32))
    cum = dot(d_high, upto) + (dot(d_mid, upto) + dot(d_low, upto))
    growth = jnp.exp(cum)
    here = pltpu.roll(rate, rate.shape[0] - 2, 0)
    rest = jnp.exp(cum[:, SPAN - 1 :] - cum) * here
    which = place_in(iota(gates.shape, 0), GATES)
    mixed = jnp.where(which < 2, cum, pltpu.roll(growth, 2, 0))
    columns = jnp.transpose(jnp.where(which < 4, mixed, pltpu.roll(rest, 4, 0)))
    cols_ref[...] = columns
    lower = lane_r >= lane_c
    strict = lane_r > lane_c
    both = [(n, r) for n in range(spans) for r in range(2)]
    keys = []
    for n in range(spans):
        k_n = unit(convolved(rows, n * SPAN + 8 - EDGE, SPAN, slice(0, DK), tap), 1.0)
        keys_ref[n * SPAN : (n + 1) * SPAN, :] = k_n
        keys.append(k_n)
    keys_t = []
    for n in range(spans):
        kt_n = jnp.transpose(keys[n].astype(F32)).astype(BF16)
        keys_t_ref[n] = kt_n
        keys_t.append(kt_n)
    grams = [dot(keys[n], keys_t[n]) for n in range(spans)]
    for n, r in both:
        at = GATES * n + r
        gap = columns[:, at : at + 1] - cum[at : at + 1, :]
        within = jnp.exp(jnp.where(lower, gap, 0.0)) * here[at : at + 1, :]
        within_ref[r, n * SPAN : (n + 1) * SPAN, :] = jnp.where(lower, within, 0.0).astype(BF16)
        system = jnp.where(strict, within * -grams[n], 0.0)
        systems_ref[r, n, 0], systems_ref[r, n, 1] = halves(system)
        small_ref[r, n] = compacted(system)
    ends_ref[...] = jnp.broadcast_to(growth[:, SPAN - 1 :], ends_ref.shape)


def inverse_kernel(
    hop_ref, keys_ref, keys_t_ref, systems_ref, small_ref, cols_ref, t_ref, lin_ref
):
    del hop_ref
    spans = keys_t_ref.shape[0]
    both = [(n, r) for n in range(spans) for r in range(2)]

    @pl.when(lax.axis_index("half") > 0)
    def _():
        compact = jnp.concatenate([small_ref[r, n] for n, r in both], axis=0)
        small = substituted(compact.reshape(len(both), SUB, SPAN))
        systems = [(systems_ref[r, n, 0], systems_ref[r, n, 1]) for n, r in both]
        inverses = inverted(systems, [small[i] for i in range(len(both))])
        scaled = []
        for i, (n, r) in enumerate(both):
            t_ref[r, n, 0], t_ref[r, n, 1] = inverses[i]
            at = GATES * n + r
            key = keys_ref[n * SPAN : (n + 1) * SPAN, :].astype(F32)
            right = (cols_ref[:, at + 2 : at + 3] * key).astype(BF16)
            scaled.append(jnp.concatenate([right, right], axis=0))
        w_mats = [dot(jnp.concatenate(t, axis=1), x) for t, x in zip(inverses, scaled)]
        weighed = []
        for (n, r), w_mat in zip(both, w_mats):
            at = GATES * n + r
            weighed.append((cols_ref[:, at + 4 : at + 5] * w_mat).astype(BF16))
        moved = [
            dot(keys_t_ref[n], jnp.concatenate(weighed[2 * n : 2 * n + 2], axis=1))
            for n in range(spans)
        ]
        for n, r in both:
            lin_ref[r, n] = moved[n][:, r * DK : (r + 1) * DK].astype(BF16)


def unwound(t_ref, n, r, x):
    both = jnp.concatenate([t_ref[r, n, 0], t_ref[r, n, 1]], axis=1)
    return dot(both, jnp.concatenate([x, x], axis=0))


def end_of(ends_ref, n, r):
    return ends_ref[GATES * n + r : GATES * n + r + 1, :]


def followed(span_map, state):
    end, moved, add = span_map
    return step(end, moved, state, halves(state)) + add


def composed(maps):
    if len(maps) == 1:
        return maps[0]
    half = len(maps) // 2
    end_a, moved_a, add_a = composed(maps[:half])
    end_b, moved_b, add_b = composed(maps[half:])
    high, low = halves(add_a)
    rights = jnp.concatenate(
        [
            jnp.concatenate([moved_a, high], axis=1),
            jnp.concatenate([jnp.zeros_like(moved_a), low], axis=1),
        ],
        axis=0,
    )
    passed = dot(jnp.concatenate([moved_b, moved_b], axis=1), rights)
    moved = end_b * moved_a.astype(F32) + end_a * moved_b.astype(F32) - passed[:, :DK]
    add = end_b * add_a - passed[:, DK:] + add_b
    return end_a * end_b, moved.astype(BF16), add


def step(end, moved, state, parts):
    both = jnp.concatenate([moved, moved], axis=1)
    return end * state - dot(both, jnp.concatenate(parts, axis=0))


def values_part(recv_ref, cv_ref, keys_t_ref, t_ref, cols_ref, rows, vs):
    sub = lax.axis_index("sub")
    tokens = (recv_ref.shape[1] - GATES) // 4
    spans = t_ref.shape[1]
    taps = value_taps(sub, cv_ref)
    widened(rows, recv_ref, [tokens, 2 * tokens], tokens)
    both = [(n, r) for n in range(spans) for r in range(2)]
    values = []
    for n, r in both:
        lanes = slice(r * DV, (r + 1) * DV)
        v_n = convolved(rows, n * SPAN + 8 - EDGE, SPAN, lanes, taps[r]).astype(BF16)
        vs[r, n * SPAN : (n + 1) * SPAN, :] = v_n
        values.append(v_n)
    solved = [unwound(t_ref, n, r, v) for (n, r), v in zip(both, values)]
    weighed = []
    for (n, r), u_mat in zip(both, solved):
        at = GATES * n + r
        weighed.append((cols_ref[:, at + 4 : at + 5] * u_mat).astype(BF16))
    moved = [
        dot(keys_t_ref[n], jnp.concatenate(weighed[2 * n : 2 * n + 2], axis=1))
        for n in range(spans)
    ]
    return [moved[n][:, r * DV : (r + 1) * DV] for n, r in both]


def opening_kernel(
    recv_ref,
    ck_ref,
    cv_ref,
    alog_ref,
    dt_ref,
    cq_ref,
    gain_ref,
    hop_ref,
    keys_ref,
    keys_t_ref,
    ends_ref,
    within_ref,
    cols_ref,
    t_ref,
    lin_ref,
    vs_ref,
    xs_ref,
    adds_ref,
    key_rows,
    rows,
    systems_ref,
    small_ref,
):
    first = lax.axis_index("half") == 0
    peers = recv_ref.shape[0]
    tokens = (recv_ref.shape[1] - GATES) // 4
    spans = keys_t_ref.shape[0]
    edges = []
    for which in (3, 0, 1, 2):
        end = (which + 1) * tokens
        edges.append(recv_ref[peers - 1, end - 16 : end, :].astype(F32)[16 - EDGE :])
    edges.append(jnp.zeros((16 - 4 * EDGE, 128), F32))
    hop_ref[2 * DK :, :] = jnp.concatenate(edges, axis=0).astype(BF16)

    @pl.when(first)
    def _():
        both = [(n, r) for n in range(spans) for r in range(2)]
        systems_of(
            recv_ref,
            ck_ref,
            alog_ref,
            dt_ref,
            keys_ref,
            keys_t_ref,
            systems_ref,
            small_ref,
            ends_ref,
            within_ref,
            cols_ref,
            None,
            key_rows,
        )
        taps = value_taps(lax.axis_index("sub"), cv_ref)
        widened(rows, recv_ref, [tokens, 2 * tokens], tokens)
        waiting = list(both)

        def meanwhile():
            for n, r in waiting[:6]:
                lanes = slice(r * DV, (r + 1) * DV)
                value = convolved(rows, n * SPAN + 8 - EDGE, SPAN, lanes, taps[r])
                vs_ref[r, n * SPAN : (n + 1) * SPAN, :] = value.astype(BF16)
            del waiting[:6]

        compact = jnp.concatenate([small_ref[r, n] for n, r in both], axis=0)
        small = substituted(compact.reshape(len(both), SUB, SPAN))
        systems = [(systems_ref[r, n, 0], systems_ref[r, n, 1]) for n, r in both]
        inverses = inverted(systems, [small[i] for i in range(len(both))], meanwhile)
        while waiting:
            meanwhile()
        rights = []
        for i, (n, r) in enumerate(both):
            t_ref[r, n, 0], t_ref[r, n, 1] = inverses[i]
            at = GATES * n + r
            here = slice(n * SPAN, (n + 1) * SPAN)
            key = (cols_ref[:, at + 2 : at + 3] * keys_ref[here, :].astype(F32)).astype(BF16)
            right = jnp.concatenate([key, vs_ref[r, here, :]], axis=1)
            rights.append(jnp.concatenate([right, right], axis=0))
        solved = [dot(jnp.concatenate(t, axis=1), x) for t, x in zip(inverses, rights)]
        weighed = []
        for (n, r), x in zip(both, solved):
            at = GATES * n + r
            weighed.append((cols_ref[:, at + 4 : at + 5] * x).astype(BF16))
        moved = [
            dot(keys_t_ref[n], jnp.concatenate(weighed[2 * n : 2 * n + 2], axis=1))
            for n in range(spans)
        ]
        adds = []
        for n, r in both:
            at = 2 * r * DK
            lin_ref[r, n] = moved[n][:, at : at + DK].astype(BF16)
            adds.append(moved[n][:, at + DK : at + 2 * DK])
            adds_ref[r, n] = adds[-1]
        maps = [
            [(end_of(ends_ref, n, r), lin_ref[r, n], adds[2 * n + r]) for n in range(spans)]
            for r in range(2)
        ]
        states = [m[0][2] for m in maps]
        done = 1
        while done < spans:
            for r in range(2):
                if done > 1:
                    xs_ref[r, done] = jnp.concatenate(halves(states[r]), axis=0)
            later = [composed(m[done : 2 * done]) for m in maps]
            states = [followed(m, x) for m, x in zip(later, states)]
            done *= 2
        for r in range(2):
            hop_ref[r * DK : (r + 1) * DK, :] = states[r].astype(BF16)

    @pl.when(jnp.logical_not(first))
    def _():
        hop_ref[0 : 2 * DK, :] = jnp.zeros((2 * DK, DV), BF16)


def states_kernel(
    recv_ref,
    cv_ref,
    keys_t_ref,
    t_ref,
    lin_ref,
    ends_ref,
    cols_ref,
    values_ref,
    states_ref,
    *rest,
):
    *last_ref, rows = rest

    @pl.when(lax.axis_index("half") > 0)
    def _():
        spans = t_ref.shape[1]
        adds = values_part(recv_ref, cv_ref, keys_t_ref, t_ref, cols_ref, rows, values_ref)
        zero_half = jnp.zeros((DK, DV), F32)
        identity = jnp.where(iota((DK, DK), 0) == iota((DK, DK), 1), 1.0, 0.0)
        states = [
            jnp.concatenate(
                [adds[r], ends_ref[r : r + 1, :] * identity - lin_ref[r, 0].astype(F32)], axis=1
            )
            for r in range(2)
        ]
        for n in range(1, spans):
            for r in range(2):
                parts = halves(states[r])
                for i in range(2):
                    both_parts = [x[:, i * DV : (i + 1) * DV] for x in parts]
                    states_ref[i, r, n] = jnp.concatenate(both_parts, axis=0)
                add = jnp.concatenate([adds[2 * n + r], zero_half], axis=1)
                end = jnp.concatenate([end_of(ends_ref, n, r)] * 2, axis=1)
                states[r] = step(end, lin_ref[r, n], states[r], parts) + add
        for ref in last_ref:
            for r in range(2):
                ref[r] = states[r]


def span_rows(n):
    return slice(n * SPAN, (n + 1) * SPAN)


def twice(x, axis):
    return jnp.concatenate([x, x], axis=axis)


def asked(recv_ref, cq_ref, keys_ref, keys_t_ref, within_ref, query_rows):
    tokens = (recv_ref.shape[1] - GATES) // 4
    spans = keys_t_ref.shape[0]
    tap = key_tap(lax.axis_index("sub"), cq_ref)
    widened(query_rows, recv_ref, [3 * tokens], tokens)
    queries = [
        unit(convolved(query_rows, n * SPAN + 8 - EDGE, SPAN, slice(0, DK), tap), DK**-0.5)
        for n in range(spans)
    ]
    readers = [
        jnp.concatenate([keys_ref[span_rows(n), :], queries[n]], axis=0) for n in range(spans)
    ]
    scores = [dot(queries[n], keys_t_ref[n]) for n in range(spans)]
    inner = [
        (within_ref[r, span_rows(n), :].astype(F32) * scores[n]).astype(BF16)
        for n in range(spans)
        for r in range(2)
    ]
    return readers, inner


def first_outputs_kernel(
    recv_ref,
    cq_ref,
    keys_ref,
    keys_t_ref,
    t_ref,
    lin_ref,
    ends_ref,
    within_ref,
    cols_ref,
    values_ref,
    xs_ref,
    adds_ref,
    oa_ref,
    query_rows,
):
    @pl.when(lax.axis_index("half") == 0)
    def _():
        spans = t_ref.shape[1]
        both = [(n, r) for n in range(spans) for r in range(2)]
        readers, inner = asked(recv_ref, cq_ref, keys_ref, keys_t_ref, within_ref, query_rows)
        stacks, states = [], []
        for n in range(1, spans):
            if n == 1:
                states = [adds_ref[r, 0] for r in range(2)]
                stack = [jnp.concatenate(halves(x), axis=0) for x in states]
            elif n & (n - 1) == 0:
                stack = [xs_ref[r, n] for r in range(2)]
                states = [x[:DK].astype(F32) + x[DK:].astype(F32) for x in stack]
            else:
                states = [
                    followed(
                        (end_of(ends_ref, n - 1, r), lin_ref[r, n - 1], adds_ref[r, n - 1]),
                        states[r],
                    )
                    for r in range(2)
                ]
                stack = [jnp.concatenate(halves(x), axis=0) for x in states]
            stacks.append(jnp.concatenate(stack, axis=1))
        reads = [dot(twice(readers[n], 1), stacks[n - 1]) for n in range(1, spans)]
        rests, seen = [], []
        for n, r in both:
            lanes = slice(r * DV, (r + 1) * DV)
            value = values_ref[r, span_rows(n), :]
            if n == 0:
                rests.append(value)
                seen.append(None)
            else:
                growth = cols_ref[:, GATES * n + 2 + r : GATES * n + 3 + r]
                read = growth * reads[n - 1][:SPAN, lanes]
                rests.append((value.astype(F32) - read).astype(BF16))
                seen.append(growth * reads[n - 1][SPAN:, lanes])
        fresh = [unwound(t_ref, n, r, x).astype(BF16) for (n, r), x in zip(both, rests)]
        spreads = [dot(w, x) for w, x in zip(inner, fresh)]
        for (n, r), x, y in zip(both, spreads, seen):
            oa_ref[r, span_rows(n), :] = x if y is None else x + y


def later_outputs_kernel(
    recv_ref,
    cq_ref,
    keys_ref,
    keys_t_ref,
    t_ref,
    within_ref,
    cols_ref,
    values_ref,
    states_ref,
    oa_ref,
    om_ref,
    query_rows,
):
    @pl.when(lax.axis_index("half") > 0)
    def _():
        spans = t_ref.shape[1]
        both = [(n, r) for n in range(spans) for r in range(2)]
        readers, inner = asked(recv_ref, cq_ref, keys_ref, keys_t_ref, within_ref, query_rows)
        zero_half = jnp.zeros((SPAN, DV), F32)
        reads = [
            dot(
                twice(readers[n], 1),
                jnp.concatenate([states_ref[0, r, n], states_ref[1, r, n]], axis=1),
            )
            if n > 0
            else None
            for n, r in both
        ]
        rests, seen = [], []
        for (n, r), read in zip(both, reads):
            value = values_ref[r, span_rows(n), :].astype(F32)
            growth = cols_ref[:, GATES * n + 2 + r : GATES * n + 3 + r]
            if n == 0:
                reader = readers[n].astype(F32)
                rest = jnp.concatenate([value, -(growth * reader[:SPAN])], axis=1)
                seen.append(jnp.concatenate([zero_half, growth * reader[SPAN:]], axis=1))
            else:
                rest = jnp.concatenate([value, zero_half], axis=1) - growth * read[:SPAN]
                seen.append(growth * read[SPAN:])
            rests.append(rest.astype(BF16))
        fresh = [unwound(t_ref, n, r, x).astype(BF16) for (n, r), x in zip(both, rests)]
        spreads = [dot(w, x) for w, x in zip(inner, fresh)]
        for (n, r), x, y in zip(both, spreads, seen):
            out = x + y
            oa_ref[r, span_rows(n), :] = out[:, :DV]
            om_ref[r, span_rows(n), :] = out[:, DV:].astype(BF16)


def first_tokens(hop_ref, recv_ref, early_ref, cq_ref, ck_ref, cv_ref, rows):
    sub = lax.axis_index("sub")
    tokens = (recv_ref.shape[1] - GATES) // 4
    taps = [key_tap(sub, cq_ref), key_tap(sub, ck_ref)] + value_taps(sub, cv_ref)
    results = []
    edges = hop_ref[2 * DK :, :].astype(F32)
    for g, first in enumerate((3, 0, 1, 2)):
        lanes = slice(g * 128, (g + 1) * 128)
        start = first * tokens
        rows[16 - EDGE : 16, lanes] = edges[EDGE * g : EDGE * (g + 1)]
        rows[16:32, lanes] = recv_ref[0, start : start + 16, :].astype(F32)
        results.append(convolved(rows, 16 - EDGE, 8, lanes, taps[g]))
    q_cols = jnp.transpose(unit(results[0], DK**-0.5).astype(F32))
    k_cols = jnp.transpose(unit(results[1], 1.0).astype(F32))
    gates = early_ref[...]
    line = iota((8, DV), 0)
    finals, outputs = [], []
    for r in range(2):
        values = results[2 + r].astype(BF16).astype(F32)
        entering = hop_ref[r * DK : (r + 1) * DK, :].astype(F32)
        state, out = entering, jnp.zeros((8, DV), F32)
        for t in range(EDGE):
            k_t, q_t = k_cols[:, t : t + 1], q_cols[:, t : t + 1]
            state = jnp.exp(gates[r : r + 1, t : t + 1]) * state
            held = jnp.sum(k_t * state, axis=0, keepdims=True)
            state = state + k_t * (
                gates[2 + r : 3 + r, t : t + 1] * (values[t : t + 1, :] - held)
            )
            out = jnp.where(line == t, jnp.sum(q_t * state, axis=0, keepdims=True), out)
        finals.append(state)
        outputs.append(out)
    return finals, outputs


def finish_kernel(
    hop_ref,
    recv_ref,
    early_ref,
    cq_ref,
    ck_ref,
    cv_ref,
    gain_ref,
    first_oa,
    oa_ref,
    om_ref,
    out_ref,
    rows,
):
    peers, tokens = out_ref.shape[0], out_ref.shape[1] // 2
    first = lax.axis_index("half") == 0
    gain = gain_ref[...]
    chunks = 4
    part, peer_part = peers * tokens // chunks, peers // chunks

    def put(c, r, core):
        scale = lax.rsqrt(jnp.mean(core * core, axis=-1, keepdims=True) + EPS)
        normed = (core * scale * gain).astype(BF16)
        here = slice(c * peer_part, (c + 1) * peer_part)
        out_ref[here, r * tokens : (r + 1) * tokens, :] = normed.reshape(peer_part, tokens, DV)

    @pl.when(first)
    def _():
        for c in range(chunks):
            for r in range(2):
                put(c, r, first_oa[r, c * part : (c + 1) * part, :])

    @pl.when(jnp.logical_not(first))
    def _():
        finals, outputs = first_tokens(hop_ref, recv_ref, early_ref, cq_ref, ck_ref, cv_ref, rows)
        replaced = iota((8, DV), 0) < EDGE
        passed = [dot(om_ref[r], finals[r].astype(BF16)) for r in range(2)]
        for c in range(chunks):
            at = c * part
            for r in range(2):
                core = oa_ref[r, at : at + part, :] + passed[r][at : at + part]
                if c == 0:
                    core = jnp.concatenate(
                        [jnp.where(replaced, outputs[r], core[0:8]), core[8:]], axis=0
                    )
                put(c, r, core)


def advance_kernel(
    hop_ref, recv_ref, early_ref, cq_ref, ck_ref, cv_ref, hop_own, last_ref, next_ref, rows
):
    finals, _ = first_tokens(hop_ref, recv_ref, early_ref, cq_ref, ck_ref, cv_ref, rows)
    first = lax.axis_index("half") == 0
    for r in range(2):
        last = last_ref[r]
        through = mm_parts(halves(last[:, DV:]), halves(finals[r]))
        own = hop_own[r * DK : (r + 1) * DK, :].astype(F32)
        moved = jnp.where(first, own, through + last[:, :DV])
        next_ref[r * DK : (r + 1) * DK, :] = moved.astype(BF16)
    next_ref[2 * DK :, :] = hop_own[2 * DK :, :]


def open_gate_kernel(hop_ref, z_ref, gate_ref):
    del hop_ref
    for at in range(0, z_ref.shape[1], DV):
        gate_ref[:, at : at + DV] = silu(z_ref[:, at : at + DV].astype(F32))


def gate_kernel(heads_axis, normed_ref, gate_ref, out_ref, made, sems):
    subs, tokens = normed_ref.shape[0] // heads_axis, gate_ref.shape[0]
    width = subs * 2 * DV
    copies = []
    for head in range(heads_axis):
        for sub in range(subs):
            for r in range(2):
                at = (2 * (head * subs + sub) + r) * DV
                gate = gate_ref[:, at : at + DV]
                here = slice(r * tokens, (r + 1) * tokens)
                value = normed_ref[sub * heads_axis + head, here, :].astype(F32)
                made[:, at : at + DV] = (value * gate).astype(BF16)
        lanes = pl.ds(head * width, width)
        copy = pltpu.make_async_copy(made.at[:, lanes], out_ref.at[:, lanes], sems.at[head])
        copy.start()
        copies.append(copy)
    for copy in copies:
        copy.wait()


VMEM = pl.BlockSpec(memory_space=pltpu.VMEM)
SMEM = pl.BlockSpec(memory_space=pltpu.SMEM)
ANY = pl.BlockSpec(memory_space=pl.ANY)


def near(x):
    return pltpu.with_memory_space_constraint(x, pltpu.VMEM)


def far(x):
    return pltpu.with_memory_space_constraint(x, pltpu.HBM)


def call(kernel, outs, in_specs, scratch=(), out_spec=VMEM, flops=1 << 26, moved=1 << 21):
    return pl.pallas_call(
        kernel,
        out_shape=outs,
        in_specs=in_specs,
        out_specs=jax.tree.map(lambda _: out_spec, outs),
        scratch_shapes=list(scratch),
        compiler_params=pltpu.CompilerParams(vmem_limit_bytes=VMEM_BYTES),
        cost_estimate=pl.CostEstimate(flops=flops, bytes_accessed=moved, transcendentals=0),
    )


def local(
    q_rows,
    k_rows,
    v_rows,
    z_rows,
    a_rows,
    b_rows,
    conv_q,
    conv_k,
    conv_v,
    a_log,
    dt_bias,
    norm_gain,
):
    shards, subs, heads_axis = (lax.axis_size(a) for a in ("half", "sub", "head"))
    peers, tokens = subs * heads_axis, q_rows.shape[0]
    total = peers * tokens
    spans = total // SPAN
    group = ("sub", "head")
    route = [(i, i + 1) for i in range(shards - 1)]
    conv_q, conv_k, conv_v = near(conv_q), near(conv_k), near(conv_v)
    gain = near(norm_gain.reshape(1, DV))
    inputs = [far(x) for x in (q_rows, k_rows, v_rows, a_rows.T, b_rows.T)]
    packed = call(
        functools.partial(pack_kernel, heads_axis),
        pltpu.VMEM((peers, GATES + 4 * tokens, 128), BF16),
        [ANY] * 5,
        [pltpu.VMEM(x.shape, BF16) for x in inputs] + [pltpu.SemaphoreType.DMA((5,))],
        flops=1 << 20,
    )(*inputs)
    blocks = near(lax.all_to_all(packed, group, 0, 0, tiled=True))
    key_shapes = (pltpu.VMEM((total, DK), BF16), pltpu.VMEM((spans, DK, SPAN), BF16))
    system_shapes = (
        pltpu.VMEM((2, spans, 2, SPAN, SPAN), BF16),
        pltpu.VMEM((2, spans, SUB, SPAN), F32),
    )
    decay_shapes = (
        pltpu.VMEM((SPAN, DK), F32),
        pltpu.VMEM((2, total, SPAN), BF16),
        pltpu.VMEM((SPAN, SPAN), F32),
    )
    map_shapes = (
        pltpu.VMEM((2, spans, 2, SPAN, SPAN), BF16),
        pltpu.VMEM((2, spans, DK, DK), BF16),
    )
    opened = call(
        opening_kernel,
        (
            pltpu.VMEM((2 * DK + 16, 128), BF16),
            *key_shapes,
            *decay_shapes,
            *map_shapes,
            pltpu.VMEM((2, total, DV), BF16),
            pltpu.VMEM((2, spans, 2 * DK, DV), BF16),
            pltpu.VMEM((2, spans, DK, DV), F32),
        ),
        [VMEM, VMEM, VMEM, SMEM, SMEM, VMEM, VMEM],
        [
            pltpu.VMEM((8 + total, DK), F32),
            pltpu.VMEM((8 + total, 2 * DV), F32),
            *system_shapes,
        ],
        flops=1 << 32,
    )(blocks, conv_k, conv_v, a_log, dt_bias, conv_q, gain)
    hop = opened[0]
    entering = near(lax.ppermute(hop, "half", route))
    hop, keys, keys_t, ends, within, cols, inverses, lins, values, starts, adds = (
        near(x) for x in opened
    )
    first_out = call(
        first_outputs_kernel,
        pltpu.VMEM((2, total, DV), F32),
        [VMEM] * 12,
        [pltpu.VMEM((8 + total, DK), F32)],
        flops=1 << 32,
    )(
        blocks,
        conv_q,
        keys,
        keys_t,
        inverses,
        lins,
        ends,
        within,
        cols,
        values,
        starts,
        adds,
    )
    open_gate = call(
        open_gate_kernel, pltpu.VMEM(z_rows.shape, F32), [VMEM] * 2, flops=1 << 30
    )(hop, near(z_rows))
    made = call(
        systems_kernel,
        (*key_shapes, *system_shapes, *decay_shapes, pltpu.VMEM((8, SPAN), F32)),
        [VMEM, VMEM, VMEM, SMEM, SMEM],
        [pltpu.VMEM((8 + total, DK), F32)],
        flops=1 << 32,
    )(hop, blocks, conv_k, a_log, dt_bias)
    keys, keys_t, systems, small, ends, within, cols, early = (near(x) for x in made)
    later_solved = call(inverse_kernel, map_shapes, [VMEM] * 6, flops=1 << 32)(
        hop, keys, keys_t, systems, small, cols
    )
    later_inverses, later_lins = (near(x) for x in later_solved)
    read_on = [pltpu.VMEM((2, DK, 2 * DV), F32)] if shards > 2 else []
    later_values, states, *last = call(
        states_kernel,
        (
            pltpu.VMEM((2, total, DV), BF16),
            pltpu.VMEM((2, 2, spans, 2 * DK, DV), BF16),
            *read_on,
        ),
        [VMEM] * 7,
        [pltpu.VMEM((8 + total, 2 * DV), F32)],
        flops=1 << 32,
    )(blocks, conv_v, keys_t, later_inverses, later_lins, ends, cols)
    out_a, out_m = call(
        later_outputs_kernel,
        (pltpu.VMEM((2, total, DV), F32), pltpu.VMEM((2, total, DV), BF16)),
        [VMEM] * 9,
        [pltpu.VMEM((8 + total, DK), F32)],
        flops=1 << 32,
    )(
        blocks,
        conv_q,
        keys,
        keys_t,
        later_inverses,
        within,
        cols,
        near(later_values),
        near(states),
    )
    for _ in range(shards - 2):
        moved = call(
            advance_kernel,
            pltpu.VMEM(hop.shape, BF16),
            [VMEM] * 8,
            [pltpu.VMEM((32, 512), F32)],
        )(entering, blocks, early, conv_q, conv_k, conv_v, hop, near(last[0]))
        entering = near(lax.ppermute(moved, "half", route))
    normed = call(
        finish_kernel,
        pltpu.VMEM((peers, 2 * tokens, DV), BF16),
        [VMEM] * 10,
        [pltpu.VMEM((32, 512), F32)],
    )(
        entering,
        blocks,
        early,
        conv_q,
        conv_k,
        conv_v,
        gain,
        near(first_out),
        near(out_a),
        near(out_m),
    )
    returned = near(lax.all_to_all(normed, group, 0, 0, tiled=True))
    return call(
        functools.partial(gate_kernel, heads_axis),
        jax.ShapeDtypeStruct(z_rows.shape, BF16),
        [VMEM] * 2,
        [pltpu.VMEM(z_rows.shape, BF16), pltpu.SemaphoreType.DMA((heads_axis,))],
        ANY,
    )(returned, near(open_gate))


def solution(mesh):
    heads_axis = mesh.shape["head"]
    subs = KH // heads_axis
    regrouped = Mesh(
        mesh.devices.reshape(mesh.shape["ctx"] // subs, subs, heads_axis), ("half", "sub", "head")
    )
    row = P(("half", "sub", "head"), None)
    placed = (row,) * 6 + (P(None, "head"),) * 3 + (P("head"),) * 2 + (P(),)
    return jax.shard_map(local, mesh=regrouped, in_specs=placed, out_specs=row, check_vma=False)
```

```python
import functools

import jax
import jax.numpy as jnp
from jax import lax
from jax.experimental import pallas as pl
from jax.experimental.pallas import tpu as pltpu
from jax.sharding import Mesh, PartitionSpec as P

DK = 128
DV = 128
CONV = 4
KH = 16
SUB = 16
SPAN = 128
EDGE = CONV - 1
EPS = 1e-06
F32 = jnp.float32
BF16 = jnp.bfloat16
VMEM_BYTES = 24 * 1024 * 1024
GATES = 8


def dot(a, b, dims=((1,), (0,))):
    return lax.dot_general(a, b, (dims, ((), ())), preferred_element_type=F32)


def halves(x):
    high = x.astype(BF16)
    return high, (x - high.astype(F32)).astype(BF16)


def mm_parts(a, b):
    left = jnp.concatenate([a[0], a[1], a[0]], axis=1)
    return dot(left, jnp.concatenate([b[0], b[0], b[1]], axis=0))


def silu(x):
    half = 0.5 * x
    return half + half * jnp.tanh(half)


def unit(y, factor):
    scale = lax.rsqrt(jnp.sum(y * y, axis=-1, keepdims=True) + EPS)
    return (y * scale * factor).astype(BF16)


def iota(shape, dim):
    return lax.broadcasted_iota(jnp.int32, shape, dim)


def block_of(x, size):
    return lax.shift_right_logical(x, jnp.full(x.shape, size.bit_length() - 1, jnp.int32))


def place_in(x, size):
    return x & (size - 1)


def pack_kernel(
    heads_axis, q_in, k_in, v_in, at_in, bt_in, out_ref, q_ref, k_ref, v_ref, at_ref, bt_ref, sems
):
    peers, tokens = out_ref.shape[0], q_ref.shape[0]
    pairs = ((at_in, at_ref), (bt_in, bt_ref), (k_in, k_ref), (v_in, v_ref), (q_in, q_ref))
    copies = [pltpu.make_async_copy(a, b, sems.at[i]) for i, (a, b) in enumerate(pairs)]
    for copy in copies:
        copy.start()
    subs = peers // heads_axis
    key_heads = [(dest % heads_axis) * subs + dest // heads_axis for dest in range(peers)]
    for copy in copies[:2]:
        copy.wait()
    value_heads = at_ref.shape[0]
    row, entry = iota((peers * GATES, value_heads), 0), iota((peers * GATES, value_heads), 1)
    dest, which = block_of(row, GATES), place_in(row, GATES)
    first = 2 * (place_in(dest, heads_axis) * subs + block_of(dest, heads_axis))
    pick_a = jnp.where((which < 2) & (entry == first + which), 1.0, 0.0).astype(BF16)
    pick_b = jnp.where(
        (which >= 2) & (which < 4) & (entry == first + which - 2), 1.0, 0.0
    ).astype(BF16)
    picked = (dot(pick_a, at_ref[...]) + dot(pick_b, bt_ref[...])).astype(BF16)
    lane_shift = tokens * lax.rem(lax.axis_index("head"), SPAN // tokens)
    place = jnp.where(
        iota((tokens, SPAN), 1) == iota((tokens, SPAN), 0) + lane_shift, 1.0, 0.0
    ).astype(BF16)
    gates = dot(picked, place).astype(BF16)
    for dest in range(peers):
        out_ref[dest, 4 * tokens :, :] = gates[GATES * dest : GATES * (dest + 1), :]

    def laid(ref, lane, start):
        for dest, key_head in enumerate(key_heads):
            at = lane(key_head) * 128
            out_ref[dest, start * tokens : (start + 1) * tokens, :] = ref[
                :, at : at + 128
            ]

    copies[2].wait()
    laid(k_ref, lambda key_head: key_head, 0)
    copies[3].wait()
    laid(v_ref, lambda key_head: 2 * key_head, 1)
    laid(v_ref, lambda key_head: 2 * key_head + 1, 2)
    copies[4].wait()
    laid(q_ref, lambda key_head: key_head, 3)


def compacted(system):
    size = system.shape[0]
    diagonal = block_of(iota((size, size), 0), SUB) == block_of(iota((size, size), 1), SUB)
    return jnp.sum(jnp.where(diagonal, system, 0.0).reshape(size // SUB, SUB, size), axis=0)


def substituted(compact):
    count, _, size = compact.shape
    flat = compact.reshape(count * SUB, size)
    lane, line = iota(flat.shape, 1), iota(flat.shape, 0)
    solved = jnp.where(place_in(lane ^ line, SUB) == 0, 1.0, 0.0).reshape(count, SUB, size)
    for m in range(SUB - 1):
        source = (lane & ~(SUB - 1)) | m
        spread = jnp.take_along_axis(flat, source, axis=1, mode="promise_in_bounds")
        solved = solved + spread.reshape(count, SUB, size) * solved[:, m : m + 1, :]
    return solved


def inverted(systems, small, meanwhile=lambda: None):
    size = systems[0][0].shape[0]
    row, col = iota((size, size), 0), iota((size, size), 1)
    placed = jnp.where(block_of(row, SUB) == block_of(col, SUB), 1.0, 0.0).astype(BF16)
    identity = jnp.where(row == col, 1.0, 0.0)
    rough = [
        jnp.concatenate([block.astype(BF16)] * (size // SUB), axis=0) * placed for block in small
    ]
    blank = jnp.zeros((size, size), BF16)
    width = SUB
    while width < size:
        odd = [(j, j + width) for j in range(width, size, 2 * width)]

        def rows_of(x):
            return jnp.concatenate([x[lo:hi] for lo, hi in odd], axis=0)

        def woven(even, x):
            pieces = []
            for j, (lo, hi) in enumerate(odd):
                pieces += [even[lo - width : lo], x[j * width : (j + 1) * width]]
            return jnp.concatenate(pieces, axis=0)

        below = rows_of(block_of(row ^ col, 2 * width)) + rows_of(col & width) == 0
        own = rows_of(identity)
        firsts = [dot(rows_of(n[0]), t) for n, t in zip(systems, rough)]
        meanwhile()
        rights = [
            woven(blank, jnp.where(below, first, own).astype(BF16)) for first in firsts
        ]
        grown = [dot(rows_of(t), right).astype(BF16) for t, right in zip(rough, rights)]
        rough = [woven(t, g) for t, g in zip(rough, grown)]
        width *= 2
    products = [
        dot(jnp.concatenate(n, axis=1), jnp.concatenate([t, t], axis=0))
        for n, t in zip(systems, rough)
    ]
    rests = [
        (identity - t.astype(F32) + product).astype(BF16) for t, product in zip(rough, products)
    ]
    return [halves(t.astype(F32) + dot(t, rest)) for t, rest in zip(rough, rests)]


def own_entry(ref, index):
    row = ref[...]
    return jnp.sum(jnp.where(iota(row.shape, 1) == index, row, 0.0), axis=1, keepdims=True)


def gate_values(gates, sub, alog_ref, dt_ref):
    second = place_in(iota(gates.shape, 0), GATES) == 1
    a_log, dt_bias = (
        jnp.where(second, own_entry(ref, 2 * sub + 1), own_entry(ref, 2 * sub))
        for ref in (alog_ref, dt_ref)
    )
    shifted = gates + dt_bias
    soft = jnp.maximum(shifted, 0.0) + jnp.log1p(jnp.exp(-jnp.abs(shifted)))
    return -jnp.exp(a_log) * soft, 1.0 / (1.0 + jnp.exp(-gates))


def convolved(rows, at, count, lanes, tap):
    summed = tap[0:1] * rows[at : at + count, lanes]
    for j in range(1, CONV):
        summed = summed + tap[j : j + 1] * rows[at + j : at + j + count, lanes]
    return silu(summed)


def key_tap(sub, tap_ref):
    return tap_ref[:, pl.ds(pl.multiple_of(sub * DK, 128), DK)]


def value_taps(sub, cv_ref):
    lane = pl.multiple_of(sub * 2 * DV, 128)
    return [cv_ref[:, pl.ds(pl.multiple_of(lane + r * DV, 128), DV)] for r in range(2)]


def widened(rows, recv_ref, starts, tokens):
    rows[0:8, :] = jnp.zeros((8, rows.shape[1]), F32)
    for s in range(recv_ref.shape[0]):
        for g, start in enumerate(starts):
            rows[8 + s * tokens : 8 + (s + 1) * tokens, g * 128 : (g + 1) * 128] = recv_ref[
                s, start : start + tokens, :
            ].astype(F32)


def systems_kernel(hop_ref, recv_ref, ck_ref, alog_ref, dt_ref, *refs):
    del hop_ref

    @pl.when(lax.axis_index("half") > 0)
    def _():
        systems_of(recv_ref, ck_ref, alog_ref, dt_ref, *refs)


def systems_of(
    recv_ref,
    ck_ref,
    alog_ref,
    dt_ref,
    keys_ref,
    keys_t_ref,
    systems_ref,
    small_ref,
    ends_ref,
    within_ref,
    cols_ref,
    early_ref,
    rows,
):
    sub = lax.axis_index("sub")
    later = lax.axis_index("half") > 0
    peers = recv_ref.shape[0]
    tokens = (recv_ref.shape[1] - GATES) // 4
    spans = peers * tokens // SPAN
    tap = key_tap(sub, ck_ref)
    widened(rows, recv_ref, [0], tokens)
    stacked = [
        sum(recv_ref[s, 4 * tokens :, :].astype(F32) for s in range(n, n + SPAN // tokens))
        for n in range(0, peers, SPAN // tokens)
    ]
    stacked.append(jnp.zeros((SPAN - spans * GATES, SPAN), F32))
    gates = jnp.concatenate(stacked, axis=0)
    decay, rate = gate_values(gates, sub, alog_ref, dt_ref)
    if early_ref is not None:
        early_ref[...] = jnp.where(iota((8, SPAN), 0) < 2, decay[0:8], rate[0:8])
    skipped = later & (iota(gates.shape, 0) < GATES) & (iota(gates.shape, 1) < EDGE)
    decay = jnp.where(skipped, 0.0, decay)
    rate = jnp.where(skipped, 0.0, rate)
    lane_r, lane_c = iota((SPAN, SPAN), 0), iota((SPAN, SPAN), 1)
    upto = jnp.where(lane_r <= lane_c, 1.0, 0.0).astype(BF16)
    d_high, _ = halves(decay)
    d_mid, d_low = halves(decay - d_high.astype(F32))
    cum = dot(d_high, upto) + (dot(d_mid, upto) + dot(d_low, upto))
    growth = jnp.exp(cum)
    here = pltpu.roll(rate, rate.shape[0] - 2, 0)
    rest = jnp.exp(cum[:, SPAN - 1 :] - cum) * here
    which = place_in(iota(gates.shape, 0), GATES)
    mixed = jnp.where(which < 2, cum, pltpu.roll(growth, 2, 0))
    columns = jnp.transpose(jnp.where(which < 4, mixed, pltpu.roll(rest, 4, 0)))
    cols_ref[...] = columns
    lower = lane_r >= lane_c
    strict = lane_r > lane_c
    both = [(n, r) for n in range(spans) for r in range(2)]
    keys = []
    for n in range(spans):
        k_n = unit(convolved(rows, n * SPAN + 8 - EDGE, SPAN, slice(0, DK), tap), 1.0)
        keys_ref[n * SPAN : (n + 1) * SPAN, :] = k_n
        keys.append(k_n)
    keys_t = []
    for n in range(spans):
        kt_n = jnp.transpose(keys[n].astype(F32)).astype(BF16)
        keys_t_ref[n] = kt_n
        keys_t.append(kt_n)
    grams = [dot(keys[n], keys_t[n]) for n in range(spans)]
    for n, r in both:
        at = GATES * n + r
        gap = columns[:, at : at + 1] - cum[at : at + 1, :]
        within = jnp.exp(jnp.where(lower, gap, 0.0)) * here[at : at + 1, :]
        within_ref[r, n * SPAN : (n + 1) * SPAN, :] = jnp.where(lower, within, 0.0).astype(BF16)
        system = jnp.where(strict, within * -grams[n], 0.0)
        systems_ref[r, n, 0], systems_ref[r, n, 1] = halves(system)
        small_ref[r, n] = compacted(system)
    ends_ref[...] = jnp.broadcast_to(growth[:, SPAN - 1 :], ends_ref.shape)


def inverse_kernel(
    hop_ref, keys_ref, keys_t_ref, systems_ref, small_ref, cols_ref, t_ref, lin_ref
):
    del hop_ref
    spans = keys_t_ref.shape[0]
    both = [(n, r) for n in range(spans) for r in range(2)]

    @pl.when(lax.axis_index("half") > 0)
    def _():
        compact = jnp.concatenate([small_ref[r, n] for n, r in both], axis=0)
        small = substituted(compact.reshape(len(both), SUB, SPAN))
        systems = [(systems_ref[r, n, 0], systems_ref[r, n, 1]) for n, r in both]
        inverses = inverted(systems, [small[i] for i in range(len(both))])
        scaled = []
        for i, (n, r) in enumerate(both):
            t_ref[r, n, 0], t_ref[r, n, 1] = inverses[i]
            at = GATES * n + r
            key = keys_ref[n * SPAN : (n + 1) * SPAN, :].astype(F32)
            right = (cols_ref[:, at + 2 : at + 3] * key).astype(BF16)
            scaled.append(jnp.concatenate([right, right], axis=0))
        w_mats = [dot(jnp.concatenate(t, axis=1), x) for t, x in zip(inverses, scaled)]
        weighed = []
        for (n, r), w_mat in zip(both, w_mats):
            at = GATES * n + r
            weighed.append((cols_ref[:, at + 4 : at + 5] * w_mat).astype(BF16))
        moved = [
            dot(keys_t_ref[n], jnp.concatenate(weighed[2 * n : 2 * n + 2], axis=1))
            for n in range(spans)
        ]
        for n, r in both:
            lin_ref[r, n] = moved[n][:, r * DK : (r + 1) * DK].astype(BF16)


def unwound(t_ref, n, r, x):
    both = jnp.concatenate([t_ref[r, n, 0], t_ref[r, n, 1]], axis=1)
    return dot(both, jnp.concatenate([x, x], axis=0))


def end_of(ends_ref, n, r):
    return ends_ref[GATES * n + r : GATES * n + r + 1, :]


def followed(span_map, state):
    end, moved, add = span_map
    return step(end, moved, state, halves(state)) + add


def composed(maps):
    if len(maps) == 1:
        return maps[0]
    half = len(maps) // 2
    end_a, moved_a, add_a = composed(maps[:half])
    end_b, moved_b, add_b = composed(maps[half:])
    high, low = halves(add_a)
    rights = jnp.concatenate(
        [
            jnp.concatenate([moved_a, high], axis=1),
            jnp.concatenate([jnp.zeros_like(moved_a), low], axis=1),
        ],
        axis=0,
    )
    passed = dot(jnp.concatenate([moved_b, moved_b], axis=1), rights)
    moved = end_b * moved_a.astype(F32) + end_a * moved_b.astype(F32) - passed[:, :DK]
    add = end_b * add_a - passed[:, DK:] + add_b
    return end_a * end_b, moved.astype(BF16), add


def step(end, moved, state, parts):
    both = jnp.concatenate([moved, moved], axis=1)
    return end * state - dot(both, jnp.concatenate(parts, axis=0))


def values_part(recv_ref, cv_ref, keys_t_ref, t_ref, cols_ref, rows, vs):
    sub = lax.axis_index("sub")
    tokens = (recv_ref.shape[1] - GATES) // 4
    spans = t_ref.shape[1]
    taps = value_taps(sub, cv_ref)
    widened(rows, recv_ref, [tokens, 2 * tokens], tokens)
    both = [(n, r) for n in range(spans) for r in range(2)]
    values = []
    for n, r in both:
        lanes = slice(r * DV, (r + 1) * DV)
        v_n = convolved(rows, n * SPAN + 8 - EDGE, SPAN, lanes, taps[r]).astype(BF16)
        vs[r, n * SPAN : (n + 1) * SPAN, :] = v_n
        values.append(v_n)
    solved = [unwound(t_ref, n, r, v) for (n, r), v in zip(both, values)]
    weighed = []
    for (n, r), u_mat in zip(both, solved):
        at = GATES * n + r
        weighed.append((cols_ref[:, at + 4 : at + 5] * u_mat).astype(BF16))
    moved = [
        dot(keys_t_ref[n], jnp.concatenate(weighed[2 * n : 2 * n + 2], axis=1))
        for n in range(spans)
    ]
    return [moved[n][:, r * DV : (r + 1) * DV] for n, r in both]


def opening_kernel(
    recv_ref,
    ck_ref,
    cv_ref,
    alog_ref,
    dt_ref,
    cq_ref,
    gain_ref,
    hop_ref,
    keys_ref,
    keys_t_ref,
    ends_ref,
    within_ref,
    cols_ref,
    t_ref,
    lin_ref,
    vs_ref,
    xs_ref,
    adds_ref,
    key_rows,
    rows,
    systems_ref,
    small_ref,
):
    first = lax.axis_index("half") == 0
    peers = recv_ref.shape[0]
    tokens = (recv_ref.shape[1] - GATES) // 4
    spans = keys_t_ref.shape[0]
    edges = []
    for which in (3, 0, 1, 2):
        end = (which + 1) * tokens
        edges.append(recv_ref[peers - 1, end - 16 : end, :].astype(F32)[16 - EDGE :])
    edges.append(jnp.zeros((16 - 4 * EDGE, 128), F32))
    hop_ref[2 * DK :, :] = jnp.concatenate(edges, axis=0).astype(BF16)

    @pl.when(first)
    def _():
        both = [(n, r) for n in range(spans) for r in range(2)]
        systems_of(
            recv_ref,
            ck_ref,
            alog_ref,
            dt_ref,
            keys_ref,
            keys_t_ref,
            systems_ref,
            small_ref,
            ends_ref,
            within_ref,
            cols_ref,
            None,
            key_rows,
        )
        taps = value_taps(lax.axis_index("sub"), cv_ref)
        widened(rows, recv_ref, [tokens, 2 * tokens], tokens)
        waiting = list(both)

        def meanwhile():
            for n, r in waiting[:6]:
                lanes = slice(r * DV, (r + 1) * DV)
                value = convolved(rows, n * SPAN + 8 - EDGE, SPAN, lanes, taps[r])
                vs_ref[r, n * SPAN : (n + 1) * SPAN, :] = value.astype(BF16)
            del waiting[:6]

        compact = jnp.concatenate([small_ref[r, n] for n, r in both], axis=0)
        small = substituted(compact.reshape(len(both), SUB, SPAN))
        systems = [(systems_ref[r, n, 0], systems_ref[r, n, 1]) for n, r in both]
        inverses = inverted(systems, [small[i] for i in range(len(both))], meanwhile)
        while waiting:
            meanwhile()
        rights = []
        for i, (n, r) in enumerate(both):
            t_ref[r, n, 0], t_ref[r, n, 1] = inverses[i]
            at = GATES * n + r
            here = slice(n * SPAN, (n + 1) * SPAN)
            key = (cols_ref[:, at + 2 : at + 3] * keys_ref[here, :].astype(F32)).astype(BF16)
            right = jnp.concatenate([key, vs_ref[r, here, :]], axis=1)
            rights.append(jnp.concatenate([right, right], axis=0))
        solved = [dot(jnp.concatenate(t, axis=1), x) for t, x in zip(inverses, rights)]
        weighed = []
        for (n, r), x in zip(both, solved):
            at = GATES * n + r
            weighed.append((cols_ref[:, at + 4 : at + 5] * x).astype(BF16))
        moved = [
            dot(keys_t_ref[n], jnp.concatenate(weighed[2 * n : 2 * n + 2], axis=1))
            for n in range(spans)
        ]
        adds = []
        for n, r in both:
            at = 2 * r * DK
            lin_ref[r, n] = moved[n][:, at : at + DK].astype(BF16)
            adds.append(moved[n][:, at + DK : at + 2 * DK])
            adds_ref[r, n] = adds[-1]
        maps = [
            [(end_of(ends_ref, n, r), lin_ref[r, n], adds[2 * n + r]) for n in range(spans)]
            for r in range(2)
        ]
        states = [m[0][2] for m in maps]
        done = 1
        while done < spans:
            for r in range(2):
                if done > 1:
                    xs_ref[r, done] = jnp.concatenate(halves(states[r]), axis=0)
            later = [composed(m[done : 2 * done]) for m in maps]
            states = [followed(m, x) for m, x in zip(later, states)]
            done *= 2
        for r in range(2):
            hop_ref[r * DK : (r + 1) * DK, :] = states[r].astype(BF16)

    @pl.when(jnp.logical_not(first))
    def _():
        hop_ref[0 : 2 * DK, :] = jnp.zeros((2 * DK, DV), BF16)


def states_kernel(
    recv_ref,
    cv_ref,
    keys_t_ref,
    t_ref,
    lin_ref,
    ends_ref,
    cols_ref,
    values_ref,
    states_ref,
    *rest,
):
    *last_ref, rows = rest

    @pl.when(lax.axis_index("half") > 0)
    def _():
        spans = t_ref.shape[1]
        adds = values_part(recv_ref, cv_ref, keys_t_ref, t_ref, cols_ref, rows, values_ref)
        zero_half = jnp.zeros((DK, DV), F32)
        identity = jnp.where(iota((DK, DK), 0) == iota((DK, DK), 1), 1.0, 0.0)
        states = [
            jnp.concatenate(
                [adds[r], ends_ref[r : r + 1, :] * identity - lin_ref[r, 0].astype(F32)], axis=1
            )
            for r in range(2)
        ]
        for n in range(1, spans):
            for r in range(2):
                parts = halves(states[r])
                for i in range(2):
                    both_parts = [x[:, i * DV : (i + 1) * DV] for x in parts]
                    states_ref[i, r, n] = jnp.concatenate(both_parts, axis=0)
                add = jnp.concatenate([adds[2 * n + r], zero_half], axis=1)
                end = jnp.concatenate([end_of(ends_ref, n, r)] * 2, axis=1)
                states[r] = step(end, lin_ref[r, n], states[r], parts) + add
        for ref in last_ref:
            for r in range(2):
                ref[r] = states[r]


def span_rows(n):
    return slice(n * SPAN, (n + 1) * SPAN)


def twice(x, axis):
    return jnp.concatenate([x, x], axis=axis)


def asked(recv_ref, cq_ref, keys_ref, keys_t_ref, within_ref, query_rows):
    tokens = (recv_ref.shape[1] - GATES) // 4
    spans = keys_t_ref.shape[0]
    tap = key_tap(lax.axis_index("sub"), cq_ref)
    widened(query_rows, recv_ref, [3 * tokens], tokens)
    queries = [
        unit(convolved(query_rows, n * SPAN + 8 - EDGE, SPAN, slice(0, DK), tap), DK**-0.5)
        for n in range(spans)
    ]
    readers = [
        jnp.concatenate([keys_ref[span_rows(n), :], queries[n]], axis=0) for n in range(spans)
    ]
    scores = [dot(queries[n], keys_t_ref[n]) for n in range(spans)]
    inner = [
        (within_ref[r, span_rows(n), :].astype(F32) * scores[n]).astype(BF16)
        for n in range(spans)
        for r in range(2)
    ]
    return readers, inner


def first_outputs_kernel(
    recv_ref,
    cq_ref,
    keys_ref,
    keys_t_ref,
    t_ref,
    lin_ref,
    ends_ref,
    within_ref,
    cols_ref,
    values_ref,
    xs_ref,
    adds_ref,
    oa_ref,
    query_rows,
):
    @pl.when(lax.axis_index("half") == 0)
    def _():
        spans = t_ref.shape[1]
        both = [(n, r) for n in range(spans) for r in range(2)]
        readers, inner = asked(recv_ref, cq_ref, keys_ref, keys_t_ref, within_ref, query_rows)
        stacks, states = [], []
        for n in range(1, spans):
            if n == 1:
                states = [adds_ref[r, 0] for r in range(2)]
                stack = [jnp.concatenate(halves(x), axis=0) for x in states]
            elif n & (n - 1) == 0:
                stack = [xs_ref[r, n] for r in range(2)]
                states = [x[:DK].astype(F32) + x[DK:].astype(F32) for x in stack]
            else:
                states = [
                    followed(
                        (end_of(ends_ref, n - 1, r), lin_ref[r, n - 1], adds_ref[r, n - 1]),
                        states[r],
                    )
                    for r in range(2)
                ]
                stack = [jnp.concatenate(halves(x), axis=0) for x in states]
            stacks.append(jnp.concatenate(stack, axis=1))
        reads = [dot(twice(readers[n], 1), stacks[n - 1]) for n in range(1, spans)]
        rests, seen = [], []
        for n, r in both:
            lanes = slice(r * DV, (r + 1) * DV)
            value = values_ref[r, span_rows(n), :]
            if n == 0:
                rests.append(value)
                seen.append(None)
            else:
                growth = cols_ref[:, GATES * n + 2 + r : GATES * n + 3 + r]
                read = growth * reads[n - 1][:SPAN, lanes]
                rests.append((value.astype(F32) - read).astype(BF16))
                seen.append(growth * reads[n - 1][SPAN:, lanes])
        fresh = [unwound(t_ref, n, r, x).astype(BF16) for (n, r), x in zip(both, rests)]
        spreads = [dot(w, x) for w, x in zip(inner, fresh)]
        for (n, r), x, y in zip(both, spreads, seen):
            oa_ref[r, span_rows(n), :] = x if y is None else x + y


def later_outputs_kernel(
    recv_ref,
    cq_ref,
    keys_ref,
    keys_t_ref,
    t_ref,
    within_ref,
    cols_ref,
    values_ref,
    states_ref,
    oa_ref,
    om_ref,
    query_rows,
):
    @pl.when(lax.axis_index("half") > 0)
    def _():
        spans = t_ref.shape[1]
        both = [(n, r) for n in range(spans) for r in range(2)]
        readers, inner = asked(recv_ref, cq_ref, keys_ref, keys_t_ref, within_ref, query_rows)
        zero_half = jnp.zeros((SPAN, DV), F32)
        reads = [
            dot(
                twice(readers[n], 1),
                jnp.concatenate([states_ref[0, r, n], states_ref[1, r, n]], axis=1),
            )
            if n > 0
            else None
            for n, r in both
        ]
        rests, seen = [], []
        for (n, r), read in zip(both, reads):
            value = values_ref[r, span_rows(n), :].astype(F32)
            growth = cols_ref[:, GATES * n + 2 + r : GATES * n + 3 + r]
            if n == 0:
                reader = readers[n].astype(F32)
                rest = jnp.concatenate([value, -(growth * reader[:SPAN])], axis=1)
                seen.append(jnp.concatenate([zero_half, growth * reader[SPAN:]], axis=1))
            else:
                rest = jnp.concatenate([value, zero_half], axis=1) - growth * read[:SPAN]
                seen.append(growth * read[SPAN:])
            rests.append(rest.astype(BF16))
        fresh = [unwound(t_ref, n, r, x).astype(BF16) for (n, r), x in zip(both, rests)]
        spreads = [dot(w, x) for w, x in zip(inner, fresh)]
        for (n, r), x, y in zip(both, spreads, seen):
            out = x + y
            oa_ref[r, span_rows(n), :] = out[:, :DV]
            om_ref[r, span_rows(n), :] = out[:, DV:].astype(BF16)


def first_tokens(hop_ref, recv_ref, early_ref, cq_ref, ck_ref, cv_ref, rows):
    sub = lax.axis_index("sub")
    tokens = (recv_ref.shape[1] - GATES) // 4
    taps = [key_tap(sub, cq_ref), key_tap(sub, ck_ref)] + value_taps(sub, cv_ref)
    results = []
    edges = hop_ref[2 * DK :, :].astype(F32)
    for g, first in enumerate((3, 0, 1, 2)):
        lanes = slice(g * 128, (g + 1) * 128)
        start = first * tokens
        rows[16 - EDGE : 16, lanes] = edges[EDGE * g : EDGE * (g + 1)]
        rows[16:32, lanes] = recv_ref[0, start : start + 16, :].astype(F32)
        results.append(convolved(rows, 16 - EDGE, 8, lanes, taps[g]))
    q_cols = jnp.transpose(unit(results[0], DK**-0.5).astype(F32))
    k_cols = jnp.transpose(unit(results[1], 1.0).astype(F32))
    gates = early_ref[...]
    line = iota((8, DV), 0)
    finals, outputs = [], []
    for r in range(2):
        values = results[2 + r].astype(BF16).astype(F32)
        entering = hop_ref[r * DK : (r + 1) * DK, :].astype(F32)
        state, out = entering, jnp.zeros((8, DV), F32)
        for t in range(EDGE):
            k_t, q_t = k_cols[:, t : t + 1], q_cols[:, t : t + 1]
            state = jnp.exp(gates[r : r + 1, t : t + 1]) * state
            held = jnp.sum(k_t * state, axis=0, keepdims=True)
            state = state + k_t * (
                gates[2 + r : 3 + r, t : t + 1] * (values[t : t + 1, :] - held)
            )
            out = jnp.where(line == t, jnp.sum(q_t * state, axis=0, keepdims=True), out)
        finals.append(state)
        outputs.append(out)
    return finals, outputs


def finish_kernel(
    hop_ref,
    recv_ref,
    early_ref,
    cq_ref,
    ck_ref,
    cv_ref,
    gain_ref,
    first_oa,
    oa_ref,
    om_ref,
    out_ref,
    rows,
):
    peers, tokens = out_ref.shape[0], out_ref.shape[1] // 2
    first = lax.axis_index("half") == 0
    gain = gain_ref[...]
    chunks = 4
    part, peer_part = peers * tokens // chunks, peers // chunks

    def put(c, r, core):
        scale = lax.rsqrt(jnp.mean(core * core, axis=-1, keepdims=True) + EPS)
        normed = (core * scale * gain).astype(BF16)
        here = slice(c * peer_part, (c + 1) * peer_part)
        out_ref[here, r * tokens : (r + 1) * tokens, :] = normed.reshape(peer_part, tokens, DV)

    @pl.when(first)
    def _():
        for c in range(chunks):
            for r in range(2):
                put(c, r, first_oa[r, c * part : (c + 1) * part, :])

    @pl.when(jnp.logical_not(first))
    def _():
        finals, outputs = first_tokens(hop_ref, recv_ref, early_ref, cq_ref, ck_ref, cv_ref, rows)
        replaced = iota((8, DV), 0) < EDGE
        passed = [dot(om_ref[r], finals[r].astype(BF16)) for r in range(2)]
        for c in range(chunks):
            at = c * part
            for r in range(2):
                core = oa_ref[r, at : at + part, :] + passed[r][at : at + part]
                if c == 0:
                    core = jnp.concatenate(
                        [jnp.where(replaced, outputs[r], core[0:8]), core[8:]], axis=0
                    )
                put(c, r, core)


def advance_kernel(
    hop_ref, recv_ref, early_ref, cq_ref, ck_ref, cv_ref, hop_own, last_ref, next_ref, rows
):
    finals, _ = first_tokens(hop_ref, recv_ref, early_ref, cq_ref, ck_ref, cv_ref, rows)
    first = lax.axis_index("half") == 0
    for r in range(2):
        last = last_ref[r]
        through = mm_parts(halves(last[:, DV:]), halves(finals[r]))
        own = hop_own[r * DK : (r + 1) * DK, :].astype(F32)
        moved = jnp.where(first, own, through + last[:, :DV])
        next_ref[r * DK : (r + 1) * DK, :] = moved.astype(BF16)
    next_ref[2 * DK :, :] = hop_own[2 * DK :, :]


def gate_kernel(heads_axis, normed_ref, z_ref, out_ref, made, sems):
    subs, tokens = normed_ref.shape[0] // heads_axis, z_ref.shape[0]
    width = subs * 2 * DV
    copies = []
    for head in range(heads_axis):
        for sub in range(subs):
            for r in range(2):
                at = (2 * (head * subs + sub) + r) * DV
                gate = silu(z_ref[:, at : at + DV].astype(F32))
                here = slice(r * tokens, (r + 1) * tokens)
                value = normed_ref[sub * heads_axis + head, here, :].astype(F32)
                made[:, at : at + DV] = (value * gate).astype(BF16)
        lanes = pl.ds(head * width, width)
        copy = pltpu.make_async_copy(made.at[:, lanes], out_ref.at[:, lanes], sems.at[head])
        copy.start()
        copies.append(copy)
    for copy in copies:
        copy.wait()


VMEM = pl.BlockSpec(memory_space=pltpu.VMEM)
ANY = pl.BlockSpec(memory_space=pl.ANY)


def near(x):
    return pltpu.with_memory_space_constraint(x, pltpu.VMEM)


def far(x):
    return pltpu.with_memory_space_constraint(x, pltpu.HBM)


def call(kernel, outs, in_specs, scratch=(), out_spec=VMEM, flops=1 << 26, moved=1 << 21):
    return pl.pallas_call(
        kernel,
        out_shape=outs,
        in_specs=in_specs,
        out_specs=jax.tree.map(lambda _: out_spec, outs),
        scratch_shapes=list(scratch),
        compiler_params=pltpu.CompilerParams(vmem_limit_bytes=VMEM_BYTES),
        cost_estimate=pl.CostEstimate(flops=flops, bytes_accessed=moved, transcendentals=0),
    )


def local(
    q_rows,
    k_rows,
    v_rows,
    z_rows,
    a_rows,
    b_rows,
    conv_q,
    conv_k,
    conv_v,
    a_log,
    dt_bias,
    norm_gain,
):
    shards, subs, heads_axis = (lax.axis_size(a) for a in ("half", "sub", "head"))
    peers, tokens = subs * heads_axis, q_rows.shape[0]
    total = peers * tokens
    spans = total // SPAN
    group = ("sub", "head")
    route = [(i, i + 1) for i in range(shards - 1)]
    conv_q, conv_k, conv_v = near(conv_q), near(conv_k), near(conv_v)
    gain = near(norm_gain.reshape(1, DV))
    a_log, dt_bias = near(a_log.reshape(1, -1)), near(dt_bias.reshape(1, -1))
    inputs = [far(x) for x in (q_rows, k_rows, v_rows, a_rows.T, b_rows.T)]
    packed = call(
        functools.partial(pack_kernel, heads_axis),
        pltpu.VMEM((peers, GATES + 4 * tokens, 128), BF16),
        [ANY] * 5,
        [pltpu.VMEM(x.shape, BF16) for x in inputs] + [pltpu.SemaphoreType.DMA((5,))],
        flops=1 << 20,
    )(*inputs)
    blocks = near(lax.all_to_all(packed, group, 0, 0, tiled=True))
    key_shapes = (pltpu.VMEM((total, DK), BF16), pltpu.VMEM((spans, DK, SPAN), BF16))
    system_shapes = (
        pltpu.VMEM((2, spans, 2, SPAN, SPAN), BF16),
        pltpu.VMEM((2, spans, SUB, SPAN), F32),
    )
    decay_shapes = (
        pltpu.VMEM((SPAN, DK), F32),
        pltpu.VMEM((2, total, SPAN), BF16),
        pltpu.VMEM((SPAN, SPAN), F32),
    )
    map_shapes = (
        pltpu.VMEM((2, spans, 2, SPAN, SPAN), BF16),
        pltpu.VMEM((2, spans, DK, DK), BF16),
    )
    opened = call(
        opening_kernel,
        (
            pltpu.VMEM((2 * DK + 16, 128), BF16),
            *key_shapes,
            *decay_shapes,
            *map_shapes,
            pltpu.VMEM((2, total, DV), BF16),
            pltpu.VMEM((2, spans, 2 * DK, DV), BF16),
            pltpu.VMEM((2, spans, DK, DV), F32),
        ),
        [VMEM] * 7,
        [
            pltpu.VMEM((8 + total, DK), F32),
            pltpu.VMEM((8 + total, 2 * DV), F32),
            *system_shapes,
        ],
        flops=1 << 32,
    )(blocks, conv_k, conv_v, a_log, dt_bias, conv_q, gain)
    hop = opened[0]
    entering = near(lax.ppermute(hop, "half", route))
    hop, keys, keys_t, ends, within, cols, inverses, lins, values, starts, adds = (
        near(x) for x in opened
    )
    first_out = call(
        first_outputs_kernel,
        pltpu.VMEM((2, total, DV), F32),
        [VMEM] * 12,
        [pltpu.VMEM((8 + total, DK), F32)],
        flops=1 << 32,
    )(
        blocks,
        conv_q,
        keys,
        keys_t,
        inverses,
        lins,
        ends,
        within,
        cols,
        values,
        starts,
        adds,
    )
    made = call(
        systems_kernel,
        (*key_shapes, *system_shapes, *decay_shapes, pltpu.VMEM((8, SPAN), F32)),
        [VMEM] * 5,
        [pltpu.VMEM((8 + total, DK), F32)],
        flops=1 << 32,
    )(hop, blocks, conv_k, a_log, dt_bias)
    keys, keys_t, systems, small, ends, within, cols, early = (near(x) for x in made)
    later_solved = call(inverse_kernel, map_shapes, [VMEM] * 6, flops=1 << 32)(
        hop, keys, keys_t, systems, small, cols
    )
    later_inverses, later_lins = (near(x) for x in later_solved)
    read_on = [pltpu.VMEM((2, DK, 2 * DV), F32)] if shards > 2 else []
    later_values, states, *last = call(
        states_kernel,
        (
            pltpu.VMEM((2, total, DV), BF16),
            pltpu.VMEM((2, 2, spans, 2 * DK, DV), BF16),
            *read_on,
        ),
        [VMEM] * 7,
        [pltpu.VMEM((8 + total, 2 * DV), F32)],
        flops=1 << 32,
    )(blocks, conv_v, keys_t, later_inverses, later_lins, ends, cols)
    out_a, out_m = call(
        later_outputs_kernel,
        (pltpu.VMEM((2, total, DV), F32), pltpu.VMEM((2, total, DV), BF16)),
        [VMEM] * 9,
        [pltpu.VMEM((8 + total, DK), F32)],
        flops=1 << 32,
    )(
        blocks,
        conv_q,
        keys,
        keys_t,
        later_inverses,
        within,
        cols,
        near(later_values),
        near(states),
    )
    for _ in range(shards - 2):
        moved = call(
            advance_kernel,
            pltpu.VMEM(hop.shape, BF16),
            [VMEM] * 8,
            [pltpu.VMEM((32, 512), F32)],
        )(entering, blocks, early, conv_q, conv_k, conv_v, hop, near(last[0]))
        entering = near(lax.ppermute(moved, "half", route))
    normed = call(
        finish_kernel,
        pltpu.VMEM((peers, 2 * tokens, DV), BF16),
        [VMEM] * 10,
        [pltpu.VMEM((32, 512), F32)],
    )(
        entering,
        blocks,
        early,
        conv_q,
        conv_k,
        conv_v,
        gain,
        near(first_out),
        near(out_a),
        near(out_m),
    )
    returned = near(lax.all_to_all(normed, group, 0, 0, tiled=True))
    return call(
        functools.partial(gate_kernel, heads_axis),
        jax.ShapeDtypeStruct(z_rows.shape, BF16),
        [VMEM] * 2,
        [pltpu.VMEM(z_rows.shape, BF16), pltpu.SemaphoreType.DMA((heads_axis,))],
        ANY,
    )(returned, z_rows)


def solution(mesh):
    heads_axis = mesh.shape["head"]
    subs = KH // heads_axis
    regrouped = Mesh(
        mesh.devices.reshape(mesh.shape["ctx"] // subs, subs, heads_axis), ("half", "sub", "head")
    )
    row = P(("half", "sub", "head"), None)
    placed = (row,) * 6 + (P(None, "head"),) * 3 + (P("head"),) * 2 + (P(),)
    return jax.shard_map(local, mesh=regrouped, in_specs=placed, out_specs=row, check_vma=False)
```

```python
import functools

import jax
import jax.numpy as jnp
from jax import lax
from jax.experimental import pallas as pl
from jax.experimental.pallas import tpu as pltpu
from jax.sharding import Mesh, PartitionSpec as P

DK = 128
DV = 128
CONV = 4
KH = 16
SUB = 16
SPAN = 128
CHUNKS = 4
EDGE = CONV - 1
EPS = 1e-06
F32 = jnp.float32
BF16 = jnp.bfloat16
VMEM_BYTES = 24 * 1024 * 1024
GATES = 8


def dot(a, b, dims=((1,), (0,))):
    return lax.dot_general(a, b, (dims, ((), ())), preferred_element_type=F32)


def halves(x):
    high = x.astype(BF16)
    return high, (x - high.astype(F32)).astype(BF16)


def mm_parts(a, b):
    left = jnp.concatenate([a[0], a[1], a[0]], axis=1)
    return dot(left, jnp.concatenate([b[0], b[0], b[1]], axis=0))


def silu(x):
    half = 0.5 * x
    return half + half * jnp.tanh(half)


def unit(y, factor):
    scale = lax.rsqrt(jnp.sum(y * y, axis=-1, keepdims=True) + EPS)
    return (y * scale * factor).astype(BF16)


def iota(shape, dim):
    return lax.broadcasted_iota(jnp.int32, shape, dim)


def block_of(x, size):
    return lax.shift_right_logical(x, jnp.full(x.shape, size.bit_length() - 1, jnp.int32))


def place_in(x, size):
    return x & (size - 1)


def pack_kernel(
    heads_axis, q_in, k_in, v_in, at_in, bt_in, out_ref, q_ref, k_ref, v_ref, at_ref, bt_ref, sems
):
    peers, tokens = out_ref.shape[0], q_ref.shape[0]
    pairs = ((at_in, at_ref), (bt_in, bt_ref), (k_in, k_ref), (v_in, v_ref), (q_in, q_ref))
    copies = [pltpu.make_async_copy(a, b, sems.at[i]) for i, (a, b) in enumerate(pairs)]
    for copy in copies:
        copy.start()
    subs = peers // heads_axis
    key_heads = [(dest % heads_axis) * subs + dest // heads_axis for dest in range(peers)]
    for copy in copies[:2]:
        copy.wait()
    value_heads = at_ref.shape[0]
    row, entry = iota((peers * GATES, value_heads), 0), iota((peers * GATES, value_heads), 1)
    dest, which = block_of(row, GATES), place_in(row, GATES)
    first = 2 * (place_in(dest, heads_axis) * subs + block_of(dest, heads_axis))
    pick_a = jnp.where((which < 2) & (entry == first + which), 1.0, 0.0).astype(BF16)
    pick_b = jnp.where(
        (which >= 2) & (which < 4) & (entry == first + which - 2), 1.0, 0.0
    ).astype(BF16)
    picked = (dot(pick_a, at_ref[...]) + dot(pick_b, bt_ref[...])).astype(BF16)
    lane_shift = tokens * lax.rem(lax.axis_index("head"), SPAN // tokens)
    place = jnp.where(
        iota((tokens, SPAN), 1) == iota((tokens, SPAN), 0) + lane_shift, 1.0, 0.0
    ).astype(BF16)
    gates = dot(picked, place).astype(BF16)
    for dest in range(peers):
        out_ref[dest, 4 * tokens :, :] = gates[GATES * dest : GATES * (dest + 1), :]

    def laid(ref, lane, start):
        for dest, key_head in enumerate(key_heads):
            at = lane(key_head) * 128
            out_ref[dest, start * tokens : (start + 1) * tokens, :] = ref[
                :, at : at + 128
            ]

    copies[2].wait()
    laid(k_ref, lambda key_head: key_head, 0)
    copies[3].wait()
    laid(v_ref, lambda key_head: 2 * key_head, 1)
    laid(v_ref, lambda key_head: 2 * key_head + 1, 2)
    copies[4].wait()
    laid(q_ref, lambda key_head: key_head, 3)


def compacted(system):
    size = system.shape[0]
    diagonal = block_of(iota((size, size), 0), SUB) == block_of(iota((size, size), 1), SUB)
    return jnp.sum(jnp.where(diagonal, system, 0.0).reshape(size // SUB, SUB, size), axis=0)


def substituted(compact):
    count, _, size = compact.shape
    flat = compact.reshape(count * SUB, size)
    lane, line = iota(flat.shape, 1), iota(flat.shape, 0)
    solved = jnp.where(place_in(lane ^ line, SUB) == 0, 1.0, 0.0).reshape(count, SUB, size)
    for m in range(SUB - 1):
        source = (lane & ~(SUB - 1)) | m
        spread = jnp.take_along_axis(flat, source, axis=1, mode="promise_in_bounds")
        solved = solved + spread.reshape(count, SUB, size) * solved[:, m : m + 1, :]
    return solved


def inverted(systems, small, meanwhile=lambda: None):
    size = systems[0][0].shape[0]
    row, col = iota((size, size), 0), iota((size, size), 1)
    placed = jnp.where(block_of(row, SUB) == block_of(col, SUB), 1.0, 0.0).astype(BF16)
    identity = jnp.where(row == col, 1.0, 0.0)
    rough = [
        jnp.concatenate([block.astype(BF16)] * (size // SUB), axis=0) * placed for block in small
    ]
    blank = jnp.zeros((size, size), BF16)
    width = SUB
    while width < size:
        odd = [(j, j + width) for j in range(width, size, 2 * width)]

        def rows_of(x):
            return jnp.concatenate([x[lo:hi] for lo, hi in odd], axis=0)

        def woven(even, x):
            pieces = []
            for j, (lo, hi) in enumerate(odd):
                pieces += [even[lo - width : lo], x[j * width : (j + 1) * width]]
            return jnp.concatenate(pieces, axis=0)

        below = rows_of(block_of(row ^ col, 2 * width)) + rows_of(col & width) == 0
        own = rows_of(identity)
        firsts = [dot(rows_of(n[0]), t) for n, t in zip(systems, rough)]
        meanwhile()
        rights = [
            woven(blank, jnp.where(below, first, own).astype(BF16)) for first in firsts
        ]
        grown = [dot(rows_of(t), right).astype(BF16) for t, right in zip(rough, rights)]
        rough = [woven(t, g) for t, g in zip(rough, grown)]
        width *= 2
    products = [
        dot(jnp.concatenate(n, axis=1), jnp.concatenate([t, t], axis=0))
        for n, t in zip(systems, rough)
    ]
    rests = [
        (identity - t.astype(F32) + product).astype(BF16) for t, product in zip(rough, products)
    ]
    return [halves(t.astype(F32) + dot(t, rest)) for t, rest in zip(rough, rests)]


def own_entry(ref, index):
    row = ref[...]
    return jnp.sum(jnp.where(iota(row.shape, 1) == index, row, 0.0), axis=1, keepdims=True)


def gate_values(gates, sub, alog_ref, dt_ref):
    second = place_in(iota(gates.shape, 0), GATES) == 1
    a_log, dt_bias = (
        jnp.where(second, own_entry(ref, 2 * sub + 1), own_entry(ref, 2 * sub))
        for ref in (alog_ref, dt_ref)
    )
    shifted = gates + dt_bias
    soft = jnp.maximum(shifted, 0.0) + jnp.log1p(jnp.exp(-jnp.abs(shifted)))
    return -jnp.exp(a_log) * soft, 1.0 / (1.0 + jnp.exp(-gates))


def convolved(rows, at, count, lanes, tap):
    summed = tap[0:1] * rows[at : at + count, lanes]
    for j in range(1, CONV):
        summed = summed + tap[j : j + 1] * rows[at + j : at + j + count, lanes]
    return silu(summed)


def key_tap(sub, tap_ref):
    return tap_ref[:, pl.ds(pl.multiple_of(sub * DK, 128), DK)]


def value_taps(sub, cv_ref):
    lane = pl.multiple_of(sub * 2 * DV, 128)
    return [cv_ref[:, pl.ds(pl.multiple_of(lane + r * DV, 128), DV)] for r in range(2)]


def widened(rows, recv_ref, starts, tokens):
    rows[0:8, :] = jnp.zeros((8, rows.shape[1]), F32)
    for s in range(recv_ref.shape[0]):
        for g, start in enumerate(starts):
            rows[8 + s * tokens : 8 + (s + 1) * tokens, g * 128 : (g + 1) * 128] = recv_ref[
                s, start : start + tokens, :
            ].astype(F32)


def systems_kernel(hop_ref, recv_ref, ck_ref, alog_ref, dt_ref, *refs):
    del hop_ref

    @pl.when(lax.axis_index("half") > 0)
    def _():
        systems_of(recv_ref, ck_ref, alog_ref, dt_ref, *refs)


def systems_of(
    recv_ref,
    ck_ref,
    alog_ref,
    dt_ref,
    keys_ref,
    keys_t_ref,
    systems_ref,
    small_ref,
    ends_ref,
    within_ref,
    cols_ref,
    early_ref,
    rows,
):
    sub = lax.axis_index("sub")
    later = lax.axis_index("half") > 0
    peers = recv_ref.shape[0]
    tokens = (recv_ref.shape[1] - GATES) // 4
    spans = peers * tokens // SPAN
    tap = key_tap(sub, ck_ref)
    widened(rows, recv_ref, [0], tokens)
    stacked = [
        sum(recv_ref[s, 4 * tokens :, :].astype(F32) for s in range(n, n + SPAN // tokens))
        for n in range(0, peers, SPAN // tokens)
    ]
    stacked.append(jnp.zeros((SPAN - spans * GATES, SPAN), F32))
    gates = jnp.concatenate(stacked, axis=0)
    decay, rate = gate_values(gates, sub, alog_ref, dt_ref)
    if early_ref is not None:
        early_ref[...] = jnp.where(iota((8, SPAN), 0) < 2, decay[0:8], rate[0:8])
    skipped = later & (iota(gates.shape, 0) < GATES) & (iota(gates.shape, 1) < EDGE)
    decay = jnp.where(skipped, 0.0, decay)
    rate = jnp.where(skipped, 0.0, rate)
    lane_r, lane_c = iota((SPAN, SPAN), 0), iota((SPAN, SPAN), 1)
    upto = jnp.where(lane_r <= lane_c, 1.0, 0.0).astype(BF16)
    d_high, _ = halves(decay)
    d_mid, d_low = halves(decay - d_high.astype(F32))
    cum = dot(d_high, upto) + (dot(d_mid, upto) + dot(d_low, upto))
    growth = jnp.exp(cum)
    here = pltpu.roll(rate, rate.shape[0] - 2, 0)
    rest = jnp.exp(cum[:, SPAN - 1 :] - cum) * here
    which = place_in(iota(gates.shape, 0), GATES)
    mixed = jnp.where(which < 2, cum, pltpu.roll(growth, 2, 0))
    columns = jnp.transpose(jnp.where(which < 4, mixed, pltpu.roll(rest, 4, 0)))
    cols_ref[...] = columns
    lower = lane_r >= lane_c
    strict = lane_r > lane_c
    both = [(n, r) for n in range(spans) for r in range(2)]
    keys = []
    for n in range(spans):
        k_n = unit(convolved(rows, n * SPAN + 8 - EDGE, SPAN, slice(0, DK), tap), 1.0)
        keys_ref[n * SPAN : (n + 1) * SPAN, :] = k_n
        keys.append(k_n)
    keys_t = []
    for n in range(spans):
        kt_n = jnp.transpose(keys[n].astype(F32)).astype(BF16)
        keys_t_ref[n] = kt_n
        keys_t.append(kt_n)
    grams = [dot(keys[n], keys_t[n]) for n in range(spans)]
    for n, r in both:
        at = GATES * n + r
        gap = columns[:, at : at + 1] - cum[at : at + 1, :]
        within = jnp.exp(jnp.where(lower, gap, 0.0)) * here[at : at + 1, :]
        within_ref[r, n * SPAN : (n + 1) * SPAN, :] = jnp.where(lower, within, 0.0).astype(BF16)
        system = jnp.where(strict, within * -grams[n], 0.0)
        systems_ref[r, n, 0], systems_ref[r, n, 1] = halves(system)
        small_ref[r, n] = compacted(system)
    ends_ref[...] = jnp.broadcast_to(growth[:, SPAN - 1 :], ends_ref.shape)


def inverse_kernel(
    hop_ref, keys_ref, keys_t_ref, systems_ref, small_ref, cols_ref, t_ref, lin_ref
):
    del hop_ref
    spans = keys_t_ref.shape[0]
    both = [(n, r) for n in range(spans) for r in range(2)]

    @pl.when(lax.axis_index("half") > 0)
    def _():
        compact = jnp.concatenate([small_ref[r, n] for n, r in both], axis=0)
        small = substituted(compact.reshape(len(both), SUB, SPAN))
        systems = [(systems_ref[r, n, 0], systems_ref[r, n, 1]) for n, r in both]
        inverses = inverted(systems, [small[i] for i in range(len(both))])
        scaled = []
        for i, (n, r) in enumerate(both):
            t_ref[r, n, 0], t_ref[r, n, 1] = inverses[i]
            at = GATES * n + r
            key = keys_ref[n * SPAN : (n + 1) * SPAN, :].astype(F32)
            right = (cols_ref[:, at + 2 : at + 3] * key).astype(BF16)
            scaled.append(jnp.concatenate([right, right], axis=0))
        w_mats = [dot(jnp.concatenate(t, axis=1), x) for t, x in zip(inverses, scaled)]
        weighed = []
        for (n, r), w_mat in zip(both, w_mats):
            at = GATES * n + r
            weighed.append((cols_ref[:, at + 4 : at + 5] * w_mat).astype(BF16))
        moved = [
            dot(keys_t_ref[n], jnp.concatenate(weighed[2 * n : 2 * n + 2], axis=1))
            for n in range(spans)
        ]
        for n, r in both:
            lin_ref[r, n] = moved[n][:, r * DK : (r + 1) * DK].astype(BF16)


def unwound(t_ref, n, r, x):
    both = jnp.concatenate([t_ref[r, n, 0], t_ref[r, n, 1]], axis=1)
    return dot(both, jnp.concatenate([x, x], axis=0))


def end_of(ends_ref, n, r):
    return ends_ref[GATES * n + r : GATES * n + r + 1, :]


def followed(span_map, state):
    end, moved, add = span_map
    return step(end, moved, state, halves(state)) + add


def composed(maps):
    if len(maps) == 1:
        return maps[0]
    half = len(maps) // 2
    end_a, moved_a, add_a = composed(maps[:half])
    end_b, moved_b, add_b = composed(maps[half:])
    high, low = halves(add_a)
    rights = jnp.concatenate(
        [
            jnp.concatenate([moved_a, high], axis=1),
            jnp.concatenate([jnp.zeros_like(moved_a), low], axis=1),
        ],
        axis=0,
    )
    passed = dot(jnp.concatenate([moved_b, moved_b], axis=1), rights)
    moved = end_b * moved_a.astype(F32) + end_a * moved_b.astype(F32) - passed[:, :DK]
    add = end_b * add_a - passed[:, DK:] + add_b
    return end_a * end_b, moved.astype(BF16), add


def step(end, moved, state, parts):
    both = jnp.concatenate([moved, moved], axis=1)
    return end * state - dot(both, jnp.concatenate(parts, axis=0))


def values_part(recv_ref, cv_ref, keys_t_ref, t_ref, cols_ref, rows, vs):
    sub = lax.axis_index("sub")
    tokens = (recv_ref.shape[1] - GATES) // 4
    spans = t_ref.shape[1]
    taps = value_taps(sub, cv_ref)
    widened(rows, recv_ref, [tokens, 2 * tokens], tokens)
    both = [(n, r) for n in range(spans) for r in range(2)]
    values = []
    for n, r in both:
        lanes = slice(r * DV, (r + 1) * DV)
        v_n = convolved(rows, n * SPAN + 8 - EDGE, SPAN, lanes, taps[r]).astype(BF16)
        vs[r, n * SPAN : (n + 1) * SPAN, :] = v_n
        values.append(v_n)
    solved = [unwound(t_ref, n, r, v) for (n, r), v in zip(both, values)]
    weighed = []
    for (n, r), u_mat in zip(both, solved):
        at = GATES * n + r
        weighed.append((cols_ref[:, at + 4 : at + 5] * u_mat).astype(BF16))
    moved = [
        dot(keys_t_ref[n], jnp.concatenate(weighed[2 * n : 2 * n + 2], axis=1))
        for n in range(spans)
    ]
    return [moved[n][:, r * DV : (r + 1) * DV] for n, r in both]


def opening_kernel(
    recv_ref,
    ck_ref,
    cv_ref,
    alog_ref,
    dt_ref,
    cq_ref,
    gain_ref,
    hop_ref,
    keys_ref,
    keys_t_ref,
    ends_ref,
    within_ref,
    cols_ref,
    t_ref,
    lin_ref,
    vs_ref,
    xs_ref,
    adds_ref,
    key_rows,
    rows,
    systems_ref,
    small_ref,
):
    first = lax.axis_index("half") == 0
    peers = recv_ref.shape[0]
    tokens = (recv_ref.shape[1] - GATES) // 4
    spans = keys_t_ref.shape[0]
    edges = []
    for which in (3, 0, 1, 2):
        end = (which + 1) * tokens
        edges.append(recv_ref[peers - 1, end - 16 : end, :].astype(F32)[16 - EDGE :])
    edges.append(jnp.zeros((16 - 4 * EDGE, 128), F32))
    hop_ref[2 * DK :, :] = jnp.concatenate(edges, axis=0).astype(BF16)

    @pl.when(first)
    def _():
        both = [(n, r) for n in range(spans) for r in range(2)]
        systems_of(
            recv_ref,
            ck_ref,
            alog_ref,
            dt_ref,
            keys_ref,
            keys_t_ref,
            systems_ref,
            small_ref,
            ends_ref,
            within_ref,
            cols_ref,
            None,
            key_rows,
        )
        taps = value_taps(lax.axis_index("sub"), cv_ref)
        widened(rows, recv_ref, [tokens, 2 * tokens], tokens)
        waiting = list(both)

        def meanwhile():
            for n, r in waiting[:6]:
                lanes = slice(r * DV, (r + 1) * DV)
                value = convolved(rows, n * SPAN + 8 - EDGE, SPAN, lanes, taps[r])
                vs_ref[r, n * SPAN : (n + 1) * SPAN, :] = value.astype(BF16)
            del waiting[:6]

        compact = jnp.concatenate([small_ref[r, n] for n, r in both], axis=0)
        small = substituted(compact.reshape(len(both), SUB, SPAN))
        systems = [(systems_ref[r, n, 0], systems_ref[r, n, 1]) for n, r in both]
        inverses = inverted(systems, [small[i] for i in range(len(both))], meanwhile)
        while waiting:
            meanwhile()
        rights = []
        for i, (n, r) in enumerate(both):
            t_ref[r, n, 0], t_ref[r, n, 1] = inverses[i]
            at = GATES * n + r
            here = slice(n * SPAN, (n + 1) * SPAN)
            key = (cols_ref[:, at + 2 : at + 3] * keys_ref[here, :].astype(F32)).astype(BF16)
            right = jnp.concatenate([key, vs_ref[r, here, :]], axis=1)
            rights.append(jnp.concatenate([right, right], axis=0))
        solved = [dot(jnp.concatenate(t, axis=1), x) for t, x in zip(inverses, rights)]
        weighed = []
        for (n, r), x in zip(both, solved):
            at = GATES * n + r
            weighed.append((cols_ref[:, at + 4 : at + 5] * x).astype(BF16))
        moved = [
            dot(keys_t_ref[n], jnp.concatenate(weighed[2 * n : 2 * n + 2], axis=1))
            for n in range(spans)
        ]
        adds = []
        for n, r in both:
            at = 2 * r * DK
            lin_ref[r, n] = moved[n][:, at : at + DK].astype(BF16)
            adds.append(moved[n][:, at + DK : at + 2 * DK])
            adds_ref[r, n] = adds[-1]
        maps = [
            [(end_of(ends_ref, n, r), lin_ref[r, n], adds[2 * n + r]) for n in range(spans)]
            for r in range(2)
        ]
        states = [m[0][2] for m in maps]
        done = 1
        while done < spans:
            for r in range(2):
                if done > 1:
                    xs_ref[r, done] = jnp.concatenate(halves(states[r]), axis=0)
            later = [composed(m[done : 2 * done]) for m in maps]
            states = [followed(m, x) for m, x in zip(later, states)]
            done *= 2
        for r in range(2):
            hop_ref[r * DK : (r + 1) * DK, :] = states[r].astype(BF16)

    @pl.when(jnp.logical_not(first))
    def _():
        hop_ref[0 : 2 * DK, :] = jnp.zeros((2 * DK, DV), BF16)


def states_kernel(
    recv_ref,
    cv_ref,
    keys_t_ref,
    t_ref,
    lin_ref,
    ends_ref,
    cols_ref,
    values_ref,
    states_ref,
    *rest,
):
    *last_ref, rows = rest

    @pl.when(lax.axis_index("half") > 0)
    def _():
        spans = t_ref.shape[1]
        adds = values_part(recv_ref, cv_ref, keys_t_ref, t_ref, cols_ref, rows, values_ref)
        zero_half = jnp.zeros((DK, DV), F32)
        identity = jnp.where(iota((DK, DK), 0) == iota((DK, DK), 1), 1.0, 0.0)
        states = [
            jnp.concatenate(
                [adds[r], ends_ref[r : r + 1, :] * identity - lin_ref[r, 0].astype(F32)], axis=1
            )
            for r in range(2)
        ]
        for n in range(1, spans):
            for r in range(2):
                parts = halves(states[r])
                for i in range(2):
                    both_parts = [x[:, i * DV : (i + 1) * DV] for x in parts]
                    states_ref[i, r, n] = jnp.concatenate(both_parts, axis=0)
                add = jnp.concatenate([adds[2 * n + r], zero_half], axis=1)
                end = jnp.concatenate([end_of(ends_ref, n, r)] * 2, axis=1)
                states[r] = step(end, lin_ref[r, n], states[r], parts) + add
        for ref in last_ref:
            for r in range(2):
                ref[r] = states[r]


def span_rows(n):
    return slice(n * SPAN, (n + 1) * SPAN)


def twice(x, axis):
    return jnp.concatenate([x, x], axis=axis)


def asked(recv_ref, cq_ref, keys_ref, keys_t_ref, within_ref, query_rows):
    tokens = (recv_ref.shape[1] - GATES) // 4
    spans = keys_t_ref.shape[0]
    tap = key_tap(lax.axis_index("sub"), cq_ref)
    widened(query_rows, recv_ref, [3 * tokens], tokens)
    queries = [
        unit(convolved(query_rows, n * SPAN + 8 - EDGE, SPAN, slice(0, DK), tap), DK**-0.5)
        for n in range(spans)
    ]
    readers = [
        jnp.concatenate([keys_ref[span_rows(n), :], queries[n]], axis=0) for n in range(spans)
    ]
    scores = [dot(queries[n], keys_t_ref[n]) for n in range(spans)]
    inner = [
        (within_ref[r, span_rows(n), :].astype(F32) * scores[n]).astype(BF16)
        for n in range(spans)
        for r in range(2)
    ]
    return readers, inner


def first_outputs_kernel(
    recv_ref,
    cq_ref,
    keys_ref,
    keys_t_ref,
    t_ref,
    lin_ref,
    ends_ref,
    within_ref,
    cols_ref,
    values_ref,
    xs_ref,
    adds_ref,
    oa_ref,
    query_rows,
):
    @pl.when(lax.axis_index("half") == 0)
    def _():
        spans = t_ref.shape[1]
        both = [(n, r) for n in range(spans) for r in range(2)]
        readers, inner = asked(recv_ref, cq_ref, keys_ref, keys_t_ref, within_ref, query_rows)
        stacks, states = [], []
        for n in range(1, spans):
            if n == 1:
                states = [adds_ref[r, 0] for r in range(2)]
                stack = [jnp.concatenate(halves(x), axis=0) for x in states]
            elif n & (n - 1) == 0:
                stack = [xs_ref[r, n] for r in range(2)]
                states = [x[:DK].astype(F32) + x[DK:].astype(F32) for x in stack]
            else:
                states = [
                    followed(
                        (end_of(ends_ref, n - 1, r), lin_ref[r, n - 1], adds_ref[r, n - 1]),
                        states[r],
                    )
                    for r in range(2)
                ]
                stack = [jnp.concatenate(halves(x), axis=0) for x in states]
            stacks.append(jnp.concatenate(stack, axis=1))
        reads = [dot(twice(readers[n], 1), stacks[n - 1]) for n in range(1, spans)]
        rests, seen = [], []
        for n, r in both:
            lanes = slice(r * DV, (r + 1) * DV)
            value = values_ref[r, span_rows(n), :]
            if n == 0:
                rests.append(value)
                seen.append(None)
            else:
                growth = cols_ref[:, GATES * n + 2 + r : GATES * n + 3 + r]
                read = growth * reads[n - 1][:SPAN, lanes]
                rests.append((value.astype(F32) - read).astype(BF16))
                seen.append(growth * reads[n - 1][SPAN:, lanes])
        fresh = [unwound(t_ref, n, r, x).astype(BF16) for (n, r), x in zip(both, rests)]
        spreads = [dot(w, x) for w, x in zip(inner, fresh)]
        for (n, r), x, y in zip(both, spreads, seen):
            oa_ref[r, span_rows(n), :] = x if y is None else x + y


def later_outputs_kernel(
    recv_ref,
    cq_ref,
    keys_ref,
    keys_t_ref,
    t_ref,
    within_ref,
    cols_ref,
    values_ref,
    states_ref,
    oa_ref,
    om_ref,
    query_rows,
):
    @pl.when(lax.axis_index("half") > 0)
    def _():
        spans = t_ref.shape[1]
        both = [(n, r) for n in range(spans) for r in range(2)]
        readers, inner = asked(recv_ref, cq_ref, keys_ref, keys_t_ref, within_ref, query_rows)
        zero_half = jnp.zeros((SPAN, DV), F32)
        reads = [
            dot(
                twice(readers[n], 1),
                jnp.concatenate([states_ref[0, r, n], states_ref[1, r, n]], axis=1),
            )
            if n > 0
            else None
            for n, r in both
        ]
        rests, seen = [], []
        for (n, r), read in zip(both, reads):
            value = values_ref[r, span_rows(n), :].astype(F32)
            growth = cols_ref[:, GATES * n + 2 + r : GATES * n + 3 + r]
            if n == 0:
                reader = readers[n].astype(F32)
                rest = jnp.concatenate([value, -(growth * reader[:SPAN])], axis=1)
                seen.append(jnp.concatenate([zero_half, growth * reader[SPAN:]], axis=1))
            else:
                rest = jnp.concatenate([value, zero_half], axis=1) - growth * read[:SPAN]
                seen.append(growth * read[SPAN:])
            rests.append(rest.astype(BF16))
        fresh = [unwound(t_ref, n, r, x).astype(BF16) for (n, r), x in zip(both, rests)]
        spreads = [dot(w, x) for w, x in zip(inner, fresh)]
        for (n, r), x, y in zip(both, spreads, seen):
            out = x + y
            oa_ref[r, span_rows(n), :] = out[:, :DV]
            om_ref[r, span_rows(n), :] = out[:, DV:].astype(BF16)


def first_tokens(hop_ref, recv_ref, early_ref, cq_ref, ck_ref, cv_ref, rows):
    sub = lax.axis_index("sub")
    tokens = (recv_ref.shape[1] - GATES) // 4
    taps = [key_tap(sub, cq_ref), key_tap(sub, ck_ref)] + value_taps(sub, cv_ref)
    results = []
    edges = hop_ref[2 * DK :, :].astype(F32)
    for g, first in enumerate((3, 0, 1, 2)):
        lanes = slice(g * 128, (g + 1) * 128)
        start = first * tokens
        rows[16 - EDGE : 16, lanes] = edges[EDGE * g : EDGE * (g + 1)]
        rows[16:32, lanes] = recv_ref[0, start : start + 16, :].astype(F32)
        results.append(convolved(rows, 16 - EDGE, 8, lanes, taps[g]))
    q_cols = jnp.transpose(unit(results[0], DK**-0.5).astype(F32))
    k_cols = jnp.transpose(unit(results[1], 1.0).astype(F32))
    gates = early_ref[...]
    line = iota((8, DV), 0)
    values = [x.astype(BF16).astype(F32) for x in results[2:]]
    states = [hop_ref[r * DK : (r + 1) * DK, :].astype(F32) for r in range(2)]
    outputs = [jnp.zeros((8, DV), F32) for r in range(2)]
    for t in range(EDGE):
        k_t, q_t = k_cols[:, t : t + 1], q_cols[:, t : t + 1]
        states = [jnp.exp(gates[r : r + 1, t : t + 1]) * states[r] for r in range(2)]
        held = [jnp.sum(k_t * x, axis=0, keepdims=True) for x in states]
        fresh = [
            gates[2 + r : 3 + r, t : t + 1] * (values[r][t : t + 1, :] - held[r])
            for r in range(2)
        ]
        states = [x + k_t * y for x, y in zip(states, fresh)]
        outputs = [
            jnp.where(line == t, jnp.sum(q_t * x, axis=0, keepdims=True), y)
            for x, y in zip(states, outputs)
        ]
    return states, outputs


def put(out_ref, gain, c, r, core):
    peer_part, tokens = out_ref.shape[0] // CHUNKS, out_ref.shape[1] // 2
    scale = lax.rsqrt(jnp.mean(core * core, axis=-1, keepdims=True) + EPS)
    normed = (core * scale * gain).astype(BF16)
    here = slice(c * peer_part, (c + 1) * peer_part)
    out_ref[here, r * tokens : (r + 1) * tokens, :] = normed.reshape(peer_part, tokens, DV)


def first_finish_kernel(gain_ref, oa_ref, out_ref):
    @pl.when(lax.axis_index("half") == 0)
    def _():
        gain = gain_ref[...]
        part = oa_ref.shape[1] // CHUNKS
        for c in range(CHUNKS):
            for r in range(2):
                put(out_ref, gain, c, r, oa_ref[r, c * part : (c + 1) * part, :])


def later_finish_kernel(
    normed_ref,
    hop_ref,
    recv_ref,
    early_ref,
    cq_ref,
    ck_ref,
    cv_ref,
    gain_ref,
    oa_ref,
    om_ref,
    out_ref,
    rows,
):
    del normed_ref

    @pl.when(lax.axis_index("half") > 0)
    def _():
        gain = gain_ref[...]
        part = oa_ref.shape[1] // CHUNKS
        finals, outputs = first_tokens(hop_ref, recv_ref, early_ref, cq_ref, ck_ref, cv_ref, rows)
        replaced = iota((8, DV), 0) < EDGE
        passed = [dot(om_ref[r], finals[r].astype(BF16)) for r in range(2)]
        for c in range(CHUNKS):
            at = c * part
            for r in range(2):
                core = oa_ref[r, at : at + part, :] + passed[r][at : at + part]
                if c == 0:
                    core = jnp.concatenate(
                        [jnp.where(replaced, outputs[r], core[0:8]), core[8:]], axis=0
                    )
                put(out_ref, gain, c, r, core)


def advance_kernel(
    hop_ref, recv_ref, early_ref, cq_ref, ck_ref, cv_ref, hop_own, last_ref, next_ref, rows
):
    finals, _ = first_tokens(hop_ref, recv_ref, early_ref, cq_ref, ck_ref, cv_ref, rows)
    first = lax.axis_index("half") == 0
    for r in range(2):
        last = last_ref[r]
        through = mm_parts(halves(last[:, DV:]), halves(finals[r]))
        own = hop_own[r * DK : (r + 1) * DK, :].astype(F32)
        moved = jnp.where(first, own, through + last[:, :DV])
        next_ref[r * DK : (r + 1) * DK, :] = moved.astype(BF16)
    next_ref[2 * DK :, :] = hop_own[2 * DK :, :]


def gate_kernel(heads_axis, normed_ref, z_ref, out_ref, made, sems):
    subs, tokens = normed_ref.shape[0] // heads_axis, z_ref.shape[0]
    width = subs * 2 * DV
    copies = []
    for head in range(heads_axis):
        for sub in range(subs):
            for r in range(2):
                at = (2 * (head * subs + sub) + r) * DV
                gate = silu(z_ref[:, at : at + DV].astype(F32))
                here = slice(r * tokens, (r + 1) * tokens)
                value = normed_ref[sub * heads_axis + head, here, :].astype(F32)
                made[:, at : at + DV] = (value * gate).astype(BF16)
        lanes = pl.ds(head * width, width)
        copy = pltpu.make_async_copy(made.at[:, lanes], out_ref.at[:, lanes], sems.at[head])
        copy.start()
        copies.append(copy)
    for copy in copies:
        copy.wait()


VMEM = pl.BlockSpec(memory_space=pltpu.VMEM)
ANY = pl.BlockSpec(memory_space=pl.ANY)


def near(x):
    return pltpu.with_memory_space_constraint(x, pltpu.VMEM)


def far(x):
    return pltpu.with_memory_space_constraint(x, pltpu.HBM)


def call(
    kernel, outs, in_specs, scratch=(), out_spec=VMEM, flops=1 << 26, moved=1 << 21, aliases=()
):
    return pl.pallas_call(
        kernel,
        out_shape=outs,
        in_specs=in_specs,
        out_specs=jax.tree.map(lambda _: out_spec, outs),
        scratch_shapes=list(scratch),
        input_output_aliases=dict(aliases),
        compiler_params=pltpu.CompilerParams(vmem_limit_bytes=VMEM_BYTES),
        cost_estimate=pl.CostEstimate(flops=flops, bytes_accessed=moved, transcendentals=0),
    )


def local(
    q_rows,
    k_rows,
    v_rows,
    z_rows,
    a_rows,
    b_rows,
    conv_q,
    conv_k,
    conv_v,
    a_log,
    dt_bias,
    norm_gain,
):
    shards, subs, heads_axis = (lax.axis_size(a) for a in ("half", "sub", "head"))
    peers, tokens = subs * heads_axis, q_rows.shape[0]
    total = peers * tokens
    spans = total // SPAN
    group = ("sub", "head")
    route = [(i, i + 1) for i in range(shards - 1)]
    conv_q, conv_k, conv_v = near(conv_q), near(conv_k), near(conv_v)
    gain = near(norm_gain.reshape(1, DV))
    a_log, dt_bias = near(a_log.reshape(1, -1)), near(dt_bias.reshape(1, -1))
    inputs = [far(x) for x in (q_rows, k_rows, v_rows, a_rows.T, b_rows.T)]
    packed = call(
        functools.partial(pack_kernel, heads_axis),
        pltpu.VMEM((peers, GATES + 4 * tokens, 128), BF16),
        [ANY] * 5,
        [pltpu.VMEM(x.shape, BF16) for x in inputs] + [pltpu.SemaphoreType.DMA((5,))],
        flops=1 << 20,
    )(*inputs)
    blocks = near(lax.all_to_all(packed, group, 0, 0, tiled=True))
    key_shapes = (pltpu.VMEM((total, DK), BF16), pltpu.VMEM((spans, DK, SPAN), BF16))
    system_shapes = (
        pltpu.VMEM((2, spans, 2, SPAN, SPAN), BF16),
        pltpu.VMEM((2, spans, SUB, SPAN), F32),
    )
    decay_shapes = (
        pltpu.VMEM((SPAN, DK), F32),
        pltpu.VMEM((2, total, SPAN), BF16),
        pltpu.VMEM((SPAN, SPAN), F32),
    )
    map_shapes = (
        pltpu.VMEM((2, spans, 2, SPAN, SPAN), BF16),
        pltpu.VMEM((2, spans, DK, DK), BF16),
    )
    opened = call(
        opening_kernel,
        (
            pltpu.VMEM((2 * DK + 16, 128), BF16),
            *key_shapes,
            *decay_shapes,
            *map_shapes,
            pltpu.VMEM((2, total, DV), BF16),
            pltpu.VMEM((2, spans, 2 * DK, DV), BF16),
            pltpu.VMEM((2, spans, DK, DV), F32),
        ),
        [VMEM] * 7,
        [
            pltpu.VMEM((8 + total, DK), F32),
            pltpu.VMEM((8 + total, 2 * DV), F32),
            *system_shapes,
        ],
        flops=1 << 32,
    )(blocks, conv_k, conv_v, a_log, dt_bias, conv_q, gain)
    hop = opened[0]
    entering = near(lax.ppermute(hop, "half", route))
    hop, keys, keys_t, ends, within, cols, inverses, lins, values, starts, adds = (
        near(x) for x in opened
    )
    first_out = call(
        first_outputs_kernel,
        pltpu.VMEM((2, total, DV), F32),
        [VMEM] * 12,
        [pltpu.VMEM((8 + total, DK), F32)],
        flops=1 << 32,
    )(
        blocks,
        conv_q,
        keys,
        keys_t,
        inverses,
        lins,
        ends,
        within,
        cols,
        values,
        starts,
        adds,
    )
    made = call(
        systems_kernel,
        (*key_shapes, *system_shapes, *decay_shapes, pltpu.VMEM((8, SPAN), F32)),
        [VMEM] * 5,
        [pltpu.VMEM((8 + total, DK), F32)],
        flops=1 << 32,
    )(hop, blocks, conv_k, a_log, dt_bias)
    keys, keys_t, systems, small, ends, within, cols, early = (near(x) for x in made)
    later_solved = call(inverse_kernel, map_shapes, [VMEM] * 6, flops=1 << 32)(
        hop, keys, keys_t, systems, small, cols
    )
    later_inverses, later_lins = (near(x) for x in later_solved)
    read_on = [pltpu.VMEM((2, DK, 2 * DV), F32)] if shards > 2 else []
    later_values, states, *last = call(
        states_kernel,
        (
            pltpu.VMEM((2, total, DV), BF16),
            pltpu.VMEM((2, 2, spans, 2 * DK, DV), BF16),
            *read_on,
        ),
        [VMEM] * 7,
        [pltpu.VMEM((8 + total, 2 * DV), F32)],
        flops=1 << 32,
    )(blocks, conv_v, keys_t, later_inverses, later_lins, ends, cols)
    out_a, out_m = call(
        later_outputs_kernel,
        (pltpu.VMEM((2, total, DV), F32), pltpu.VMEM((2, total, DV), BF16)),
        [VMEM] * 9,
        [pltpu.VMEM((8 + total, DK), F32)],
        flops=1 << 32,
    )(
        blocks,
        conv_q,
        keys,
        keys_t,
        later_inverses,
        within,
        cols,
        near(later_values),
        near(states),
    )
    for _ in range(shards - 2):
        moved = call(
            advance_kernel,
            pltpu.VMEM(hop.shape, BF16),
            [VMEM] * 8,
            [pltpu.VMEM((32, 512), F32)],
        )(entering, blocks, early, conv_q, conv_k, conv_v, hop, near(last[0]))
        entering = near(lax.ppermute(moved, "half", route))
    normed_shape = pltpu.VMEM((peers, 2 * tokens, DV), BF16)
    first_normed = call(first_finish_kernel, normed_shape, [VMEM] * 2, flops=1 << 30)(
        gain, near(first_out)
    )
    normed = call(
        later_finish_kernel,
        normed_shape,
        [VMEM] * 10,
        [pltpu.VMEM((32, 512), F32)],
        aliases=((0, 0),),
    )(
        near(first_normed),
        entering,
        blocks,
        early,
        conv_q,
        conv_k,
        conv_v,
        gain,
        near(out_a),
        near(out_m),
    )
    returned = near(lax.all_to_all(normed, group, 0, 0, tiled=True))
    return call(
        functools.partial(gate_kernel, heads_axis),
        jax.ShapeDtypeStruct(z_rows.shape, BF16),
        [VMEM] * 2,
        [pltpu.VMEM(z_rows.shape, BF16), pltpu.SemaphoreType.DMA((heads_axis,))],
        ANY,
    )(returned, z_rows)


def solution(mesh):
    heads_axis = mesh.shape["head"]
    subs = KH // heads_axis
    regrouped = Mesh(
        mesh.devices.reshape(mesh.shape["ctx"] // subs, subs, heads_axis), ("half", "sub", "head")
    )
    row = P(("half", "sub", "head"), None)
    placed = (row,) * 6 + (P(None, "head"),) * 3 + (P("head"),) * 2 + (P(),)
    return jax.shard_map(local, mesh=regrouped, in_specs=placed, out_specs=row, check_vma=False)
```

```python
import functools

import jax
import jax.numpy as jnp
from jax import lax
from jax.experimental import pallas as pl
from jax.experimental.pallas import tpu as pltpu
from jax.sharding import Mesh, PartitionSpec as P

DK = 128
DV = 128
CONV = 4
KH = 16
SUB = 16
SPAN = 128
CHUNKS = 4
EDGE = CONV - 1
EPS = 1e-06
F32 = jnp.float32
BF16 = jnp.bfloat16
VMEM_BYTES = 24 * 1024 * 1024
GATES = 8


def dot(a, b, dims=((1,), (0,))):
    return lax.dot_general(a, b, (dims, ((), ())), preferred_element_type=F32)


def halves(x):
    high = x.astype(BF16)
    return high, (x - high.astype(F32)).astype(BF16)


def mm_parts(a, b):
    left = jnp.concatenate([a[0], a[1], a[0]], axis=1)
    return dot(left, jnp.concatenate([b[0], b[0], b[1]], axis=0))


def silu(x):
    half = 0.5 * x
    return half + half * jnp.tanh(half)


def unit(y, factor):
    scale = lax.rsqrt(jnp.sum(y * y, axis=-1, keepdims=True) + EPS)
    return (y * scale * factor).astype(BF16)


def iota(shape, dim):
    return lax.broadcasted_iota(jnp.int32, shape, dim)


def block_of(x, size):
    return lax.shift_right_logical(x, jnp.full(x.shape, size.bit_length() - 1, jnp.int32))


def place_in(x, size):
    return x & (size - 1)


def pack_kernel(
    heads_axis, q_in, k_in, v_in, at_in, bt_in, out_ref, q_ref, k_ref, v_ref, at_ref, bt_ref, sems
):
    peers, tokens = out_ref.shape[0], q_ref.shape[0]
    pairs = [(at_in, at_ref), (bt_in, bt_ref)]
    for source, target, pieces in ((k_in, k_ref, 2), (v_in, v_ref, 4), (q_in, q_ref, 2)):
        width = source.shape[1] // pieces
        for i in range(pieces):
            lanes = pl.ds(i * width, width)
            pairs.append((source.at[:, lanes], target.at[:, lanes]))
    copies = [pltpu.make_async_copy(a, b, sems.at[i]) for i, (a, b) in enumerate(pairs)]
    for copy in copies:
        copy.start()
    subs = peers // heads_axis
    key_heads = [(dest % heads_axis) * subs + dest // heads_axis for dest in range(peers)]
    for copy in copies[:2]:
        copy.wait()
    value_heads = at_ref.shape[0]
    row, entry = iota((peers * GATES, value_heads), 0), iota((peers * GATES, value_heads), 1)
    dest, which = block_of(row, GATES), place_in(row, GATES)
    first = 2 * (place_in(dest, heads_axis) * subs + block_of(dest, heads_axis))
    pick_a = jnp.where((which < 2) & (entry == first + which), 1.0, 0.0).astype(BF16)
    pick_b = jnp.where(
        (which >= 2) & (which < 4) & (entry == first + which - 2), 1.0, 0.0
    ).astype(BF16)
    picked = (dot(pick_a, at_ref[...]) + dot(pick_b, bt_ref[...])).astype(BF16)
    lane_shift = tokens * lax.rem(lax.axis_index("head"), SPAN // tokens)
    place = jnp.where(
        iota((tokens, SPAN), 1) == iota((tokens, SPAN), 0) + lane_shift, 1.0, 0.0
    ).astype(BF16)
    gates = dot(picked, place).astype(BF16)
    for dest in range(peers):
        out_ref[dest, 4 * tokens :, :] = gates[GATES * dest : GATES * (dest + 1), :]

    def laid(ref, lane, start, piece, pieces):
        for dest, key_head in enumerate(key_heads):
            if key_head * pieces // peers == piece:
                at = lane(key_head) * 128
                out_ref[dest, start * tokens : (start + 1) * tokens, :] = ref[:, at : at + 128]

    for i in range(2):
        copies[2 + i].wait()
        laid(k_ref, lambda key_head: key_head, 0, i, 2)
    for i in range(4):
        copies[4 + i].wait()
        laid(v_ref, lambda key_head: 2 * key_head, 1, i, 4)
        laid(v_ref, lambda key_head: 2 * key_head + 1, 2, i, 4)
    for i in range(2):
        copies[8 + i].wait()
        laid(q_ref, lambda key_head: key_head, 3, i, 2)


def compacted(system):
    size = system.shape[0]
    diagonal = block_of(iota((size, size), 0), SUB) == block_of(iota((size, size), 1), SUB)
    return jnp.sum(jnp.where(diagonal, system, 0.0).reshape(size // SUB, SUB, size), axis=0)


def substituted(compact):
    count, _, size = compact.shape
    flat = compact.reshape(count * SUB, size)
    lane, line = iota(flat.shape, 1), iota(flat.shape, 0)
    solved = jnp.where(place_in(lane ^ line, SUB) == 0, 1.0, 0.0).reshape(count, SUB, size)
    for m in range(SUB - 1):
        source = (lane & ~(SUB - 1)) | m
        spread = jnp.take_along_axis(flat, source, axis=1, mode="promise_in_bounds")
        solved = solved + spread.reshape(count, SUB, size) * solved[:, m : m + 1, :]
    return solved


def inverted(systems, small, meanwhile=lambda: None):
    size = systems[0][0].shape[0]
    row, col = iota((size, size), 0), iota((size, size), 1)
    placed = jnp.where(block_of(row, SUB) == block_of(col, SUB), 1.0, 0.0).astype(BF16)
    identity = jnp.where(row == col, 1.0, 0.0)
    rough = [
        jnp.concatenate([block.astype(BF16)] * (size // SUB), axis=0) * placed for block in small
    ]
    blank = jnp.zeros((size, size), BF16)
    width = SUB
    while width < size:
        odd = [(j, j + width) for j in range(width, size, 2 * width)]

        def rows_of(x):
            return jnp.concatenate([x[lo:hi] for lo, hi in odd], axis=0)

        def woven(even, x):
            pieces = []
            for j, (lo, hi) in enumerate(odd):
                pieces += [even[lo - width : lo], x[j * width : (j + 1) * width]]
            return jnp.concatenate(pieces, axis=0)

        below = rows_of(block_of(row ^ col, 2 * width)) + rows_of(col & width) == 0
        own = rows_of(identity)
        firsts = [dot(rows_of(n[0]), t) for n, t in zip(systems, rough)]
        meanwhile()
        rights = [
            woven(blank, jnp.where(below, first, own).astype(BF16)) for first in firsts
        ]
        grown = [dot(rows_of(t), right).astype(BF16) for t, right in zip(rough, rights)]
        rough = [woven(t, g) for t, g in zip(rough, grown)]
        width *= 2
    products = [
        dot(jnp.concatenate(n, axis=1), jnp.concatenate([t, t], axis=0))
        for n, t in zip(systems, rough)
    ]
    rests = [
        (identity - t.astype(F32) + product).astype(BF16) for t, product in zip(rough, products)
    ]
    return [halves(t.astype(F32) + dot(t, rest)) for t, rest in zip(rough, rests)]


def own_entry(ref, index):
    row = ref[...]
    return jnp.sum(jnp.where(iota(row.shape, 1) == index, row, 0.0), axis=1, keepdims=True)


def gate_values(gates, sub, alog_ref, dt_ref):
    second = place_in(iota(gates.shape, 0), GATES) == 1
    a_log, dt_bias = (
        jnp.where(second, own_entry(ref, 2 * sub + 1), own_entry(ref, 2 * sub))
        for ref in (alog_ref, dt_ref)
    )
    shifted = gates + dt_bias
    soft = jnp.maximum(shifted, 0.0) + jnp.log1p(jnp.exp(-jnp.abs(shifted)))
    return -jnp.exp(a_log) * soft, 1.0 / (1.0 + jnp.exp(-gates))


def convolved(rows, at, count, lanes, tap):
    summed = tap[0:1] * rows[at : at + count, lanes]
    for j in range(1, CONV):
        summed = summed + tap[j : j + 1] * rows[at + j : at + j + count, lanes]
    return silu(summed)


def key_tap(sub, tap_ref):
    return tap_ref[:, pl.ds(pl.multiple_of(sub * DK, 128), DK)]


def value_taps(sub, cv_ref):
    lane = pl.multiple_of(sub * 2 * DV, 128)
    return [cv_ref[:, pl.ds(pl.multiple_of(lane + r * DV, 128), DV)] for r in range(2)]


def widened(rows, recv_ref, starts, tokens):
    rows[0:8, :] = jnp.zeros((8, rows.shape[1]), F32)
    for s in range(recv_ref.shape[0]):
        for g, start in enumerate(starts):
            rows[8 + s * tokens : 8 + (s + 1) * tokens, g * 128 : (g + 1) * 128] = recv_ref[
                s, start : start + tokens, :
            ].astype(F32)


def systems_kernel(hop_ref, recv_ref, ck_ref, alog_ref, dt_ref, *refs):
    del hop_ref

    @pl.when(lax.axis_index("half") > 0)
    def _():
        systems_of(recv_ref, ck_ref, alog_ref, dt_ref, *refs)


def systems_of(
    recv_ref,
    ck_ref,
    alog_ref,
    dt_ref,
    keys_ref,
    keys_t_ref,
    systems_ref,
    small_ref,
    ends_ref,
    within_ref,
    cols_ref,
    early_ref,
    rows,
):
    sub = lax.axis_index("sub")
    later = lax.axis_index("half") > 0
    peers = recv_ref.shape[0]
    tokens = (recv_ref.shape[1] - GATES) // 4
    spans = peers * tokens // SPAN
    tap = key_tap(sub, ck_ref)
    widened(rows, recv_ref, [0], tokens)
    stacked = [
        sum(recv_ref[s, 4 * tokens :, :].astype(F32) for s in range(n, n + SPAN // tokens))
        for n in range(0, peers, SPAN // tokens)
    ]
    stacked.append(jnp.zeros((SPAN - spans * GATES, SPAN), F32))
    gates = jnp.concatenate(stacked, axis=0)
    decay, rate = gate_values(gates, sub, alog_ref, dt_ref)
    if early_ref is not None:
        early_ref[...] = jnp.where(iota((8, SPAN), 0) < 2, decay[0:8], rate[0:8])
    skipped = later & (iota(gates.shape, 0) < GATES) & (iota(gates.shape, 1) < EDGE)
    decay = jnp.where(skipped, 0.0, decay)
    rate = jnp.where(skipped, 0.0, rate)
    lane_r, lane_c = iota((SPAN, SPAN), 0), iota((SPAN, SPAN), 1)
    upto = jnp.where(lane_r <= lane_c, 1.0, 0.0).astype(BF16)
    d_high, _ = halves(decay)
    d_mid, d_low = halves(decay - d_high.astype(F32))
    cum = dot(d_high, upto) + (dot(d_mid, upto) + dot(d_low, upto))
    growth = jnp.exp(cum)
    here = pltpu.roll(rate, rate.shape[0] - 2, 0)
    rest = jnp.exp(cum[:, SPAN - 1 :] - cum) * here
    which = place_in(iota(gates.shape, 0), GATES)
    mixed = jnp.where(which < 2, cum, pltpu.roll(growth, 2, 0))
    columns = jnp.transpose(jnp.where(which < 4, mixed, pltpu.roll(rest, 4, 0)))
    cols_ref[...] = columns
    if early_ref is None:
        within_ref[0], within_ref[1] = cum, here
    lower = lane_r >= lane_c
    strict = lane_r > lane_c
    both = [(n, r) for n in range(spans) for r in range(2)]
    keys = []
    for n in range(spans):
        k_n = unit(convolved(rows, n * SPAN + 8 - EDGE, SPAN, slice(0, DK), tap), 1.0)
        keys_ref[n * SPAN : (n + 1) * SPAN, :] = k_n
        keys.append(k_n)
    keys_t = []
    for n in range(spans):
        kt_n = jnp.transpose(keys[n].astype(F32)).astype(BF16)
        keys_t_ref[n] = kt_n
        keys_t.append(kt_n)
    grams = [dot(keys[n], keys_t[n]) for n in range(spans)]
    for n, r in both:
        at = GATES * n + r
        gap = columns[:, at : at + 1] - cum[at : at + 1, :]
        within = jnp.exp(jnp.where(lower, gap, 0.0)) * here[at : at + 1, :]
        if early_ref is not None:
            kept = jnp.where(lower, within, 0.0).astype(BF16)
            within_ref[r, n * SPAN : (n + 1) * SPAN, :] = kept
        system = jnp.where(strict, within * -grams[n], 0.0)
        systems_ref[r, n, 0], systems_ref[r, n, 1] = halves(system)
        small_ref[r, n] = compacted(system)
    ends_ref[...] = jnp.broadcast_to(growth[:, SPAN - 1 :], ends_ref.shape)


def inverse_kernel(
    hop_ref, keys_ref, keys_t_ref, systems_ref, small_ref, cols_ref, t_ref, lin_ref
):
    del hop_ref
    spans = keys_t_ref.shape[0]
    both = [(n, r) for n in range(spans) for r in range(2)]

    @pl.when(lax.axis_index("half") > 0)
    def _():
        compact = jnp.concatenate([small_ref[r, n] for n, r in both], axis=0)
        small = substituted(compact.reshape(len(both), SUB, SPAN))
        systems = [(systems_ref[r, n, 0], systems_ref[r, n, 1]) for n, r in both]
        inverses = inverted(systems, [small[i] for i in range(len(both))])
        scaled = []
        for i, (n, r) in enumerate(both):
            t_ref[r, n, 0], t_ref[r, n, 1] = inverses[i]
            at = GATES * n + r
            key = keys_ref[n * SPAN : (n + 1) * SPAN, :].astype(F32)
            right = (cols_ref[:, at + 2 : at + 3] * key).astype(BF16)
            scaled.append(jnp.concatenate([right, right], axis=0))
        w_mats = [dot(jnp.concatenate(t, axis=1), x) for t, x in zip(inverses, scaled)]
        weighed = []
        for (n, r), w_mat in zip(both, w_mats):
            at = GATES * n + r
            weighed.append((cols_ref[:, at + 4 : at + 5] * w_mat).astype(BF16))
        moved = [
            dot(keys_t_ref[n], jnp.concatenate(weighed[2 * n : 2 * n + 2], axis=1))
            for n in range(spans)
        ]
        for n, r in both:
            lin_ref[r, n] = moved[n][:, r * DK : (r + 1) * DK].astype(BF16)


def unwound(t_ref, n, r, x):
    both = jnp.concatenate([t_ref[r, n, 0], t_ref[r, n, 1]], axis=1)
    return dot(both, jnp.concatenate([x, x], axis=0))


def end_of(ends_ref, n, r):
    return ends_ref[GATES * n + r : GATES * n + r + 1, :]


def followed(span_map, state):
    end, moved, add = span_map
    return step(end, moved, state, halves(state)) + add


def composed(maps):
    if len(maps) == 1:
        return maps[0]
    half = len(maps) // 2
    end_a, moved_a, add_a = composed(maps[:half])
    end_b, moved_b, add_b = composed(maps[half:])
    high, low = halves(add_a)
    rights = jnp.concatenate(
        [
            jnp.concatenate([moved_a, high], axis=1),
            jnp.concatenate([jnp.zeros_like(moved_a), low], axis=1),
        ],
        axis=0,
    )
    passed = dot(jnp.concatenate([moved_b, moved_b], axis=1), rights)
    moved = end_b * moved_a.astype(F32) + end_a * moved_b.astype(F32) - passed[:, :DK]
    add = end_b * add_a - passed[:, DK:] + add_b
    return end_a * end_b, moved.astype(BF16), add


def step(end, moved, state, parts):
    both = jnp.concatenate([moved, moved], axis=1)
    return end * state - dot(both, jnp.concatenate(parts, axis=0))


def values_part(recv_ref, cv_ref, keys_t_ref, t_ref, cols_ref, rows, vs):
    sub = lax.axis_index("sub")
    tokens = (recv_ref.shape[1] - GATES) // 4
    spans = t_ref.shape[1]
    taps = value_taps(sub, cv_ref)
    widened(rows, recv_ref, [tokens, 2 * tokens], tokens)
    both = [(n, r) for n in range(spans) for r in range(2)]
    values = []
    for n, r in both:
        lanes = slice(r * DV, (r + 1) * DV)
        v_n = convolved(rows, n * SPAN + 8 - EDGE, SPAN, lanes, taps[r]).astype(BF16)
        vs[r, n * SPAN : (n + 1) * SPAN, :] = v_n
        values.append(v_n)
    solved = [unwound(t_ref, n, r, v) for (n, r), v in zip(both, values)]
    weighed = []
    for (n, r), u_mat in zip(both, solved):
        at = GATES * n + r
        weighed.append((cols_ref[:, at + 4 : at + 5] * u_mat).astype(BF16))
    moved = [
        dot(keys_t_ref[n], jnp.concatenate(weighed[2 * n : 2 * n + 2], axis=1))
        for n in range(spans)
    ]
    return [moved[n][:, r * DV : (r + 1) * DV] for n, r in both]


def opening_kernel(
    recv_ref,
    ck_ref,
    cv_ref,
    alog_ref,
    dt_ref,
    cq_ref,
    gain_ref,
    hop_ref,
    keys_ref,
    keys_t_ref,
    ends_ref,
    within_ref,
    cols_ref,
    t_ref,
    lin_ref,
    vs_ref,
    xs_ref,
    adds_ref,
    key_rows,
    rows,
    systems_ref,
    small_ref,
):
    first = lax.axis_index("half") == 0
    peers = recv_ref.shape[0]
    tokens = (recv_ref.shape[1] - GATES) // 4
    spans = keys_t_ref.shape[0]
    edges = []
    for which in (3, 0, 1, 2):
        end = (which + 1) * tokens
        edges.append(recv_ref[peers - 1, end - 16 : end, :].astype(F32)[16 - EDGE :])
    edges.append(jnp.zeros((16 - 4 * EDGE, 128), F32))
    hop_ref[2 * DK :, :] = jnp.concatenate(edges, axis=0).astype(BF16)

    @pl.when(first)
    def _():
        both = [(n, r) for n in range(spans) for r in range(2)]
        systems_of(
            recv_ref,
            ck_ref,
            alog_ref,
            dt_ref,
            keys_ref,
            keys_t_ref,
            systems_ref,
            small_ref,
            ends_ref,
            within_ref,
            cols_ref,
            None,
            key_rows,
        )
        taps = value_taps(lax.axis_index("sub"), cv_ref)
        widened(rows, recv_ref, [tokens, 2 * tokens], tokens)
        waiting = list(both)

        def meanwhile():
            for n, r in waiting[:6]:
                lanes = slice(r * DV, (r + 1) * DV)
                value = convolved(rows, n * SPAN + 8 - EDGE, SPAN, lanes, taps[r])
                vs_ref[r, n * SPAN : (n + 1) * SPAN, :] = value.astype(BF16)
            del waiting[:6]

        compact = jnp.concatenate([small_ref[r, n] for n, r in both], axis=0)
        small = substituted(compact.reshape(len(both), SUB, SPAN))
        systems = [(systems_ref[r, n, 0], systems_ref[r, n, 1]) for n, r in both]
        inverses = inverted(systems, [small[i] for i in range(len(both))], meanwhile)
        while waiting:
            meanwhile()
        rights = []
        for i, (n, r) in enumerate(both):
            t_ref[r, n, 0], t_ref[r, n, 1] = inverses[i]
            at = GATES * n + r
            here = slice(n * SPAN, (n + 1) * SPAN)
            key = (cols_ref[:, at + 2 : at + 3] * keys_ref[here, :].astype(F32)).astype(BF16)
            right = jnp.concatenate([key, vs_ref[r, here, :]], axis=1)
            rights.append(jnp.concatenate([right, right], axis=0))
        solved = [dot(jnp.concatenate(t, axis=1), x) for t, x in zip(inverses, rights)]
        weighed = []
        for (n, r), x in zip(both, solved):
            at = GATES * n + r
            weighed.append((cols_ref[:, at + 4 : at + 5] * x).astype(BF16))
        moved = [
            dot(keys_t_ref[n], jnp.concatenate(weighed[2 * n : 2 * n + 2], axis=1))
            for n in range(spans)
        ]
        adds = []
        for n, r in both:
            at = 2 * r * DK
            lin_ref[r, n] = moved[n][:, at : at + DK].astype(BF16)
            adds.append(moved[n][:, at + DK : at + 2 * DK])
            if n == 0 or (n + 1) & n:
                adds_ref[r, n] = adds[-1]
        maps = [
            [(end_of(ends_ref, n, r), lin_ref[r, n], adds[2 * n + r]) for n in range(spans)]
            for r in range(2)
        ]
        states = [m[0][2] for m in maps]
        done = 1
        while done < spans:
            for r in range(2):
                if done > 1:
                    xs_ref[r, done] = jnp.concatenate(halves(states[r]), axis=0)
            later = [composed(m[done : 2 * done]) for m in maps]
            states = [followed(m, x) for m, x in zip(later, states)]
            done *= 2
        for r in range(2):
            hop_ref[r * DK : (r + 1) * DK, :] = states[r].astype(BF16)

    @pl.when(jnp.logical_not(first))
    def _():
        hop_ref[0 : 2 * DK, :] = jnp.zeros((2 * DK, DV), BF16)


def states_kernel(
    recv_ref,
    cv_ref,
    keys_t_ref,
    t_ref,
    lin_ref,
    ends_ref,
    cols_ref,
    values_ref,
    states_ref,
    *rest,
):
    *last_ref, rows = rest

    @pl.when(lax.axis_index("half") > 0)
    def _():
        spans = t_ref.shape[1]
        adds = values_part(recv_ref, cv_ref, keys_t_ref, t_ref, cols_ref, rows, values_ref)
        zero_half = jnp.zeros((DK, DV), F32)
        identity = jnp.where(iota((DK, DK), 0) == iota((DK, DK), 1), 1.0, 0.0)
        states = [
            jnp.concatenate(
                [adds[r], ends_ref[r : r + 1, :] * identity - lin_ref[r, 0].astype(F32)], axis=1
            )
            for r in range(2)
        ]
        for n in range(1, spans):
            for r in range(2):
                parts = halves(states[r])
                for i in range(2):
                    both_parts = [x[:, i * DV : (i + 1) * DV] for x in parts]
                    states_ref[i, r, n] = jnp.concatenate(both_parts, axis=0)
                add = jnp.concatenate([adds[2 * n + r], zero_half], axis=1)
                end = jnp.concatenate([end_of(ends_ref, n, r)] * 2, axis=1)
                states[r] = step(end, lin_ref[r, n], states[r], parts) + add
        for ref in last_ref:
            for r in range(2):
                ref[r] = states[r]


def span_rows(n):
    return slice(n * SPAN, (n + 1) * SPAN)


def twice(x, axis):
    return jnp.concatenate([x, x], axis=axis)


def asked(recv_ref, cq_ref, keys_ref, keys_t_ref, within, query_rows):
    tokens = (recv_ref.shape[1] - GATES) // 4
    spans = keys_t_ref.shape[0]
    tap = key_tap(lax.axis_index("sub"), cq_ref)
    widened(query_rows, recv_ref, [3 * tokens], tokens)
    queries = [
        unit(convolved(query_rows, n * SPAN + 8 - EDGE, SPAN, slice(0, DK), tap), DK**-0.5)
        for n in range(spans)
    ]
    readers = [
        jnp.concatenate([keys_ref[span_rows(n), :], queries[n]], axis=0) for n in range(spans)
    ]
    scores = [dot(queries[n], keys_t_ref[n]) for n in range(spans)]
    inner = [
        (within(n, r) * scores[n]).astype(BF16)
        for n in range(spans)
        for r in range(2)
    ]
    return readers, inner


def first_outputs_kernel(
    recv_ref,
    cq_ref,
    keys_ref,
    keys_t_ref,
    t_ref,
    lin_ref,
    ends_ref,
    within_ref,
    cols_ref,
    values_ref,
    xs_ref,
    adds_ref,
    oa_ref,
    query_rows,
):
    @pl.when(lax.axis_index("half") == 0)
    def _():
        spans = t_ref.shape[1]
        both = [(n, r) for n in range(spans) for r in range(2)]
        lower = iota((SPAN, SPAN), 0) >= iota((SPAN, SPAN), 1)

        def within(n, r):
            line = slice(GATES * n + r, GATES * n + r + 1)
            gap = cols_ref[:, line] - within_ref[0, line, :]
            decayed = jnp.exp(jnp.where(lower, gap, 0.0)) * within_ref[1, line, :]
            return jnp.where(lower, decayed, 0.0)

        readers, inner = asked(recv_ref, cq_ref, keys_ref, keys_t_ref, within, query_rows)
        stacks, states = [], []
        for n in range(1, spans):
            if n == 1:
                states = [adds_ref[r, 0] for r in range(2)]
                stack = [jnp.concatenate(halves(x), axis=0) for x in states]
            elif n & (n - 1) == 0:
                stack = [xs_ref[r, n] for r in range(2)]
                states = [x[:DK].astype(F32) + x[DK:].astype(F32) for x in stack]
            else:
                states = [
                    followed(
                        (end_of(ends_ref, n - 1, r), lin_ref[r, n - 1], adds_ref[r, n - 1]),
                        states[r],
                    )
                    for r in range(2)
                ]
                stack = [jnp.concatenate(halves(x), axis=0) for x in states]
            stacks.append(jnp.concatenate(stack, axis=1))
        reads = [dot(twice(readers[n], 1), stacks[n - 1]) for n in range(1, spans)]
        rests, seen = [], []
        for n, r in both:
            lanes = slice(r * DV, (r + 1) * DV)
            value = values_ref[r, span_rows(n), :]
            if n == 0:
                rests.append(value)
                seen.append(None)
            else:
                growth = cols_ref[:, GATES * n + 2 + r : GATES * n + 3 + r]
                read = growth * reads[n - 1][:SPAN, lanes]
                rests.append((value.astype(F32) - read).astype(BF16))
                seen.append(growth * reads[n - 1][SPAN:, lanes])
        fresh = [unwound(t_ref, n, r, x).astype(BF16) for (n, r), x in zip(both, rests)]
        spreads = [dot(w, x) for w, x in zip(inner, fresh)]
        for (n, r), x, y in zip(both, spreads, seen):
            oa_ref[r, span_rows(n), :] = x if y is None else x + y


def later_outputs_kernel(
    recv_ref,
    cq_ref,
    keys_ref,
    keys_t_ref,
    t_ref,
    within_ref,
    cols_ref,
    values_ref,
    states_ref,
    oa_ref,
    om_ref,
    query_rows,
):
    @pl.when(lax.axis_index("half") > 0)
    def _():
        spans = t_ref.shape[1]
        both = [(n, r) for n in range(spans) for r in range(2)]
        readers, inner = asked(
            recv_ref,
            cq_ref,
            keys_ref,
            keys_t_ref,
            lambda n, r: within_ref[r, span_rows(n), :].astype(F32),
            query_rows,
        )
        zero_half = jnp.zeros((SPAN, DV), F32)
        reads = [
            dot(
                twice(readers[n], 1),
                jnp.concatenate([states_ref[0, r, n], states_ref[1, r, n]], axis=1),
            )
            if n > 0
            else None
            for n, r in both
        ]
        rests, seen = [], []
        for (n, r), read in zip(both, reads):
            value = values_ref[r, span_rows(n), :].astype(F32)
            growth = cols_ref[:, GATES * n + 2 + r : GATES * n + 3 + r]
            if n == 0:
                reader = readers[n].astype(F32)
                rest = jnp.concatenate([value, -(growth * reader[:SPAN])], axis=1)
                seen.append(jnp.concatenate([zero_half, growth * reader[SPAN:]], axis=1))
            else:
                rest = jnp.concatenate([value, zero_half], axis=1) - growth * read[:SPAN]
                seen.append(growth * read[SPAN:])
            rests.append(rest.astype(BF16))
        fresh = [unwound(t_ref, n, r, x).astype(BF16) for (n, r), x in zip(both, rests)]
        spreads = [dot(w, x) for w, x in zip(inner, fresh)]
        for (n, r), x, y in zip(both, spreads, seen):
            out = x + y
            oa_ref[r, span_rows(n), :] = out[:, :DV]
            om_ref[r, span_rows(n), :] = out[:, DV:].astype(BF16)


def first_tokens(hop_ref, recv_ref, early_ref, cq_ref, ck_ref, cv_ref, rows):
    sub = lax.axis_index("sub")
    tokens = (recv_ref.shape[1] - GATES) // 4
    taps = [key_tap(sub, cq_ref), key_tap(sub, ck_ref)] + value_taps(sub, cv_ref)
    results = []
    edges = hop_ref[2 * DK :, :].astype(F32)
    for g, first in enumerate((3, 0, 1, 2)):
        lanes = slice(g * 128, (g + 1) * 128)
        start = first * tokens
        rows[16 - EDGE : 16, lanes] = edges[EDGE * g : EDGE * (g + 1)]
        rows[16:32, lanes] = recv_ref[0, start : start + 16, :].astype(F32)
        results.append(convolved(rows, 16 - EDGE, 8, lanes, taps[g]))
    q_cols = jnp.transpose(unit(results[0], DK**-0.5).astype(F32))
    k_cols = jnp.transpose(unit(results[1], 1.0).astype(F32))
    gates = early_ref[...]
    line = iota((8, DV), 0)
    values = [x.astype(BF16).astype(F32) for x in results[2:]]
    states = [hop_ref[r * DK : (r + 1) * DK, :].astype(F32) for r in range(2)]
    outputs = [jnp.zeros((8, DV), F32) for r in range(2)]
    for t in range(EDGE):
        k_t, q_t = k_cols[:, t : t + 1], q_cols[:, t : t + 1]
        states = [jnp.exp(gates[r : r + 1, t : t + 1]) * states[r] for r in range(2)]
        held = [jnp.sum(k_t * x, axis=0, keepdims=True) for x in states]
        fresh = [
            gates[2 + r : 3 + r, t : t + 1] * (values[r][t : t + 1, :] - held[r])
            for r in range(2)
        ]
        states = [x + k_t * y for x, y in zip(states, fresh)]
        outputs = [
            jnp.where(line == t, jnp.sum(q_t * x, axis=0, keepdims=True), y)
            for x, y in zip(states, outputs)
        ]
    return states, outputs


def put(out_ref, gain, c, r, core):
    peer_part, tokens = out_ref.shape[0] // CHUNKS, out_ref.shape[1] // 2
    scale = lax.rsqrt(jnp.mean(core * core, axis=-1, keepdims=True) + EPS)
    normed = (core * scale * gain).astype(BF16)
    here = slice(c * peer_part, (c + 1) * peer_part)
    out_ref[here, r * tokens : (r + 1) * tokens, :] = normed.reshape(peer_part, tokens, DV)


def first_finish_kernel(gain_ref, oa_ref, out_ref):
    @pl.when(lax.axis_index("half") == 0)
    def _():
        gain = gain_ref[...]
        part = oa_ref.shape[1] // CHUNKS
        for c in range(CHUNKS):
            for r in range(2):
                put(out_ref, gain, c, r, oa_ref[r, c * part : (c + 1) * part, :])


def later_finish_kernel(
    normed_ref,
    hop_ref,
    recv_ref,
    early_ref,
    cq_ref,
    ck_ref,
    cv_ref,
    gain_ref,
    oa_ref,
    om_ref,
    out_ref,
    rows,
):
    del normed_ref

    @pl.when(lax.axis_index("half") > 0)
    def _():
        gain = gain_ref[...]
        part = oa_ref.shape[1] // CHUNKS
        finals, outputs = first_tokens(hop_ref, recv_ref, early_ref, cq_ref, ck_ref, cv_ref, rows)
        replaced = iota((8, DV), 0) < EDGE
        passed = [dot(om_ref[r], finals[r].astype(BF16)) for r in range(2)]
        for c in range(CHUNKS):
            at = c * part
            for r in range(2):
                core = oa_ref[r, at : at + part, :] + passed[r][at : at + part]
                if c == 0:
                    core = jnp.concatenate(
                        [jnp.where(replaced, outputs[r], core[0:8]), core[8:]], axis=0
                    )
                put(out_ref, gain, c, r, core)


def advance_kernel(
    hop_ref, recv_ref, early_ref, cq_ref, ck_ref, cv_ref, hop_own, last_ref, next_ref, rows
):
    finals, _ = first_tokens(hop_ref, recv_ref, early_ref, cq_ref, ck_ref, cv_ref, rows)
    first = lax.axis_index("half") == 0
    for r in range(2):
        last = last_ref[r]
        through = mm_parts(halves(last[:, DV:]), halves(finals[r]))
        own = hop_own[r * DK : (r + 1) * DK, :].astype(F32)
        moved = jnp.where(first, own, through + last[:, :DV])
        next_ref[r * DK : (r + 1) * DK, :] = moved.astype(BF16)
    next_ref[2 * DK :, :] = hop_own[2 * DK :, :]


def gate_kernel(heads_axis, normed_ref, z_ref, out_ref, made, sems):
    subs, tokens = normed_ref.shape[0] // heads_axis, z_ref.shape[0]
    width = subs * 2 * DV
    copies = []
    for head in range(heads_axis):
        for sub in range(subs):
            for r in range(2):
                at = (2 * (head * subs + sub) + r) * DV
                gate = silu(z_ref[:, at : at + DV].astype(F32))
                here = slice(r * tokens, (r + 1) * tokens)
                value = normed_ref[sub * heads_axis + head, here, :].astype(F32)
                made[:, at : at + DV] = (value * gate).astype(BF16)
            if sub % 2 == 1:
                lanes = pl.ds(head * width + (sub - 1) * 2 * DV, 4 * DV)
                copy = pltpu.make_async_copy(
                    made.at[:, lanes], out_ref.at[:, lanes], sems.at[len(copies)]
                )
                copy.start()
                copies.append(copy)
    for copy in copies:
        copy.wait()


VMEM = pl.BlockSpec(memory_space=pltpu.VMEM)
ANY = pl.BlockSpec(memory_space=pl.ANY)


def near(x):
    return pltpu.with_memory_space_constraint(x, pltpu.VMEM)


def far(x):
    return pltpu.with_memory_space_constraint(x, pltpu.HBM)


def call(
    kernel, outs, in_specs, scratch=(), out_spec=VMEM, flops=1 << 26, moved=1 << 21, aliases=()
):
    return pl.pallas_call(
        kernel,
        out_shape=outs,
        in_specs=in_specs,
        out_specs=jax.tree.map(lambda _: out_spec, outs),
        scratch_shapes=list(scratch),
        input_output_aliases=dict(aliases),
        compiler_params=pltpu.CompilerParams(vmem_limit_bytes=VMEM_BYTES),
        cost_estimate=pl.CostEstimate(flops=flops, bytes_accessed=moved, transcendentals=0),
    )


def local(
    q_rows,
    k_rows,
    v_rows,
    z_rows,
    a_rows,
    b_rows,
    conv_q,
    conv_k,
    conv_v,
    a_log,
    dt_bias,
    norm_gain,
):
    shards, subs, heads_axis = (lax.axis_size(a) for a in ("half", "sub", "head"))
    peers, tokens = subs * heads_axis, q_rows.shape[0]
    total = peers * tokens
    spans = total // SPAN
    group = ("sub", "head")
    route = [(i, i + 1) for i in range(shards - 1)]
    conv_q, conv_k, conv_v = near(conv_q), near(conv_k), near(conv_v)
    gain = near(norm_gain.reshape(1, DV))
    a_log, dt_bias = near(a_log.reshape(1, -1)), near(dt_bias.reshape(1, -1))
    inputs = [far(x) for x in (q_rows, k_rows, v_rows, a_rows.T, b_rows.T)]
    packed = call(
        functools.partial(pack_kernel, heads_axis),
        pltpu.VMEM((peers, GATES + 4 * tokens, 128), BF16),
        [ANY] * 5,
        [pltpu.VMEM(x.shape, BF16) for x in inputs] + [pltpu.SemaphoreType.DMA((10,))],
        flops=1 << 20,
    )(*inputs)
    blocks = near(lax.all_to_all(packed, group, 0, 0, tiled=True))
    key_shapes = (pltpu.VMEM((total, DK), BF16), pltpu.VMEM((spans, DK, SPAN), BF16))
    system_shapes = (
        pltpu.VMEM((2, spans, 2, SPAN, SPAN), BF16),
        pltpu.VMEM((2, spans, SUB, SPAN), F32),
    )
    decay_shapes = (
        pltpu.VMEM((SPAN, DK), F32),
        pltpu.VMEM((2, total, SPAN), BF16),
        pltpu.VMEM((SPAN, SPAN), F32),
    )
    map_shapes = (
        pltpu.VMEM((2, spans, 2, SPAN, SPAN), BF16),
        pltpu.VMEM((2, spans, DK, DK), BF16),
    )
    opened = call(
        opening_kernel,
        (
            pltpu.VMEM((2 * DK + 16, 128), BF16),
            *key_shapes,
            decay_shapes[0],
            pltpu.VMEM((2, SPAN, SPAN), F32),
            decay_shapes[2],
            *map_shapes,
            pltpu.VMEM((2, total, DV), BF16),
            pltpu.VMEM((2, spans, 2 * DK, DV), BF16),
            pltpu.VMEM((2, spans, DK, DV), F32),
        ),
        [VMEM] * 7,
        [
            pltpu.VMEM((8 + total, DK), F32),
            pltpu.VMEM((8 + total, 2 * DV), F32),
            *system_shapes,
        ],
        flops=1 << 32,
    )(blocks, conv_k, conv_v, a_log, dt_bias, conv_q, gain)
    hop = opened[0]
    entering = near(lax.ppermute(hop, "half", route))
    hop, keys, keys_t, ends, within, cols, inverses, lins, values, starts, adds = (
        near(x) for x in opened
    )
    first_out = call(
        first_outputs_kernel,
        pltpu.VMEM((2, total, DV), F32),
        [VMEM] * 12,
        [pltpu.VMEM((8 + total, DK), F32)],
        flops=1 << 32,
    )(
        blocks,
        conv_q,
        keys,
        keys_t,
        inverses,
        lins,
        ends,
        within,
        cols,
        values,
        starts,
        adds,
    )
    made = call(
        systems_kernel,
        (*key_shapes, *system_shapes, *decay_shapes, pltpu.VMEM((8, SPAN), F32)),
        [VMEM] * 5,
        [pltpu.VMEM((8 + total, DK), F32)],
        flops=1 << 32,
    )(hop, blocks, conv_k, a_log, dt_bias)
    keys, keys_t, systems, small, ends, within, cols, early = (near(x) for x in made)
    later_solved = call(inverse_kernel, map_shapes, [VMEM] * 6, flops=1 << 32)(
        hop, keys, keys_t, systems, small, cols
    )
    later_inverses, later_lins = (near(x) for x in later_solved)
    read_on = [pltpu.VMEM((2, DK, 2 * DV), F32)] if shards > 2 else []
    later_values, states, *last = call(
        states_kernel,
        (
            pltpu.VMEM((2, total, DV), BF16),
            pltpu.VMEM((2, 2, spans, 2 * DK, DV), BF16),
            *read_on,
        ),
        [VMEM] * 7,
        [pltpu.VMEM((8 + total, 2 * DV), F32)],
        flops=1 << 32,
    )(blocks, conv_v, keys_t, later_inverses, later_lins, ends, cols)
    out_a, out_m = call(
        later_outputs_kernel,
        (pltpu.VMEM((2, total, DV), F32), pltpu.VMEM((2, total, DV), BF16)),
        [VMEM] * 9,
        [pltpu.VMEM((8 + total, DK), F32)],
        flops=1 << 32,
    )(
        blocks,
        conv_q,
        keys,
        keys_t,
        later_inverses,
        within,
        cols,
        near(later_values),
        near(states),
    )
    for _ in range(shards - 2):
        moved = call(
            advance_kernel,
            pltpu.VMEM(hop.shape, BF16),
            [VMEM] * 8,
            [pltpu.VMEM((32, 512), F32)],
        )(entering, blocks, early, conv_q, conv_k, conv_v, hop, near(last[0]))
        entering = near(lax.ppermute(moved, "half", route))
    normed_shape = pltpu.VMEM((peers, 2 * tokens, DV), BF16)
    first_normed = call(first_finish_kernel, normed_shape, [VMEM] * 2, flops=1 << 30)(
        gain, near(first_out)
    )
    normed = call(
        later_finish_kernel,
        normed_shape,
        [VMEM] * 10,
        [pltpu.VMEM((32, 512), F32)],
        aliases=((0, 0),),
    )(
        near(first_normed),
        entering,
        blocks,
        early,
        conv_q,
        conv_k,
        conv_v,
        gain,
        near(out_a),
        near(out_m),
    )
    returned = near(lax.all_to_all(normed, group, 0, 0, tiled=True))
    return call(
        functools.partial(gate_kernel, heads_axis),
        jax.ShapeDtypeStruct(z_rows.shape, BF16),
        [VMEM] * 2,
        [pltpu.VMEM(z_rows.shape, BF16), pltpu.SemaphoreType.DMA((peers // 2,))],
        ANY,
    )(returned, z_rows)


def solution(mesh):
    heads_axis = mesh.shape["head"]
    subs = KH // heads_axis
    regrouped = Mesh(
        mesh.devices.reshape(mesh.shape["ctx"] // subs, subs, heads_axis), ("half", "sub", "head")
    )
    row = P(("half", "sub", "head"), None)
    placed = (row,) * 6 + (P(None, "head"),) * 3 + (P("head"),) * 2 + (P(),)
    return jax.shard_map(local, mesh=regrouped, in_specs=placed, out_specs=row, check_vma=False)
```

```python
import functools

import jax
import jax.numpy as jnp
from jax import lax
from jax.experimental import pallas as pl
from jax.experimental.pallas import tpu as pltpu
from jax.sharding import Mesh, PartitionSpec as P

DK = 128
DV = 128
CONV = 4
KH = 16
SUB = 16
SPAN = 128
CHUNKS = 4
EDGE = CONV - 1
EPS = 1e-06
F32 = jnp.float32
BF16 = jnp.bfloat16
VMEM_BYTES = 24 * 1024 * 1024
GATES = 8


def dot(a, b, dims=((1,), (0,))):
    return lax.dot_general(a, b, (dims, ((), ())), preferred_element_type=F32)


def halves(x):
    high = x.astype(BF16)
    return high, (x - high.astype(F32)).astype(BF16)


def mm_parts(a, b):
    left = jnp.concatenate([a[0], a[1], a[0]], axis=1)
    return dot(left, jnp.concatenate([b[0], b[0], b[1]], axis=0))


def silu(x):
    half = 0.5 * x
    return half + half * jnp.tanh(half)


def unit(y, factor):
    scale = lax.rsqrt(jnp.sum(y * y, axis=-1, keepdims=True) + EPS)
    return (y * scale * factor).astype(BF16)


def iota(shape, dim):
    return lax.broadcasted_iota(jnp.int32, shape, dim)


def block_of(x, size):
    return lax.shift_right_logical(x, jnp.full(x.shape, size.bit_length() - 1, jnp.int32))


def place_in(x, size):
    return x & (size - 1)


def pack_kernel(
    heads_axis, q_in, k_in, v_in, at_in, bt_in, out_ref, q_ref, k_ref, v_ref, at_ref, bt_ref, sems
):
    peers, tokens = out_ref.shape[0], q_ref.shape[0]
    pairs = ((at_in, at_ref), (bt_in, bt_ref), (k_in, k_ref), (v_in, v_ref), (q_in, q_ref))
    copies = [pltpu.make_async_copy(a, b, sems.at[i]) for i, (a, b) in enumerate(pairs)]
    for copy in copies:
        copy.start()
    subs = peers // heads_axis
    key_heads = [(dest % heads_axis) * subs + dest // heads_axis for dest in range(peers)]
    for copy in copies[:2]:
        copy.wait()
    value_heads = at_ref.shape[0]
    row, entry = iota((peers * GATES, value_heads), 0), iota((peers * GATES, value_heads), 1)
    dest, which = block_of(row, GATES), place_in(row, GATES)
    first = 2 * (place_in(dest, heads_axis) * subs + block_of(dest, heads_axis))
    pick_a = jnp.where((which < 2) & (entry == first + which), 1.0, 0.0).astype(BF16)
    pick_b = jnp.where(
        (which >= 2) & (which < 4) & (entry == first + which - 2), 1.0, 0.0
    ).astype(BF16)
    picked = (dot(pick_a, at_ref[...]) + dot(pick_b, bt_ref[...])).astype(BF16)
    lane_shift = tokens * lax.rem(lax.axis_index("head"), SPAN // tokens)
    place = jnp.where(
        iota((tokens, SPAN), 1) == iota((tokens, SPAN), 0) + lane_shift, 1.0, 0.0
    ).astype(BF16)
    gates = dot(picked, place).astype(BF16)
    for dest in range(peers):
        out_ref[dest, 4 * tokens :, :] = gates[GATES * dest : GATES * (dest + 1), :]

    def laid(ref, lane, start):
        for dest, key_head in enumerate(key_heads):
            at = lane(key_head) * 128
            out_ref[dest, start * tokens : (start + 1) * tokens, :] = ref[
                :, at : at + 128
            ]

    copies[2].wait()
    laid(k_ref, lambda key_head: key_head, 0)
    copies[3].wait()
    laid(v_ref, lambda key_head: 2 * key_head, 1)
    laid(v_ref, lambda key_head: 2 * key_head + 1, 2)
    copies[4].wait()
    laid(q_ref, lambda key_head: key_head, 3)


def compacted(system):
    size = system.shape[0]
    diagonal = block_of(iota((size, size), 0), SUB) == block_of(iota((size, size), 1), SUB)
    return jnp.sum(jnp.where(diagonal, system, 0.0).reshape(size // SUB, SUB, size), axis=0)


def substituted(compact):
    count, _, size = compact.shape
    flat = compact.reshape(count * SUB, size)
    lane, line = iota(flat.shape, 1), iota(flat.shape, 0)
    solved = jnp.where(place_in(lane ^ line, SUB) == 0, 1.0, 0.0).reshape(count, SUB, size)
    for m in range(SUB - 1):
        source = (lane & ~(SUB - 1)) | m
        spread = jnp.take_along_axis(flat, source, axis=1, mode="promise_in_bounds")
        solved = solved + spread.reshape(count, SUB, size) * solved[:, m : m + 1, :]
    return solved


def inverted(systems, small, meanwhile=lambda: None):
    size = systems[0][0].shape[0]
    row, col = iota((size, size), 0), iota((size, size), 1)
    placed = jnp.where(block_of(row, SUB) == block_of(col, SUB), 1.0, 0.0).astype(BF16)
    identity = jnp.where(row == col, 1.0, 0.0)
    rough = [
        jnp.concatenate([block.astype(BF16)] * (size // SUB), axis=0) * placed for block in small
    ]
    blank = jnp.zeros((size, size), BF16)
    width = SUB
    while width < size:
        odd = [(j, j + width) for j in range(width, size, 2 * width)]

        def rows_of(x):
            return jnp.concatenate([x[lo:hi] for lo, hi in odd], axis=0)

        def woven(even, x):
            pieces = []
            for j, (lo, hi) in enumerate(odd):
                pieces += [even[lo - width : lo], x[j * width : (j + 1) * width]]
            return jnp.concatenate(pieces, axis=0)

        below = rows_of(block_of(row ^ col, 2 * width)) + rows_of(col & width) == 0
        own = rows_of(identity)
        firsts = [dot(rows_of(n[0]), t) for n, t in zip(systems, rough)]
        meanwhile()
        rights = [
            woven(blank, jnp.where(below, first, own).astype(BF16)) for first in firsts
        ]
        grown = [dot(rows_of(t), right).astype(BF16) for t, right in zip(rough, rights)]
        rough = [woven(t, g) for t, g in zip(rough, grown)]
        width *= 2
    products = [
        dot(jnp.concatenate(n, axis=1), jnp.concatenate([t, t], axis=0))
        for n, t in zip(systems, rough)
    ]
    rests = [
        (identity - t.astype(F32) + product).astype(BF16) for t, product in zip(rough, products)
    ]
    return [halves(t.astype(F32) + dot(t, rest)) for t, rest in zip(rough, rests)]


def own_entry(ref, index):
    row = ref[...]
    return jnp.sum(jnp.where(iota(row.shape, 1) == index, row, 0.0), axis=1, keepdims=True)


def gate_values(gates, sub, alog_ref, dt_ref):
    second = place_in(iota(gates.shape, 0), GATES) == 1
    a_log, dt_bias = (
        jnp.where(second, own_entry(ref, 2 * sub + 1), own_entry(ref, 2 * sub))
        for ref in (alog_ref, dt_ref)
    )
    shifted = gates + dt_bias
    soft = jnp.maximum(shifted, 0.0) + jnp.log1p(jnp.exp(-jnp.abs(shifted)))
    return -jnp.exp(a_log) * soft, 1.0 / (1.0 + jnp.exp(-gates))


def convolved(rows, at, count, lanes, tap):
    summed = tap[0:1] * rows[at : at + count, lanes]
    for j in range(1, CONV):
        summed = summed + tap[j : j + 1] * rows[at + j : at + j + count, lanes]
    return silu(summed)


def key_tap(sub, tap_ref):
    return tap_ref[:, pl.ds(pl.multiple_of(sub * DK, 128), DK)]


def value_taps(sub, cv_ref):
    lane = pl.multiple_of(sub * 2 * DV, 128)
    return [cv_ref[:, pl.ds(pl.multiple_of(lane + r * DV, 128), DV)] for r in range(2)]


def widened(rows, recv_ref, starts, tokens):
    rows[0:8, :] = jnp.zeros((8, rows.shape[1]), F32)
    for s in range(recv_ref.shape[0]):
        for g, start in enumerate(starts):
            rows[8 + s * tokens : 8 + (s + 1) * tokens, g * 128 : (g + 1) * 128] = recv_ref[
                s, start : start + tokens, :
            ].astype(F32)


def systems_kernel(hop_ref, recv_ref, ck_ref, alog_ref, dt_ref, *refs):
    del hop_ref

    @pl.when(lax.axis_index("half") > 0)
    def _():
        systems_of(recv_ref, ck_ref, alog_ref, dt_ref, *refs)


def systems_of(
    recv_ref,
    ck_ref,
    alog_ref,
    dt_ref,
    keys_ref,
    keys_t_ref,
    systems_ref,
    small_ref,
    ends_ref,
    within_ref,
    cols_ref,
    early_ref,
    rows,
):
    sub = lax.axis_index("sub")
    later = lax.axis_index("half") > 0
    peers = recv_ref.shape[0]
    tokens = (recv_ref.shape[1] - GATES) // 4
    spans = peers * tokens // SPAN
    tap = key_tap(sub, ck_ref)
    widened(rows, recv_ref, [0], tokens)
    stacked = [
        sum(recv_ref[s, 4 * tokens :, :].astype(F32) for s in range(n, n + SPAN // tokens))
        for n in range(0, peers, SPAN // tokens)
    ]
    stacked.append(jnp.zeros((SPAN - spans * GATES, SPAN), F32))
    gates = jnp.concatenate(stacked, axis=0)
    decay, rate = gate_values(gates, sub, alog_ref, dt_ref)
    if early_ref is not None:
        early_ref[...] = jnp.where(iota((8, SPAN), 0) < 2, decay[0:8], rate[0:8])
    skipped = later & (iota(gates.shape, 0) < GATES) & (iota(gates.shape, 1) < EDGE)
    decay = jnp.where(skipped, 0.0, decay)
    rate = jnp.where(skipped, 0.0, rate)
    lane_r, lane_c = iota((SPAN, SPAN), 0), iota((SPAN, SPAN), 1)
    upto = jnp.where(lane_r <= lane_c, 1.0, 0.0).astype(BF16)
    d_high, _ = halves(decay)
    d_mid, d_low = halves(decay - d_high.astype(F32))
    cum = dot(d_high, upto) + (dot(d_mid, upto) + dot(d_low, upto))
    growth = jnp.exp(cum)
    here = pltpu.roll(rate, rate.shape[0] - 2, 0)
    rest = jnp.exp(cum[:, SPAN - 1 :] - cum) * here
    which = place_in(iota(gates.shape, 0), GATES)
    mixed = jnp.where(which < 2, cum, pltpu.roll(growth, 2, 0))
    columns = jnp.transpose(jnp.where(which < 4, mixed, pltpu.roll(rest, 4, 0)))
    cols_ref[...] = columns
    lower = lane_r >= lane_c
    strict = lane_r > lane_c
    both = [(n, r) for n in range(spans) for r in range(2)]
    keys = []
    for n in range(spans):
        k_n = unit(convolved(rows, n * SPAN + 8 - EDGE, SPAN, slice(0, DK), tap), 1.0)
        keys_ref[n * SPAN : (n + 1) * SPAN, :] = k_n
        keys.append(k_n)
    keys_t = []
    for n in range(spans):
        kt_n = jnp.transpose(keys[n].astype(F32)).astype(BF16)
        keys_t_ref[n] = kt_n
        keys_t.append(kt_n)
    grams = [dot(keys[n], keys_t[n]) for n in range(spans)]
    for n, r in both:
        at = GATES * n + r
        gap = columns[:, at : at + 1] - cum[at : at + 1, :]
        within = jnp.exp(jnp.where(lower, gap, 0.0)) * here[at : at + 1, :]
        within_ref[r, n * SPAN : (n + 1) * SPAN, :] = jnp.where(lower, within, 0.0).astype(BF16)
        system = jnp.where(strict, within * -grams[n], 0.0)
        systems_ref[r, n, 0], systems_ref[r, n, 1] = halves(system)
        small_ref[r, n] = compacted(system)
    ends_ref[...] = jnp.broadcast_to(growth[:, SPAN - 1 :], ends_ref.shape)


def inverse_kernel(
    hop_ref, keys_ref, keys_t_ref, systems_ref, small_ref, cols_ref, t_ref, lin_ref
):
    del hop_ref
    spans = keys_t_ref.shape[0]
    both = [(n, r) for n in range(spans) for r in range(2)]

    @pl.when(lax.axis_index("half") > 0)
    def _():
        compact = jnp.concatenate([small_ref[r, n] for n, r in both], axis=0)
        small = substituted(compact.reshape(len(both), SUB, SPAN))
        systems = [(systems_ref[r, n, 0], systems_ref[r, n, 1]) for n, r in both]
        inverses = inverted(systems, [small[i] for i in range(len(both))])
        scaled = []
        for i, (n, r) in enumerate(both):
            t_ref[r, n, 0], t_ref[r, n, 1] = inverses[i]
            at = GATES * n + r
            key = keys_ref[n * SPAN : (n + 1) * SPAN, :].astype(F32)
            right = (cols_ref[:, at + 2 : at + 3] * key).astype(BF16)
            scaled.append(jnp.concatenate([right, right], axis=0))
        w_mats = [dot(jnp.concatenate(t, axis=1), x) for t, x in zip(inverses, scaled)]
        weighed = []
        for (n, r), w_mat in zip(both, w_mats):
            at = GATES * n + r
            weighed.append((cols_ref[:, at + 4 : at + 5] * w_mat).astype(BF16))
        moved = [
            dot(keys_t_ref[n], jnp.concatenate(weighed[2 * n : 2 * n + 2], axis=1))
            for n in range(spans)
        ]
        for n, r in both:
            lin_ref[r, n] = moved[n][:, r * DK : (r + 1) * DK].astype(BF16)


def unwound(t_ref, n, r, x):
    both = jnp.concatenate([t_ref[r, n, 0], t_ref[r, n, 1]], axis=1)
    return dot(both, jnp.concatenate([x, x], axis=0))


def end_of(ends_ref, n, r):
    return ends_ref[GATES * n + r : GATES * n + r + 1, :]


def followed(span_map, state):
    end, moved, add = span_map
    return step(end, moved, state, halves(state)) + add


def composed(maps):
    if len(maps) == 1:
        return maps[0]
    half = len(maps) // 2
    end_a, moved_a, add_a = composed(maps[:half])
    end_b, moved_b, add_b = composed(maps[half:])
    high, low = halves(add_a)
    rights = jnp.concatenate(
        [
            jnp.concatenate([moved_a, high], axis=1),
            jnp.concatenate([jnp.zeros_like(moved_a), low], axis=1),
        ],
        axis=0,
    )
    passed = dot(jnp.concatenate([moved_b, moved_b], axis=1), rights)
    moved = end_b * moved_a.astype(F32) + end_a * moved_b.astype(F32) - passed[:, :DK]
    add = end_b * add_a - passed[:, DK:] + add_b
    return end_a * end_b, moved.astype(BF16), add


def step(end, moved, state, parts):
    both = jnp.concatenate([moved, moved], axis=1)
    return end * state - dot(both, jnp.concatenate(parts, axis=0))


def values_part(recv_ref, cv_ref, keys_t_ref, t_ref, cols_ref, rows, vs):
    sub = lax.axis_index("sub")
    tokens = (recv_ref.shape[1] - GATES) // 4
    spans = t_ref.shape[1]
    taps = value_taps(sub, cv_ref)
    widened(rows, recv_ref, [tokens, 2 * tokens], tokens)
    both = [(n, r) for n in range(spans) for r in range(2)]
    values = []
    for n, r in both:
        lanes = slice(r * DV, (r + 1) * DV)
        v_n = convolved(rows, n * SPAN + 8 - EDGE, SPAN, lanes, taps[r]).astype(BF16)
        vs[r, n * SPAN : (n + 1) * SPAN, :] = v_n
        values.append(v_n)
    solved = [unwound(t_ref, n, r, v) for (n, r), v in zip(both, values)]
    weighed = []
    for (n, r), u_mat in zip(both, solved):
        at = GATES * n + r
        weighed.append((cols_ref[:, at + 4 : at + 5] * u_mat).astype(BF16))
    moved = [
        dot(keys_t_ref[n], jnp.concatenate(weighed[2 * n : 2 * n + 2], axis=1))
        for n in range(spans)
    ]
    return [moved[n][:, r * DV : (r + 1) * DV] for n, r in both]


def opening_kernel(
    recv_ref,
    ck_ref,
    cv_ref,
    alog_ref,
    dt_ref,
    cq_ref,
    gain_ref,
    hop_ref,
    keys_ref,
    keys_t_ref,
    ends_ref,
    within_ref,
    cols_ref,
    t_ref,
    lin_ref,
    vs_ref,
    xs_ref,
    adds_ref,
    key_rows,
    rows,
    systems_ref,
    small_ref,
):
    first = lax.axis_index("half") == 0
    peers = recv_ref.shape[0]
    tokens = (recv_ref.shape[1] - GATES) // 4
    spans = keys_t_ref.shape[0]
    edges = []
    for which in (3, 0, 1, 2):
        end = (which + 1) * tokens
        edges.append(recv_ref[peers - 1, end - 16 : end, :].astype(F32)[16 - EDGE :])
    edges.append(jnp.zeros((16 - 4 * EDGE, 128), F32))
    hop_ref[2 * DK :, :] = jnp.concatenate(edges, axis=0).astype(BF16)

    @pl.when(first)
    def _():
        both = [(n, r) for n in range(spans) for r in range(2)]
        taps = value_taps(lax.axis_index("sub"), cv_ref)
        widened(rows, recv_ref, [tokens, 2 * tokens], tokens)
        waiting = list(both)

        def meanwhile():
            for n, r in waiting[:6]:
                lanes = slice(r * DV, (r + 1) * DV)
                value = convolved(rows, n * SPAN + 8 - EDGE, SPAN, lanes, taps[r])
                vs_ref[r, n * SPAN : (n + 1) * SPAN, :] = value.astype(BF16)
            del waiting[:6]

        meanwhile()
        systems_of(
            recv_ref,
            ck_ref,
            alog_ref,
            dt_ref,
            keys_ref,
            keys_t_ref,
            systems_ref,
            small_ref,
            ends_ref,
            within_ref,
            cols_ref,
            None,
            key_rows,
        )
        compact = jnp.concatenate([small_ref[r, n] for n, r in both], axis=0)
        small = substituted(compact.reshape(len(both), SUB, SPAN))
        systems = [(systems_ref[r, n, 0], systems_ref[r, n, 1]) for n, r in both]
        inverses = inverted(systems, [small[i] for i in range(len(both))], meanwhile)
        while waiting:
            meanwhile()
        rights = []
        for i, (n, r) in enumerate(both):
            t_ref[r, n, 0], t_ref[r, n, 1] = inverses[i]
            at = GATES * n + r
            here = slice(n * SPAN, (n + 1) * SPAN)
            key = (cols_ref[:, at + 2 : at + 3] * keys_ref[here, :].astype(F32)).astype(BF16)
            right = jnp.concatenate([key, vs_ref[r, here, :]], axis=1)
            rights.append(jnp.concatenate([right, right], axis=0))
        solved = [dot(jnp.concatenate(t, axis=1), x) for t, x in zip(inverses, rights)]
        weighed = []
        for (n, r), x in zip(both, solved):
            at = GATES * n + r
            weighed.append((cols_ref[:, at + 4 : at + 5] * x).astype(BF16))
        moved = [
            dot(keys_t_ref[n], jnp.concatenate(weighed[2 * n : 2 * n + 2], axis=1))
            for n in range(spans)
        ]
        adds = []
        for n, r in both:
            at = 2 * r * DK
            lin_ref[r, n] = moved[n][:, at : at + DK].astype(BF16)
            adds.append(moved[n][:, at + DK : at + 2 * DK])
            adds_ref[r, n] = adds[-1]
        maps = [
            [(end_of(ends_ref, n, r), lin_ref[r, n], adds[2 * n + r]) for n in range(spans)]
            for r in range(2)
        ]
        states = [m[0][2] for m in maps]
        done = 1
        while done < spans:
            for r in range(2):
                if done > 1:
                    xs_ref[r, done] = jnp.concatenate(halves(states[r]), axis=0)
            later = [composed(m[done : 2 * done]) for m in maps]
            states = [followed(m, x) for m, x in zip(later, states)]
            done *= 2
        for r in range(2):
            hop_ref[r * DK : (r + 1) * DK, :] = states[r].astype(BF16)

    @pl.when(jnp.logical_not(first))
    def _():
        hop_ref[0 : 2 * DK, :] = jnp.zeros((2 * DK, DV), BF16)


def states_kernel(
    recv_ref,
    cv_ref,
    keys_t_ref,
    t_ref,
    lin_ref,
    ends_ref,
    cols_ref,
    values_ref,
    states_ref,
    *rest,
):
    *last_ref, rows = rest

    @pl.when(lax.axis_index("half") > 0)
    def _():
        spans = t_ref.shape[1]
        adds = values_part(recv_ref, cv_ref, keys_t_ref, t_ref, cols_ref, rows, values_ref)
        zero_half = jnp.zeros((DK, DV), F32)
        identity = jnp.where(iota((DK, DK), 0) == iota((DK, DK), 1), 1.0, 0.0)
        states = [
            jnp.concatenate(
                [adds[r], ends_ref[r : r + 1, :] * identity - lin_ref[r, 0].astype(F32)], axis=1
            )
            for r in range(2)
        ]
        for n in range(1, spans):
            for r in range(2):
                parts = halves(states[r])
                for i in range(2):
                    both_parts = [x[:, i * DV : (i + 1) * DV] for x in parts]
                    states_ref[i, r, n] = jnp.concatenate(both_parts, axis=0)
                add = jnp.concatenate([adds[2 * n + r], zero_half], axis=1)
                end = jnp.concatenate([end_of(ends_ref, n, r)] * 2, axis=1)
                states[r] = step(end, lin_ref[r, n], states[r], parts) + add
        for ref in last_ref:
            for r in range(2):
                ref[r] = states[r]


def span_rows(n):
    return slice(n * SPAN, (n + 1) * SPAN)


def twice(x, axis):
    return jnp.concatenate([x, x], axis=axis)


def asked(recv_ref, cq_ref, keys_ref, keys_t_ref, within_ref, query_rows):
    tokens = (recv_ref.shape[1] - GATES) // 4
    spans = keys_t_ref.shape[0]
    tap = key_tap(lax.axis_index("sub"), cq_ref)
    widened(query_rows, recv_ref, [3 * tokens], tokens)
    queries = [
        unit(convolved(query_rows, n * SPAN + 8 - EDGE, SPAN, slice(0, DK), tap), DK**-0.5)
        for n in range(spans)
    ]
    readers = [
        jnp.concatenate([keys_ref[span_rows(n), :], queries[n]], axis=0) for n in range(spans)
    ]
    scores = [dot(queries[n], keys_t_ref[n]) for n in range(spans)]
    inner = [
        (within_ref[r, span_rows(n), :].astype(F32) * scores[n]).astype(BF16)
        for n in range(spans)
        for r in range(2)
    ]
    return readers, inner


def first_outputs_kernel(
    recv_ref,
    cq_ref,
    keys_ref,
    keys_t_ref,
    t_ref,
    lin_ref,
    ends_ref,
    within_ref,
    cols_ref,
    values_ref,
    xs_ref,
    adds_ref,
    oa_ref,
    query_rows,
):
    @pl.when(lax.axis_index("half") == 0)
    def _():
        spans = t_ref.shape[1]
        both = [(n, r) for n in range(spans) for r in range(2)]
        readers, inner = asked(recv_ref, cq_ref, keys_ref, keys_t_ref, within_ref, query_rows)
        stacks, states = [], []
        for n in range(1, spans):
            if n == 1:
                states = [adds_ref[r, 0] for r in range(2)]
                stack = [jnp.concatenate(halves(x), axis=0) for x in states]
            elif n & (n - 1) == 0:
                stack = [xs_ref[r, n] for r in range(2)]
                states = [x[:DK].astype(F32) + x[DK:].astype(F32) for x in stack]
            else:
                states = [
                    followed(
                        (end_of(ends_ref, n - 1, r), lin_ref[r, n - 1], adds_ref[r, n - 1]),
                        states[r],
                    )
                    for r in range(2)
                ]
                stack = [jnp.concatenate(halves(x), axis=0) for x in states]
            stacks.append(jnp.concatenate(stack, axis=1))
        reads = [dot(twice(readers[n], 1), stacks[n - 1]) for n in range(1, spans)]
        rests, seen = [], []
        for n, r in both:
            lanes = slice(r * DV, (r + 1) * DV)
            value = values_ref[r, span_rows(n), :]
            if n == 0:
                rests.append(value)
                seen.append(None)
            else:
                growth = cols_ref[:, GATES * n + 2 + r : GATES * n + 3 + r]
                read = growth * reads[n - 1][:SPAN, lanes]
                rests.append((value.astype(F32) - read).astype(BF16))
                seen.append(growth * reads[n - 1][SPAN:, lanes])
        fresh = [unwound(t_ref, n, r, x).astype(BF16) for (n, r), x in zip(both, rests)]
        spreads = [dot(w, x) for w, x in zip(inner, fresh)]
        for (n, r), x, y in zip(both, spreads, seen):
            oa_ref[r, span_rows(n), :] = x if y is None else x + y


def later_outputs_kernel(
    recv_ref,
    cq_ref,
    keys_ref,
    keys_t_ref,
    t_ref,
    within_ref,
    cols_ref,
    values_ref,
    states_ref,
    oa_ref,
    om_ref,
    query_rows,
):
    @pl.when(lax.axis_index("half") > 0)
    def _():
        spans = t_ref.shape[1]
        both = [(n, r) for n in range(spans) for r in range(2)]
        readers, inner = asked(recv_ref, cq_ref, keys_ref, keys_t_ref, within_ref, query_rows)
        zero_half = jnp.zeros((SPAN, DV), F32)
        reads = [
            dot(
                twice(readers[n], 1),
                jnp.concatenate([states_ref[0, r, n], states_ref[1, r, n]], axis=1),
            )
            if n > 0
            else None
            for n, r in both
        ]
        rests, seen = [], []
        for (n, r), read in zip(both, reads):
            value = values_ref[r, span_rows(n), :].astype(F32)
            growth = cols_ref[:, GATES * n + 2 + r : GATES * n + 3 + r]
            if n == 0:
                reader = readers[n].astype(F32)
                rest = jnp.concatenate([value, -(growth * reader[:SPAN])], axis=1)
                seen.append(jnp.concatenate([zero_half, growth * reader[SPAN:]], axis=1))
            else:
                rest = jnp.concatenate([value, zero_half], axis=1) - growth * read[:SPAN]
                seen.append(growth * read[SPAN:])
            rests.append(rest.astype(BF16))
        fresh = [unwound(t_ref, n, r, x).astype(BF16) for (n, r), x in zip(both, rests)]
        spreads = [dot(w, x) for w, x in zip(inner, fresh)]
        for (n, r), x, y in zip(both, spreads, seen):
            out = x + y
            oa_ref[r, span_rows(n), :] = out[:, :DV]
            om_ref[r, span_rows(n), :] = out[:, DV:].astype(BF16)


def first_tokens(hop_ref, recv_ref, early_ref, cq_ref, ck_ref, cv_ref, rows):
    sub = lax.axis_index("sub")
    tokens = (recv_ref.shape[1] - GATES) // 4
    taps = [key_tap(sub, cq_ref), key_tap(sub, ck_ref)] + value_taps(sub, cv_ref)
    results = []
    edges = hop_ref[2 * DK :, :].astype(F32)
    for g, first in enumerate((3, 0, 1, 2)):
        lanes = slice(g * 128, (g + 1) * 128)
        start = first * tokens
        rows[16 - EDGE : 16, lanes] = edges[EDGE * g : EDGE * (g + 1)]
        rows[16:32, lanes] = recv_ref[0, start : start + 16, :].astype(F32)
        results.append(convolved(rows, 16 - EDGE, 8, lanes, taps[g]))
    q_cols = jnp.transpose(unit(results[0], DK**-0.5).astype(F32))
    k_cols = jnp.transpose(unit(results[1], 1.0).astype(F32))
    gates = early_ref[...]
    line = iota((8, DV), 0)
    values = [x.astype(BF16).astype(F32) for x in results[2:]]
    states = [hop_ref[r * DK : (r + 1) * DK, :].astype(F32) for r in range(2)]
    outputs = [jnp.zeros((8, DV), F32) for r in range(2)]
    for t in range(EDGE):
        k_t, q_t = k_cols[:, t : t + 1], q_cols[:, t : t + 1]
        states = [jnp.exp(gates[r : r + 1, t : t + 1]) * states[r] for r in range(2)]
        held = [jnp.sum(k_t * x, axis=0, keepdims=True) for x in states]
        fresh = [
            gates[2 + r : 3 + r, t : t + 1] * (values[r][t : t + 1, :] - held[r])
            for r in range(2)
        ]
        states = [x + k_t * y for x, y in zip(states, fresh)]
        outputs = [
            jnp.where(line == t, jnp.sum(q_t * x, axis=0, keepdims=True), y)
            for x, y in zip(states, outputs)
        ]
    return states, outputs


def put(out_ref, gain, c, r, core):
    peer_part, tokens = out_ref.shape[0] // CHUNKS, out_ref.shape[1] // 2
    scale = lax.rsqrt(jnp.mean(core * core, axis=-1, keepdims=True) + EPS)
    normed = (core * scale * gain).astype(BF16)
    here = slice(c * peer_part, (c + 1) * peer_part)
    out_ref[here, r * tokens : (r + 1) * tokens, :] = normed.reshape(peer_part, tokens, DV)


def first_finish_kernel(gain_ref, oa_ref, out_ref):
    @pl.when(lax.axis_index("half") == 0)
    def _():
        gain = gain_ref[...]
        part = oa_ref.shape[1] // CHUNKS
        for c in range(CHUNKS):
            for r in range(2):
                put(out_ref, gain, c, r, oa_ref[r, c * part : (c + 1) * part, :])


def later_finish_kernel(
    normed_ref,
    hop_ref,
    recv_ref,
    early_ref,
    cq_ref,
    ck_ref,
    cv_ref,
    gain_ref,
    oa_ref,
    om_ref,
    out_ref,
    rows,
):
    del normed_ref

    @pl.when(lax.axis_index("half") > 0)
    def _():
        gain = gain_ref[...]
        part = oa_ref.shape[1] // CHUNKS
        finals, outputs = first_tokens(hop_ref, recv_ref, early_ref, cq_ref, ck_ref, cv_ref, rows)
        replaced = iota((8, DV), 0) < EDGE
        passed = [dot(om_ref[r], finals[r].astype(BF16)) for r in range(2)]
        for c in range(CHUNKS):
            at = c * part
            for r in range(2):
                core = oa_ref[r, at : at + part, :] + passed[r][at : at + part]
                if c == 0:
                    core = jnp.concatenate(
                        [jnp.where(replaced, outputs[r], core[0:8]), core[8:]], axis=0
                    )
                put(out_ref, gain, c, r, core)


def advance_kernel(
    hop_ref, recv_ref, early_ref, cq_ref, ck_ref, cv_ref, hop_own, last_ref, next_ref, rows
):
    finals, _ = first_tokens(hop_ref, recv_ref, early_ref, cq_ref, ck_ref, cv_ref, rows)
    first = lax.axis_index("half") == 0
    for r in range(2):
        last = last_ref[r]
        through = mm_parts(halves(last[:, DV:]), halves(finals[r]))
        own = hop_own[r * DK : (r + 1) * DK, :].astype(F32)
        moved = jnp.where(first, own, through + last[:, :DV])
        next_ref[r * DK : (r + 1) * DK, :] = moved.astype(BF16)
    next_ref[2 * DK :, :] = hop_own[2 * DK :, :]


def gate_kernel(heads_axis, normed_ref, z_ref, out_ref, made, sems):
    subs, tokens = normed_ref.shape[0] // heads_axis, z_ref.shape[0]
    width = subs * 2 * DV
    copies = []
    for head in range(heads_axis):
        for sub in range(subs):
            for r in range(2):
                at = (2 * (head * subs + sub) + r) * DV
                gate = silu(z_ref[:, at : at + DV].astype(F32))
                here = slice(r * tokens, (r + 1) * tokens)
                value = normed_ref[sub * heads_axis + head, here, :].astype(F32)
                made[:, at : at + DV] = (value * gate).astype(BF16)
        lanes = pl.ds(head * width, width)
        copy = pltpu.make_async_copy(made.at[:, lanes], out_ref.at[:, lanes], sems.at[head])
        copy.start()
        copies.append(copy)
    for copy in copies:
        copy.wait()


VMEM = pl.BlockSpec(memory_space=pltpu.VMEM)
ANY = pl.BlockSpec(memory_space=pl.ANY)


def near(x):
    return pltpu.with_memory_space_constraint(x, pltpu.VMEM)


def far(x):
    return pltpu.with_memory_space_constraint(x, pltpu.HBM)


def call(
    kernel, outs, in_specs, scratch=(), out_spec=VMEM, flops=1 << 26, moved=1 << 21, aliases=()
):
    return pl.pallas_call(
        kernel,
        out_shape=outs,
        in_specs=in_specs,
        out_specs=jax.tree.map(lambda _: out_spec, outs),
        scratch_shapes=list(scratch),
        input_output_aliases=dict(aliases),
        compiler_params=pltpu.CompilerParams(vmem_limit_bytes=VMEM_BYTES),
        cost_estimate=pl.CostEstimate(flops=flops, bytes_accessed=moved, transcendentals=0),
    )


def local(
    q_rows,
    k_rows,
    v_rows,
    z_rows,
    a_rows,
    b_rows,
    conv_q,
    conv_k,
    conv_v,
    a_log,
    dt_bias,
    norm_gain,
):
    shards, subs, heads_axis = (lax.axis_size(a) for a in ("half", "sub", "head"))
    peers, tokens = subs * heads_axis, q_rows.shape[0]
    total = peers * tokens
    spans = total // SPAN
    group = ("sub", "head")
    route = [(i, i + 1) for i in range(shards - 1)]
    conv_q, conv_k, conv_v = near(conv_q), near(conv_k), near(conv_v)
    gain = near(norm_gain.reshape(1, DV))
    a_log, dt_bias = near(a_log.reshape(1, -1)), near(dt_bias.reshape(1, -1))
    inputs = [far(x) for x in (q_rows, k_rows, v_rows, a_rows.T, b_rows.T)]
    packed = call(
        functools.partial(pack_kernel, heads_axis),
        pltpu.VMEM((peers, GATES + 4 * tokens, 128), BF16),
        [ANY] * 5,
        [pltpu.VMEM(x.shape, BF16) for x in inputs] + [pltpu.SemaphoreType.DMA((5,))],
        flops=1 << 20,
    )(*inputs)
    blocks = near(lax.all_to_all(packed, group, 0, 0, tiled=True))
    key_shapes = (pltpu.VMEM((total, DK), BF16), pltpu.VMEM((spans, DK, SPAN), BF16))
    system_shapes = (
        pltpu.VMEM((2, spans, 2, SPAN, SPAN), BF16),
        pltpu.VMEM((2, spans, SUB, SPAN), F32),
    )
    decay_shapes = (
        pltpu.VMEM((SPAN, DK), F32),
        pltpu.VMEM((2, total, SPAN), BF16),
        pltpu.VMEM((SPAN, SPAN), F32),
    )
    map_shapes = (
        pltpu.VMEM((2, spans, 2, SPAN, SPAN), BF16),
        pltpu.VMEM((2, spans, DK, DK), BF16),
    )
    opened = call(
        opening_kernel,
        (
            pltpu.VMEM((2 * DK + 16, 128), BF16),
            *key_shapes,
            *decay_shapes,
            *map_shapes,
            pltpu.VMEM((2, total, DV), BF16),
            pltpu.VMEM((2, spans, 2 * DK, DV), BF16),
            pltpu.VMEM((2, spans, DK, DV), F32),
        ),
        [VMEM] * 7,
        [
            pltpu.VMEM((8 + total, DK), F32),
            pltpu.VMEM((8 + total, 2 * DV), F32),
            *system_shapes,
        ],
        flops=1 << 32,
    )(blocks, conv_k, conv_v, a_log, dt_bias, conv_q, gain)
    hop = opened[0]
    entering = near(lax.ppermute(hop, "half", route))
    hop, keys, keys_t, ends, within, cols, inverses, lins, values, starts, adds = (
        near(x) for x in opened
    )
    first_out = call(
        first_outputs_kernel,
        pltpu.VMEM((2, total, DV), F32),
        [VMEM] * 12,
        [pltpu.VMEM((8 + total, DK), F32)],
        flops=1 << 32,
    )(
        blocks,
        conv_q,
        keys,
        keys_t,
        inverses,
        lins,
        ends,
        within,
        cols,
        values,
        starts,
        adds,
    )
    made = call(
        systems_kernel,
        (*key_shapes, *system_shapes, *decay_shapes, pltpu.VMEM((8, SPAN), F32)),
        [VMEM] * 5,
        [pltpu.VMEM((8 + total, DK), F32)],
        flops=1 << 32,
    )(hop, blocks, conv_k, a_log, dt_bias)
    keys, keys_t, systems, small, ends, within, cols, early = (near(x) for x in made)
    later_solved = call(inverse_kernel, map_shapes, [VMEM] * 6, flops=1 << 32)(
        hop, keys, keys_t, systems, small, cols
    )
    later_inverses, later_lins = (near(x) for x in later_solved)
    read_on = [pltpu.VMEM((2, DK, 2 * DV), F32)] if shards > 2 else []
    later_values, states, *last = call(
        states_kernel,
        (
            pltpu.VMEM((2, total, DV), BF16),
            pltpu.VMEM((2, 2, spans, 2 * DK, DV), BF16),
            *read_on,
        ),
        [VMEM] * 7,
        [pltpu.VMEM((8 + total, 2 * DV), F32)],
        flops=1 << 32,
    )(blocks, conv_v, keys_t, later_inverses, later_lins, ends, cols)
    out_a, out_m = call(
        later_outputs_kernel,
        (pltpu.VMEM((2, total, DV), F32), pltpu.VMEM((2, total, DV), BF16)),
        [VMEM] * 9,
        [pltpu.VMEM((8 + total, DK), F32)],
        flops=1 << 32,
    )(
        blocks,
        conv_q,
        keys,
        keys_t,
        later_inverses,
        within,
        cols,
        near(later_values),
        near(states),
    )
    for _ in range(shards - 2):
        moved = call(
            advance_kernel,
            pltpu.VMEM(hop.shape, BF16),
            [VMEM] * 8,
            [pltpu.VMEM((32, 512), F32)],
        )(entering, blocks, early, conv_q, conv_k, conv_v, hop, near(last[0]))
        entering = near(lax.ppermute(moved, "half", route))
    normed_shape = pltpu.VMEM((peers, 2 * tokens, DV), BF16)
    first_normed = call(first_finish_kernel, normed_shape, [VMEM] * 2, flops=1 << 30)(
        gain, near(first_out)
    )
    normed = call(
        later_finish_kernel,
        normed_shape,
        [VMEM] * 10,
        [pltpu.VMEM((32, 512), F32)],
        aliases=((0, 0),),
    )(
        near(first_normed),
        entering,
        blocks,
        early,
        conv_q,
        conv_k,
        conv_v,
        gain,
        near(out_a),
        near(out_m),
    )
    returned = near(lax.all_to_all(normed, group, 0, 0, tiled=True))
    return call(
        functools.partial(gate_kernel, heads_axis),
        jax.ShapeDtypeStruct(z_rows.shape, BF16),
        [VMEM] * 2,
        [pltpu.VMEM(z_rows.shape, BF16), pltpu.SemaphoreType.DMA((heads_axis,))],
        ANY,
    )(returned, z_rows)


def solution(mesh):
    heads_axis = mesh.shape["head"]
    subs = KH // heads_axis
    regrouped = Mesh(
        mesh.devices.reshape(mesh.shape["ctx"] // subs, subs, heads_axis), ("half", "sub", "head")
    )
    row = P(("half", "sub", "head"), None)
    placed = (row,) * 6 + (P(None, "head"),) * 3 + (P("head"),) * 2 + (P(),)
    return jax.shard_map(local, mesh=regrouped, in_specs=placed, out_specs=row, check_vma=False)
```
